32 devices in a mesh: seq: 4 (over x, core), shard: 8 (over z, y).
Axes of the slice: x: 2, y: 2, z: 4, core: 2. Of those that a mesh axis runs over, the one named last changes fastest.
Arguments:
- latents: bfloat16 [8, 1024, 768], P('shard', 'seq'), may hold values from -6 to 6
- cotangent: bfloat16 [8, 1024, 768], P('shard', 'seq'), may hold values from -6 to 6
- class_labels: int32 [8], replicated, may hold values from 0 to 999
- time_buckets: int32 [8], replicated, may hold values from 0 to 999
- class_table: bfloat16 [1000, 768], replicated, may hold values from -5 to 5
- time_table: bfloat16 [1000, 768], replicated, may hold values from -5 to 5
- ada_weight: float32 [768, 4608], P('shard'), may hold values from -0.21875 to 0.21875
- qkv_weight: float32 [768, 2304], P('shard'), may hold values from -0.21875 to 0.21875
- out_weight: float32 [768, 768], P('shard'), may hold values from -1 to 1
- up_weight: float32 [768, 3072], P('shard'), may hold values from -0.21875 to 0.21875
- down_weight: float32 [3072, 768], P('shard'), may hold values from -0.109375 to 0.109375
- biases: float32 [14, 768], P(None, 'shard'), may hold values from -0.5 to 0.5
- ada_first: float32 [768, 4608], P('shard'), may hold values from -80 to 80
- qkv_first: float32 [768, 2304], P('shard'), may hold values from -256 to 256
- out_first: float32 [768, 768], P('shard'), may hold values from -16 to 16
- up_first: float32 [768, 3072], P('shard'), may hold values from -32 to 32
- down_first: float32 [3072, 768], P('shard'), may hold values from -64 to 64
- bias_first: float32 [14, 768], P(None, 'shard'), may hold values from -64 to 64
- ada_second: float32 [768, 4608], P('shard'), may hold values from 18.432 to 73.728
- qkv_second: float32 [768, 2304], P('shard'), may hold values from 131.072 to 524.288
- out_second: float32 [768, 768], P('shard'), may hold values from 0.73728 to 2.94912
- up_second: float32 [768, 3072], P('shard'), may hold values from 2.048 to 8.192
- down_second: float32 [3072, 768], P('shard'), may hold values from 8.192 to 32.768
- bias_second: float32 [14, 768], P(None, 'shard'), may hold values from 8.192 to 32.768
Outputs:
- block_out: bfloat16 [8, 1024, 768], P('shard', 'seq')
- latents_grad: float32 [8, 1024, 768], P('shard', 'seq')
- class_grad: float32 [1000, 768], P(None, 'shard')
- time_grad: float32 [1000, 768], P(None, 'shard')
- ada_new: float32 [768, 4608], P('shard')
- qkv_new: float32 [768, 2304], P('shard')
- out_new: float32 [768, 768], P('shard')
- up_new: float32 [768, 3072], P('shard')
- down_new: float32 [3072, 768], P('shard')
- bias_new: float32 [14, 768], P(None, 'shard')
- ada_first_new: float32 [768, 4608], P('shard')
- qkv_first_new: float32 [768, 2304], P('shard')
- out_first_new: float32 [768, 768], P('shard')
- up_first_new: float32 [768, 3072], P('shard')
- down_first_new: float32 [3072, 768], P('shard')
- bias_first_new: float32 [14, 768], P(None, 'shard')
- ada_second_new: float32 [768, 4608], P('shard')
- qkv_second_new: float32 [768, 2304], P('shard')
- out_second_new: float32 [768, 768], P('shard')
- up_second_new: float32 [768, 3072], P('shard')
- down_second_new: float32 [3072, 768], P('shard')
- bias_second_new: float32 [14, 768], P(None, 'shard')
The draws below stay inside these ranges and needn't reach their ends.
All inputs are finite; a program needn't handle non-finite values.
Results may differ from the reference program's by a relative error of at most 0.013.
The reference program's roundings to bfloat16 on the way count: a program that leaves them out, or rounds other values in their place, can miss the bound.
Values may be sent and summed in bfloat16 or wider, within the bound.
No kernel may reach another device: no remote copies, remote signals or barrier semaphores. Data moves between devices by JAX's collectives and lax.ppermute only.
A program may use at most 192 MiB of HBM per device.

```python
import math
import jax
import jax.numpy as jnp
from jax import lax

D = 768
HEADS = 12
FF = 3072
NCLASS = 1000
NSTEPS = 1000
TOK_LAT = 1024
ADAM_STEP = 10
LATENTS = 8


def plant(drawn, own_key, least, largest):
    shape = drawn.shape
    index_at = [jax.random.randint(jax.random.fold_in(own_key, axis), (), 0, shape[axis]) for axis in range(len(shape))]
    drawn = drawn.at[tuple(index_at)].set(least)
    longest = shape.index(max(shape))
    index_at[longest] = (index_at[longest] + 1) % shape[longest]
    return drawn.at[tuple(index_at)].set(largest)


def shard_levels(stream_key, shape, split, least, largest):
    level, own = 1.0, jax.random.fold_in(stream_key, 6)
    for dim, blocks in split:
        draws = jnp.exp(jax.random.uniform(jax.random.fold_in(own, dim), (blocks,), jnp.float32, least / len(split), largest / len(split)))
        level = level * jnp.repeat(draws, shape[dim] // blocks).reshape([-1 if axis == dim else 1 for axis in range(len(shape))])
    return level


def normal_values(own_key, shape, deviation, most, cuts=(), kind=jnp.bfloat16):
    entries = deviation * jax.random.normal(own_key, shape, jnp.float32)
    if cuts:
        entries = entries * shard_levels(own_key, shape, cuts, -0.22, 0.18)
    return jnp.clip(entries, -most, most).astype(kind)


def setup_inputs(seed: int = 0) -> dict:
    key_list = jax.random.split(jax.random.key(seed), 25)
    latents = normal_values(key_list[0], (LATENTS, TOK_LAT, D), 1.0, 6.0, ((0, 8), (1, 4)))
    cotangent = normal_values(key_list[1], (LATENTS, TOK_LAT, D), 1.0, 6.0, ((0, 8), (1, 4)))
    class_labels = plant(jax.random.randint(key_list[2], (LATENTS,), 0, NCLASS), jax.random.fold_in(key_list[2], 1), 0, NCLASS - 1).astype(jnp.int32)
    time_buckets = plant(jax.random.randint(key_list[3], (LATENTS,), 0, NSTEPS), jax.random.fold_in(key_list[3], 1), 0, NSTEPS - 1).astype(jnp.int32)
    class_table = normal_values(key_list[4], (NCLASS, D), 1.0, 5.0)
    time_table = normal_values(key_list[5], (NSTEPS, D), 1.0, 5.0)
    ada_weight = normal_values(key_list[6], (D, 6 * D), D ** -0.5, 0.21875, ((0, 8),), jnp.float32)
    qkv_weight = normal_values(key_list[7], (D, 3 * D), D ** -0.5, 0.21875, ((0, 8),), jnp.float32)
    out_weight = normal_values(key_list[8], (D, D), (D // 24) ** -0.5, 1.0, ((0, 8),), jnp.float32)
    up_weight = normal_values(key_list[9], (D, FF), D ** -0.5, 0.21875, ((0, 8),), jnp.float32)
    down_weight = normal_values(key_list[10], (FF, D), FF ** -0.5, 0.109375, ((0, 8),), jnp.float32)
    biases = normal_values(key_list[11], (14, D), 0.1, 0.5, ((1, 8),), jnp.float32)
    ada_first = normal_values(key_list[12], (D, 6 * D), (0.16 * (LATENTS * TOK_LAT) ** 0.5), 80.0, ((0, 8),), jnp.float32)
    qkv_first = normal_values(key_list[13], (D, 3 * D), (0.44 * (LATENTS * TOK_LAT) ** 0.5), 256.0, ((0, 8),), jnp.float32)
    out_first = normal_values(key_list[14], (D, D), (0.033 * (LATENTS * TOK_LAT) ** 0.5), 16.0, ((0, 8),), jnp.float32)
    up_first = normal_values(key_list[15], (D, FF), (0.055 * (LATENTS * TOK_LAT) ** 0.5), 32.0, ((0, 8),), jnp.float32)
    down_first = normal_values(key_list[16], (FF, D), (0.11 * (LATENTS * TOK_LAT) ** 0.5), 64.0, ((0, 8),), jnp.float32)
    bias_first = normal_values(key_list[17], (14, D), (0.11 * (LATENTS * TOK_LAT) ** 0.5), 64.0, ((1, 8),), jnp.float32)
    ada_second = jnp.clip(jnp.exp(math.log(73.728) - 1.3862944 * jax.random.uniform(key_list[18], (D, 6 * D), jnp.float32) ** shard_levels(key_list[18], (D, 6 * D), ((0, 8),), -0.2, 0.2)), 18.432, 73.728)
    qkv_second = jnp.clip(jnp.exp(math.log(524.288) - 1.3862944 * jax.random.uniform(key_list[19], (D, 3 * D), jnp.float32) ** shard_levels(key_list[19], (D, 3 * D), ((0, 8),), -0.2, 0.2)), 131.072, 524.288)
    out_second = jnp.clip(jnp.exp(math.log(2.94912) - 1.3862944 * jax.random.uniform(key_list[20], (D, D), jnp.float32) ** shard_levels(key_list[20], (D, D), ((0, 8),), -0.2, 0.2)), 0.73728, 2.94912)
    up_second = jnp.clip(jnp.exp(math.log(8.192) - 1.3862944 * jax.random.uniform(key_list[21], (D, FF), jnp.float32) ** shard_levels(key_list[21], (D, FF), ((0, 8),), -0.2, 0.2)), 2.048, 8.192)
    down_second = jnp.clip(jnp.exp(math.log(32.768) - 1.3862944 * jax.random.uniform(key_list[22], (FF, D), jnp.float32) ** shard_levels(key_list[22], (FF, D), ((0, 8),), -0.2, 0.2)), 8.192, 32.768)
    bias_second = jnp.clip(jnp.exp(math.log(32.768) - 1.3862944 * jax.random.uniform(key_list[23], (14, D), jnp.float32) ** shard_levels(key_list[23], (14, D), ((1, 8),), -0.2, 0.2)), 8.192, 32.768)
    return {"latents": latents, "cotangent": cotangent, "class_labels": class_labels, "time_buckets": time_buckets, "class_table": class_table, "time_table": time_table, "ada_weight": ada_weight, "qkv_weight": qkv_weight, "out_weight": out_weight, "up_weight": up_weight, "down_weight": down_weight, "biases": biases, "ada_first": ada_first, "qkv_first": qkv_first, "out_first": out_first, "up_first": up_first, "down_first": down_first, "bias_first": bias_first, "ada_second": ada_second, "qkv_second": qkv_second, "out_second": out_second, "up_second": up_second, "down_second": down_second, "bias_second": bias_second}


norm_eps = 1e-06
beta_one = 0.9
beta_two = 0.999
learn_rate = 0.05
adam_eps = 1e-08
per_group = 2
highest = lax.Precision.HIGHEST

@jax.custom_vjp
def low(v):
    return lax.optimization_barrier(v.astype(jnp.bfloat16)).astype(jnp.float32)

@jax.custom_vjp
def low_back(v):
    return v

def low_keep(v):
    return (low(v), None)

def low_pass(kept, grad):
    return (grad,)

def back_keep(v):
    return (v, None)

def back_low(kept, grad):
    return (low(grad),)
low.defvjp(low_keep, low_pass)
low_back.defvjp(back_keep, back_low)

def layer_norm(values_in):
    centred = values_in - lax.optimization_barrier(jnp.mean(values_in, -1, keepdims=True))
    return centred * lax.rsqrt(lax.optimization_barrier(jnp.mean(centred * centred, -1, keepdims=True)) + norm_eps)

def block(stream, mod_rows, qkv_w, out_w, up_w, down_w, bias_low):
    model_width = stream.shape[-1]
    head_dim = model_width // HEADS
    pieces = [mod_rows[:, slot][:, None, :] for slot in range(6)]
    shift_a, scale_a, gate_a, shift_m, scale_m, gate_m = pieces
    modulated_a = low(layer_norm(stream) * (1.0 + scale_a) + shift_a)
    projected = jnp.einsum('bsd,de->bse', modulated_a, qkv_w, precision=highest)
    queries = low_back(low(projected[..., :model_width] + bias_low[6]))
    keys = low_back(low(projected[..., model_width:2 * model_width]))
    values = low_back(low(projected[..., 2 * model_width:] + bias_low[7]))
    head_shape = stream.shape[:2] + (HEADS, head_dim)
    queries = queries.reshape(head_shape)
    keys = keys.reshape(head_shape)
    values = values.reshape(head_shape)
    scores = low_back(jnp.einsum('bqhe,bkhe->bhqk', queries, keys, precision=highest) * head_dim ** (-0.5))
    probs = low(jax.nn.softmax(scores, axis=-1))
    attended = low_back(low(jnp.einsum('bhqk,bkhe->bqhe', probs, values, precision=highest)))
    attended = attended.reshape(stream.shape)
    branch_a = low_back(jnp.einsum('bsd,de->bse', attended, out_w, precision=highest) + bias_low[8])
    residual = stream + gate_a * branch_a
    modulated_m = low(layer_norm(residual) * (1.0 + scale_m) + shift_m)
    hidden = low_back(jnp.einsum('bsd,df->bsf', modulated_m, up_w, precision=highest) + bias_low[9:13].reshape(-1))
    activated = low(jax.nn.gelu(hidden, approximate=True))
    branch_m = low_back(jnp.einsum('bsf,fd->bsd', activated, down_w, precision=highest) + bias_low[13])
    return residual + gate_m * branch_m

def forward(stream, class_table, time_table, ada_weight, qkv_weight, out_weight, up_weight, down_weight, biases, class_labels, time_buckets):
    model_width = stream.shape[-1]
    bias_low = low(biases)
    cond = class_table[class_labels] + time_table[time_buckets]
    silu_cond = low(jax.nn.silu(cond))
    modulation = jnp.dot(silu_cond, low(ada_weight), precision=highest) + bias_low[0:6].reshape(6 * model_width)
    modulation = low_back(modulation).reshape(-1, 6, model_width)
    weights = (low(qkv_weight), low(out_weight), low(up_weight), low(down_weight))
    groups = stream.shape[0] // per_group
    grouped = stream.reshape((groups, per_group) + stream.shape[1:])
    mod_grouped = modulation.reshape(groups, per_group, 6, model_width)
    step_fn = jax.checkpoint(block)

    def run(carry, pieces):
        return (carry, step_fn(pieces[0], pieces[1], weights[0], weights[1], weights[2], weights[3], bias_low))
    _, outs = lax.scan(run, jnp.zeros((), jnp.float32), (grouped, mod_grouped))
    return outs.reshape(stream.shape)

def adam_step(weight, first, second, grad):
    first_new = beta_one * first + (1.0 - beta_one) * grad
    second_new = beta_two * second + (1.0 - beta_two) * grad * grad
    corr_one = 1.0 - beta_one ** ADAM_STEP
    corr_two = 1.0 - beta_two ** ADAM_STEP
    weight_new = weight - learn_rate * (first_new / corr_one) / (jnp.sqrt(second_new / corr_two) + adam_eps)
    return (weight_new, first_new, second_new)

def reference(latents, cotangent, class_labels, time_buckets, class_table, time_table, ada_weight, qkv_weight, out_weight, up_weight, down_weight, biases, ada_first, qkv_first, out_first, up_first, down_first, bias_first, ada_second, qkv_second, out_second, up_second, down_second, bias_second):
    primals = (latents.astype(jnp.float32), class_table.astype(jnp.float32), time_table.astype(jnp.float32), ada_weight, qkv_weight, out_weight, up_weight, down_weight, biases)

    def wrapped(*args):
        return forward(*args, class_labels, time_buckets)
    result, pull = jax.vjp(wrapped, *primals)
    grads = pull(cotangent.astype(jnp.float32))
    params = (ada_weight, qkv_weight, out_weight, up_weight, down_weight, biases)
    firsts = (ada_first, qkv_first, out_first, up_first, down_first, bias_first)
    seconds = (ada_second, qkv_second, out_second, up_second, down_second, bias_second)
    updates = [adam_step(params[slot], firsts[slot], seconds[slot], grads[3 + slot]) for slot in range(6)]
    return (result.astype(jnp.bfloat16), grads[0], grads[1], grads[2], updates[0][0], updates[1][0], updates[2][0], updates[3][0], updates[4][0], updates[5][0], updates[0][1], updates[1][1], updates[2][1], updates[3][1], updates[4][1], updates[5][1], updates[0][2], updates[1][2], updates[2][2], updates[3][2], updates[4][2], updates[5][2])
```

```python
from functools import partial

import jax
import jax.numpy as jnp
from jax import lax
from jax.sharding import PartitionSpec as P

HEADS = 12
ADAM_STEP = 10


norm_eps = 1e-06
beta_one = 0.9
beta_two = 0.999
learn_rate = 0.05
adam_eps = 1e-08

low_type = jnp.bfloat16
full_type = jnp.float32


def layer_norm(values_in):
    centred = values_in - jnp.mean(values_in, -1, keepdims=True)
    inverse = lax.rsqrt(jnp.mean(centred * centred, -1, keepdims=True) + norm_eps)
    return (centred * inverse, inverse)


def norm_back(gradient, normed, inverse):
    return inverse * (
        gradient
        - jnp.mean(gradient, -1, keepdims=True)
        - normed * jnp.mean(gradient * normed, -1, keepdims=True)
    )


def dot(left, right, dims):
    return lax.dot_general(left, right, (dims, ((), ())), preferred_element_type=full_type)


def mm(left, right):
    return dot(left, right, ((1,), (0,)))


def mm_nt(left, right):
    return dot(left, right, ((1,), (1,)))


def mm_tn(left, right):
    return dot(left, right, ((0,), (0,)))


def attend_forward(queries, keys, values, score_scale):
    scores = (
        jnp.einsum("hqe,hke->hqk", queries, keys, preferred_element_type=full_type) * score_scale
    )
    row_max = jnp.max(scores, -1, keepdims=True)
    expo_scores = jnp.exp(scores - row_max)
    row_total = jnp.sum(expo_scores, -1, keepdims=True)
    probs_low = (expo_scores / row_total).astype(low_type)
    result = jnp.einsum("hqk,hke->hqe", probs_low, values, preferred_element_type=full_type)
    return (result.astype(low_type), row_max + jnp.log(row_total))


def attend_backward(queries, keys, values, log_total, grad_out, score_scale):
    scores = (
        jnp.einsum("hqe,hke->hqk", queries, keys, preferred_element_type=full_type) * score_scale
    )
    probs_full = jnp.exp(scores - log_total)
    probs_low = probs_full.astype(low_type)
    grad_values = jnp.einsum("hqk,hqe->hke", probs_low, grad_out, preferred_element_type=full_type)
    grad_probs = jnp.einsum("hqe,hke->hqk", grad_out, values, preferred_element_type=full_type)
    grad_scores = probs_full * (grad_probs - jnp.sum(probs_full * grad_probs, -1, keepdims=True))
    grad_scores = grad_scores.astype(low_type)
    grad_queries = (
        jnp.einsum("hqk,hke->hqe", grad_scores, keys, preferred_element_type=full_type)
        * score_scale
    )
    grad_keys = (
        jnp.einsum("hqk,hqe->hke", grad_scores, queries, preferred_element_type=full_type)
        * score_scale
    )
    return (
        grad_queries.astype(low_type),
        grad_keys.astype(low_type),
        grad_values.astype(low_type),
    )


def adam_step(weight, first, second, grad):
    first_new = beta_one * first + (1.0 - beta_one) * grad
    second_new = beta_two * second + (1.0 - beta_two) * grad * grad
    corr_one = 1.0 - beta_one**ADAM_STEP
    corr_two = 1.0 - beta_two**ADAM_STEP
    weight_new = weight - learn_rate * (first_new / corr_one) / (
        jnp.sqrt(second_new / corr_two) + adam_eps
    )
    return (weight_new, first_new, second_new)


def swap(value, distance):
    return lax.ppermute(value, "seq", [(p, p ^ distance) for p in range(4)])


def gather_rel(value):
    far = swap(value, 2)
    near = swap(value, 1)
    cross = swap(far, 1)
    return [value, near, far, cross]


def scatter_rel(blocks):
    near_own = swap(blocks[1].astype(low_type), 1)
    near_far = swap(blocks[3].astype(low_type), 1)
    far = blocks[2] + near_far.astype(full_type)
    far_own = swap(far.astype(low_type), 2)
    return blocks[0] + near_own.astype(full_type) + far_own.astype(full_type)


def split_rows(value):
    return [value[r * value.shape[0] // 4 : (r + 1) * value.shape[0] // 4] for r in range(4)]


def reorder(blocks, own):
    stacked = jnp.stack(blocks)
    return jnp.concatenate(
        [lax.dynamic_index_in_dim(stacked, own ^ j, 0, keepdims=True) for j in range(4)]
    )


def token_sum(tensor):
    return jnp.sum(tensor.astype(full_type), axis=0)


def shards(
    latents,
    cotangent,
    class_labels,
    time_buckets,
    class_table,
    time_table,
    ada_weight,
    qkv_weight,
    out_weight,
    up_weight,
    down_weight,
    biases,
    ada_first,
    qkv_first,
    out_first,
    up_first,
    down_first,
    bias_first,
    ada_second,
    qkv_second,
    out_second,
    up_second,
    down_second,
    bias_second,
    n_shard,
    n_seq,
):
    assert n_seq == 4 and latents.shape[0] == 1 and class_labels.shape[0] == n_shard
    s_own = lax.axis_index("shard")
    q_own = lax.axis_index("seq")
    tok_dev, width = latents.shape[1:]
    head_dim = width // HEADS
    score_scale = head_dim ** (-0.5)
    heads_own = HEADS // n_seq
    feats = heads_own * head_dim
    rows = ada_weight.shape[0]
    ff = up_weight.shape[1]
    ff_cell = ff // (n_shard * n_seq)
    ff_own = ff // n_seq

    qkv_part = lax.dynamic_index_in_dim(
        qkv_weight.reshape(rows, 3, n_seq, feats), q_own, 2, keepdims=False
    )
    qkv_q = lax.all_gather(
        qkv_part.reshape(rows, 3 * feats).astype(low_type), "shard", axis=0, tiled=True
    )
    out_part = lax.dynamic_slice_in_dim(out_weight, q_own * feats, feats, 1).astype(low_type)
    out_q = lax.all_gather(out_part, "shard", axis=0, tiled=True)
    up_part = lax.dynamic_index_in_dim(
        up_weight.reshape(rows, n_shard, n_seq, ff_cell), q_own, 2, keepdims=False
    )
    up_q = lax.all_gather(
        up_part.reshape(rows, ff_own).astype(low_type), "shard", axis=0, tiled=True
    )
    down_part = lax.dynamic_slice_in_dim(down_weight, q_own * ff_cell, ff_cell, 0)
    down_q = lax.all_gather(down_part.astype(low_type), "shard", axis=0, tiled=True)

    cond = jnp.take(class_table, class_labels, axis=0).astype(full_type) + jnp.take(
        time_table, time_buckets, axis=0
    ).astype(full_type)
    cond_cols = lax.dynamic_slice_in_dim(cond, s_own * rows, rows, 1)
    silu_cols = jax.nn.silu(cond_cols).astype(low_type)
    ada_low = ada_weight.astype(low_type)
    mod_partial = mm(silu_cols, ada_low)
    bias_low = biases.astype(low_type).astype(full_type).reshape(1, -1)
    payload = jnp.concatenate(
        [mod_partial, jnp.broadcast_to(bias_low, (n_shard, bias_low.shape[1]))], 1
    )
    arrived = lax.all_to_all(payload, "shard", split_axis=0, concat_axis=0, tiled=True)
    mod_sum = jnp.sum(arrived[:, : 6 * width], 0)
    bias_full = jnp.transpose(
        arrived[:, 6 * width :].reshape(n_shard, biases.shape[0], rows), (1, 0, 2)
    ).reshape(biases.shape[0], width)
    modulation = mod_sum.reshape(6, width) + bias_full[0:6]
    shift_a, scale_a, gate_a, shift_m, scale_m, gate_m = [modulation[i] for i in range(6)]

    stream = jnp.concatenate(gather_rel(latents[0])).astype(full_type)
    grad_y = jnp.concatenate(gather_rel(cotangent[0])).astype(full_type)

    out_rel = jnp.concatenate(gather_rel(out_q), 1)
    out_cols = reorder(jnp.split(out_rel, 4, 1), q_own)
    out_abs = jnp.transpose(out_cols, (1, 0, 2)).reshape(width, width)
    out_rows = out_abs.reshape(n_seq, feats, width)
    out_rel_rows = [
        lax.dynamic_index_in_dim(out_rows, q_own ^ r, 0, keepdims=False) for r in range(4)
    ]
    out_w = jnp.concatenate(out_rel_rows)
    out_own = out_rel_rows[0]

    normed_a, inverse_a = layer_norm(stream)
    modulated_a = (normed_a * (1.0 + scale_a) + shift_a).astype(low_type)
    projected = mm(modulated_a, qkv_q)
    bias_query = lax.dynamic_slice_in_dim(bias_full[6], q_own * feats, feats)
    bias_value = lax.dynamic_slice_in_dim(bias_full[7], q_own * feats, feats)
    queries = (projected[:, :feats] + bias_query).astype(low_type)
    keys = projected[:, feats : 2 * feats].astype(low_type)
    values = (projected[:, 2 * feats :] + bias_value).astype(low_type)
    n_tok = queries.shape[0]

    def by_head(value):
        return jnp.transpose(value.reshape(n_tok, heads_own, head_dim), (1, 0, 2))

    def by_token(value):
        return jnp.transpose(value, (1, 0, 2)).reshape(n_tok, feats)

    queries_h, keys_h, values_h = by_head(queries), by_head(keys), by_head(values)
    attended_h, log_total = attend_forward(queries_h, keys_h, values_h, score_scale)
    pieces = gather_rel(by_token(attended_h))
    ordered = []
    for d in range(4):
        blocks = split_rows(pieces[d])
        ordered.append(jnp.concatenate([blocks[d ^ r] for r in range(4)]))
    attended = jnp.concatenate(ordered, 1)

    branch_a = mm(attended, out_w) + bias_full[8]
    residual = stream + gate_a * branch_a
    normed_m, inverse_m = layer_norm(residual)
    modulated_m = (normed_m * (1.0 + scale_m) + shift_m).astype(low_type)
    bias_ff = lax.dynamic_index_in_dim(
        bias_full[9:13].reshape(n_shard, n_seq, ff_cell), q_own, 1, keepdims=False
    ).reshape(ff_own)
    hidden = mm(modulated_m, up_q) + bias_ff
    activated = jax.nn.gelu(hidden, approximate=True).astype(low_type)
    branch_part = mm(activated, down_q)
    branch_own = scatter_rel(split_rows(branch_part)) + bias_full[13]
    block_out = (residual[:tok_dev] + gate_m * branch_own).astype(low_type)
    grad_gate_m = token_sum(grad_y * branch_part) + token_sum(grad_y[:tok_dev]) * bias_full[13]

    grad_branch_m = (gate_m * grad_y).astype(low_type)
    grad_down = mm_tn(activated, grad_branch_m)
    grad_act = mm_nt(grad_branch_m, down_q)
    _, gelu_pull = jax.vjp(partial(jax.nn.gelu, approximate=True), hidden)
    grad_hidden = gelu_pull(grad_act)[0].astype(low_type)
    grad_up = mm_tn(modulated_m, grad_hidden)
    grad_mod_m = mm_nt(grad_hidden, up_q)
    grad_scale_m = token_sum(grad_mod_m * normed_m)
    grad_shift_m = token_sum(grad_mod_m)
    grad_mod_own = scatter_rel(split_rows(grad_mod_m))
    grad_residual = grad_y[:tok_dev] + norm_back(
        grad_mod_own * (1.0 + scale_m), normed_m[:tok_dev], inverse_m[:tok_dev]
    )
    grad_gate_a = token_sum(grad_residual * branch_a[:tok_dev])
    grad_branch_own = (gate_a * grad_residual).astype(low_type)
    grad_branch_a = jnp.concatenate(gather_rel(grad_branch_own))
    grad_out = mm_tn(attended, lax.dynamic_slice_in_dim(grad_branch_a, q_own * feats, feats, 1))
    grad_out = reorder(split_rows(grad_out), q_own).reshape(width, feats)
    grad_att = mm_nt(grad_branch_a, out_own).astype(low_type)

    grads_h = attend_backward(
        queries_h, keys_h, values_h, log_total, by_head(grad_att), score_scale
    )
    grad_qkv = jnp.concatenate([by_token(piece) for piece in grads_h], 1)
    grad_qkv_weight = mm_tn(modulated_a, grad_qkv)
    grad_mod_a = mm_nt(grad_qkv, qkv_q)
    grad_scale_a = token_sum(grad_mod_a * normed_a)
    grad_shift_a = token_sum(grad_mod_a)
    grad_mod_a_own = scatter_rel(split_rows(grad_mod_a))
    latents_grad = grad_residual + norm_back(
        grad_mod_a_own * (1.0 + scale_a), normed_a[:tok_dev], inverse_a[:tok_dev]
    )

    qkv_sums = token_sum(grad_qkv)
    small = jnp.concatenate(
        [
            grad_shift_a,
            grad_scale_a,
            grad_gate_a,
            grad_shift_m,
            grad_scale_m,
            grad_gate_m,
            qkv_sums[:feats],
            qkv_sums[2 * feats :],
            token_sum(grad_branch_own),
            token_sum(grad_hidden),
            token_sum(grad_branch_m[:tok_dev]),
        ]
    )
    every = lax.all_gather(small, ("shard", "seq"), axis=0).reshape(n_shard, n_seq, -1)
    grad_modulation = jnp.sum(every[:, :, : 6 * width], 1).astype(low_type)
    rest = jnp.sum(every[:, :, 6 * width :], 0)
    cuts = [feats, 2 * feats, 2 * feats + width, 2 * feats + width + ff_own]
    sum_query, sum_value, sum_out, sum_ff, sum_down = jnp.split(rest, cuts, 1)
    bias_ada = jnp.sum(grad_modulation.astype(full_type), 0).reshape(6, width)
    bias_grad_all = jnp.concatenate(
        [
            bias_ada,
            sum_query.reshape(1, width),
            sum_value.reshape(1, width),
            jnp.sum(sum_out, 0, keepdims=True),
            jnp.transpose(sum_ff.reshape(n_seq, n_shard, ff_cell), (1, 0, 2)).reshape(-1, width),
            jnp.sum(sum_down, 0, keepdims=True),
        ]
    )
    bias_grad = lax.dynamic_slice_in_dim(bias_grad_all, s_own * rows, rows, 1)
    grad_ada = mm_tn(silu_cols, grad_modulation)
    grad_silu = mm_nt(grad_modulation, ada_low)
    _, silu_pull = jax.vjp(jax.nn.silu, cond_cols)
    grad_cols = silu_pull(grad_silu)[0]

    def owned(gradient):
        return lax.psum_scatter(
            gradient.astype(low_type), "shard", scatter_dimension=0, tiled=True
        )

    down_grad = lax.all_gather(owned(grad_down), "seq", axis=0)
    up_grad = lax.all_gather(owned(grad_up), "seq", axis=0)
    out_grad = lax.all_gather(owned(grad_out), "seq", axis=0)
    qkv_grad = lax.all_gather(owned(grad_qkv_weight), "seq", axis=0)
    down_grad = down_grad.astype(full_type).reshape(n_seq * ff_cell, width)
    up_grad = jnp.transpose(
        up_grad.astype(full_type).reshape(n_seq, rows, n_shard, ff_cell), (1, 2, 0, 3)
    ).reshape(rows, ff)
    out_grad = jnp.transpose(out_grad.astype(full_type), (1, 0, 2)).reshape(rows, width)
    qkv_grad = jnp.transpose(
        qkv_grad.astype(full_type).reshape(n_seq, rows, 3, feats), (1, 2, 0, 3)
    ).reshape(rows, 3 * width)

    class_hot = (
        class_labels[:, None] == jnp.arange(class_table.shape[0], dtype=jnp.int32)[None, :]
    ).astype(full_type)
    time_hot = (
        time_buckets[:, None] == jnp.arange(time_table.shape[0], dtype=jnp.int32)[None, :]
    ).astype(full_type)
    class_grad = jnp.einsum("ln,lc->nc", class_hot, grad_cols, precision=lax.Precision.HIGHEST)
    time_grad = jnp.einsum("ln,lc->nc", time_hot, grad_cols, precision=lax.Precision.HIGHEST)
    updates = [
        adam_step(ada_weight, ada_first, ada_second, grad_ada),
        adam_step(qkv_weight, qkv_first, qkv_second, qkv_grad),
        adam_step(out_weight, out_first, out_second, out_grad),
        adam_step(up_weight, up_first, up_second, up_grad),
        adam_step(down_weight, down_first, down_second, down_grad),
        adam_step(biases, bias_first, bias_second, bias_grad),
    ]
    return (
        block_out[None],
        latents_grad[None],
        class_grad,
        time_grad,
        *[update[0] for update in updates],
        *[update[1] for update in updates],
        *[update[2] for update in updates],
    )


def solution(mesh):
    tokens = P("shard", "seq", None)
    rows = P("shard", None)
    cols = P(None, "shard")
    state = (rows, rows, rows, rows, rows, cols)
    return jax.shard_map(
        partial(shards, n_shard=mesh.shape["shard"], n_seq=mesh.shape["seq"]),
        mesh=mesh,
        in_specs=(tokens, tokens, P(), P(), P(), P()) + 3 * state,
        out_specs=(tokens, tokens, cols, cols) + 3 * state,
        check_vma=False,
    )
```

```python
from functools import partial

import jax
import jax.numpy as jnp
from jax import lax
from jax.experimental import pallas as pl
from jax.experimental.pallas import tpu as pltpu
from jax.sharding import PartitionSpec as P

HEADS = 12
ADAM_STEP = 10
BLOCK = 256


norm_eps = 1e-06
beta_one = 0.9
beta_two = 0.999
learn_rate = 0.05
adam_eps = 1e-08

low_type = jnp.bfloat16
full_type = jnp.float32


def layer_norm(values_in):
    centred = values_in - jnp.mean(values_in, -1, keepdims=True)
    inverse = lax.rsqrt(jnp.mean(centred * centred, -1, keepdims=True) + norm_eps)
    return (centred * inverse, inverse)


def norm_back(gradient, normed, inverse):
    return inverse * (
        gradient
        - jnp.mean(gradient, -1, keepdims=True)
        - normed * jnp.mean(gradient * normed, -1, keepdims=True)
    )


def dot(left, right, dims):
    return lax.dot_general(left, right, (dims, ((), ())), preferred_element_type=full_type)


def mm(left, right):
    return dot(left, right, ((1,), (0,)))


def mm_nt(left, right):
    return dot(left, right, ((1,), (1,)))


def mm_tn(left, right):
    return dot(left, right, ((0,), (0,)))


def attend_forward_kernel(heads, mod_ref, weight_ref, bias_ref, qkv_ref, att_ref, log_ref):
    n_tok = mod_ref.shape[0]
    feats = att_ref.shape[0]
    dim = feats // heads
    scale = dim ** (-0.5)
    projected = mm(mod_ref[...], weight_ref[...]) + bias_ref[...]
    qkv_ref[...] = projected.astype(low_type)
    log_ref[...] = jnp.zeros(log_ref.shape, full_type)

    def step(block, _):
        here = pl.ds(pl.multiple_of(block * BLOCK, BLOCK), BLOCK)
        for head in range(heads):
            queries = qkv_ref[here, head * dim : (head + 1) * dim] * scale
            keys = qkv_ref[:, feats + head * dim : feats + (head + 1) * dim]
            values = qkv_ref[:, 2 * feats + head * dim : 2 * feats + (head + 1) * dim]
            scores = mm_nt(queries.astype(low_type), keys)
            row_max = jnp.max(scores, -1, keepdims=True)
            expo = jnp.exp(scores - row_max)
            total = jnp.sum(expo, -1, keepdims=True)
            probs = (expo * (1.0 / total)).astype(low_type)
            att_ref[head * dim : (head + 1) * dim, here] = jnp.transpose(
                mm(probs, values)
            ).astype(low_type)
            logs = jnp.broadcast_to(row_max + jnp.log(total), (BLOCK, 128))
            log_ref[head : head + 1, here] = jnp.transpose(logs)[0:1]
        return 0

    lax.fori_loop(0, n_tok // BLOCK, step, 0)


def attend_backward_kernel(heads, qkv_ref, log_ref, grad_ref, out_ref, keys_t, sum_k, sum_v):
    n_tok = qkv_ref.shape[0]
    feats = grad_ref.shape[1]
    dim = feats // heads
    scale = dim ** (-0.5)
    keys_t[...] = jnp.transpose(qkv_ref[:, feats : 2 * feats])
    sum_k[...] = jnp.zeros(sum_k.shape, full_type)
    sum_v[...] = jnp.zeros(sum_v.shape, full_type)

    def step(block, _):
        here = pl.ds(pl.multiple_of(block * BLOCK, BLOCK), BLOCK)
        for head in range(heads):
            cut = slice(head * dim, (head + 1) * dim)
            queries = (qkv_ref[here, cut] * scale).astype(low_type)
            keys = qkv_ref[:, feats + head * dim : feats + (head + 1) * dim]
            values = qkv_ref[:, 2 * feats + head * dim : 2 * feats + (head + 1) * dim]
            grad = grad_ref[here, cut]
            probs = jnp.exp(mm_nt(keys, queries) - log_ref[head : head + 1, here])
            grad_probs = mm_nt(values, grad)
            delta = jnp.sum(probs * grad_probs, 0, keepdims=True)
            grad_scores = (probs * (grad_probs - delta)).astype(low_type)
            sum_v[:, cut] += mm(probs.astype(low_type), grad)
            sum_k[:, cut] += mm(grad_scores, queries)
            grad_q = mm(keys_t[cut, :], grad_scores) * scale
            out_ref[here, cut] = jnp.transpose(grad_q).astype(low_type)
        return 0

    lax.fori_loop(0, n_tok // BLOCK, step, 0)
    out_ref[:, feats : 2 * feats] = sum_k[...].astype(low_type)
    out_ref[:, 2 * feats :] = sum_v[...].astype(low_type)


def attend_forward(modulated, weight, bias, heads):
    n_tok = modulated.shape[0]
    feats = weight.shape[1] // 3
    return pl.pallas_call(
        partial(attend_forward_kernel, heads),
        out_shape=(
            jax.ShapeDtypeStruct((n_tok, 3 * feats), low_type),
            jax.ShapeDtypeStruct((feats, n_tok), low_type),
            jax.ShapeDtypeStruct((8, n_tok), full_type),
        ),
        compiler_params=pltpu.CompilerParams(vmem_limit_bytes=48 * 2**20),
        cost_estimate=pl.CostEstimate(
            flops=2 * n_tok * weight.size + 4 * n_tok * n_tok * feats,
            bytes_accessed=2 * (modulated.size + weight.size + 4 * n_tok * feats),
            transcendentals=heads * n_tok * n_tok,
        ),
        name="attend_forward",
    )(modulated, weight, bias)


def attend_backward(qkv, logs, grad_att, heads):
    n_tok, feats = grad_att.shape
    return pl.pallas_call(
        partial(attend_backward_kernel, heads),
        out_shape=jax.ShapeDtypeStruct((n_tok, 3 * feats), low_type),
        scratch_shapes=[
            pltpu.VMEM((feats, n_tok), low_type),
            pltpu.VMEM((n_tok, feats), full_type),
            pltpu.VMEM((n_tok, feats), full_type),
        ],
        compiler_params=pltpu.CompilerParams(vmem_limit_bytes=48 * 2**20),
        cost_estimate=pl.CostEstimate(
            flops=10 * n_tok * n_tok * feats,
            bytes_accessed=2 * 7 * n_tok * feats,
            transcendentals=heads * n_tok * n_tok,
        ),
        name="attend_backward",
    )(qkv, logs, grad_att)


def adam_step(weight, first, second, grad):
    first_new = beta_one * first + (1.0 - beta_one) * grad
    second_new = beta_two * second + (1.0 - beta_two) * grad * grad
    corr_one = 1.0 - beta_one**ADAM_STEP
    corr_two = 1.0 - beta_two**ADAM_STEP
    weight_new = weight - learn_rate * (first_new / corr_one) / (
        jnp.sqrt(second_new / corr_two) + adam_eps
    )
    return (weight_new, first_new, second_new)


def swap(value, distance):
    return lax.ppermute(value, "seq", [(p, p ^ distance) for p in range(4)])


def gather_rel(value):
    far = swap(value, 2)
    near = swap(value, 1)
    cross = swap(far, 1)
    return [value, near, far, cross]


def scatter_rel(blocks):
    near_own = swap(blocks[1].astype(low_type), 1)
    near_far = swap(blocks[3].astype(low_type), 1)
    far = blocks[2] + near_far.astype(full_type)
    far_own = swap(far.astype(low_type), 2)
    return blocks[0] + near_own.astype(full_type) + far_own.astype(full_type)


def split_rows(value):
    return [value[r * value.shape[0] // 4 : (r + 1) * value.shape[0] // 4] for r in range(4)]


def reorder(blocks, own):
    stacked = jnp.stack(blocks)
    return jnp.concatenate(
        [lax.dynamic_index_in_dim(stacked, own ^ j, 0, keepdims=True) for j in range(4)]
    )


def permute_blocks(value, distance):
    size = value.shape[1] // 4
    return jnp.concatenate(
        [value[:, (r ^ distance) * size : ((r ^ distance) + 1) * size] for r in range(4)], 1
    )


def spread(value, axis, count):
    return lax.all_to_all(
        jnp.broadcast_to(value[None], (count,) + value.shape), axis, 0, 0, tiled=True
    )


def owned(gradient, count):
    pieces = gradient.astype(low_type).reshape(count, -1, gradient.shape[-1])
    arrived = lax.all_to_all(pieces, "shard", 0, 0, tiled=True)
    return jnp.sum(arrived.astype(full_type), 0).astype(low_type)


def token_sum(tensor):
    return jnp.sum(tensor.astype(full_type), axis=0)


def shards(
    latents,
    cotangent,
    class_labels,
    time_buckets,
    class_table,
    time_table,
    ada_weight,
    qkv_weight,
    out_weight,
    up_weight,
    down_weight,
    biases,
    ada_first,
    qkv_first,
    out_first,
    up_first,
    down_first,
    bias_first,
    ada_second,
    qkv_second,
    out_second,
    up_second,
    down_second,
    bias_second,
    n_shard,
    n_seq,
):
    assert n_seq == 4 and latents.shape[0] == 1 and class_labels.shape[0] == n_shard
    s_own = lax.axis_index("shard")
    q_own = lax.axis_index("seq")
    tok_dev, width = latents.shape[1:]
    head_dim = width // HEADS
    score_scale = head_dim ** (-0.5)
    heads_own = HEADS // n_seq
    feats = heads_own * head_dim
    rows = ada_weight.shape[0]
    ff = up_weight.shape[1]
    ff_cell = ff // (n_shard * n_seq)
    ff_own = ff // n_seq

    qkv_part = lax.dynamic_index_in_dim(
        qkv_weight.reshape(rows, 3, n_seq, feats), q_own, 2, keepdims=False
    )
    qkv_q = spread(qkv_part.reshape(rows, 3 * feats).astype(low_type), "shard", n_shard)
    qkv_q = qkv_q.reshape(width, 3 * feats)
    out_part = lax.dynamic_slice_in_dim(out_weight, q_own * feats, feats, 1).astype(low_type)
    out_q = spread(out_part, "shard", n_shard).reshape(width, feats)
    up_part = lax.dynamic_index_in_dim(
        up_weight.reshape(rows, n_shard, n_seq, ff_cell), q_own, 2, keepdims=False
    )
    up_q = spread(up_part.reshape(rows, ff_own).astype(low_type), "shard", n_shard)
    up_q = up_q.reshape(width, ff_own)
    down_part = lax.dynamic_slice_in_dim(down_weight, q_own * ff_cell, ff_cell, 0)
    down_q = spread(down_part.astype(low_type), "shard", n_shard).reshape(ff_own, width)

    cond = jnp.take(class_table, class_labels, axis=0).astype(full_type) + jnp.take(
        time_table, time_buckets, axis=0
    ).astype(full_type)
    cond_cols = lax.dynamic_slice_in_dim(cond, s_own * rows, rows, 1)
    silu_cols = jax.nn.silu(cond_cols).astype(low_type)
    ada_low = ada_weight.astype(low_type)
    mod_partial = mm(silu_cols, ada_low)
    bias_low = biases.astype(low_type).astype(full_type).reshape(1, -1)
    payload = jnp.concatenate(
        [mod_partial, jnp.broadcast_to(bias_low, (n_shard, bias_low.shape[1]))], 1
    )
    arrived = lax.all_to_all(payload, "shard", split_axis=0, concat_axis=0, tiled=True)
    mod_sum = jnp.sum(arrived[:, : 6 * width], 0)
    bias_full = jnp.transpose(
        arrived[:, 6 * width :].reshape(n_shard, biases.shape[0], rows), (1, 0, 2)
    ).reshape(biases.shape[0], width)
    modulation = mod_sum.reshape(6, width) + bias_full[0:6]
    shift_a, scale_a, gate_a, shift_m, scale_m, gate_m = [modulation[i] for i in range(6)]

    stream = jnp.concatenate(gather_rel(latents[0])).astype(full_type)
    grad_y = jnp.concatenate(gather_rel(cotangent[0])).astype(full_type)

    out_cols = spread(out_q, "seq", n_seq)
    out_rows = jnp.transpose(out_cols, (1, 0, 2)).reshape(n_seq, feats, width)
    out_rel_rows = [
        lax.dynamic_index_in_dim(out_rows, q_own ^ r, 0, keepdims=False) for r in range(4)
    ]
    out_w = jnp.concatenate(out_rel_rows)
    out_own = out_rel_rows[0]

    normed_a, inverse_a = layer_norm(stream)
    modulated_a = (normed_a * (1.0 + scale_a) + shift_a).astype(low_type)
    bias_query = lax.dynamic_slice_in_dim(bias_full[6], q_own * feats, feats)
    bias_value = lax.dynamic_slice_in_dim(bias_full[7], q_own * feats, feats)
    bias_qkv = jnp.concatenate([bias_query, jnp.zeros_like(bias_query), bias_value])[None]
    qkv, att_own, logs = attend_forward(modulated_a, qkv_q, bias_qkv, heads_own)
    att_far = swap(permute_blocks(att_own, 2), 2)
    att_near = swap(permute_blocks(att_own, 1), 1)
    att_cross = swap(permute_blocks(att_far, 1), 1)
    attended = jnp.concatenate([att_own, att_near, att_far, att_cross])

    branch_a = mm_tn(attended, out_w) + bias_full[8]
    residual = stream + gate_a * branch_a
    normed_m, inverse_m = layer_norm(residual)
    modulated_m = (normed_m * (1.0 + scale_m) + shift_m).astype(low_type)
    bias_ff = lax.dynamic_index_in_dim(
        bias_full[9:13].reshape(n_shard, n_seq, ff_cell), q_own, 1, keepdims=False
    ).reshape(ff_own)
    hidden = mm(modulated_m, up_q) + bias_ff
    activated = jax.nn.gelu(hidden, approximate=True).astype(low_type)
    branch_part = mm(activated, down_q)
    branch_own = scatter_rel(split_rows(branch_part)) + bias_full[13]
    block_out = (residual[:tok_dev] + gate_m * branch_own).astype(low_type)
    grad_gate_m = token_sum(grad_y * branch_part) + token_sum(grad_y[:tok_dev]) * bias_full[13]

    grad_branch_m = (gate_m * grad_y).astype(low_type)
    grad_down = mm_tn(activated, grad_branch_m)
    grad_act = mm_nt(grad_branch_m, down_q)
    _, gelu_pull = jax.vjp(partial(jax.nn.gelu, approximate=True), hidden)
    grad_hidden = gelu_pull(grad_act)[0].astype(low_type)
    grad_up = mm_tn(modulated_m, grad_hidden)
    grad_mod_m = mm_nt(grad_hidden, up_q)
    grad_scale_m = token_sum(grad_mod_m * normed_m)
    grad_shift_m = token_sum(grad_mod_m)
    grad_mod_own = scatter_rel(split_rows(grad_mod_m))
    grad_residual = grad_y[:tok_dev] + norm_back(
        grad_mod_own * (1.0 + scale_m), normed_m[:tok_dev], inverse_m[:tok_dev]
    )
    grad_gate_a = token_sum(grad_residual * branch_a[:tok_dev])
    grad_branch_own = (gate_a * grad_residual).astype(low_type)
    grad_branch_a = jnp.concatenate(gather_rel(grad_branch_own))
    grad_out = mm(attended, lax.dynamic_slice_in_dim(grad_branch_a, q_own * feats, feats, 1))
    grad_out = reorder(split_rows(grad_out), q_own).reshape(width, feats)
    grad_att = mm_nt(grad_branch_a, out_own).astype(low_type)

    grad_qkv = attend_backward(qkv, logs, grad_att, heads_own)
    grad_qkv_weight = mm_tn(modulated_a, grad_qkv)
    grad_mod_a = mm_nt(grad_qkv, qkv_q)
    grad_scale_a = token_sum(grad_mod_a * normed_a)
    grad_shift_a = token_sum(grad_mod_a)
    grad_mod_a_own = scatter_rel(split_rows(grad_mod_a))
    latents_grad = grad_residual + norm_back(
        grad_mod_a_own * (1.0 + scale_a), normed_a[:tok_dev], inverse_a[:tok_dev]
    )

    def placed(own_part):
        whole = jnp.zeros((n_seq, own_part.shape[0]), full_type)
        return lax.dynamic_update_index_in_dim(whole, own_part, q_own, 0).reshape(-1)

    qkv_sums = token_sum(grad_qkv)
    small = jnp.concatenate(
        [
            grad_shift_a,
            grad_scale_a,
            grad_gate_a,
            grad_shift_m,
            grad_scale_m,
            grad_gate_m,
            placed(qkv_sums[:feats]),
            placed(qkv_sums[2 * feats :]),
            token_sum(grad_branch_own),
            placed(token_sum(grad_hidden)),
            token_sum(grad_branch_m[:tok_dev]),
        ]
    )
    small = small + swap(small, 1)
    small = small + swap(small, 2)
    every = spread(small, "shard", n_shard)
    grad_modulation = every[:, : 6 * width].astype(low_type)
    rest = jnp.sum(every[:, 6 * width :], 0)
    cuts = [width, 2 * width, 3 * width, 3 * width + ff]
    sum_query, sum_value, sum_out, sum_ff, sum_down = jnp.split(rest, cuts)
    bias_ada = jnp.sum(grad_modulation.astype(full_type), 0).reshape(6, width)
    bias_grad_all = jnp.concatenate(
        [
            bias_ada,
            sum_query.reshape(1, width),
            sum_value.reshape(1, width),
            sum_out[None],
            jnp.transpose(sum_ff.reshape(n_seq, n_shard, ff_cell), (1, 0, 2)).reshape(-1, width),
            sum_down[None],
        ]
    )
    bias_grad = lax.dynamic_slice_in_dim(bias_grad_all, s_own * rows, rows, 1)
    grad_ada = mm_tn(silu_cols, grad_modulation)
    grad_silu = mm_nt(grad_modulation, ada_low)
    _, silu_pull = jax.vjp(jax.nn.silu, cond_cols)
    grad_cols = silu_pull(grad_silu)[0]

    down_grad = spread(owned(grad_down, n_shard), "seq", n_seq)
    up_grad = spread(owned(grad_up, n_shard), "seq", n_seq)
    out_grad = spread(owned(grad_out, n_shard), "seq", n_seq)
    qkv_grad = spread(owned(grad_qkv_weight, n_shard), "seq", n_seq)
    down_grad = down_grad.astype(full_type).reshape(n_seq * ff_cell, width)
    up_grad = jnp.transpose(
        up_grad.astype(full_type).reshape(n_seq, rows, n_shard, ff_cell), (1, 2, 0, 3)
    ).reshape(rows, ff)
    out_grad = jnp.transpose(out_grad.astype(full_type), (1, 0, 2)).reshape(rows, width)
    qkv_grad = jnp.transpose(
        qkv_grad.astype(full_type).reshape(n_seq, rows, 3, feats), (1, 2, 0, 3)
    ).reshape(rows, 3 * width)

    class_hot = (
        class_labels[:, None] == jnp.arange(class_table.shape[0], dtype=jnp.int32)[None, :]
    ).astype(full_type)
    time_hot = (
        time_buckets[:, None] == jnp.arange(time_table.shape[0], dtype=jnp.int32)[None, :]
    ).astype(full_type)
    class_grad = jnp.einsum("ln,lc->nc", class_hot, grad_cols, precision=lax.Precision.HIGHEST)
    time_grad = jnp.einsum("ln,lc->nc", time_hot, grad_cols, precision=lax.Precision.HIGHEST)
    updates = [
        adam_step(ada_weight, ada_first, ada_second, grad_ada),
        adam_step(qkv_weight, qkv_first, qkv_second, qkv_grad),
        adam_step(out_weight, out_first, out_second, out_grad),
        adam_step(up_weight, up_first, up_second, up_grad),
        adam_step(down_weight, down_first, down_second, down_grad),
        adam_step(biases, bias_first, bias_second, bias_grad),
    ]
    return (
        block_out[None],
        latents_grad[None],
        class_grad,
        time_grad,
        *[update[0] for update in updates],
        *[update[1] for update in updates],
        *[update[2] for update in updates],
    )


def solution(mesh):
    tokens = P("shard", "seq", None)
    rows = P("shard", None)
    cols = P(None, "shard")
    state = (rows, rows, rows, rows, rows, cols)
    return jax.shard_map(
        partial(shards, n_shard=mesh.shape["shard"], n_seq=mesh.shape["seq"]),
        mesh=mesh,
        in_specs=(tokens, tokens, P(), P(), P(), P()) + 3 * state,
        out_specs=(tokens, tokens, cols, cols) + 3 * state,
        check_vma=False,
    )
```

```python
import math
from functools import partial

import jax
import jax.numpy as jnp
from jax import lax
from jax.experimental import pallas as pl
from jax.experimental.pallas import tpu as pltpu
from jax.sharding import PartitionSpec as P

HEADS = 12
ADAM_STEP = 10
BLOCK = 256


norm_eps = 1e-06
beta_one = 0.9
beta_two = 0.999
learn_rate = 0.05
adam_eps = 1e-08

low_type = jnp.bfloat16
full_type = jnp.float32


def layer_norm(values_in):
    centred = values_in - jnp.mean(values_in, -1, keepdims=True)
    inverse = lax.rsqrt(jnp.mean(centred * centred, -1, keepdims=True) + norm_eps)
    return (centred * inverse, inverse)


def norm_back(gradient, normed, inverse):
    return inverse * (
        gradient
        - jnp.mean(gradient, -1, keepdims=True)
        - normed * jnp.mean(gradient * normed, -1, keepdims=True)
    )


def dot(left, right, dims):
    return lax.dot_general(left, right, (dims, ((), ())), preferred_element_type=full_type)


def mm(left, right):
    return dot(left, right, ((1,), (0,)))


def mm_nt(left, right):
    return dot(left, right, ((1,), (1,)))


def mm_tn(left, right):
    return dot(left, right, ((0,), (0,)))


def vmem_call(kernel, name, out_shape, scratch, flops, exps, operands, n_scalar=1):
    specs = [pl.BlockSpec(memory_space=pltpu.SMEM)] * n_scalar
    specs += [pl.BlockSpec(memory_space=pltpu.VMEM)] * (len(operands) - n_scalar)
    moved = sum(x.size * x.dtype.itemsize for x in operands)
    moved += sum(x.size * x.dtype.itemsize for x in out_shape)
    return pl.pallas_call(
        kernel,
        out_shape=out_shape,
        in_specs=specs,
        out_specs=tuple(pl.BlockSpec(memory_space=pltpu.VMEM) for _ in out_shape),
        scratch_shapes=scratch,
        compiler_params=pltpu.CompilerParams(vmem_limit_bytes=50 * 2**20),
        cost_estimate=pl.CostEstimate(flops=flops, bytes_accessed=moved, transcendentals=exps),
        name=name,
    )(*operands)


def assemble(table_ref, pieces, target):
    size = pieces[0].shape[0]
    for slot, piece in enumerate(pieces):
        start = pl.multiple_of(table_ref[slot] * size, size)
        target[pl.ds(start, size), :] = piece[...]


def attend_forward_kernel(heads, n_piece, table_ref, *refs):
    stream = refs[:4]
    mod_ref, bias_ref = refs[4:6]
    pieces = refs[6 : 6 + n_piece]
    low_ref, weight_ref, qkv_ref, att_ref, log_ref = refs[6 + n_piece :]
    n_tok = low_ref.shape[0]
    feats = att_ref.shape[0]
    dim = feats // heads
    scale = dim ** (-0.5)
    assemble(table_ref, pieces, weight_ref)
    for r in range(4):
        normed, _ = layer_norm(stream[r][...].astype(full_type))
        here = slice(r * n_tok // 4, (r + 1) * n_tok // 4)
        low = (normed * (1.0 + mod_ref[1:2, :]) + mod_ref[0:1, :]).astype(low_type)
        low_ref[here, :] = low
        qkv_ref[here, :] = (mm(low, weight_ref[...]) + bias_ref[...]).astype(low_type)
    log_ref[...] = jnp.zeros(log_ref.shape, full_type)

    def step(block, _):
        here = pl.ds(pl.multiple_of(block * BLOCK, BLOCK), BLOCK)
        for head in range(heads):
            queries = qkv_ref[here, head * dim : (head + 1) * dim] * scale
            keys = qkv_ref[:, feats + head * dim : feats + (head + 1) * dim]
            values = qkv_ref[:, 2 * feats + head * dim : 2 * feats + (head + 1) * dim]
            scores = mm_nt(queries.astype(low_type), keys)
            row_max = jnp.max(scores, -1, keepdims=True)
            expo = jnp.exp(scores - row_max)
            total = jnp.sum(expo, -1, keepdims=True)
            probs = (expo * (1.0 / total)).astype(low_type)
            att_ref[head * dim : (head + 1) * dim, here] = jnp.transpose(
                mm(probs, values)
            ).astype(low_type)
            logs = jnp.broadcast_to(row_max + jnp.log(total), (BLOCK, 128))
            log_ref[head : head + 1, here] = jnp.transpose(logs)[0:1]
        return 0

    lax.fori_loop(0, n_tok // BLOCK, step, 0)


def gelu_both(value):
    root = (2.0 / math.pi) ** 0.5
    square = value * value
    bend = jnp.tanh(root * value * (1.0 + 0.044715 * square))
    half = 0.5 * (1.0 + bend)
    slope = half + 0.5 * value * (1.0 - bend * bend) * (root * (1.0 + 3 * 0.044715 * square))
    return (value * half, slope)


def mlp_kernel(n_piece, table_ref, *refs):
    att = refs[:4]
    stream = refs[4:8]
    cot = refs[8:12]
    mod_ref, bias_ref = refs[12:14]
    pieces = refs[14 : 14 + n_piece]
    (
        att_all,
        out_own,
        residual_ref,
        branch_ref,
        part_ref,
        back_ref,
        grads_ref,
        sums_ref,
        weights,
        low_ref,
        act_ref,
        hid_ref,
        cot_ref,
    ) = refs[14 + n_piece :]
    feats, n_tok = att[0].shape
    width = stream[0].shape[1]
    size = n_tok // 4
    own = table_ref[n_piece]
    assemble(table_ref, pieces, weights)
    for r in range(4):
        start = pl.multiple_of((own ^ r) * feats, feats)
        att_all[pl.ds(start, feats), :] = att[r][...]
    out_own[...] = weights[pl.ds(pl.multiple_of(own * feats, feats), feats), :width]
    shift_m, scale_m, gate_m = [mod_ref[i : i + 1, :] for i in (3, 4, 5)]
    totals = [jnp.zeros((1, width), full_type) for _ in range(5)]
    for r in range(4):
        here = slice(r * size, (r + 1) * size)
        branch = mm_tn(att_all[:, here], weights[:, :width]) + bias_ref[0:1, :]
        residual = stream[r][...].astype(full_type) + mod_ref[2:3, :] * branch
        if r == 0:
            residual_ref[...] = residual
            branch_ref[...] = branch
        normed, _ = layer_norm(residual)
        low = (normed * (1.0 + scale_m) + shift_m).astype(low_type)
        low_ref[here, :] = low
        hidden = mm(low, weights[:, width : 2 * width]) + bias_ref[2:3, :]
        active, slope = gelu_both(hidden)
        active = active.astype(low_type)
        act_ref[here, :] = active
        part = mm(active, weights[:, 2 * width :])
        part_ref[here, :] = part.astype(low_type)
        grad_y = cot[r][...].astype(full_type)
        totals[0] += jnp.sum(grad_y * part, 0, keepdims=True)
        if r == 0:
            totals[0] += jnp.sum(grad_y, 0, keepdims=True) * bias_ref[1:2, :]
        grad_low = (gate_m * grad_y).astype(low_type)
        cot_ref[here, :] = grad_low
        grad_hid = (mm_nt(grad_low, weights[:, 2 * width :]) * slope).astype(low_type)
        hid_ref[here, :] = grad_hid
        back = mm_nt(grad_hid, weights[:, width : 2 * width])
        back_ref[here, :] = back.astype(low_type)
        totals[1] += jnp.sum(back * normed, 0, keepdims=True)
        totals[2] += jnp.sum(back, 0, keepdims=True)
        totals[3] += jnp.sum(grad_hid.astype(full_type), 0, keepdims=True)
        totals[4] += jnp.sum(grad_low.astype(full_type), 0, keepdims=True)
    sums_ref[...] = jnp.concatenate(totals + [jnp.zeros((3, width), full_type)], 0)
    grads_ref[:, :width] = mm_tn(low_ref[...], hid_ref[...]).astype(low_type)
    grads_ref[:, width:] = mm_tn(act_ref[...], cot_ref[...]).astype(low_type)


def attend_backward_kernel(heads, table_ref, *refs):
    grad = refs[:4]
    stream = refs[4:8]
    att_all, out_own, qkv_ref, log_ref, weight_ref, low_ref = refs[8:14]
    back_ref, grads_ref, sums_ref, bias_ref = refs[14:18]
    all_ref, cols_ref, grad_ref, out_ref, keys_t, sum_k, sum_v = refs[18:]
    n_tok, width = low_ref.shape
    feats = out_own.shape[0]
    size = n_tok // 4
    dim = feats // heads
    scale = dim ** (-0.5)
    own = table_ref[0]
    for r in range(4):
        here = slice(r * size, (r + 1) * size)
        all_ref[here, :] = grad[r][...]
        grad_ref[here, :] = mm_nt(grad[r][...], out_own[...]).astype(low_type)
    for j in range(4):

        @pl.when(own == j)
        def _():
            cols_ref[...] = all_ref[:, j * feats : (j + 1) * feats]

    grads_ref[:, 3 * feats :] = mm(att_all[...], cols_ref[...]).astype(low_type)
    keys_t[...] = jnp.transpose(qkv_ref[:, feats : 2 * feats])
    sum_k[...] = jnp.zeros(sum_k.shape, full_type)
    sum_v[...] = jnp.zeros(sum_v.shape, full_type)

    def step(block, _):
        here = pl.ds(pl.multiple_of(block * BLOCK, BLOCK), BLOCK)
        for head in range(heads):
            cut = slice(head * dim, (head + 1) * dim)
            queries = (qkv_ref[here, cut] * scale).astype(low_type)
            keys = qkv_ref[:, feats + head * dim : feats + (head + 1) * dim]
            values = qkv_ref[:, 2 * feats + head * dim : 2 * feats + (head + 1) * dim]
            grad_att = grad_ref[here, cut]
            probs = jnp.exp(mm_nt(keys, queries) - log_ref[head : head + 1, here])
            grad_probs = mm_nt(values, grad_att)
            delta = jnp.sum(probs * grad_probs, 0, keepdims=True)
            grad_scores = (probs * (grad_probs - delta)).astype(low_type)
            sum_v[:, cut] += mm(probs.astype(low_type), grad_att)
            sum_k[:, cut] += mm(grad_scores, queries)
            grad_q = mm(keys_t[cut, :], grad_scores) * scale
            out_ref[here, cut] = jnp.transpose(grad_q).astype(low_type)
        return 0

    lax.fori_loop(0, n_tok // BLOCK, step, 0)
    out_ref[:, feats : 2 * feats] = sum_k[...].astype(low_type)
    out_ref[:, 2 * feats :] = sum_v[...].astype(low_type)
    grads_ref[:, : 3 * feats] = mm_tn(low_ref[...], out_ref[...]).astype(low_type)
    totals = [jnp.zeros((1, width), full_type) for _ in range(2)]
    for r in range(4):
        here = slice(r * size, (r + 1) * size)
        back = mm_nt(out_ref[here, :], weight_ref[...])
        back_ref[here, :] = back.astype(low_type)
        normed, _ = layer_norm(stream[r][...].astype(full_type))
        totals[0] += jnp.sum(back, 0, keepdims=True)
        totals[1] += jnp.sum(back * normed, 0, keepdims=True)
    sums_ref[...] = jnp.concatenate(totals + [jnp.zeros((6, width), full_type)], 0)
    bias_ref[...] = jnp.sum(out_ref[...].astype(full_type), 0, keepdims=True)


def adam_step(weight, first, second, grad):
    first_new = beta_one * first + (1.0 - beta_one) * grad
    second_new = beta_two * second + (1.0 - beta_two) * grad * grad
    corr_one = 1.0 - beta_one**ADAM_STEP
    corr_two = 1.0 - beta_two**ADAM_STEP
    weight_new = weight - learn_rate * (first_new / corr_one) / (
        jnp.sqrt(second_new / corr_two) + adam_eps
    )
    return (weight_new, first_new, second_new)


def swap(value, distance):
    return lax.ppermute(value, "seq", [(p, p ^ distance) for p in range(4)])


def gather_rel(value):
    far = swap(value, 2)
    near = swap(value, 1)
    cross = swap(far, 1)
    return [value, near, far, cross]


def scatter_rel(low):
    blocks = split_rows(low)
    near_own = swap(blocks[1], 1).astype(full_type)
    near_far = swap(blocks[3], 1).astype(full_type)
    far_own = swap((blocks[2].astype(full_type) + near_far).astype(low_type), 2)
    return blocks[0].astype(full_type) + near_own + far_own.astype(full_type)


def split_rows(value):
    return [value[r * value.shape[0] // 4 : (r + 1) * value.shape[0] // 4] for r in range(4)]


def reorder(blocks, own):
    odd, high = (own & 1) == 1, own >= 2
    pairs = [jnp.where(odd, blocks[j ^ 1], blocks[j]) for j in range(4)]
    return [jnp.where(high, pairs[j ^ 2], pairs[j]) for j in range(4)]


CYCLE = (0, 2, 4, 6, 7, 5, 3, 1)


def ring_gather(value, count):
    if count != len(CYCLE):
        return [spread(value, "shard", count).reshape(-1, value.shape[-1])]
    right = [(CYCLE[i], CYCLE[(i + 1) % count]) for i in range(count)]
    left = [(to, start) for start, to in right]
    pieces = [value]
    ahead = behind = value
    for hop in range(count // 2):
        ahead = lax.ppermute(ahead, "shard", right)
        pieces.append(ahead)
        if hop < count // 2 - 1:
            behind = lax.ppermute(behind, "shard", left)
            pieces.append(behind)
    return pieces


def ring_table(own, count):
    if count != len(CYCLE):
        return jnp.zeros((1,), jnp.int32)
    lines = []
    for s in range(count):
        at = CYCLE.index(s)
        line = [s]
        for hop in range(1, count // 2 + 1):
            line.append(CYCLE[(at - hop) % count])
            if hop < count // 2:
                line.append(CYCLE[(at + hop) % count])
        lines.append(line)
    return lax.dynamic_index_in_dim(jnp.array(lines, jnp.int32), own, 0, keepdims=False)


def permute_blocks(value, distance):
    size = value.shape[1] // 4
    return jnp.concatenate(
        [value[:, (r ^ distance) * size : ((r ^ distance) + 1) * size] for r in range(4)], 1
    )


def spread(value, axis, count):
    return lax.all_to_all(
        jnp.broadcast_to(value[None], (count,) + value.shape), axis, 0, 0, tiled=True
    )


def owned(gradient, count, own):
    arrived = lax.all_to_all(
        gradient.reshape(count, -1, gradient.shape[-1]), "shard", 0, 0, tiled=True
    )
    total = jnp.sum(arrived.astype(full_type), 0).astype(low_type)
    return [piece.astype(full_type) for piece in reorder(gather_rel(total), own)]


def every_shard(value, count):
    rows, distance = value[None], 1
    while distance < count:
        pairs = [(p, p ^ distance) for p in range(count)]
        rows = jnp.concatenate([rows, lax.ppermute(rows, "shard", pairs)])
        distance *= 2
    return rows


def token_sum(tensor):
    return jnp.sum(tensor.astype(full_type), axis=0)


def shards(
    latents,
    cotangent,
    class_labels,
    time_buckets,
    class_table,
    time_table,
    ada_weight,
    qkv_weight,
    out_weight,
    up_weight,
    down_weight,
    biases,
    ada_first,
    qkv_first,
    out_first,
    up_first,
    down_first,
    bias_first,
    ada_second,
    qkv_second,
    out_second,
    up_second,
    down_second,
    bias_second,
    n_shard,
    n_seq,
):
    assert n_seq == 4 and latents.shape[0] == 1 and class_labels.shape[0] == n_shard
    s_own = lax.axis_index("shard")
    q_own = lax.axis_index("seq")
    tok_dev, width = latents.shape[1:]
    head_dim = width // HEADS
    score_scale = head_dim ** (-0.5)
    heads_own = HEADS // n_seq
    feats = heads_own * head_dim
    rows = ada_weight.shape[0]
    ff = up_weight.shape[1]
    ff_cell = ff // (n_shard * n_seq)
    ff_own = ff // n_seq

    table = jnp.concatenate([ring_table(s_own, n_shard), q_own[None].astype(jnp.int32)])
    qkv_part = lax.dynamic_index_in_dim(
        qkv_weight.reshape(rows, 3, n_seq, feats), q_own, 2, keepdims=False
    ).reshape(rows, 3 * feats)
    qkv_pieces = ring_gather(qkv_part.astype(low_type), n_shard)
    up_part = lax.dynamic_index_in_dim(
        up_weight.reshape(rows, n_shard, n_seq, ff_cell), q_own, 2, keepdims=False
    ).reshape(rows, ff_own)
    down_part = lax.dynamic_slice_in_dim(down_weight, q_own * ff_cell, ff_cell, 0)
    rest_part = jnp.concatenate([out_weight, up_part, down_part], 1).astype(low_type)
    rest_pieces = ring_gather(rest_part, n_shard)
    n_piece = len(qkv_pieces)

    cond = jnp.take(class_table, class_labels, axis=0).astype(full_type) + jnp.take(
        time_table, time_buckets, axis=0
    ).astype(full_type)
    cond_cols = lax.dynamic_slice_in_dim(cond, s_own * rows, rows, 1)
    silu_cols = jax.nn.silu(cond_cols).astype(low_type)
    ada_low = ada_weight.astype(low_type)
    mod_partial = mm(silu_cols, ada_low)
    bias_low = biases.astype(low_type).astype(full_type).reshape(1, -1)
    payload = jnp.concatenate(
        [mod_partial, jnp.broadcast_to(bias_low, (n_shard, bias_low.shape[1]))], 1
    )
    arrived = lax.all_to_all(payload, "shard", split_axis=0, concat_axis=0, tiled=True)
    mod_sum = jnp.sum(arrived[:, : 6 * width], 0)
    bias_full = jnp.transpose(
        arrived[:, 6 * width :].reshape(n_shard, biases.shape[0], rows), (1, 0, 2)
    ).reshape(biases.shape[0], width)
    modulation = mod_sum.reshape(6, width) + bias_full[0:6]
    shift_a, scale_a, gate_a, shift_m, scale_m, gate_m = [modulation[i] for i in range(6)]

    stream = gather_rel(latents[0])
    grad_y = gather_rel(cotangent[0])
    n_tok = n_seq * tok_dev

    bias_query = lax.dynamic_slice_in_dim(bias_full[6], q_own * feats, feats)
    bias_value = lax.dynamic_slice_in_dim(bias_full[7], q_own * feats, feats)
    bias_qkv = jnp.concatenate([bias_query, jnp.zeros_like(bias_query), bias_value])[None]
    pair_count = heads_own * n_tok * n_tok
    modulated_a, qkv_w, qkv, att_own, logs = vmem_call(
        partial(attend_forward_kernel, heads_own, n_piece),
        "attend_forward",
        (
            jax.ShapeDtypeStruct((n_tok, width), low_type),
            jax.ShapeDtypeStruct((width, 3 * feats), low_type),
            jax.ShapeDtypeStruct((n_tok, 3 * feats), low_type),
            jax.ShapeDtypeStruct((feats, n_tok), low_type),
            jax.ShapeDtypeStruct((8, n_tok), full_type),
        ),
        [],
        6 * n_tok * width * feats + 4 * pair_count * head_dim,
        pair_count,
        [table, *stream, modulation, bias_qkv, *qkv_pieces],
    )
    att_far = swap(permute_blocks(att_own, 2), 2)
    att_near = swap(permute_blocks(att_own, 1), 1)
    att_cross = swap(permute_blocks(att_far, 1), 1)

    bias_ff = lax.dynamic_index_in_dim(
        bias_full[9:13].reshape(n_shard, n_seq, ff_cell), q_own, 1, keepdims=False
    ).reshape(ff_own)
    bias_mlp = jnp.stack([bias_full[8], bias_full[13], bias_ff])
    attended, out_own, residual, branch_a, branch_part, grad_mod_part, grads_mlp, sums_mlp = (
        vmem_call(
            partial(mlp_kernel, n_piece),
            "mlp",
            (
                jax.ShapeDtypeStruct((width, n_tok), low_type),
                jax.ShapeDtypeStruct((feats, width), low_type),
                jax.ShapeDtypeStruct((tok_dev, width), full_type),
                jax.ShapeDtypeStruct((tok_dev, width), full_type),
                jax.ShapeDtypeStruct((n_tok, width), low_type),
                jax.ShapeDtypeStruct((n_tok, width), low_type),
                jax.ShapeDtypeStruct((width, 2 * ff_own), low_type),
                jax.ShapeDtypeStruct((8, width), full_type),
            ),
            [pltpu.VMEM((width, 3 * width), low_type)]
            + [pltpu.VMEM((n_tok, width), low_type)] * 4,
            14 * n_tok * width * width,
            n_tok * width,
            [
                table,
                att_own,
                att_near,
                att_far,
                att_cross,
                *stream,
                *grad_y,
                modulation,
                bias_mlp,
                *rest_pieces,
            ],
        )
    )
    grad_mod_own = scatter_rel(grad_mod_part)
    normed_m, inverse_m = layer_norm(residual)
    grad_residual = grad_y[0].astype(full_type) + norm_back(
        grad_mod_own * (1.0 + scale_m), normed_m, inverse_m
    )
    grad_branch_own = (gate_a * grad_residual).astype(low_type)
    grad_branch_a = gather_rel(grad_branch_own)
    grad_mod_a_part, grads_att, sums_att, sums_qkv = vmem_call(
        partial(attend_backward_kernel, heads_own),
        "attend_backward",
        (
            jax.ShapeDtypeStruct((n_tok, width), low_type),
            jax.ShapeDtypeStruct((width, 4 * feats), low_type),
            jax.ShapeDtypeStruct((8, width), full_type),
            jax.ShapeDtypeStruct((1, 3 * feats), full_type),
        ),
        [
            pltpu.VMEM((n_tok, width), low_type),
            pltpu.VMEM((n_tok, feats), low_type),
            pltpu.VMEM((n_tok, feats), low_type),
            pltpu.VMEM((n_tok, 3 * feats), low_type),
            pltpu.VMEM((feats, n_tok), low_type),
            pltpu.VMEM((n_tok, feats), full_type),
            pltpu.VMEM((n_tok, feats), full_type),
        ],
        16 * n_tok * width * feats + 10 * pair_count * head_dim,
        pair_count,
        [
            q_own[None].astype(jnp.int32),
            *grad_branch_a,
            *stream,
            attended,
            out_own,
            qkv,
            logs,
            qkv_w,
            modulated_a,
        ],
    )
    grad_gate_a = token_sum(grad_residual * branch_a)
    grad_gate_m, grad_scale_m, grad_shift_m, sum_hidden, sum_branch_m = [
        sums_mlp[i] for i in range(5)
    ]
    grad_shift_a, grad_scale_a = sums_att[0], sums_att[1]
    qkv_sums = sums_qkv[0]
    normed_a, inverse_a = layer_norm(latents[0].astype(full_type))
    latents_grad = grad_residual + norm_back(
        scatter_rel(grad_mod_a_part) * (1.0 + scale_a), normed_a, inverse_a
    )
    branch_own = scatter_rel(branch_part) + bias_full[13]
    block_out = (residual + gate_m * branch_own).astype(low_type)

    def placed(own_part):
        whole = jnp.zeros((n_seq, own_part.shape[0]), full_type)
        return lax.dynamic_update_index_in_dim(whole, own_part, q_own, 0).reshape(-1)

    small = jnp.concatenate(
        [
            grad_shift_a,
            grad_scale_a,
            grad_gate_a,
            grad_shift_m,
            grad_scale_m,
            grad_gate_m,
            placed(qkv_sums[:feats]),
            placed(qkv_sums[2 * feats :]),
            token_sum(grad_branch_own),
            placed(sum_hidden),
            jnp.where(q_own == 0, sum_branch_m, 0.0),
        ]
    )
    small = small + swap(small, 1)
    small = small + swap(small, 2)
    every = every_shard(small, n_shard)
    grad_modulation = every[:, : 6 * width].astype(low_type)
    rest = jnp.sum(every[:, 6 * width :], 0)
    cuts = [width, 2 * width, 3 * width, 3 * width + ff]
    sum_query, sum_value, sum_out, sum_ff, sum_down = jnp.split(rest, cuts)
    bias_ada = jnp.sum(grad_modulation.astype(full_type), 0).reshape(6, width)
    bias_grad_all = jnp.concatenate(
        [
            bias_ada,
            sum_query.reshape(1, width),
            sum_value.reshape(1, width),
            sum_out[None],
            jnp.transpose(sum_ff.reshape(n_seq, n_shard, ff_cell), (1, 0, 2)).reshape(-1, width),
            sum_down[None],
        ]
    )
    bias_grad = lax.dynamic_slice_in_dim(bias_grad_all, s_own * rows, rows, 1)
    others = s_own ^ jnp.arange(n_shard, dtype=jnp.int32)
    cond_rel = jnp.take(cond_cols, others, axis=0)
    labels_rel = jnp.take(class_labels, others)
    buckets_rel = jnp.take(time_buckets, others)
    grad_ada = mm_tn(jax.nn.silu(cond_rel).astype(low_type), grad_modulation)
    grad_silu = mm_nt(grad_modulation, ada_low)
    _, silu_pull = jax.vjp(jax.nn.silu, cond_rel)
    grad_cols = silu_pull(grad_silu)[0]

    mlp_quarters = owned(grads_mlp, n_shard, q_own)
    att_quarters = owned(grads_att, n_shard, q_own)
    down_grad = jnp.concatenate([piece[:, ff_own:] for piece in mlp_quarters])
    up_grad = jnp.transpose(
        jnp.stack([piece[:, :ff_own].reshape(rows, n_shard, ff_cell) for piece in mlp_quarters]),
        (1, 2, 0, 3),
    ).reshape(rows, ff)
    out_grad = jnp.concatenate([piece[:, 3 * feats :] for piece in att_quarters], 1)
    qkv_grad = jnp.stack(
        [piece[:, : 3 * feats].reshape(rows, 3, feats) for piece in att_quarters], 2
    ).reshape(rows, 3 * width)

    class_hot = (
        labels_rel[:, None] == jnp.arange(class_table.shape[0], dtype=jnp.int32)[None, :]
    ).astype(full_type)
    time_hot = (
        buckets_rel[:, None] == jnp.arange(time_table.shape[0], dtype=jnp.int32)[None, :]
    ).astype(full_type)
    class_grad = jnp.einsum("ln,lc->nc", class_hot, grad_cols, precision=lax.Precision.HIGHEST)
    time_grad = jnp.einsum("ln,lc->nc", time_hot, grad_cols, precision=lax.Precision.HIGHEST)
    updates = [
        adam_step(ada_weight, ada_first, ada_second, grad_ada),
        adam_step(qkv_weight, qkv_first, qkv_second, qkv_grad),
        adam_step(out_weight, out_first, out_second, out_grad),
        adam_step(up_weight, up_first, up_second, up_grad),
        adam_step(down_weight, down_first, down_second, down_grad),
        adam_step(biases, bias_first, bias_second, bias_grad),
    ]
    return (
        block_out[None],
        latents_grad[None],
        class_grad,
        time_grad,
        *[update[0] for update in updates],
        *[update[1] for update in updates],
        *[update[2] for update in updates],
    )


def solution(mesh):
    tokens = P("shard", "seq", None)
    rows = P("shard", None)
    cols = P(None, "shard")
    state = (rows, rows, rows, rows, rows, cols)
    return jax.shard_map(
        partial(shards, n_shard=mesh.shape["shard"], n_seq=mesh.shape["seq"]),
        mesh=mesh,
        in_specs=(tokens, tokens, P(), P(), P(), P()) + 3 * state,
        out_specs=(tokens, tokens, cols, cols) + 3 * state,
        check_vma=False,
    )
```

```python
import math
from functools import partial

import jax
import jax.numpy as jnp
from jax import lax
from jax.experimental import pallas as pl
from jax.experimental.pallas import tpu as pltpu
from jax.sharding import PartitionSpec as P

HEADS = 12
ADAM_STEP = 10
BLOCK = 256


norm_eps = 1e-06
beta_one = 0.9
beta_two = 0.999
learn_rate = 0.05
adam_eps = 1e-08

low_type = jnp.bfloat16
full_type = jnp.float32


def layer_norm(values_in):
    centred = values_in - jnp.mean(values_in, -1, keepdims=True)
    inverse = lax.rsqrt(jnp.mean(centred * centred, -1, keepdims=True) + norm_eps)
    return (centred * inverse, inverse)


def norm_back(gradient, normed, inverse):
    return inverse * (
        gradient
        - jnp.mean(gradient, -1, keepdims=True)
        - normed * jnp.mean(gradient * normed, -1, keepdims=True)
    )


def dot(left, right, dims):
    return lax.dot_general(left, right, (dims, ((), ())), preferred_element_type=full_type)


def mm(left, right):
    return dot(left, right, ((1,), (0,)))


def mm_nt(left, right):
    return dot(left, right, ((1,), (1,)))


def mm_tn(left, right):
    return dot(left, right, ((0,), (0,)))


def vmem_call(kernel, name, out_shape, scratch, flops, exps, operands, n_scalar=1):
    specs = [pl.BlockSpec(memory_space=pltpu.SMEM)] * n_scalar
    specs += [pl.BlockSpec(memory_space=pltpu.VMEM)] * (len(operands) - n_scalar)
    moved = sum(x.size * x.dtype.itemsize for x in operands)
    moved += sum(x.size * x.dtype.itemsize for x in out_shape)
    return pl.pallas_call(
        kernel,
        out_shape=out_shape,
        in_specs=specs,
        out_specs=tuple(pl.BlockSpec(memory_space=pltpu.VMEM) for _ in out_shape),
        scratch_shapes=scratch,
        compiler_params=pltpu.CompilerParams(vmem_limit_bytes=50 * 2**20),
        cost_estimate=pl.CostEstimate(flops=flops, bytes_accessed=moved, transcendentals=exps),
        name=name,
    )(*operands)


def cut_kernel(table_ref, qkv_ref, out_ref, up_ref, down_ref, first_ref, rest_ref):
    rows, width = out_ref.shape
    feats = width // 4
    cell = down_ref.shape[0] // 4
    n_shard = up_ref.shape[1] // (4 * cell)
    for j in range(4):

        @pl.when(table_ref[0] == j)
        def _():
            for part in range(3):
                start = part * width + j * feats
                first_ref[:, part * feats : (part + 1) * feats] = qkv_ref[
                    :, start : start + feats
                ].astype(low_type)
            first_ref[:, 3 * feats :] = out_ref[:, j * feats : (j + 1) * feats].astype(low_type)
            for s in range(n_shard):
                start = (s * 4 + j) * cell
                rest_ref[:, s * cell : (s + 1) * cell] = up_ref[:, start : start + cell].astype(
                    low_type
                )
            rest_ref[:, width:] = down_ref[j * cell : (j + 1) * cell, :].astype(low_type)


def adam_mlp_kernel(table_ref, *refs):
    grads, state, outs = refs[:4], refs[4:10], refs[10:16]
    grad_up, grad_down = refs[16:]
    width = grad_down.shape[1]
    cell = grad_down.shape[0] // 4
    n_shard = grad_up.shape[1] // (4 * cell)
    for j in range(4):

        @pl.when(table_ref[0] == j)
        def _():
            for r in range(4):
                grad = grads[r][...].astype(full_type)
                for s in range(n_shard):
                    start = (s * 4 + (j ^ r)) * cell
                    grad_up[:, start : start + cell] = grad[:, s * cell : (s + 1) * cell]
                grad_down[(j ^ r) * cell : ((j ^ r) + 1) * cell, :] = grad[:, width:]

    for grad, part in ((grad_up, slice(0, 6, 2)), (grad_down, slice(1, 6, 2))):
        results = adam_step(*[ref[...] for ref in state[part]], grad[...])
        for ref, result in zip(outs[part], results):
            ref[...] = result


def adam_att_kernel(table_ref, *refs):
    grads, state, outs = refs[:4], refs[4:10], refs[10:16]
    grad_qkv, grad_out = refs[16:]
    width = grad_out.shape[1]
    feats = width // 4
    for j in range(4):

        @pl.when(table_ref[0] == j)
        def _():
            for r in range(4):
                grad = grads[r][...].astype(full_type)
                for part in range(3):
                    start = part * width + (j ^ r) * feats
                    grad_qkv[:, start : start + feats] = grad[:, part * feats : (part + 1) * feats]
                grad_out[:, (j ^ r) * feats : ((j ^ r) + 1) * feats] = grad[:, 3 * feats :]

    for grad, part in ((grad_qkv, slice(0, 6, 2)), (grad_out, slice(1, 6, 2))):
        results = adam_step(*[ref[...] for ref in state[part]], grad[...])
        for ref, result in zip(outs[part], results):
            ref[...] = result


def adam_call(kernel, name, own, grads, state):
    results = vmem_call(
        kernel,
        name,
        tuple(jax.ShapeDtypeStruct(x.shape, full_type) for x in state),
        [pltpu.VMEM(x.shape, full_type) for x in state[:2]],
        20 * (state[0].size + state[1].size),
        state[0].size + state[1].size,
        [own, *grads, *state],
    )
    return results[0::2], results[1::2]


def project_kernel(n_piece, table_ref, *refs):
    stream = refs[:4]
    mod_ref, bias_ref = refs[4:6]
    pieces = refs[6 : 6 + n_piece]
    low_ref, weight_ref, out_ref, qkv_ref = refs[6 + n_piece :]
    n_tok, cols = qkv_ref.shape
    size = pieces[0].shape[0]
    for slot, piece in enumerate(pieces):
        place = pl.ds(pl.multiple_of(table_ref[slot] * size, size), size)
        weight_ref[place, :] = piece[:, :cols]
        out_ref[place, :] = piece[:, cols:]
    for r in range(4):
        normed, _ = layer_norm(stream[r][...].astype(full_type))
        here = slice(r * n_tok // 4, (r + 1) * n_tok // 4)
        low = (normed * (1.0 + mod_ref[1:2, :]) + mod_ref[0:1, :]).astype(low_type)
        low_ref[here, :] = low
        qkv_ref[here, :] = (mm(low, weight_ref[...]) + bias_ref[...]).astype(low_type)


def attend_forward_kernel(heads, qkv_ref, att_ref, log_ref):
    n_tok = qkv_ref.shape[0]
    feats = att_ref.shape[0]
    dim = feats // heads
    scale = dim ** (-0.5)
    log_ref[...] = jnp.zeros(log_ref.shape, full_type)

    def step(block, _):
        here = pl.ds(pl.multiple_of(block * BLOCK, BLOCK), BLOCK)
        for head in range(heads):
            queries = qkv_ref[here, head * dim : (head + 1) * dim] * scale
            keys = qkv_ref[:, feats + head * dim : feats + (head + 1) * dim]
            values = qkv_ref[:, 2 * feats + head * dim : 2 * feats + (head + 1) * dim]
            scores = mm_nt(queries.astype(low_type), keys)
            row_max = jnp.max(scores, -1, keepdims=True)
            expo = jnp.exp(scores - row_max)
            total = jnp.sum(expo, -1, keepdims=True)
            probs = (expo * (1.0 / total)).astype(low_type)
            att_ref[head * dim : (head + 1) * dim, here] = jnp.transpose(
                mm(probs, values)
            ).astype(low_type)
            logs = jnp.broadcast_to(row_max + jnp.log(total), (BLOCK, 128))
            log_ref[head : head + 1, here] = jnp.transpose(logs)[0:1]
        return 0

    lax.fori_loop(0, n_tok // BLOCK, step, 0)


def gelu_both(value):
    root = (2.0 / math.pi) ** 0.5
    square = value * value
    bend = jnp.tanh(root * value * (1.0 + 0.044715 * square))
    half = 0.5 * (1.0 + bend)
    slope = half + 0.5 * value * (1.0 - bend * bend) * (root * (1.0 + 3 * 0.044715 * square))
    return (value * half, slope)


def deal(table_ref, pieces, source):
    size = pieces[0].shape[0]
    for slot, piece in enumerate(pieces):
        piece[...] = source[pl.ds(pl.multiple_of(table_ref[slot] * size, size), size), :]


def mlp_kernel(n_piece, table_ref, *refs):
    att = refs[:4]
    stream = refs[4:8]
    cot = refs[8:12]
    mod_ref, bias_ref = refs[12:14]
    out_parts = refs[14:18]
    weights = refs[18]
    (
        att_all,
        out_own,
        residual_ref,
        branch_ref,
        normed_ref,
        inverse_ref,
        part_ref,
        back_ref,
        sums_ref,
    ) = refs[19:28]
    pieces = refs[28 : 28 + n_piece]
    grads_ref, out_all, low_ref, act_ref, hid_ref, cot_ref = refs[28 + n_piece :]
    feats, n_tok = att[0].shape
    width = stream[0].shape[1]
    size = n_tok // 4
    own = table_ref[n_piece]
    for r in range(4):
        start = pl.multiple_of((own ^ r) * feats, feats)
        att_all[pl.ds(start, feats), :] = att[r][...]
    for r in range(4):
        for j in range(4):

            @pl.when((own ^ r) == j)
            def _():
                out_all[:, j * feats : (j + 1) * feats] = out_parts[r][...]

    out_own[...] = out_all[pl.ds(pl.multiple_of(own * feats, feats), feats), :]
    shift_m, scale_m, gate_m = [mod_ref[i : i + 1, :] for i in (3, 4, 5)]
    totals = [jnp.zeros((1, width), full_type) for _ in range(5)]
    for r in range(4):
        here = slice(r * size, (r + 1) * size)
        branch = mm_tn(att_all[:, here], out_all[...]) + bias_ref[0:1, :]
        residual = stream[r][...].astype(full_type) + mod_ref[2:3, :] * branch
        if r == 0:
            residual_ref[...] = residual
            branch_ref[...] = branch
        normed, inverse = layer_norm(residual)
        if r == 0:
            normed_ref[...] = normed
            inverse_ref[...] = inverse
        low = (normed * (1.0 + scale_m) + shift_m).astype(low_type)
        low_ref[here, :] = low
        hidden = mm(low, weights[:, :width]) + bias_ref[2:3, :]
        active, slope = gelu_both(hidden)
        active = active.astype(low_type)
        act_ref[here, :] = active
        part = mm(active, weights[:, width:])
        part_ref[here, :] = part.astype(low_type)
        grad_y = cot[r][...].astype(full_type)
        totals[0] += jnp.sum(grad_y * part, 0, keepdims=True)
        if r == 0:
            totals[0] += jnp.sum(grad_y, 0, keepdims=True) * bias_ref[1:2, :]
        grad_low = (gate_m * grad_y).astype(low_type)
        cot_ref[here, :] = grad_low
        grad_hid = (mm_nt(grad_low, weights[:, width:]) * slope).astype(low_type)
        hid_ref[here, :] = grad_hid
        back = mm_nt(grad_hid, weights[:, :width])
        back_ref[here, :] = back.astype(low_type)
        totals[1] += jnp.sum(back * normed, 0, keepdims=True)
        totals[2] += jnp.sum(back, 0, keepdims=True)
        totals[3] += jnp.sum(grad_hid.astype(full_type), 0, keepdims=True)
        totals[4] += jnp.sum(grad_low.astype(full_type), 0, keepdims=True)
    sums_ref[...] = jnp.concatenate(totals + [jnp.zeros((3, width), full_type)], 0)
    grads_ref[:, :width] = mm_tn(low_ref[...], hid_ref[...]).astype(low_type)
    grads_ref[:, width:] = mm_tn(act_ref[...], cot_ref[...]).astype(low_type)
    deal(table_ref, pieces, grads_ref)


def attend_backward_kernel(heads, n_piece, table_ref, *refs):
    grad = refs[:4]
    stream = refs[4:8]
    att_all, out_own, qkv_ref, log_ref, weight_ref, low_ref = refs[8:14]
    back_ref, sums_ref, bias_ref = refs[14:17]
    pieces = refs[17 : 17 + n_piece]
    grads_ref, all_ref, cols_ref, grad_ref, out_ref, keys_t, sum_k, sum_v = refs[17 + n_piece :]
    n_tok, width = low_ref.shape
    feats = out_own.shape[0]
    size = n_tok // 4
    dim = feats // heads
    scale = dim ** (-0.5)
    own = table_ref[n_piece]
    for r in range(4):
        here = slice(r * size, (r + 1) * size)
        all_ref[here, :] = grad[r][...]
        grad_ref[here, :] = mm_nt(grad[r][...], out_own[...]).astype(low_type)
    for j in range(4):

        @pl.when(own == j)
        def _():
            cols_ref[...] = all_ref[:, j * feats : (j + 1) * feats]

    grads_ref[:, 3 * feats :] = mm(att_all[...], cols_ref[...]).astype(low_type)
    keys_t[...] = jnp.transpose(qkv_ref[:, feats : 2 * feats])
    sum_k[...] = jnp.zeros(sum_k.shape, full_type)
    sum_v[...] = jnp.zeros(sum_v.shape, full_type)

    def step(block, _):
        here = pl.ds(pl.multiple_of(block * BLOCK, BLOCK), BLOCK)
        for head in range(heads):
            cut = slice(head * dim, (head + 1) * dim)
            queries = (qkv_ref[here, cut] * scale).astype(low_type)
            keys = qkv_ref[:, feats + head * dim : feats + (head + 1) * dim]
            values = qkv_ref[:, 2 * feats + head * dim : 2 * feats + (head + 1) * dim]
            grad_att = grad_ref[here, cut]
            probs = jnp.exp(mm_nt(keys, queries) - log_ref[head : head + 1, here])
            grad_probs = mm_nt(values, grad_att)
            delta = jnp.sum(probs * grad_probs, 0, keepdims=True)
            grad_scores = (probs * (grad_probs - delta)).astype(low_type)
            sum_v[:, cut] += mm(probs.astype(low_type), grad_att)
            sum_k[:, cut] += mm(grad_scores, queries)
            grad_q = mm(keys_t[cut, :], grad_scores) * scale
            out_ref[here, cut] = jnp.transpose(grad_q).astype(low_type)
        return 0

    lax.fori_loop(0, n_tok // BLOCK, step, 0)
    out_ref[:, feats : 2 * feats] = sum_k[...].astype(low_type)
    out_ref[:, 2 * feats :] = sum_v[...].astype(low_type)
    grads_ref[:, : 3 * feats] = mm_tn(low_ref[...], out_ref[...]).astype(low_type)
    deal(table_ref, pieces, grads_ref)
    totals = [jnp.zeros((1, width), full_type) for _ in range(2)]
    for r in range(4):
        here = slice(r * size, (r + 1) * size)
        back = mm_nt(out_ref[here, :], weight_ref[...])
        back_ref[here, :] = back.astype(low_type)
        normed, _ = layer_norm(stream[r][...].astype(full_type))
        totals[0] += jnp.sum(back, 0, keepdims=True)
        totals[1] += jnp.sum(back * normed, 0, keepdims=True)
    sums_ref[...] = jnp.concatenate(totals + [jnp.zeros((6, width), full_type)], 0)
    bias_ref[...] = jnp.sum(out_ref[...].astype(full_type), 0, keepdims=True)


def adam_step(weight, first, second, grad):
    first_new = beta_one * first + (1.0 - beta_one) * grad
    second_new = beta_two * second + (1.0 - beta_two) * grad * grad
    corr_one = 1.0 - beta_one**ADAM_STEP
    corr_two = 1.0 - beta_two**ADAM_STEP
    weight_new = weight - learn_rate * (first_new / corr_one) / (
        jnp.sqrt(second_new / corr_two) + adam_eps
    )
    return (weight_new, first_new, second_new)


def swap(value, distance):
    return lax.ppermute(value, "seq", [(p, p ^ distance) for p in range(4)])


def gather_rel(value):
    far = swap(value, 2)
    near = swap(value, 1)
    cross = swap(far, 1)
    return [value, near, far, cross]


def scatter_rel(low):
    blocks = split_rows(low)
    near_own = swap(blocks[1], 1).astype(full_type)
    near_far = swap(blocks[3], 1).astype(full_type)
    far_own = swap((blocks[2].astype(full_type) + near_far).astype(low_type), 2)
    return blocks[0].astype(full_type) + near_own + far_own.astype(full_type)


def split_rows(value):
    return [value[r * value.shape[0] // 4 : (r + 1) * value.shape[0] // 4] for r in range(4)]


def reorder(blocks, own):
    odd, high = (own & 1) == 1, own >= 2
    pairs = [jnp.where(odd, blocks[j ^ 1], blocks[j]) for j in range(4)]
    return [jnp.where(high, pairs[j ^ 2], pairs[j]) for j in range(4)]


CYCLE = (0, 2, 4, 6, 7, 5, 3, 1)


def ring_pairs(count):
    right = [(CYCLE[i], CYCLE[(i + 1) % count]) for i in range(count)]
    return right, [(to, start) for start, to in right]


def ring_gather(value, count, follower):
    if count != len(CYCLE):
        return [spread(value, "shard", count).reshape(-1, value.shape[-1])], follower
    right, left = ring_pairs(count)
    pieces = [value]
    ahead = behind = value
    for hop in range(count // 2):
        ahead = lax.ppermute(ahead, "shard", right)
        pieces.append(ahead)
        if hop < count // 2 - 1:
            behind = lax.ppermute(behind, "shard", left)
            pieces.append(behind)
        if hop == 0:
            ahead, behind, follower = lax.optimization_barrier((ahead, behind, follower))
    return pieces, follower


def ring_scatter(pieces, count):
    if len(pieces) == 1:
        whole = pieces[0].reshape(count, -1, pieces[0].shape[-1])
        arrived = lax.all_to_all(whole, "shard", 0, 0, tiled=True)
        return jnp.sum(arrived.astype(full_type), 0).astype(low_type)
    right, left = ring_pairs(count)
    ahead, behind = pieces[count - 1], pieces[count - 3]
    for hop in range(count // 2, 0, -1):
        ahead = lax.ppermute(ahead, "shard", right)
        if hop > 1:
            ahead = (ahead.astype(full_type) + pieces[2 * hop - 2].astype(full_type)).astype(
                low_type
            )
    for hop in range(count // 2 - 1, 0, -1):
        behind = lax.ppermute(behind, "shard", left)
        if hop > 1:
            behind = (behind.astype(full_type) + pieces[2 * hop - 3].astype(full_type)).astype(
                low_type
            )
    return (
        pieces[0].astype(full_type) + ahead.astype(full_type) + behind.astype(full_type)
    ).astype(low_type)


def ring_table(own, count):
    if count != len(CYCLE):
        return jnp.zeros((1,), jnp.int32)
    lines = []
    for s in range(count):
        at = CYCLE.index(s)
        line = [s]
        for hop in range(1, count // 2 + 1):
            line.append(CYCLE[(at - hop) % count])
            if hop < count // 2:
                line.append(CYCLE[(at + hop) % count])
        lines.append(line)
    return lax.dynamic_index_in_dim(jnp.array(lines, jnp.int32), own, 0, keepdims=False)


def permute_blocks(value, distance):
    size = value.shape[1] // 4
    return jnp.concatenate(
        [value[:, (r ^ distance) * size : ((r ^ distance) + 1) * size] for r in range(4)], 1
    )


def spread(value, axis, count):
    return lax.all_to_all(
        jnp.broadcast_to(value[None], (count,) + value.shape), axis, 0, 0, tiled=True
    )


def token_sum(tensor):
    return jnp.sum(tensor.astype(full_type), axis=0)


def shards(
    latents,
    cotangent,
    class_labels,
    time_buckets,
    class_table,
    time_table,
    ada_weight,
    qkv_weight,
    out_weight,
    up_weight,
    down_weight,
    biases,
    ada_first,
    qkv_first,
    out_first,
    up_first,
    down_first,
    bias_first,
    ada_second,
    qkv_second,
    out_second,
    up_second,
    down_second,
    bias_second,
    n_shard,
    n_seq,
):
    assert n_seq == 4 and latents.shape[0] == 1 and class_labels.shape[0] == n_shard
    s_own = lax.axis_index("shard")
    q_own = lax.axis_index("seq")
    tok_dev, width = latents.shape[1:]
    head_dim = width // HEADS
    score_scale = head_dim ** (-0.5)
    heads_own = HEADS // n_seq
    feats = heads_own * head_dim
    rows = ada_weight.shape[0]
    ff = up_weight.shape[1]
    ff_cell = ff // (n_shard * n_seq)
    ff_own = ff // n_seq

    table = jnp.concatenate([ring_table(s_own, n_shard), q_own[None].astype(jnp.int32)])
    own_index = q_own[None].astype(jnp.int32)
    first_part, rest_part = vmem_call(
        cut_kernel,
        "cut",
        (
            jax.ShapeDtypeStruct((rows, 4 * feats), low_type),
            jax.ShapeDtypeStruct((rows, width + ff_own), low_type),
        ),
        [],
        0,
        0,
        [own_index, qkv_weight, out_weight, up_weight, down_weight],
    )
    rest_all = lax.all_gather(rest_part, "shard", axis=0, tiled=True)
    first_pieces, class_labels_late = ring_gather(first_part, n_shard, class_labels)
    n_piece = len(first_pieces)

    cond = jnp.take(class_table, class_labels_late, axis=0).astype(full_type) + jnp.take(
        time_table, time_buckets, axis=0
    ).astype(full_type)
    cond_cols = lax.dynamic_slice_in_dim(cond, s_own * rows, rows, 1)
    silu_cols = jax.nn.silu(cond_cols).astype(low_type)
    ada_low = ada_weight.astype(low_type)
    mod_partial = mm(silu_cols, ada_low)
    bias_low = biases.astype(low_type).astype(full_type).reshape(1, -1)
    payload = jnp.concatenate(
        [mod_partial, jnp.broadcast_to(bias_low, (n_shard, bias_low.shape[1]))], 1
    )
    arrived = lax.all_to_all(payload, "shard", split_axis=0, concat_axis=0, tiled=True)
    mod_sum = jnp.sum(arrived[:, : 6 * width], 0)
    bias_full = jnp.transpose(
        arrived[:, 6 * width :].reshape(n_shard, biases.shape[0], rows), (1, 0, 2)
    ).reshape(biases.shape[0], width)
    modulation = mod_sum.reshape(6, width) + bias_full[0:6]
    shift_a, scale_a, gate_a, shift_m, scale_m, gate_m = [modulation[i] for i in range(6)]

    stream = gather_rel(latents[0])
    n_tok = n_seq * tok_dev

    bias_query = lax.dynamic_slice_in_dim(bias_full[6], q_own * feats, feats)
    bias_value = lax.dynamic_slice_in_dim(bias_full[7], q_own * feats, feats)
    bias_qkv = jnp.concatenate([bias_query, jnp.zeros_like(bias_query), bias_value])[None]
    pair_count = heads_own * n_tok * n_tok
    modulated_a, qkv_w, out_q, qkv = vmem_call(
        partial(project_kernel, n_piece),
        "project",
        (
            jax.ShapeDtypeStruct((n_tok, width), low_type),
            jax.ShapeDtypeStruct((width, 3 * feats), low_type),
            jax.ShapeDtypeStruct((width, feats), low_type),
            jax.ShapeDtypeStruct((n_tok, 3 * feats), low_type),
        ),
        [],
        6 * n_tok * width * feats,
        n_tok,
        [table, *stream, modulation, bias_qkv, *first_pieces],
    )
    out_parts = gather_rel(out_q)
    cot_own, qkv = lax.optimization_barrier((cotangent[0], qkv))
    grad_y = gather_rel(cot_own)
    att_own, logs = vmem_call(
        partial(attend_forward_kernel, heads_own),
        "attend_forward",
        (
            jax.ShapeDtypeStruct((feats, n_tok), low_type),
            jax.ShapeDtypeStruct((8, n_tok), full_type),
        ),
        [],
        4 * pair_count * head_dim,
        pair_count,
        [qkv],
        0,
    )
    att_far = swap(permute_blocks(att_own, 2), 2)
    att_near = swap(permute_blocks(att_own, 1), 1)
    att_cross = swap(permute_blocks(att_far, 1), 1)

    bias_ff = lax.dynamic_index_in_dim(
        bias_full[9:13].reshape(n_shard, n_seq, ff_cell), q_own, 1, keepdims=False
    ).reshape(ff_own)
    bias_mlp = jnp.stack([bias_full[8], bias_full[13], bias_ff])
    attended, out_own, residual, branch_a, normed_m, inverse_m, *mlp_out = (
        vmem_call(
            partial(mlp_kernel, n_piece),
            "mlp",
            (
                jax.ShapeDtypeStruct((width, n_tok), low_type),
                jax.ShapeDtypeStruct((feats, width), low_type),
                jax.ShapeDtypeStruct((tok_dev, width), full_type),
                jax.ShapeDtypeStruct((tok_dev, width), full_type),
                jax.ShapeDtypeStruct((tok_dev, width), full_type),
                jax.ShapeDtypeStruct((tok_dev, 1), full_type),
                jax.ShapeDtypeStruct((n_tok, width), low_type),
                jax.ShapeDtypeStruct((n_tok, width), low_type),
                jax.ShapeDtypeStruct((8, width), full_type),
            )
            + n_piece * (jax.ShapeDtypeStruct((width // n_piece, width + ff_own), low_type),),
            [
                pltpu.VMEM((width, width + ff_own), low_type),
                pltpu.VMEM((width, width), low_type),
            ]
            + [pltpu.VMEM((n_tok, width), low_type)] * 4,
            14 * n_tok * width * width,
            n_tok * width,
            [
                table,
                att_own,
                att_near,
                att_far,
                att_cross,
                *stream,
                *grad_y,
                modulation,
                bias_mlp,
                *out_parts,
                rest_all,
            ],
        )
    )
    branch_part, grad_mod_part, sums_mlp, *grads_mlp = mlp_out
    mlp_total = ring_scatter(grads_mlp, n_shard)
    grad_mod_own = scatter_rel(grad_mod_part)
    grad_residual = grad_y[0].astype(full_type) + norm_back(
        grad_mod_own * (1.0 + scale_m), normed_m, inverse_m
    )
    grad_branch_own = (gate_a * grad_residual).astype(low_type)
    grad_branch_a = gather_rel(grad_branch_own)
    branch_part, mlp_total, *grad_branch_a = lax.optimization_barrier(
        (branch_part, mlp_total, *grad_branch_a)
    )
    grad_mod_a_part, sums_att, sums_qkv, *grads_att = vmem_call(
        partial(attend_backward_kernel, heads_own, n_piece),
        "attend_backward",
        (
            jax.ShapeDtypeStruct((n_tok, width), low_type),
            jax.ShapeDtypeStruct((8, width), full_type),
            jax.ShapeDtypeStruct((1, 3 * feats), full_type),
        )
        + n_piece * (jax.ShapeDtypeStruct((width // n_piece, 4 * feats), low_type),),
        [
            pltpu.VMEM((width, 4 * feats), low_type),
            pltpu.VMEM((n_tok, width), low_type),
            pltpu.VMEM((n_tok, feats), low_type),
            pltpu.VMEM((n_tok, feats), low_type),
            pltpu.VMEM((n_tok, 3 * feats), low_type),
            pltpu.VMEM((feats, n_tok), low_type),
            pltpu.VMEM((n_tok, feats), full_type),
            pltpu.VMEM((n_tok, feats), full_type),
        ],
        16 * n_tok * width * feats + 10 * pair_count * head_dim,
        pair_count,
        [
            table,
            *grad_branch_a,
            *stream,
            attended,
            out_own,
            qkv,
            logs,
            qkv_w,
            modulated_a,
        ],
    )
    grad_gate_a = token_sum(grad_residual * branch_a)
    grad_gate_m, grad_scale_m, grad_shift_m, sum_hidden, sum_branch_m = [
        sums_mlp[i] for i in range(5)
    ]
    grad_shift_a, grad_scale_a = sums_att[0], sums_att[1]
    qkv_sums = sums_qkv[0]
    normed_a, inverse_a = layer_norm(latents[0].astype(full_type))
    latents_grad = grad_residual + norm_back(
        scatter_rel(grad_mod_a_part) * (1.0 + scale_a), normed_a, inverse_a
    )
    branch_own = scatter_rel(branch_part) + bias_full[13]
    block_out = (residual + gate_m * branch_own).astype(low_type)

    def placed(own_part):
        whole = jnp.zeros((n_seq, own_part.shape[0]), full_type)
        return lax.dynamic_update_index_in_dim(whole, own_part, q_own, 0).reshape(-1)

    small = jnp.concatenate(
        [
            grad_shift_a,
            grad_scale_a,
            grad_gate_a,
            grad_shift_m,
            grad_scale_m,
            grad_gate_m,
            placed(qkv_sums[:feats]),
            placed(qkv_sums[2 * feats :]),
            token_sum(grad_branch_own),
            placed(sum_hidden),
            jnp.where(q_own == 0, sum_branch_m, 0.0),
        ]
    )
    small = small + swap(small, 1)
    small = small + swap(small, 2)
    every = spread(small, "shard", n_shard)
    grad_modulation = every[:, : 6 * width].astype(low_type)
    rest = jnp.sum(every[:, 6 * width :], 0)
    cuts = [width, 2 * width, 3 * width, 3 * width + ff]
    sum_query, sum_value, sum_out, sum_ff, sum_down = jnp.split(rest, cuts)
    bias_ada = jnp.sum(grad_modulation.astype(full_type), 0).reshape(6, width)
    bias_grad_all = jnp.concatenate(
        [
            bias_ada,
            sum_query.reshape(1, width),
            sum_value.reshape(1, width),
            sum_out[None],
            jnp.transpose(sum_ff.reshape(n_seq, n_shard, ff_cell), (1, 0, 2)).reshape(-1, width),
            sum_down[None],
        ]
    )
    bias_grad = lax.dynamic_slice_in_dim(bias_grad_all, s_own * rows, rows, 1)
    grad_ada = mm_tn(silu_cols, grad_modulation)
    grad_silu = mm_nt(grad_modulation, ada_low)
    _, silu_pull = jax.vjp(jax.nn.silu, cond_cols)
    grad_cols = silu_pull(grad_silu)[0]

    mlp_up, mlp_down = adam_call(
        adam_mlp_kernel,
        "adam_mlp",
        own_index,
        gather_rel(mlp_total),
        [up_weight, down_weight, up_first, down_first, up_second, down_second],
    )
    att_qkv, att_out = adam_call(
        adam_att_kernel,
        "adam_att",
        own_index,
        gather_rel(ring_scatter(grads_att, n_shard)),
        [qkv_weight, out_weight, qkv_first, out_first, qkv_second, out_second],
    )

    class_hot = (
        class_labels[:, None] == jnp.arange(class_table.shape[0], dtype=jnp.int32)[None, :]
    ).astype(full_type)
    time_hot = (
        time_buckets[:, None] == jnp.arange(time_table.shape[0], dtype=jnp.int32)[None, :]
    ).astype(full_type)
    class_grad = jnp.einsum("ln,lc->nc", class_hot, grad_cols, precision=lax.Precision.HIGHEST)
    time_grad = jnp.einsum("ln,lc->nc", time_hot, grad_cols, precision=lax.Precision.HIGHEST)
    updates = [
        adam_step(ada_weight, ada_first, ada_second, grad_ada),
        att_qkv,
        att_out,
        mlp_up,
        mlp_down,
        adam_step(biases, bias_first, bias_second, bias_grad),
    ]
    return (
        block_out[None],
        latents_grad[None],
        class_grad,
        time_grad,
        *[update[0] for update in updates],
        *[update[1] for update in updates],
        *[update[2] for update in updates],
    )


def solution(mesh):
    tokens = P("shard", "seq", None)
    rows = P("shard", None)
    cols = P(None, "shard")
    state = (rows, rows, rows, rows, rows, cols)
    return jax.shard_map(
        partial(shards, n_shard=mesh.shape["shard"], n_seq=mesh.shape["seq"]),
        mesh=mesh,
        in_specs=(tokens, tokens, P(), P(), P(), P()) + 3 * state,
        out_specs=(tokens, tokens, cols, cols) + 3 * state,
        check_vma=False,
    )
```

```python
import math
from functools import partial

import jax
import jax.numpy as jnp
from jax import lax
from jax.experimental import pallas as pl
from jax.experimental.pallas import tpu as pltpu
from jax.sharding import PartitionSpec as P

HEADS = 12
ADAM_STEP = 10
BLOCK = 256


norm_eps = 1e-06
beta_one = 0.9
beta_two = 0.999
learn_rate = 0.05
adam_eps = 1e-08

low_type = jnp.bfloat16
full_type = jnp.float32


def layer_norm(values_in):
    centred = values_in - jnp.mean(values_in, -1, keepdims=True)
    inverse = lax.rsqrt(jnp.mean(centred * centred, -1, keepdims=True) + norm_eps)
    return (centred * inverse, inverse)


def norm_back(gradient, normed, inverse):
    return inverse * (
        gradient
        - jnp.mean(gradient, -1, keepdims=True)
        - normed * jnp.mean(gradient * normed, -1, keepdims=True)
    )


def dot(left, right, dims):
    return lax.dot_general(left, right, (dims, ((), ())), preferred_element_type=full_type)


def mm(left, right):
    return dot(left, right, ((1,), (0,)))


def mm_nt(left, right):
    return dot(left, right, ((1,), (1,)))


def mm_tn(left, right):
    return dot(left, right, ((0,), (0,)))


def vmem_call(kernel, name, out_shape, scratch, flops, exps, operands, n_scalar=1, space=None):
    specs = [pl.BlockSpec(memory_space=pltpu.SMEM)] * n_scalar
    specs += [pl.BlockSpec(memory_space=space or pltpu.VMEM)] * (len(operands) - n_scalar)
    moved = sum(x.size * x.dtype.itemsize for x in operands)
    moved += sum(x.size * x.dtype.itemsize for x in out_shape)
    return pl.pallas_call(
        kernel,
        out_shape=out_shape,
        in_specs=specs,
        out_specs=tuple(pl.BlockSpec(memory_space=pltpu.VMEM) for _ in out_shape),
        scratch_shapes=scratch,
        compiler_params=pltpu.CompilerParams(vmem_limit_bytes=50 * 2**20),
        cost_estimate=pl.CostEstimate(flops=flops, bytes_accessed=moved, transcendentals=exps),
        name=name,
    )(*operands)


def assemble(table_ref, pieces, target):
    size = pieces[0].shape[0]
    for slot, piece in enumerate(pieces):
        target[pl.ds(pl.multiple_of(table_ref[slot] * size, size), size), :] = piece[...]


def cut_kernel(table_ref, qkv_all, out_all, up_all, down_all, first_ref, rest_ref, *scratch):
    held, sems = scratch[:4], scratch[4]
    qkv_ref, out_ref, up_ref, down_ref = held
    copies = []
    for source, target in zip((qkv_all, out_all, up_all, down_all), held):
        step = 768 if source.shape[1] > 768 else 256
        for start in range(0, source.shape[1], step):
            cut = (slice(None), pl.ds(start, step))
            copies.append(
                pltpu.make_async_copy(source.at[cut], target.at[cut], sems.at[len(copies)])
            )
    for copy in copies:
        copy.start()
    for copy in copies:
        copy.wait()
    rows, width = out_ref.shape
    feats = width // 4
    cell = down_ref.shape[0] // 4
    n_shard = up_ref.shape[1] // (4 * cell)
    for j in range(4):

        @pl.when(table_ref[0] == j)
        def _():
            for part in range(3):
                start = part * width + j * feats
                first_ref[:, part * feats : (part + 1) * feats] = qkv_ref[
                    :, start : start + feats
                ].astype(low_type)
            first_ref[:, 3 * feats :] = out_ref[:, j * feats : (j + 1) * feats].astype(low_type)
            for s in range(n_shard):
                start = (s * 4 + j) * cell
                rest_ref[:, s * cell : (s + 1) * cell] = up_ref[:, start : start + cell].astype(
                    low_type
                )
            rest_ref[:, width:] = down_ref[j * cell : (j + 1) * cell, :].astype(low_type)


def adam_mlp_kernel(table_ref, *refs):
    grads, state, outs = refs[:4], refs[4:10], refs[10:16]
    grad_up, grad_down = refs[16:]
    width = grad_down.shape[1]
    cell = grad_down.shape[0] // 4
    n_shard = grad_up.shape[1] // (4 * cell)
    for j in range(4):

        @pl.when(table_ref[0] == j)
        def _():
            for r in range(4):
                grad = grads[r][...].astype(full_type)
                for s in range(n_shard):
                    start = (s * 4 + (j ^ r)) * cell
                    grad_up[:, start : start + cell] = grad[:, s * cell : (s + 1) * cell]
                grad_down[(j ^ r) * cell : ((j ^ r) + 1) * cell, :] = grad[:, width:]

    for grad, part in ((grad_up, slice(0, 6, 2)), (grad_down, slice(1, 6, 2))):
        results = adam_step(*[ref[...] for ref in state[part]], grad[...])
        for ref, result in zip(outs[part], results):
            ref[...] = result


def adam_att_kernel(table_ref, *refs):
    grads, state, outs = refs[:4], refs[4:10], refs[10:16]
    grad_qkv, grad_out = refs[16:]
    width = grad_out.shape[1]
    feats = width // 4
    for j in range(4):

        @pl.when(table_ref[0] == j)
        def _():
            for r in range(4):
                grad = grads[r][...].astype(full_type)
                for part in range(3):
                    start = part * width + (j ^ r) * feats
                    grad_qkv[:, start : start + feats] = grad[:, part * feats : (part + 1) * feats]
                grad_out[:, (j ^ r) * feats : ((j ^ r) + 1) * feats] = grad[:, 3 * feats :]

    for grad, part in ((grad_qkv, slice(0, 6, 2)), (grad_out, slice(1, 6, 2))):
        results = adam_step(*[ref[...] for ref in state[part]], grad[...])
        for ref, result in zip(outs[part], results):
            ref[...] = result


def adam_call(kernel, name, own, grads, state):
    results = vmem_call(
        kernel,
        name,
        tuple(jax.ShapeDtypeStruct(x.shape, full_type) for x in state),
        [pltpu.VMEM(x.shape, full_type) for x in state[:2]],
        20 * (state[0].size + state[1].size),
        state[0].size + state[1].size,
        [own, *grads, *state],
    )
    return results[0::2], results[1::2]


def project_kernel(n_piece, table_ref, *refs):
    stream = refs[:4]
    mod_ref, bias_ref = refs[4:6]
    pieces = refs[6 : 6 + n_piece]
    low_ref, weight_ref, out_ref, qkv_ref = refs[6 + n_piece :]
    n_tok, cols = qkv_ref.shape
    size = pieces[0].shape[0]
    for slot, piece in enumerate(pieces):
        place = pl.ds(pl.multiple_of(table_ref[slot] * size, size), size)
        weight_ref[place, :] = piece[:, :cols]
        out_ref[place, :] = piece[:, cols:]
    for r in range(4):
        here = slice(r * n_tok // 4, (r + 1) * n_tok // 4)
        normed, _ = layer_norm(stream[r][: n_tok // 4, :].astype(full_type))
        low = (normed * (1.0 + mod_ref[1:2, :]) + mod_ref[0:1, :]).astype(low_type)
        low_ref[here, :] = low
        qkv_ref[here, :] = (mm(low, weight_ref[...]) + bias_ref[...]).astype(low_type)


def attend_forward_kernel(heads, qkv_ref, att_ref, log_ref):
    n_tok = qkv_ref.shape[0]
    feats = att_ref.shape[0]
    dim = feats // heads
    scale = dim ** (-0.5)
    log_ref[...] = jnp.zeros(log_ref.shape, full_type)

    def step(block, _):
        here = pl.ds(pl.multiple_of(block * BLOCK, BLOCK), BLOCK)
        for head in range(heads):
            queries = qkv_ref[here, head * dim : (head + 1) * dim] * scale
            keys = qkv_ref[:, feats + head * dim : feats + (head + 1) * dim]
            values = qkv_ref[:, 2 * feats + head * dim : 2 * feats + (head + 1) * dim]
            scores = mm_nt(queries.astype(low_type), keys)
            row_max = jnp.max(scores, -1, keepdims=True)
            expo = jnp.exp(scores - row_max)
            total = jnp.sum(expo, -1, keepdims=True)
            probs = (expo * (1.0 / total)).astype(low_type)
            att_ref[head * dim : (head + 1) * dim, here] = jnp.transpose(
                mm(probs, values)
            ).astype(low_type)
            logs = jnp.broadcast_to(row_max + jnp.log(total), (BLOCK, 128))
            log_ref[head : head + 1, here] = jnp.transpose(logs)[0:1]
        return 0

    lax.fori_loop(0, n_tok // BLOCK, step, 0)


def gelu_both(value):
    root = (2.0 / math.pi) ** 0.5
    square = value * value
    bend = jnp.tanh(root * value * (1.0 + 0.044715 * square))
    half = 0.5 * (1.0 + bend)
    slope = half + 0.5 * value * (1.0 - bend * bend) * (root * (1.0 + 3 * 0.044715 * square))
    return (value * half, slope)


def deal(table_ref, pieces, source):
    size = pieces[0].shape[0]
    for slot, piece in enumerate(pieces):
        piece[...] = source[pl.ds(pl.multiple_of(table_ref[slot] * size, size), size), :]


def mlp_kernel(n_piece, table_ref, *refs):
    att = refs[:4]
    tokens = refs[4:8]
    mod_ref, bias_ref = refs[8:10]
    out_parts = refs[10:14]
    pieces = refs[14 : 14 + n_piece]
    (
        att_all,
        out_own,
        residual_ref,
        branch_ref,
        normed_ref,
        inverse_ref,
        part_ref,
        back_ref,
        sums_ref,
    ) = refs[14 + n_piece : 23 + n_piece]
    dealt = refs[23 + n_piece : 23 + 2 * n_piece]
    weights, grads_ref, out_all, low_ref, act_ref, hid_ref, cot_ref = refs[23 + 2 * n_piece :]
    feats, n_tok = att[0].shape
    width = tokens[0].shape[1]
    size = n_tok // 4
    own = table_ref[n_piece]
    assemble(table_ref, pieces, weights)
    for r in range(4):
        start = pl.multiple_of((own ^ r) * feats, feats)
        att_all[pl.ds(start, feats), :] = att[r][...]
    for r in range(4):
        for j in range(4):

            @pl.when((own ^ r) == j)
            def _():
                out_all[:, j * feats : (j + 1) * feats] = out_parts[r][...]

    out_own[...] = out_all[pl.ds(pl.multiple_of(own * feats, feats), feats), :]
    shift_m, scale_m, gate_m = [mod_ref[i : i + 1, :] for i in (3, 4, 5)]
    totals = [jnp.zeros((1, width), full_type) for _ in range(5)]
    for r in range(4):
        here = slice(r * size, (r + 1) * size)
        branch = mm_tn(att_all[:, here], out_all[...]) + bias_ref[0:1, :]
        residual = tokens[r][:size, :].astype(full_type) + mod_ref[2:3, :] * branch
        if r == 0:
            residual_ref[...] = residual
            branch_ref[...] = branch
        normed, inverse = layer_norm(residual)
        if r == 0:
            normed_ref[...] = normed
            inverse_ref[...] = inverse
        low = (normed * (1.0 + scale_m) + shift_m).astype(low_type)
        low_ref[here, :] = low
        hidden = mm(low, weights[:, :width]) + bias_ref[2:3, :]
        active, slope = gelu_both(hidden)
        active = active.astype(low_type)
        act_ref[here, :] = active
        part = mm(active, weights[:, width:])
        part_ref[here, :] = part.astype(low_type)
        grad_y = tokens[r][size:, :].astype(full_type)
        totals[0] += jnp.sum(grad_y * part, 0, keepdims=True)
        if r == 0:
            totals[0] += jnp.sum(grad_y, 0, keepdims=True) * bias_ref[1:2, :]
        grad_low = (gate_m * grad_y).astype(low_type)
        cot_ref[here, :] = grad_low
        grad_hid = (mm_nt(grad_low, weights[:, width:]) * slope).astype(low_type)
        hid_ref[here, :] = grad_hid
        back = mm_nt(grad_hid, weights[:, :width])
        back_ref[here, :] = back.astype(low_type)
        totals[1] += jnp.sum(back * normed, 0, keepdims=True)
        totals[2] += jnp.sum(back, 0, keepdims=True)
        totals[3] += jnp.sum(grad_hid.astype(full_type), 0, keepdims=True)
        totals[4] += jnp.sum(grad_low.astype(full_type), 0, keepdims=True)
    sums_ref[...] = jnp.zeros(sums_ref.shape, full_type)
    sums_ref[3:4, :] = totals[2]
    sums_ref[4:5, :] = totals[1]
    sums_ref[5:6, :] = totals[0]
    sums_ref[pl.ds(9 + own, 1), :] = totals[3]
    sums_ref[13:14, :] = jnp.where(own == 0, totals[4], 0.0)
    grads_ref[:, :width] = mm_tn(low_ref[...], hid_ref[...]).astype(low_type)
    grads_ref[:, width:] = mm_tn(act_ref[...], cot_ref[...]).astype(low_type)
    deal(table_ref, dealt, grads_ref)


def attend_backward_kernel(heads, own_ref, *refs):
    grad = refs[:4]
    att_all, out_own, qkv_ref, log_ref, low_ref = refs[4:9]
    out_ref, grads_ref, sums_ref = refs[9:12]
    all_ref, cols_ref, grad_ref, keys_t, sum_k, sum_v = refs[12:]
    n_tok, width = low_ref.shape
    feats = out_own.shape[0]
    size = n_tok // 4
    dim = feats // heads
    scale = dim ** (-0.5)
    own = own_ref[0]
    for r in range(4):
        here = slice(r * size, (r + 1) * size)
        all_ref[here, :] = grad[r][...]
        grad_ref[here, :] = mm_nt(grad[r][...], out_own[...]).astype(low_type)
    for j in range(4):

        @pl.when(own == j)
        def _():
            cols_ref[...] = all_ref[:, j * feats : (j + 1) * feats]

    grads_ref[:, 3 * feats :] = mm(att_all[...], cols_ref[...]).astype(low_type)
    keys_t[...] = jnp.transpose(qkv_ref[:, feats : 2 * feats])
    sum_k[...] = jnp.zeros(sum_k.shape, full_type)
    sum_v[...] = jnp.zeros(sum_v.shape, full_type)

    def step(block, _):
        here = pl.ds(pl.multiple_of(block * BLOCK, BLOCK), BLOCK)
        for head in range(heads):
            cut = slice(head * dim, (head + 1) * dim)
            queries = (qkv_ref[here, cut] * scale).astype(low_type)
            keys = qkv_ref[:, feats + head * dim : feats + (head + 1) * dim]
            values = qkv_ref[:, 2 * feats + head * dim : 2 * feats + (head + 1) * dim]
            grad_att = grad_ref[here, cut]
            probs = jnp.exp(mm_nt(keys, queries) - log_ref[head : head + 1, here])
            grad_probs = mm_nt(values, grad_att)
            delta = jnp.sum(probs * grad_probs, 0, keepdims=True)
            grad_scores = (probs * (grad_probs - delta)).astype(low_type)
            sum_v[:, cut] += mm(probs.astype(low_type), grad_att)
            sum_k[:, cut] += mm(grad_scores, queries)
            grad_q = mm(keys_t[cut, :], grad_scores) * scale
            out_ref[here, cut] = jnp.transpose(grad_q).astype(low_type)
        return 0

    lax.fori_loop(0, n_tok // BLOCK, step, 0)
    out_ref[:, feats : 2 * feats] = sum_k[...].astype(low_type)
    out_ref[:, 2 * feats :] = sum_v[...].astype(low_type)
    grads_ref[:, : 3 * feats] = mm_tn(low_ref[...], out_ref[...]).astype(low_type)
    sums_ref[...] = jnp.zeros(sums_ref.shape, full_type)
    bias = jnp.sum(out_ref[...].astype(full_type), 0, keepdims=True)
    total = jnp.sum(all_ref[...].astype(full_type), 0, keepdims=True)
    sums_ref[8:9, :] = jnp.where(own == 0, total, 0.0)
    for j in range(4):

        @pl.when(own == j)
        def _():
            sums_ref[6:7, j * feats : (j + 1) * feats] = bias[:, :feats]
            sums_ref[7:8, j * feats : (j + 1) * feats] = bias[:, 2 * feats :]


def project_backward_kernel(*refs):
    tokens = refs[:4]
    grad_ref, weight_ref, gate_ref, sums_mlp, sums_att, back_ref, sums_ref = refs[4:]
    n_tok, width = back_ref.shape
    size = n_tok // 4
    totals = [jnp.zeros((1, width), full_type) for _ in range(2)]
    for r in range(4):
        here = slice(r * size, (r + 1) * size)
        back = mm_nt(grad_ref[here, :], weight_ref[...])
        back_ref[here, :] = back.astype(low_type)
        normed, _ = layer_norm(tokens[r][:size, :].astype(full_type))
        totals[0] += jnp.sum(back, 0, keepdims=True)
        totals[1] += jnp.sum(back * normed, 0, keepdims=True)
    sums_ref[...] = sums_mlp[...] + sums_att[...]
    sums_ref[0:1, :] = totals[0]
    sums_ref[1:2, :] = totals[1]
    sums_ref[2:3, :] = gate_ref[...]


def adam_step(weight, first, second, grad):
    first_new = beta_one * first + (1.0 - beta_one) * grad
    second_new = beta_two * second + (1.0 - beta_two) * grad * grad
    corr_one = 1.0 - beta_one**ADAM_STEP
    corr_two = 1.0 - beta_two**ADAM_STEP
    weight_new = weight - learn_rate * (first_new / corr_one) / (
        jnp.sqrt(second_new / corr_two) + adam_eps
    )
    return (weight_new, first_new, second_new)


def swap(value, distance):
    return lax.ppermute(value, "seq", [(p, p ^ distance) for p in range(4)])


def gather_rel(value):
    far = swap(value, 2)
    near = swap(value, 1)
    cross = swap(far, 1)
    return [value, near, far, cross]


def scatter_rel(low, follower=()):
    blocks = split_rows(low)
    near = [swap(blocks[1], 1), swap(blocks[3], 1)]
    if follower:
        *near, follower = lax.optimization_barrier((*near, follower))
    near_own, near_far = [x.astype(full_type) for x in near]
    far_own = swap((blocks[2].astype(full_type) + near_far).astype(low_type), 2)
    total = blocks[0].astype(full_type) + near_own + far_own.astype(full_type)
    return (total, follower) if follower else total


def split_rows(value):
    return [value[r * value.shape[0] // 4 : (r + 1) * value.shape[0] // 4] for r in range(4)]


def reorder(blocks, own):
    odd, high = (own & 1) == 1, own >= 2
    pairs = [jnp.where(odd, blocks[j ^ 1], blocks[j]) for j in range(4)]
    return [jnp.where(high, pairs[j ^ 2], pairs[j]) for j in range(4)]


CYCLE = (0, 2, 4, 6, 7, 5, 3, 1)


def ring_pairs(count):
    right = [(CYCLE[i], CYCLE[(i + 1) % count]) for i in range(count)]
    return right, [(to, start) for start, to in right]


def ring_hop(pieces, count):
    if count != len(CYCLE):
        return pieces
    right, left = ring_pairs(count)
    hop = len(pieces) // 2
    ahead, behind = (pieces[-2], pieces[-1]) if hop else (pieces[0], pieces[0])
    more = [lax.ppermute(ahead, "shard", right)]
    if hop < count // 2 - 1:
        more.append(lax.ppermute(behind, "shard", left))
    return pieces + more


def ring_begin(value, count):
    if count != len(CYCLE):
        return [spread(value, "shard", count).reshape(-1, value.shape[-1])]
    return ring_hop([value], count)


def ring_scatter(pieces, count):
    if len(pieces) == 1:
        whole = pieces[0].reshape(count, -1, pieces[0].shape[-1])
        arrived = lax.all_to_all(whole, "shard", 0, 0, tiled=True)
        return jnp.sum(arrived.astype(full_type), 0).astype(low_type)
    right, left = ring_pairs(count)
    ahead, behind = pieces[count - 1], pieces[count - 3]
    for hop in range(count // 2, 0, -1):
        ahead = lax.ppermute(ahead, "shard", right)
        if hop > 1:
            ahead = (ahead.astype(full_type) + pieces[2 * hop - 2].astype(full_type)).astype(
                low_type
            )
    for hop in range(count // 2 - 1, 0, -1):
        behind = lax.ppermute(behind, "shard", left)
        if hop > 1:
            behind = (behind.astype(full_type) + pieces[2 * hop - 3].astype(full_type)).astype(
                low_type
            )
    return (
        pieces[0].astype(full_type) + ahead.astype(full_type) + behind.astype(full_type)
    ).astype(low_type)


def ring_table(own, count):
    if count != len(CYCLE):
        return jnp.zeros((1,), jnp.int32)
    lines = []
    for s in range(count):
        at = CYCLE.index(s)
        line = [s]
        for hop in range(1, count // 2 + 1):
            line.append(CYCLE[(at - hop) % count])
            if hop < count // 2:
                line.append(CYCLE[(at + hop) % count])
        lines.append(line)
    return lax.dynamic_index_in_dim(jnp.array(lines, jnp.int32), own, 0, keepdims=False)


def permute_blocks(value, distance):
    size = value.shape[1] // 4
    return jnp.concatenate(
        [value[:, (r ^ distance) * size : ((r ^ distance) + 1) * size] for r in range(4)], 1
    )


def spread(value, axis, count):
    return lax.all_to_all(
        jnp.broadcast_to(value[None], (count,) + value.shape), axis, 0, 0, tiled=True
    )


def token_sum(tensor):
    return jnp.sum(tensor.astype(full_type), axis=0)


def shards(
    latents,
    cotangent,
    class_labels,
    time_buckets,
    class_table,
    time_table,
    ada_weight,
    qkv_weight,
    out_weight,
    up_weight,
    down_weight,
    biases,
    ada_first,
    qkv_first,
    out_first,
    up_first,
    down_first,
    bias_first,
    ada_second,
    qkv_second,
    out_second,
    up_second,
    down_second,
    bias_second,
    n_shard,
    n_seq,
):
    assert n_seq == 4 and latents.shape[0] == 1 and class_labels.shape[0] == n_shard
    s_own = lax.axis_index("shard")
    q_own = lax.axis_index("seq")
    tok_dev, width = latents.shape[1:]
    head_dim = width // HEADS
    score_scale = head_dim ** (-0.5)
    heads_own = HEADS // n_seq
    feats = heads_own * head_dim
    rows = ada_weight.shape[0]
    ff = up_weight.shape[1]
    ff_cell = ff // (n_shard * n_seq)
    ff_own = ff // n_seq

    table = jnp.concatenate([ring_table(s_own, n_shard), q_own[None].astype(jnp.int32)])
    own_index = q_own[None].astype(jnp.int32)
    first_part, rest_part = vmem_call(
        cut_kernel,
        "cut",
        (
            jax.ShapeDtypeStruct((rows, 4 * feats), low_type),
            jax.ShapeDtypeStruct((rows, width + ff_own), low_type),
        ),
        [pltpu.VMEM(x.shape, full_type) for x in (qkv_weight, out_weight, up_weight, down_weight)]
        + [pltpu.SemaphoreType.DMA((16,))],
        0,
        0,
        [own_index, qkv_weight, out_weight, up_weight, down_weight],
        space=pl.ANY,
    )
    first_pieces = ring_begin(first_part, n_shard)

    cond = jnp.take(class_table, class_labels, axis=0).astype(full_type) + jnp.take(
        time_table, time_buckets, axis=0
    ).astype(full_type)
    cond_cols = lax.dynamic_slice_in_dim(cond, s_own * rows, rows, 1)
    silu_cols = jax.nn.silu(cond_cols).astype(low_type)
    ada_low = ada_weight.astype(low_type)
    mod_partial = mm(silu_cols, ada_low)
    bias_low = biases.astype(low_type).astype(full_type).reshape(1, -1)
    payload = jnp.concatenate(
        [mod_partial, jnp.broadcast_to(bias_low, (n_shard, bias_low.shape[1]))], 1
    )
    payload, *first_pieces = lax.optimization_barrier((payload, *first_pieces))
    arrived = lax.all_to_all(payload, "shard", split_axis=0, concat_axis=0, tiled=True)
    for _ in range(3):
        first_pieces = ring_hop(first_pieces, n_shard)
    n_piece = len(first_pieces)
    mod_sum = jnp.sum(arrived[:, : 6 * width], 0)
    bias_full = jnp.transpose(
        arrived[:, 6 * width :].reshape(n_shard, biases.shape[0], rows), (1, 0, 2)
    ).reshape(biases.shape[0], width)
    modulation = mod_sum.reshape(6, width) + bias_full[0:6]
    shift_a, scale_a, gate_a, shift_m, scale_m, gate_m = [modulation[i] for i in range(6)]

    tokens = gather_rel(jnp.concatenate([latents[0], cotangent[0]]))
    n_tok = n_seq * tok_dev

    bias_query = lax.dynamic_slice_in_dim(bias_full[6], q_own * feats, feats)
    bias_value = lax.dynamic_slice_in_dim(bias_full[7], q_own * feats, feats)
    bias_qkv = jnp.concatenate([bias_query, jnp.zeros_like(bias_query), bias_value])[None]
    pair_count = heads_own * n_tok * n_tok
    modulated_a, qkv_w, out_q, qkv = vmem_call(
        partial(project_kernel, n_piece),
        "project",
        (
            jax.ShapeDtypeStruct((n_tok, width), low_type),
            jax.ShapeDtypeStruct((width, 3 * feats), low_type),
            jax.ShapeDtypeStruct((width, feats), low_type),
            jax.ShapeDtypeStruct((n_tok, 3 * feats), low_type),
        ),
        [],
        6 * n_tok * width * feats,
        n_tok,
        [table, *tokens, modulation, bias_qkv, *first_pieces],
    )
    out_parts = gather_rel(out_q)
    rest_pieces = ring_begin(rest_part, n_shard)
    qkv, *rest_pieces = lax.optimization_barrier((qkv, *rest_pieces))
    rest_pieces = ring_hop(rest_pieces, n_shard)
    att_own, logs = vmem_call(
        partial(attend_forward_kernel, heads_own),
        "attend_forward",
        (
            jax.ShapeDtypeStruct((feats, n_tok), low_type),
            jax.ShapeDtypeStruct((8, n_tok), full_type),
        ),
        [],
        4 * pair_count * head_dim,
        pair_count,
        [qkv],
        0,
    )
    att_own, out_parts, rest_pieces = lax.optimization_barrier((att_own, out_parts, rest_pieces))
    for _ in range(2):
        rest_pieces = ring_hop(rest_pieces, n_shard)
    att_far = swap(permute_blocks(att_own, 2), 2)
    att_near = swap(permute_blocks(att_own, 1), 1)
    att_cross = swap(permute_blocks(att_far, 1), 1)

    bias_ff = lax.dynamic_index_in_dim(
        bias_full[9:13].reshape(n_shard, n_seq, ff_cell), q_own, 1, keepdims=False
    ).reshape(ff_own)
    bias_mlp = jnp.stack([bias_full[8], bias_full[13], bias_ff])
    attended, out_own, residual, branch_a, normed_m, inverse_m, *mlp_out = (
        vmem_call(
            partial(mlp_kernel, n_piece),
            "mlp",
            (
                jax.ShapeDtypeStruct((width, n_tok), low_type),
                jax.ShapeDtypeStruct((feats, width), low_type),
                jax.ShapeDtypeStruct((tok_dev, width), full_type),
                jax.ShapeDtypeStruct((tok_dev, width), full_type),
                jax.ShapeDtypeStruct((tok_dev, width), full_type),
                jax.ShapeDtypeStruct((tok_dev, 1), full_type),
                jax.ShapeDtypeStruct((n_tok, width), low_type),
                jax.ShapeDtypeStruct((n_tok, width), low_type),
                jax.ShapeDtypeStruct((16, width), full_type),
            )
            + n_piece * (jax.ShapeDtypeStruct((width // n_piece, width + ff_own), low_type),),
            [
                pltpu.VMEM((width, width + ff_own), low_type),
                pltpu.VMEM((width, width + ff_own), low_type),
                pltpu.VMEM((width, width), low_type),
            ]
            + [pltpu.VMEM((n_tok, width), low_type)] * 4,
            14 * n_tok * width * width,
            n_tok * width,
            [
                table,
                att_own,
                att_near,
                att_far,
                att_cross,
                *tokens,
                modulation,
                bias_mlp,
                *out_parts,
                *rest_pieces,
            ],
        )
    )
    branch_part, grad_mod_part, sums_mlp, *grads_mlp = mlp_out
    grad_mod_own, grads_mlp = scatter_rel(grad_mod_part, grads_mlp)
    mlp_total = ring_scatter(grads_mlp, n_shard)
    grad_residual = cotangent[0].astype(full_type) + norm_back(
        grad_mod_own * (1.0 + scale_m), normed_m, inverse_m
    )
    grad_branch_own = (gate_a * grad_residual).astype(low_type)
    grad_branch_a = gather_rel(grad_branch_own)
    branch_part, mlp_total, *grad_branch_a = lax.optimization_barrier(
        (branch_part, mlp_total, *grad_branch_a)
    )
    grad_gate_a = token_sum(grad_residual * branch_a)
    grad_qkv, grads_att, sums_att = vmem_call(
        partial(attend_backward_kernel, heads_own),
        "attend_backward",
        (
            jax.ShapeDtypeStruct((n_tok, 3 * feats), low_type),
            jax.ShapeDtypeStruct((width, 4 * feats), low_type),
            jax.ShapeDtypeStruct((16, width), full_type),
        ),
        [
            pltpu.VMEM((n_tok, width), low_type),
            pltpu.VMEM((n_tok, feats), low_type),
            pltpu.VMEM((n_tok, feats), low_type),
            pltpu.VMEM((feats, n_tok), low_type),
            pltpu.VMEM((n_tok, feats), full_type),
            pltpu.VMEM((n_tok, feats), full_type),
        ],
        10 * n_tok * width * feats + 10 * pair_count * head_dim,
        pair_count,
        [own_index, *grad_branch_a, attended, out_own, qkv, logs, modulated_a],
    )
    grad_mod_a_part, small = vmem_call(
        project_backward_kernel,
        "project_backward",
        (
            jax.ShapeDtypeStruct((n_tok, width), low_type),
            jax.ShapeDtypeStruct((16, width), full_type),
        ),
        [],
        6 * n_tok * width * feats,
        n_tok,
        [*tokens, grad_qkv, qkv_w, grad_gate_a[None], sums_mlp, sums_att],
        0,
    )
    arrived_att = lax.all_to_all(
        grads_att.reshape(n_shard, rows, 4 * feats), "shard", 0, 0, tiled=True
    )
    normed_a, inverse_a = layer_norm(latents[0].astype(full_type))
    latents_grad = grad_residual + norm_back(
        scatter_rel(grad_mod_a_part) * (1.0 + scale_a), normed_a, inverse_a
    )
    branch_own = scatter_rel(branch_part) + bias_full[13]
    block_out = (residual + gate_m * branch_own).astype(low_type)

    small = small + swap(small, 1)
    small = small + swap(small, 2)
    small, arrived_att = lax.optimization_barrier((small, arrived_att))
    every = spread(small, "shard", n_shard)
    grad_modulation = every[:, :6].reshape(n_shard, 6 * width).astype(low_type)
    rest = jnp.sum(every[:, 6:14], 0)
    rest_ff = jnp.transpose(rest[3:7].reshape(n_seq, n_shard, ff_cell), (1, 0, 2))
    bias_ada = jnp.sum(grad_modulation.astype(full_type), 0).reshape(6, width)
    bias_grad_all = jnp.concatenate([bias_ada, rest[:3], rest_ff.reshape(-1, width), rest[7:8]])
    bias_grad = lax.dynamic_slice_in_dim(bias_grad_all, s_own * rows, rows, 1)
    grad_ada = mm_tn(silu_cols, grad_modulation)
    grad_silu = mm_nt(grad_modulation, ada_low)
    _, silu_pull = jax.vjp(jax.nn.silu, cond_cols)
    grad_cols = silu_pull(grad_silu)[0]

    att_total = jnp.sum(arrived_att.astype(full_type), 0).astype(low_type)
    mlp_up, mlp_down = adam_call(
        adam_mlp_kernel,
        "adam_mlp",
        own_index,
        gather_rel(mlp_total),
        [up_weight, down_weight, up_first, down_first, up_second, down_second],
    )
    att_qkv, att_out = adam_call(
        adam_att_kernel,
        "adam_att",
        own_index,
        gather_rel(att_total),
        [qkv_weight, out_weight, qkv_first, out_first, qkv_second, out_second],
    )

    class_hot = (
        class_labels[:, None] == jnp.arange(class_table.shape[0], dtype=jnp.int32)[None, :]
    ).astype(full_type)
    time_hot = (
        time_buckets[:, None] == jnp.arange(time_table.shape[0], dtype=jnp.int32)[None, :]
    ).astype(full_type)
    class_grad = jnp.einsum("ln,lc->nc", class_hot, grad_cols, precision=lax.Precision.HIGHEST)
    time_grad = jnp.einsum("ln,lc->nc", time_hot, grad_cols, precision=lax.Precision.HIGHEST)
    updates = [
        adam_step(ada_weight, ada_first, ada_second, grad_ada),
        att_qkv,
        att_out,
        mlp_up,
        mlp_down,
        adam_step(biases, bias_first, bias_second, bias_grad),
    ]
    return (
        block_out[None],
        latents_grad[None],
        class_grad,
        time_grad,
        *[update[0] for update in updates],
        *[update[1] for update in updates],
        *[update[2] for update in updates],
    )


def solution(mesh):
    tokens = P("shard", "seq", None)
    rows = P("shard", None)
    cols = P(None, "shard")
    state = (rows, rows, rows, rows, rows, cols)
    return jax.shard_map(
        partial(shards, n_shard=mesh.shape["shard"], n_seq=mesh.shape["seq"]),
        mesh=mesh,
        in_specs=(tokens, tokens, P(), P(), P(), P()) + 3 * state,
        out_specs=(tokens, tokens, cols, cols) + 3 * state,
        check_vma=False,
    )
```

```python
import math
from functools import partial

import jax
import jax.numpy as jnp
from jax import lax
from jax.experimental import pallas as pl
from jax.experimental.pallas import tpu as pltpu
from jax.sharding import PartitionSpec as P

HEADS = 12
ADAM_STEP = 10
BLOCK = 256


norm_eps = 1e-06
beta_one = 0.9
beta_two = 0.999
learn_rate = 0.05
adam_eps = 1e-08

low_type = jnp.bfloat16
full_type = jnp.float32


def layer_norm(values_in):
    centred = values_in - jnp.mean(values_in, -1, keepdims=True)
    inverse = lax.rsqrt(jnp.mean(centred * centred, -1, keepdims=True) + norm_eps)
    return (centred * inverse, inverse)


def norm_back(gradient, normed, inverse):
    return inverse * (
        gradient
        - jnp.mean(gradient, -1, keepdims=True)
        - normed * jnp.mean(gradient * normed, -1, keepdims=True)
    )


def dot(left, right, dims):
    return lax.dot_general(left, right, (dims, ((), ())), preferred_element_type=full_type)


def mm(left, right):
    return dot(left, right, ((1,), (0,)))


def mm_nt(left, right):
    return dot(left, right, ((1,), (1,)))


def mm_tn(left, right):
    return dot(left, right, ((0,), (0,)))


def vmem_call(kernel, name, out_shape, scratch, flops, exps, operands, n_scalar=1, space=None, grant=32):
    specs = [pl.BlockSpec(memory_space=pltpu.SMEM)] * n_scalar
    specs += [pl.BlockSpec(memory_space=space or pltpu.VMEM)] * (len(operands) - n_scalar)
    moved = sum(x.size * x.dtype.itemsize for x in operands)
    moved += sum(x.size * x.dtype.itemsize for x in out_shape)
    return pl.pallas_call(
        kernel,
        out_shape=out_shape,
        in_specs=specs,
        out_specs=tuple(pl.BlockSpec(memory_space=pltpu.VMEM) for _ in out_shape),
        scratch_shapes=scratch,
        compiler_params=pltpu.CompilerParams(vmem_limit_bytes=grant * 2**20),
        cost_estimate=pl.CostEstimate(flops=flops, bytes_accessed=moved, transcendentals=exps),
        name=name,
    )(*operands)


def assemble(table_ref, pieces, target):
    size = pieces[0].shape[0]
    for slot, piece in enumerate(pieces):
        target[pl.ds(pl.multiple_of(table_ref[slot] * size, size), size), :] = piece[...]


def cut_kernel(table_ref, qkv_all, out_all, up_all, down_all, first_ref, rest_ref, *scratch):
    held, sems = scratch[:4], scratch[4]
    qkv_ref, out_ref, up_ref, down_ref = held
    copies = []
    for source, target in zip((qkv_all, out_all, up_all, down_all), held):
        step = 768 if source.shape[1] > 768 else 256
        for start in range(0, source.shape[1], step):
            cut = (slice(None), pl.ds(start, step))
            copies.append(
                pltpu.make_async_copy(source.at[cut], target.at[cut], sems.at[len(copies)])
            )
    for copy in copies:
        copy.start()
    for copy in copies:
        copy.wait()
    rows, width = out_ref.shape
    feats = width // 4
    cell = down_ref.shape[0] // 4
    n_shard = up_ref.shape[1] // (4 * cell)
    for j in range(4):

        @pl.when(table_ref[0] == j)
        def _():
            for part in range(3):
                start = part * width + j * feats
                first_ref[:, part * feats : (part + 1) * feats] = qkv_ref[
                    :, start : start + feats
                ].astype(low_type)
            first_ref[:, 3 * feats :] = out_ref[:, j * feats : (j + 1) * feats].astype(low_type)
            for s in range(n_shard):
                start = (s * 4 + j) * cell
                rest_ref[:, s * cell : (s + 1) * cell] = up_ref[:, start : start + cell].astype(
                    low_type
                )
            rest_ref[:, width:] = down_ref[j * cell : (j + 1) * cell, :].astype(low_type)


def adam_mlp_kernel(table_ref, *refs):
    grads, state, outs = refs[:4], refs[4:10], refs[10:16]
    grad_up, grad_down = refs[16:]
    width = grad_down.shape[1]
    cell = grad_down.shape[0] // 4
    n_shard = grad_up.shape[1] // (4 * cell)
    for j in range(4):

        @pl.when(table_ref[0] == j)
        def _():
            for r in range(4):
                grad = grads[r][...].astype(full_type)
                for s in range(n_shard):
                    start = (s * 4 + (j ^ r)) * cell
                    grad_up[:, start : start + cell] = grad[:, s * cell : (s + 1) * cell]
                grad_down[(j ^ r) * cell : ((j ^ r) + 1) * cell, :] = grad[:, width:]

    for grad, part in ((grad_up, slice(0, 6, 2)), (grad_down, slice(1, 6, 2))):
        results = adam_step(*[ref[...] for ref in state[part]], grad[...])
        for ref, result in zip(outs[part], results):
            ref[...] = result


def adam_att_kernel(table_ref, *refs):
    grads, state, outs = refs[:4], refs[4:10], refs[10:16]
    grad_qkv, grad_out = refs[16:]
    width = grad_out.shape[1]
    feats = width // 4
    for j in range(4):

        @pl.when(table_ref[0] == j)
        def _():
            for r in range(4):
                grad = grads[r][...].astype(full_type)
                for part in range(3):
                    start = part * width + (j ^ r) * feats
                    grad_qkv[:, start : start + feats] = grad[:, part * feats : (part + 1) * feats]
                grad_out[:, (j ^ r) * feats : ((j ^ r) + 1) * feats] = grad[:, 3 * feats :]

    for grad, part in ((grad_qkv, slice(0, 6, 2)), (grad_out, slice(1, 6, 2))):
        results = adam_step(*[ref[...] for ref in state[part]], grad[...])
        for ref, result in zip(outs[part], results):
            ref[...] = result


def adam_call(kernel, name, own, grads, state):
    results = vmem_call(
        kernel,
        name,
        tuple(jax.ShapeDtypeStruct(x.shape, full_type) for x in state),
        [pltpu.VMEM(x.shape, full_type) for x in state[:2]],
        20 * (state[0].size + state[1].size),
        state[0].size + state[1].size,
        [own, *grads, *state],
    )
    return results[0::2], results[1::2]


def project_kernel(n_piece, table_ref, *refs):
    stream = refs[:4]
    mod_ref, bias_ref = refs[4:6]
    pieces = refs[6 : 6 + n_piece]
    low_ref, weight_ref, out_ref, qkv_ref = refs[6 + n_piece :]
    n_tok, cols = qkv_ref.shape
    size = pieces[0].shape[0]
    for slot, piece in enumerate(pieces):
        place = pl.ds(pl.multiple_of(table_ref[slot] * size, size), size)
        weight_ref[place, :] = piece[:, :cols]
        out_ref[place, :] = piece[:, cols:]
    for r in range(4):
        here = slice(r * n_tok // 4, (r + 1) * n_tok // 4)
        normed, _ = layer_norm(stream[r][: n_tok // 4, :].astype(full_type))
        low = (normed * (1.0 + mod_ref[1:2, :]) + mod_ref[0:1, :]).astype(low_type)
        low_ref[here, :] = low
        qkv_ref[here, :] = (mm(low, weight_ref[...]) + bias_ref[...]).astype(low_type)


def attend_forward_kernel(heads, qkv_ref, att_ref, log_ref):
    n_tok = qkv_ref.shape[0]
    feats = att_ref.shape[0]
    dim = feats // heads
    scale = dim ** (-0.5)
    log_ref[...] = jnp.zeros(log_ref.shape, full_type)

    def step(block, _):
        here = pl.ds(pl.multiple_of(block * BLOCK, BLOCK), BLOCK)
        for head in range(heads):
            queries = qkv_ref[here, head * dim : (head + 1) * dim] * scale
            keys = qkv_ref[:, feats + head * dim : feats + (head + 1) * dim]
            values = qkv_ref[:, 2 * feats + head * dim : 2 * feats + (head + 1) * dim]
            scores = mm_nt(queries.astype(low_type), keys)
            row_max = jnp.max(scores, -1, keepdims=True)
            expo = jnp.exp(scores - row_max)
            total = jnp.sum(expo, -1, keepdims=True)
            probs = (expo * (1.0 / total)).astype(low_type)
            att_ref[head * dim : (head + 1) * dim, here] = jnp.transpose(
                mm(probs, values)
            ).astype(low_type)
            logs = jnp.broadcast_to(row_max + jnp.log(total), (BLOCK, 128))
            log_ref[head : head + 1, here] = jnp.transpose(logs)[0:1]
        return 0

    lax.fori_loop(0, n_tok // BLOCK, step, 0)


def gelu_both(value):
    root = (2.0 / math.pi) ** 0.5
    square = value * value
    bend = jnp.tanh(root * value * (1.0 + 0.044715 * square))
    half = 0.5 * (1.0 + bend)
    slope = half + 0.5 * value * (1.0 - bend * bend) * (root * (1.0 + 3 * 0.044715 * square))
    return (value * half, slope)


def deal(table_ref, pieces, source):
    size = pieces[0].shape[0]
    for slot, piece in enumerate(pieces):
        piece[...] = source[pl.ds(pl.multiple_of(table_ref[slot] * size, size), size), :]


def mlp_kernel(n_piece, table_ref, *refs):
    att = refs[:4]
    tokens = refs[4:8]
    mod_ref, bias_ref = refs[8:10]
    out_parts = refs[10:14]
    pieces = refs[14 : 14 + n_piece]
    (
        att_all,
        out_own,
        residual_ref,
        branch_ref,
        *more,
        sums_ref,
    ) = refs[14 + n_piece : 31 + n_piece]
    normed_refs, inverse_refs, part_refs, back_refs = more[:2], more[2:4], more[4:8], more[8:12]
    dealt = refs[31 + n_piece : 31 + 2 * n_piece]
    weights, grads_ref, out_all, low_ref, act_ref, hid_ref, cot_ref = refs[31 + 2 * n_piece :]
    feats, n_tok = att[0].shape
    width = tokens[0].shape[1]
    size = n_tok // 4
    own = table_ref[n_piece]
    assemble(table_ref, pieces, weights)
    for r in range(4):
        start = pl.multiple_of((own ^ r) * feats, feats)
        att_all[pl.ds(start, feats), :] = att[r][...]
    for r in range(4):
        for j in range(4):

            @pl.when((own ^ r) == j)
            def _():
                out_all[:, j * feats : (j + 1) * feats] = out_parts[r][...]

    out_own[...] = out_all[pl.ds(pl.multiple_of(own * feats, feats), feats), :]
    shift_m, scale_m, gate_m = [mod_ref[i : i + 1, :] for i in (3, 4, 5)]
    totals = [jnp.zeros((1, width), full_type) for _ in range(5)]
    for r in range(4):
        here = slice(r * size, (r + 1) * size)
        branch = mm_tn(att_all[:, here], out_all[...]) + bias_ref[0:1, :]
        residual = tokens[r][:size, :].astype(full_type) + mod_ref[2:3, :] * branch
        if r == 0:
            residual_ref[...] = residual
            branch_ref[...] = branch
        normed, inverse = layer_norm(residual)
        if r % 2 == 0:
            normed_refs[r // 2][...] = normed
            inverse_refs[r // 2][...] = inverse
        low = (normed * (1.0 + scale_m) + shift_m).astype(low_type)
        low_ref[here, :] = low
        hidden = mm(low, weights[:, :width]) + bias_ref[2:3, :]
        active, slope = gelu_both(hidden)
        active = active.astype(low_type)
        act_ref[here, :] = active
        part = mm(active, weights[:, width:])
        part_refs[r][...] = part.astype(low_type)
        grad_y = tokens[r][size:, :].astype(full_type)
        totals[0] += jnp.sum(grad_y * part, 0, keepdims=True)
        if r == 0:
            totals[0] += jnp.sum(grad_y, 0, keepdims=True) * bias_ref[1:2, :]
        grad_low = (gate_m * grad_y).astype(low_type)
        cot_ref[here, :] = grad_low
        grad_hid = (mm_nt(grad_low, weights[:, width:]) * slope).astype(low_type)
        hid_ref[here, :] = grad_hid
        back = mm_nt(grad_hid, weights[:, :width])
        back_refs[r][...] = back.astype(low_type)
        totals[1] += jnp.sum(back * normed, 0, keepdims=True)
        totals[2] += jnp.sum(back, 0, keepdims=True)
        totals[3] += jnp.sum(grad_hid.astype(full_type), 0, keepdims=True)
        totals[4] += jnp.sum(grad_low.astype(full_type), 0, keepdims=True)
    sums_ref[...] = jnp.zeros(sums_ref.shape, full_type)
    sums_ref[3:4, :] = totals[2]
    sums_ref[4:5, :] = totals[1]
    sums_ref[5:6, :] = totals[0]
    sums_ref[pl.ds(9 + own, 1), :] = totals[3]
    sums_ref[13:14, :] = jnp.where(own == 0, totals[4], 0.0)
    grads_ref[:, :width] = mm_tn(low_ref[...], hid_ref[...]).astype(low_type)
    grads_ref[:, width:] = mm_tn(act_ref[...], cot_ref[...]).astype(low_type)
    deal(table_ref, dealt, grads_ref)


def attend_backward_kernel(heads, own_ref, *refs):
    grad = refs[:4]
    att_all, out_own, qkv_ref, log_ref, low_ref = refs[4:9]
    out_ref, grads_ref, sums_ref = refs[9:12]
    all_ref, cols_ref, grad_ref, keys_t, sum_k, sum_v = refs[12:]
    n_tok, width = low_ref.shape
    feats = out_own.shape[0]
    size = n_tok // 4
    dim = feats // heads
    scale = dim ** (-0.5)
    own = own_ref[0]
    for r in range(4):
        here = slice(r * size, (r + 1) * size)
        all_ref[here, :] = grad[r][...]
        grad_ref[here, :] = mm_nt(grad[r][...], out_own[...]).astype(low_type)
    for j in range(4):

        @pl.when(own == j)
        def _():
            cols_ref[...] = all_ref[:, j * feats : (j + 1) * feats]

    grads_ref[:, 3 * feats :] = mm(att_all[...], cols_ref[...]).astype(low_type)
    keys_t[...] = jnp.transpose(qkv_ref[:, feats : 2 * feats])
    sum_k[...] = jnp.zeros(sum_k.shape, full_type)
    sum_v[...] = jnp.zeros(sum_v.shape, full_type)

    def step(block, _):
        here = pl.ds(pl.multiple_of(block * BLOCK, BLOCK), BLOCK)
        for head in range(heads):
            cut = slice(head * dim, (head + 1) * dim)
            queries = (qkv_ref[here, cut] * scale).astype(low_type)
            keys = qkv_ref[:, feats + head * dim : feats + (head + 1) * dim]
            values = qkv_ref[:, 2 * feats + head * dim : 2 * feats + (head + 1) * dim]
            grad_att = grad_ref[here, cut]
            probs = jnp.exp(mm_nt(keys, queries) - log_ref[head : head + 1, here])
            grad_probs = mm_nt(values, grad_att)
            delta = jnp.sum(probs * grad_probs, 0, keepdims=True)
            grad_scores = (probs * (grad_probs - delta)).astype(low_type)
            sum_v[:, cut] += mm(probs.astype(low_type), grad_att)
            sum_k[:, cut] += mm(grad_scores, queries)
            grad_q = mm(keys_t[cut, :], grad_scores) * scale
            out_ref[here, cut] = jnp.transpose(grad_q).astype(low_type)
        return 0

    lax.fori_loop(0, n_tok // BLOCK, step, 0)
    out_ref[:, feats : 2 * feats] = sum_k[...].astype(low_type)
    out_ref[:, 2 * feats :] = sum_v[...].astype(low_type)
    grads_ref[:, : 3 * feats] = mm_tn(low_ref[...], out_ref[...]).astype(low_type)
    sums_ref[...] = jnp.zeros(sums_ref.shape, full_type)
    bias = jnp.sum(out_ref[...].astype(full_type), 0, keepdims=True)
    total = jnp.sum(all_ref[...].astype(full_type), 0, keepdims=True)
    sums_ref[8:9, :] = jnp.where(own == 0, total, 0.0)
    for j in range(4):

        @pl.when(own == j)
        def _():
            sums_ref[6:7, j * feats : (j + 1) * feats] = bias[:, :feats]
            sums_ref[7:8, j * feats : (j + 1) * feats] = bias[:, 2 * feats :]


def project_backward_kernel(*refs):
    tokens = refs[:4]
    grad_ref, weight_ref, gate_ref, sums_mlp, sums_att = refs[4:9]
    back_refs, sums_ref = refs[9:13], refs[13]
    size, width = back_refs[0].shape
    totals = [jnp.zeros((1, width), full_type) for _ in range(2)]
    for r in range(4):
        here = slice(r * size, (r + 1) * size)
        back = mm_nt(grad_ref[here, :], weight_ref[...])
        back_refs[r][...] = back.astype(low_type)
        normed, _ = layer_norm(tokens[r][:size, :].astype(full_type))
        totals[0] += jnp.sum(back, 0, keepdims=True)
        totals[1] += jnp.sum(back * normed, 0, keepdims=True)
    sums_ref[...] = sums_mlp[...] + sums_att[...]
    sums_ref[0:1, :] = totals[0]
    sums_ref[1:2, :] = totals[1]
    sums_ref[2:3, :] = gate_ref[...]


def adam_step(weight, first, second, grad):
    first_new = beta_one * first + (1.0 - beta_one) * grad
    second_new = beta_two * second + (1.0 - beta_two) * grad * grad
    corr_one = 1.0 - beta_one**ADAM_STEP
    corr_two = 1.0 - beta_two**ADAM_STEP
    weight_new = weight - learn_rate * (first_new / corr_one) / (
        jnp.sqrt(second_new / corr_two) + adam_eps
    )
    return (weight_new, first_new, second_new)


def swap(value, distance):
    return lax.ppermute(value, "seq", [(p, p ^ distance) for p in range(4)])


def gather_rel(value):
    far = swap(value, 2)
    near = swap(value, 1)
    cross = swap(far, 1)
    return [value, near, far, cross]


def scatter_rel(blocks):
    near_own, near_far = [swap(blocks[r], 1).astype(full_type) for r in (1, 3)]
    far_own = swap((blocks[2].astype(full_type) + near_far).astype(low_type), 2)
    return blocks[0].astype(full_type) + near_own + far_own.astype(full_type)


CYCLE = (0, 2, 4, 6, 7, 5, 3, 1)


def ring_pairs(count):
    right = [(CYCLE[i], CYCLE[(i + 1) % count]) for i in range(count)]
    return right, [(to, start) for start, to in right]


def ring_hop(pieces, count):
    if count != len(CYCLE):
        return pieces
    right, left = ring_pairs(count)
    hop = len(pieces) // 2
    ahead, behind = (pieces[-2], pieces[-1]) if hop else (pieces[0], pieces[0])
    more = [lax.ppermute(ahead, "shard", right)]
    if hop < count // 2 - 1:
        more.append(lax.ppermute(behind, "shard", left))
    return pieces + more


def ring_begin(value, count):
    if count != len(CYCLE):
        return [spread(value, "shard", count).reshape(-1, value.shape[-1])]
    return ring_hop([value], count)


def ring_scatter(pieces, count):
    if len(pieces) == 1:
        whole = pieces[0].reshape(count, -1, pieces[0].shape[-1])
        arrived = lax.all_to_all(whole, "shard", 0, 0, tiled=True)
        return jnp.sum(arrived.astype(full_type), 0).astype(low_type)
    right, left = ring_pairs(count)
    ahead, behind = pieces[count - 1], pieces[count - 3]
    for hop in range(count // 2, 0, -1):
        ahead = lax.ppermute(ahead, "shard", right)
        if hop > 1:
            ahead = (ahead.astype(full_type) + pieces[2 * hop - 2].astype(full_type)).astype(
                low_type
            )
    for hop in range(count // 2 - 1, 0, -1):
        behind = lax.ppermute(behind, "shard", left)
        if hop > 1:
            behind = (behind.astype(full_type) + pieces[2 * hop - 3].astype(full_type)).astype(
                low_type
            )
    return (
        pieces[0].astype(full_type) + ahead.astype(full_type) + behind.astype(full_type)
    ).astype(low_type)


def ring_table(own, count):
    if count != len(CYCLE):
        return jnp.zeros((1,), jnp.int32)
    lines = []
    for s in range(count):
        at = CYCLE.index(s)
        line = [s]
        for hop in range(1, count // 2 + 1):
            line.append(CYCLE[(at - hop) % count])
            if hop < count // 2:
                line.append(CYCLE[(at + hop) % count])
        lines.append(line)
    return lax.dynamic_index_in_dim(jnp.array(lines, jnp.int32), own, 0, keepdims=False)


def permute_blocks(value, distance):
    size = value.shape[1] // 4
    return jnp.concatenate(
        [value[:, (r ^ distance) * size : ((r ^ distance) + 1) * size] for r in range(4)], 1
    )


def spread(value, axis, count):
    return lax.all_to_all(
        jnp.broadcast_to(value[None], (count,) + value.shape), axis, 0, 0, tiled=True
    )


def token_sum(tensor):
    return jnp.sum(tensor.astype(full_type), axis=0)


def shards(
    latents,
    cotangent,
    class_labels,
    time_buckets,
    class_table,
    time_table,
    ada_weight,
    qkv_weight,
    out_weight,
    up_weight,
    down_weight,
    biases,
    ada_first,
    qkv_first,
    out_first,
    up_first,
    down_first,
    bias_first,
    ada_second,
    qkv_second,
    out_second,
    up_second,
    down_second,
    bias_second,
    n_shard,
    n_seq,
):
    assert n_seq == 4 and latents.shape[0] == 1 and class_labels.shape[0] == n_shard
    s_own = lax.axis_index("shard")
    q_own = lax.axis_index("seq")
    tok_dev, width = latents.shape[1:]
    head_dim = width // HEADS
    score_scale = head_dim ** (-0.5)
    heads_own = HEADS // n_seq
    feats = heads_own * head_dim
    rows = ada_weight.shape[0]
    ff = up_weight.shape[1]
    ff_cell = ff // (n_shard * n_seq)
    ff_own = ff // n_seq

    table = jnp.concatenate([ring_table(s_own, n_shard), q_own[None].astype(jnp.int32)])
    own_index = q_own[None].astype(jnp.int32)
    first_part, rest_part = vmem_call(
        cut_kernel,
        "cut",
        (
            jax.ShapeDtypeStruct((rows, 4 * feats), low_type),
            jax.ShapeDtypeStruct((rows, width + ff_own), low_type),
        ),
        [pltpu.VMEM(x.shape, full_type) for x in (qkv_weight, out_weight, up_weight, down_weight)]
        + [pltpu.SemaphoreType.DMA((16,))],
        0,
        0,
        [own_index, qkv_weight, out_weight, up_weight, down_weight],
        space=pl.ANY,
        grant=60,
    )
    first_pieces = ring_begin(first_part, n_shard)

    cond = jnp.take(class_table, class_labels, axis=0).astype(full_type) + jnp.take(
        time_table, time_buckets, axis=0
    ).astype(full_type)
    cond_cols = lax.dynamic_slice_in_dim(cond, s_own * rows, rows, 1)
    silu_cols = jax.nn.silu(cond_cols).astype(low_type)
    ada_low = ada_weight.astype(low_type)
    mod_partial = mm(silu_cols, ada_low)
    bias_low = biases.astype(low_type).astype(full_type).reshape(1, -1)
    payload = jnp.concatenate(
        [mod_partial, jnp.broadcast_to(bias_low, (n_shard, bias_low.shape[1]))], 1
    )
    payload, *first_pieces = lax.optimization_barrier((payload, *first_pieces))
    arrived = lax.all_to_all(payload, "shard", split_axis=0, concat_axis=0, tiled=True)
    for _ in range(2):
        first_pieces = ring_hop(first_pieces, n_shard)
    both = jnp.concatenate([latents[0], cotangent[0]])
    far, first_pieces = lax.optimization_barrier((swap(both, 2), first_pieces))
    tokens = [both, swap(both, 1), far, swap(far, 1)]
    first_pieces = ring_hop(first_pieces, n_shard)
    n_piece = len(first_pieces)
    mod_sum = jnp.sum(arrived[:, : 6 * width], 0)
    bias_full = jnp.transpose(
        arrived[:, 6 * width :].reshape(n_shard, biases.shape[0], rows), (1, 0, 2)
    ).reshape(biases.shape[0], width)
    modulation = mod_sum.reshape(6, width) + bias_full[0:6]
    shift_a, scale_a, gate_a, shift_m, scale_m, gate_m = [modulation[i] for i in range(6)]

    n_tok = n_seq * tok_dev

    bias_query = lax.dynamic_slice_in_dim(bias_full[6], q_own * feats, feats)
    bias_value = lax.dynamic_slice_in_dim(bias_full[7], q_own * feats, feats)
    bias_qkv = jnp.concatenate([bias_query, jnp.zeros_like(bias_query), bias_value])[None]
    pair_count = heads_own * n_tok * n_tok
    modulated_a, qkv_w, out_q, qkv = vmem_call(
        partial(project_kernel, n_piece),
        "project",
        (
            jax.ShapeDtypeStruct((n_tok, width), low_type),
            jax.ShapeDtypeStruct((width, 3 * feats), low_type),
            jax.ShapeDtypeStruct((width, feats), low_type),
            jax.ShapeDtypeStruct((n_tok, 3 * feats), low_type),
        ),
        [],
        6 * n_tok * width * feats,
        n_tok,
        [table, *tokens, modulation, bias_qkv, *first_pieces],
    )
    out_far = swap(out_q, 2)
    rest_pieces = ring_begin(rest_part, n_shard)
    qkv, *rest_pieces = lax.optimization_barrier((qkv, *rest_pieces))
    rest_pieces = ring_hop(rest_pieces, n_shard)
    att_own, logs = vmem_call(
        partial(attend_forward_kernel, heads_own),
        "attend_forward",
        (
            jax.ShapeDtypeStruct((feats, n_tok), low_type),
            jax.ShapeDtypeStruct((8, n_tok), full_type),
        ),
        [],
        4 * pair_count * head_dim,
        pair_count,
        [qkv],
        0,
    )
    att_own, out_far, rest_pieces = lax.optimization_barrier((att_own, out_far, rest_pieces))
    out_parts = [out_q, swap(out_q, 1), out_far, swap(out_far, 1)]
    rest_pieces = ring_hop(rest_pieces, n_shard)
    att_far = swap(permute_blocks(att_own, 2), 2)
    att_far, rest_pieces = lax.optimization_barrier((att_far, rest_pieces))
    rest_pieces = ring_hop(rest_pieces, n_shard)
    att_near = swap(permute_blocks(att_own, 1), 1)
    att_cross = swap(permute_blocks(att_far, 1), 1)

    bias_ff = lax.dynamic_index_in_dim(
        bias_full[9:13].reshape(n_shard, n_seq, ff_cell), q_own, 1, keepdims=False
    ).reshape(ff_own)
    bias_mlp = jnp.stack([bias_full[8], bias_full[13], bias_ff])
    attended, out_own, residual, branch_a, *mlp_out = (
        vmem_call(
            partial(mlp_kernel, n_piece),
            "mlp",
            (
                jax.ShapeDtypeStruct((width, n_tok), low_type),
                jax.ShapeDtypeStruct((feats, width), low_type),
            )
            + 4 * (jax.ShapeDtypeStruct((tok_dev, width), full_type),)
            + 2 * (jax.ShapeDtypeStruct((tok_dev, 1), full_type),)
            + 8 * (jax.ShapeDtypeStruct((tok_dev, width), low_type),)
            + (jax.ShapeDtypeStruct((16, width), full_type),)
            + n_piece * (jax.ShapeDtypeStruct((width // n_piece, width + ff_own), low_type),),
            [
                pltpu.VMEM((width, width + ff_own), low_type),
                pltpu.VMEM((width, width + ff_own), low_type),
                pltpu.VMEM((width, width), low_type),
            ]
            + [pltpu.VMEM((n_tok, width), low_type)] * 4,
            14 * n_tok * width * width,
            n_tok * width,
            [
                table,
                att_own,
                att_near,
                att_far,
                att_cross,
                *tokens,
                modulation,
                bias_mlp,
                *out_parts,
                *rest_pieces,
            ],
        )
    )
    normed_m, inverse_m = mlp_out[:2], mlp_out[2:4]
    branch_part, back, sums_mlp, grads_mlp = mlp_out[4:8], mlp_out[8:12], mlp_out[12], mlp_out[13:]
    near_zero, near_two, grads_mlp = lax.optimization_barrier(
        (swap(back[1], 1), swap(back[3], 1), grads_mlp)
    )
    chip = [
        (mine.astype(full_type) + theirs.astype(full_type)).astype(low_type)
        for mine, theirs in ((back[0], near_zero), (back[2], near_two))
    ]
    across = [swap(chip[1], 2), swap(chip[0], 2)]
    mlp_total = ring_scatter(grads_mlp, n_shard)
    grad_residuals = [
        tokens[2 * i][tok_dev:].astype(full_type)
        + norm_back(
            (chip[i].astype(full_type) + across[i].astype(full_type)) * (1.0 + scale_m),
            normed_m[i],
            inverse_m[i],
        )
        for i in range(2)
    ]
    grad_residual = grad_residuals[0]
    grad_low = [(gate_a * part).astype(low_type) for part in grad_residuals]
    grad_branch_a = [grad_low[0], swap(grad_low[0], 1), grad_low[1], swap(grad_low[1], 1)]
    across, branch_part = lax.optimization_barrier((across, branch_part))
    branch_near = swap(branch_part[1], 1)
    branch_chip = branch_part[2].astype(full_type) + swap(branch_part[3], 1).astype(full_type)
    branch_far = swap(branch_chip.astype(low_type), 2)
    mlp_total, grad_branch_a = lax.optimization_barrier((mlp_total, grad_branch_a))
    mlp_far = swap(mlp_total, 2)
    grad_gate_a = token_sum(grad_residual * branch_a)
    grad_qkv, grads_att, sums_att = vmem_call(
        partial(attend_backward_kernel, heads_own),
        "attend_backward",
        (
            jax.ShapeDtypeStruct((n_tok, 3 * feats), low_type),
            jax.ShapeDtypeStruct((width, 4 * feats), low_type),
            jax.ShapeDtypeStruct((16, width), full_type),
        ),
        [
            pltpu.VMEM((n_tok, width), low_type),
            pltpu.VMEM((n_tok, feats), low_type),
            pltpu.VMEM((n_tok, feats), low_type),
            pltpu.VMEM((feats, n_tok), low_type),
            pltpu.VMEM((n_tok, feats), full_type),
            pltpu.VMEM((n_tok, feats), full_type),
        ],
        10 * n_tok * width * feats + 10 * pair_count * head_dim,
        pair_count,
        [own_index, *grad_branch_a, attended, out_own, qkv, logs, modulated_a],
    )
    grad_qkv, mlp_far, branch_far = lax.optimization_barrier((grad_qkv, mlp_far, branch_far))
    *grad_mod_a_part, small = vmem_call(
        project_backward_kernel,
        "project_backward",
        4 * (jax.ShapeDtypeStruct((tok_dev, width), low_type),)
        + (jax.ShapeDtypeStruct((16, width), full_type),),
        [],
        6 * n_tok * width * feats,
        n_tok,
        [*tokens, grad_qkv, qkv_w, grad_gate_a[None], sums_mlp, sums_att],
        0,
    )
    arrived_att = lax.all_to_all(
        grads_att.reshape(n_shard, rows, 4 * feats), "shard", 0, 0, tiled=True
    )
    normed_a, inverse_a = layer_norm(latents[0].astype(full_type))
    latents_grad = grad_residual + norm_back(
        scatter_rel(grad_mod_a_part) * (1.0 + scale_a), normed_a, inverse_a
    )
    branch_own = sum(x.astype(full_type) for x in (branch_part[0], branch_near, branch_far))
    branch_own = branch_own + bias_full[13]
    block_out = (residual + gate_m * branch_own).astype(low_type)

    small = small + swap(small, 1)
    small = small + swap(small, 2)
    small, arrived_att = lax.optimization_barrier((small, arrived_att))
    every = spread(small, "shard", n_shard)
    grad_modulation = every[:, :6].reshape(n_shard, 6 * width).astype(low_type)
    rest = jnp.sum(every[:, 6:14], 0)
    rest_ff = jnp.transpose(rest[3:7].reshape(n_seq, n_shard, ff_cell), (1, 0, 2))
    bias_ada = jnp.sum(grad_modulation.astype(full_type), 0).reshape(6, width)
    bias_grad_all = jnp.concatenate([bias_ada, rest[:3], rest_ff.reshape(-1, width), rest[7:8]])
    bias_grad = lax.dynamic_slice_in_dim(bias_grad_all, s_own * rows, rows, 1)
    grad_ada = mm_tn(silu_cols, grad_modulation)
    grad_silu = mm_nt(grad_modulation, ada_low)
    _, silu_pull = jax.vjp(jax.nn.silu, cond_cols)
    grad_cols = silu_pull(grad_silu)[0]

    att_total = jnp.sum(arrived_att.astype(full_type), 0).astype(low_type)
    mlp_up, mlp_down = adam_call(
        adam_mlp_kernel,
        "adam_mlp",
        own_index,
        [mlp_total, swap(mlp_total, 1), mlp_far, swap(mlp_far, 1)],
        [up_weight, down_weight, up_first, down_first, up_second, down_second],
    )
    att_qkv, att_out = adam_call(
        adam_att_kernel,
        "adam_att",
        own_index,
        gather_rel(att_total),
        [qkv_weight, out_weight, qkv_first, out_first, qkv_second, out_second],
    )

    class_hot = (
        class_labels[:, None] == jnp.arange(class_table.shape[0], dtype=jnp.int32)[None, :]
    ).astype(full_type)
    time_hot = (
        time_buckets[:, None] == jnp.arange(time_table.shape[0], dtype=jnp.int32)[None, :]
    ).astype(full_type)
    class_grad = jnp.einsum("ln,lc->nc", class_hot, grad_cols, precision=lax.Precision.HIGHEST)
    time_grad = jnp.einsum("ln,lc->nc", time_hot, grad_cols, precision=lax.Precision.HIGHEST)
    updates = [
        adam_step(ada_weight, ada_first, ada_second, grad_ada),
        att_qkv,
        att_out,
        mlp_up,
        mlp_down,
        adam_step(biases, bias_first, bias_second, bias_grad),
    ]
    return (
        block_out[None],
        latents_grad[None],
        class_grad,
        time_grad,
        *[update[0] for update in updates],
        *[update[1] for update in updates],
        *[update[2] for update in updates],
    )


def solution(mesh):
    tokens = P("shard", "seq", None)
    rows = P("shard", None)
    cols = P(None, "shard")
    state = (rows, rows, rows, rows, rows, cols)
    return jax.shard_map(
        partial(shards, n_shard=mesh.shape["shard"], n_seq=mesh.shape["seq"]),
        mesh=mesh,
        in_specs=(tokens, tokens, P(), P(), P(), P()) + 3 * state,
        out_specs=(tokens, tokens, cols, cols) + 3 * state,
        check_vma=False,
    )
```

```python
import math
from functools import partial

import jax
import jax.numpy as jnp
from jax import lax
from jax.experimental import pallas as pl
from jax.experimental.pallas import tpu as pltpu
from jax.sharding import PartitionSpec as P

HEADS = 12
ADAM_STEP = 10
BLOCK = 256


norm_eps = 1e-06
beta_one = 0.9
beta_two = 0.999
learn_rate = 0.05
adam_eps = 1e-08

low_type = jnp.bfloat16
full_type = jnp.float32


def layer_norm(values_in):
    centred = values_in - jnp.mean(values_in, -1, keepdims=True)
    inverse = lax.rsqrt(jnp.mean(centred * centred, -1, keepdims=True) + norm_eps)
    return (centred * inverse, inverse)


def norm_back(gradient, normed, inverse):
    return inverse * (
        gradient
        - jnp.mean(gradient, -1, keepdims=True)
        - normed * jnp.mean(gradient * normed, -1, keepdims=True)
    )


def dot(left, right, dims):
    return lax.dot_general(left, right, (dims, ((), ())), preferred_element_type=full_type)


def mm(left, right):
    return dot(left, right, ((1,), (0,)))


def mm_nt(left, right):
    return dot(left, right, ((1,), (1,)))


def mm_tn(left, right):
    return dot(left, right, ((0,), (0,)))


def vmem_call(kernel, name, out_shape, scratch, flops, exps, operands, n_scalar=1, space=None, grant=50):
    specs = [pl.BlockSpec(memory_space=pltpu.SMEM)] * n_scalar
    specs += [pl.BlockSpec(memory_space=space or pltpu.VMEM)] * (len(operands) - n_scalar)
    moved = sum(x.size * x.dtype.itemsize for x in operands)
    moved += sum(x.size * x.dtype.itemsize for x in out_shape)
    return pl.pallas_call(
        kernel,
        out_shape=out_shape,
        in_specs=specs,
        out_specs=tuple(pl.BlockSpec(memory_space=pltpu.VMEM) for _ in out_shape),
        scratch_shapes=scratch,
        compiler_params=pltpu.CompilerParams(vmem_limit_bytes=grant * 2**20),
        cost_estimate=pl.CostEstimate(flops=flops, bytes_accessed=moved, transcendentals=exps),
        name=name,
    )(*operands)


def assemble(table_ref, pieces, target):
    size = pieces[0].shape[0]
    for slot, piece in enumerate(pieces):
        target[pl.ds(pl.multiple_of(table_ref[slot] * size, size), size), :] = piece[...]


def cut_kernel(table_ref, qkv_all, out_all, up_all, down_all, first_ref, rest_ref, *scratch):
    held, sems = scratch[:4], scratch[4]
    qkv_ref, out_ref, up_ref, down_ref = held
    copies = []
    for source, target in zip((qkv_all, out_all, up_all, down_all), held):
        step = 768 if source.shape[1] > 768 else 256
        for start in range(0, source.shape[1], step):
            cut = (slice(None), pl.ds(start, step))
            copies.append(
                pltpu.make_async_copy(source.at[cut], target.at[cut], sems.at[len(copies)])
            )
    for copy in copies:
        copy.start()
    for copy in copies:
        copy.wait()
    rows, width = out_ref.shape
    feats = width // 4
    cell = down_ref.shape[0] // 4
    n_shard = up_ref.shape[1] // (4 * cell)
    for j in range(4):

        @pl.when(table_ref[0] == j)
        def _():
            for part in range(3):
                start = part * width + j * feats
                first_ref[:, part * feats : (part + 1) * feats] = qkv_ref[
                    :, start : start + feats
                ].astype(low_type)
            first_ref[:, 3 * feats :] = out_ref[:, j * feats : (j + 1) * feats].astype(low_type)
            for s in range(n_shard):
                start = (s * 4 + j) * cell
                rest_ref[:, s * cell : (s + 1) * cell] = up_ref[:, start : start + cell].astype(
                    low_type
                )
            rest_ref[:, width:] = down_ref[j * cell : (j + 1) * cell, :].astype(low_type)


def adam_mlp_kernel(table_ref, *refs):
    grads, state, outs = refs[:4], refs[4:10], refs[10:16]
    grad_up, grad_down = refs[16:]
    width = grad_down.shape[1]
    cell = grad_down.shape[0] // 4
    n_shard = grad_up.shape[1] // (4 * cell)
    for j in range(4):

        @pl.when(table_ref[0] == j)
        def _():
            for r in range(4):
                grad = grads[r][...].astype(full_type)
                for s in range(n_shard):
                    start = (s * 4 + (j ^ r)) * cell
                    grad_up[:, start : start + cell] = grad[:, s * cell : (s + 1) * cell]
                grad_down[(j ^ r) * cell : ((j ^ r) + 1) * cell, :] = grad[:, width:]

    for grad, part in ((grad_up, slice(0, 6, 2)), (grad_down, slice(1, 6, 2))):
        results = adam_step(*[ref[...] for ref in state[part]], grad[...])
        for ref, result in zip(outs[part], results):
            ref[...] = result


def adam_att_kernel(table_ref, *refs):
    grads, state, outs = refs[:4], refs[4:10], refs[10:16]
    grad_qkv, grad_out = refs[16:]
    width = grad_out.shape[1]
    feats = width // 4
    for j in range(4):

        @pl.when(table_ref[0] == j)
        def _():
            for r in range(4):
                grad = grads[r][...].astype(full_type)
                for part in range(3):
                    start = part * width + (j ^ r) * feats
                    grad_qkv[:, start : start + feats] = grad[:, part * feats : (part + 1) * feats]
                grad_out[:, (j ^ r) * feats : ((j ^ r) + 1) * feats] = grad[:, 3 * feats :]

    for grad, part in ((grad_qkv, slice(0, 6, 2)), (grad_out, slice(1, 6, 2))):
        results = adam_step(*[ref[...] for ref in state[part]], grad[...])
        for ref, result in zip(outs[part], results):
            ref[...] = result


def finish_kernel(n_shard, place_ref, label_ref, bucket_ref, *refs):
    every_ref, silu_ref, cond_ref = refs[:3]
    ada, bias = refs[3:6], refs[6:9]
    ada_out, bias_out, class_ref, time_ref = refs[9:12], refs[12:15], refs[15], refs[16]
    sums_ref, bias_grad, cols_ref = refs[17:]
    rows = cond_ref.shape[1]
    width = every_ref.shape[2]
    grad_silu = jnp.zeros((n_shard, rows), full_type)
    for slot in range(6):
        cut = slice(slot * width, (slot + 1) * width)
        grad_mod = every_ref[:, slot, :].astype(low_type)
        weight = ada[0][:, cut]
        results = adam_step(
            weight, ada[1][:, cut], ada[2][:, cut], mm_tn(silu_ref[...], grad_mod)
        )
        for ref, result in zip(ada_out, results):
            ref[:, cut] = result
        grad_silu += mm_nt(grad_mod, weight.astype(low_type))
        sums_ref[slot : slot + 1, :] = jnp.sum(grad_mod.astype(full_type), 0, keepdims=True)
    for slot in range(6, 14):
        sums_ref[slot : slot + 1, :] = jnp.sum(every_ref[:, slot, :], 0, keepdims=True)
    for s in range(n_shard):

        @pl.when(place_ref[0] == s)
        def _():
            for slot in range(14):
                row, cell = slot, s
                if 9 <= slot < 13:
                    row, cell = 9 + s % 4, (n_shard * (slot - 9) + s) // 4
                bias_grad[slot : slot + 1, :] = sums_ref[
                    row : row + 1, cell * rows : (cell + 1) * rows
                ]

    results = adam_step(*[ref[...] for ref in bias], bias_grad[...])
    for ref, result in zip(bias_out, results):
        ref[...] = result
    cond = cond_ref[...]
    gate = 1.0 / (1.0 + jnp.exp(-cond))
    cols_ref[...] = grad_silu * (gate * (1.0 + cond * (1.0 - gate)))
    for index_ref, table in ((label_ref, class_ref), (bucket_ref, time_ref)):
        table[...] = jnp.zeros(table.shape, full_type)
        for latent in range(n_shard):
            place = pl.ds(index_ref[latent], 1)
            table[place, :] = table[place, :] + cols_ref[latent : latent + 1, :]


def adam_call(kernel, name, own, grads, state):
    results = vmem_call(
        kernel,
        name,
        tuple(jax.ShapeDtypeStruct(x.shape, full_type) for x in state),
        [pltpu.VMEM(x.shape, full_type) for x in state[:2]],
        20 * (state[0].size + state[1].size),
        state[0].size + state[1].size,
        [own, *grads, *state],
    )
    return results[0::2], results[1::2]


def project_kernel(n_piece, table_ref, *refs):
    stream = refs[:4]
    mod_ref, bias_ref = refs[4:6]
    pieces = refs[6 : 6 + n_piece]
    low_ref, weight_ref, out_ref, qkv_ref = refs[6 + n_piece :]
    n_tok, cols = qkv_ref.shape
    size = pieces[0].shape[0]
    for slot, piece in enumerate(pieces):
        place = pl.ds(pl.multiple_of(table_ref[slot] * size, size), size)
        weight_ref[place, :] = piece[:, :cols]
        out_ref[place, :] = piece[:, cols:]
    for r in range(4):
        here = slice(r * n_tok // 4, (r + 1) * n_tok // 4)
        normed, _ = layer_norm(stream[r][: n_tok // 4, :].astype(full_type))
        low = (normed * (1.0 + mod_ref[1:2, :]) + mod_ref[0:1, :]).astype(low_type)
        low_ref[here, :] = low
        qkv_ref[here, :] = (mm(low, weight_ref[...]) + bias_ref[...]).astype(low_type)


def attend_forward_kernel(heads, qkv_ref, att_ref, log_ref):
    n_tok = qkv_ref.shape[0]
    feats = att_ref.shape[0]
    dim = feats // heads
    scale = dim ** (-0.5)
    log_ref[...] = jnp.zeros(log_ref.shape, full_type)

    def step(block, _):
        here = pl.ds(pl.multiple_of(block * BLOCK, BLOCK), BLOCK)
        for head in range(heads):
            queries = qkv_ref[here, head * dim : (head + 1) * dim] * scale
            keys = qkv_ref[:, feats + head * dim : feats + (head + 1) * dim]
            values = qkv_ref[:, 2 * feats + head * dim : 2 * feats + (head + 1) * dim]
            scores = mm_nt(queries.astype(low_type), keys)
            row_max = jnp.max(scores, -1, keepdims=True)
            expo = jnp.exp(scores - row_max)
            total = jnp.sum(expo, -1, keepdims=True)
            probs = (expo * (1.0 / total)).astype(low_type)
            att_ref[head * dim : (head + 1) * dim, here] = jnp.transpose(
                mm(probs, values)
            ).astype(low_type)
            logs = jnp.broadcast_to(row_max + jnp.log(total), (BLOCK, 128))
            log_ref[head : head + 1, here] = jnp.transpose(logs)[0:1]
        return 0

    lax.fori_loop(0, n_tok // BLOCK, step, 0)


def gelu_both(value):
    root = (2.0 / math.pi) ** 0.5
    square = value * value
    bend = jnp.tanh(root * value * (1.0 + 0.044715 * square))
    half = 0.5 * (1.0 + bend)
    slope = half + 0.5 * value * (1.0 - bend * bend) * (root * (1.0 + 3 * 0.044715 * square))
    return (value * half, slope)


def deal(table_ref, pieces, source):
    size = pieces[0].shape[0]
    for slot, piece in enumerate(pieces):
        piece[...] = source[pl.ds(pl.multiple_of(table_ref[slot] * size, size), size), :]


def mlp_kernel(n_piece, table_ref, *refs):
    att = refs[:4]
    tokens = refs[4:8]
    mod_ref, bias_ref = refs[8:10]
    out_parts = refs[10:14]
    pieces = refs[14 : 14 + n_piece]
    (
        att_all,
        out_own,
        residual_ref,
        branch_ref,
        *more,
        sums_ref,
    ) = refs[14 + n_piece : 31 + n_piece]
    normed_refs, inverse_refs, part_refs, back_refs = more[:2], more[2:4], more[4:8], more[8:12]
    dealt = refs[31 + n_piece : 31 + 2 * n_piece]
    weights, grads_ref, out_all, low_ref, act_ref, hid_ref, cot_ref = refs[31 + 2 * n_piece :]
    feats, n_tok = att[0].shape
    width = tokens[0].shape[1]
    size = n_tok // 4
    own = table_ref[n_piece]
    assemble(table_ref, pieces, weights)
    for r in range(4):
        start = pl.multiple_of((own ^ r) * feats, feats)
        att_all[pl.ds(start, feats), :] = att[r][...]
    for r in range(4):
        for j in range(4):

            @pl.when((own ^ r) == j)
            def _():
                out_all[:, j * feats : (j + 1) * feats] = out_parts[r][...]

    out_own[...] = out_all[pl.ds(pl.multiple_of(own * feats, feats), feats), :]
    shift_m, scale_m, gate_m = [mod_ref[i : i + 1, :] for i in (3, 4, 5)]
    totals = [jnp.zeros((1, width), full_type) for _ in range(5)]
    for r in range(4):
        here = slice(r * size, (r + 1) * size)
        branch = mm_tn(att_all[:, here], out_all[...]) + bias_ref[0:1, :]
        residual = tokens[r][:size, :].astype(full_type) + mod_ref[2:3, :] * branch
        if r == 0:
            residual_ref[...] = residual
            branch_ref[...] = branch
        normed, inverse = layer_norm(residual)
        if r % 2 == 0:
            normed_refs[r // 2][...] = normed
            inverse_refs[r // 2][...] = inverse
        low = (normed * (1.0 + scale_m) + shift_m).astype(low_type)
        low_ref[here, :] = low
        hidden = mm(low, weights[:, :width]) + bias_ref[2:3, :]
        active, slope = gelu_both(hidden)
        active = active.astype(low_type)
        act_ref[here, :] = active
        part = mm(active, weights[:, width:])
        part_refs[r][...] = part.astype(low_type)
        grad_y = tokens[r][size:, :].astype(full_type)
        totals[0] += jnp.sum(grad_y * part, 0, keepdims=True)
        if r == 0:
            totals[0] += jnp.sum(grad_y, 0, keepdims=True) * bias_ref[1:2, :]
        grad_low = (gate_m * grad_y).astype(low_type)
        cot_ref[here, :] = grad_low
        grad_hid = (mm_nt(grad_low, weights[:, width:]) * slope).astype(low_type)
        hid_ref[here, :] = grad_hid
        back = mm_nt(grad_hid, weights[:, :width])
        back_refs[r][...] = back.astype(low_type)
        totals[1] += jnp.sum(back * normed, 0, keepdims=True)
        totals[2] += jnp.sum(back, 0, keepdims=True)
        totals[3] += jnp.sum(grad_hid.astype(full_type), 0, keepdims=True)
        totals[4] += jnp.sum(grad_low.astype(full_type), 0, keepdims=True)
    sums_ref[...] = jnp.zeros(sums_ref.shape, full_type)
    sums_ref[3:4, :] = totals[2]
    sums_ref[4:5, :] = totals[1]
    sums_ref[5:6, :] = totals[0]
    sums_ref[pl.ds(9 + own, 1), :] = totals[3]
    sums_ref[13:14, :] = jnp.where(own == 0, totals[4], 0.0)
    grads_ref[:, :width] = mm_tn(low_ref[...], hid_ref[...]).astype(low_type)
    grads_ref[:, width:] = mm_tn(act_ref[...], cot_ref[...]).astype(low_type)
    deal(table_ref, dealt, grads_ref)


def attend_backward_kernel(heads, own_ref, *refs):
    grad = refs[:4]
    att_all, out_own, qkv_ref, log_ref, low_ref = refs[4:9]
    out_ref, grads_ref, sums_ref = refs[9:12]
    all_ref, cols_ref, grad_ref, keys_t, sum_k, sum_v = refs[12:]
    n_tok, width = low_ref.shape
    feats = out_own.shape[0]
    size = n_tok // 4
    dim = feats // heads
    scale = dim ** (-0.5)
    own = own_ref[0]
    for r in range(4):
        here = slice(r * size, (r + 1) * size)
        all_ref[here, :] = grad[r][...]
        grad_ref[here, :] = mm_nt(grad[r][...], out_own[...]).astype(low_type)
    for j in range(4):

        @pl.when(own == j)
        def _():
            cols_ref[...] = all_ref[:, j * feats : (j + 1) * feats]

    grads_ref[:, 3 * feats :] = mm(att_all[...], cols_ref[...]).astype(low_type)
    keys_t[...] = jnp.transpose(qkv_ref[:, feats : 2 * feats])
    sum_k[...] = jnp.zeros(sum_k.shape, full_type)
    sum_v[...] = jnp.zeros(sum_v.shape, full_type)

    def step(block, _):
        here = pl.ds(pl.multiple_of(block * BLOCK, BLOCK), BLOCK)
        for head in range(heads):
            cut = slice(head * dim, (head + 1) * dim)
            queries = (qkv_ref[here, cut] * scale).astype(low_type)
            keys = qkv_ref[:, feats + head * dim : feats + (head + 1) * dim]
            values = qkv_ref[:, 2 * feats + head * dim : 2 * feats + (head + 1) * dim]
            grad_att = grad_ref[here, cut]
            probs = jnp.exp(mm_nt(keys, queries) - log_ref[head : head + 1, here])
            grad_probs = mm_nt(values, grad_att)
            delta = jnp.sum(probs * grad_probs, 0, keepdims=True)
            grad_scores = (probs * (grad_probs - delta)).astype(low_type)
            sum_v[:, cut] += mm(probs.astype(low_type), grad_att)
            sum_k[:, cut] += mm(grad_scores, queries)
            grad_q = mm(keys_t[cut, :], grad_scores) * scale
            out_ref[here, cut] = jnp.transpose(grad_q).astype(low_type)
        return 0

    lax.fori_loop(0, n_tok // BLOCK, step, 0)
    out_ref[:, feats : 2 * feats] = sum_k[...].astype(low_type)
    out_ref[:, 2 * feats :] = sum_v[...].astype(low_type)
    grads_ref[:, : 3 * feats] = mm_tn(low_ref[...], out_ref[...]).astype(low_type)
    sums_ref[...] = jnp.zeros(sums_ref.shape, full_type)
    bias = jnp.sum(out_ref[...].astype(full_type), 0, keepdims=True)
    total = jnp.sum(all_ref[...].astype(full_type), 0, keepdims=True)
    sums_ref[8:9, :] = jnp.where(own == 0, total, 0.0)
    for j in range(4):

        @pl.when(own == j)
        def _():
            sums_ref[6:7, j * feats : (j + 1) * feats] = bias[:, :feats]
            sums_ref[7:8, j * feats : (j + 1) * feats] = bias[:, 2 * feats :]


def project_backward_kernel(*refs):
    tokens = refs[:4]
    grad_ref, weight_ref, gate_ref, sums_mlp, sums_att = refs[4:9]
    back_refs, sums_ref = refs[9:13], refs[13]
    size, width = back_refs[0].shape
    totals = [jnp.zeros((1, width), full_type) for _ in range(2)]
    for r in range(4):
        here = slice(r * size, (r + 1) * size)
        back = mm_nt(grad_ref[here, :], weight_ref[...])
        back_refs[r][...] = back.astype(low_type)
        normed, _ = layer_norm(tokens[r][:size, :].astype(full_type))
        totals[0] += jnp.sum(back, 0, keepdims=True)
        totals[1] += jnp.sum(back * normed, 0, keepdims=True)
    sums_ref[...] = sums_mlp[...] + sums_att[...]
    sums_ref[0:1, :] = totals[0]
    sums_ref[1:2, :] = totals[1]
    sums_ref[2:3, :] = gate_ref[...]


def adam_step(weight, first, second, grad):
    first_new = beta_one * first + (1.0 - beta_one) * grad
    second_new = beta_two * second + (1.0 - beta_two) * grad * grad
    corr_one = 1.0 - beta_one**ADAM_STEP
    corr_two = 1.0 - beta_two**ADAM_STEP
    weight_new = weight - learn_rate * (first_new / corr_one) / (
        jnp.sqrt(second_new / corr_two) + adam_eps
    )
    return (weight_new, first_new, second_new)


def swap(value, distance):
    return lax.ppermute(value, "seq", [(p, p ^ distance) for p in range(4)])


def gather_rel(value):
    far = swap(value, 2)
    near = swap(value, 1)
    cross = swap(far, 1)
    return [value, near, far, cross]


def scatter_rel(blocks):
    near_own, near_far = [swap(blocks[r], 1).astype(full_type) for r in (1, 3)]
    far_own = swap((blocks[2].astype(full_type) + near_far).astype(low_type), 2)
    return blocks[0].astype(full_type) + near_own + far_own.astype(full_type)


CYCLE = (0, 2, 4, 6, 7, 5, 3, 1)


def ring_pairs(count):
    right = [(CYCLE[i], CYCLE[(i + 1) % count]) for i in range(count)]
    return right, [(to, start) for start, to in right]


def ring_hop(pieces, count):
    if count != len(CYCLE):
        return pieces
    right, left = ring_pairs(count)
    hop = len(pieces) // 2
    ahead, behind = (pieces[-2], pieces[-1]) if hop else (pieces[0], pieces[0])
    more = [lax.ppermute(ahead, "shard", right)]
    if hop < count // 2 - 1:
        more.append(lax.ppermute(behind, "shard", left))
    return pieces + more


def ring_begin(value, count):
    if count != len(CYCLE):
        return [spread(value, "shard", count).reshape(-1, value.shape[-1])]
    return ring_hop([value], count)


def ring_scatter(pieces, count):
    if len(pieces) == 1:
        whole = pieces[0].reshape(count, -1, pieces[0].shape[-1])
        arrived = lax.all_to_all(whole, "shard", 0, 0, tiled=True)
        return [jnp.sum(arrived.astype(full_type), 0).astype(low_type)]
    right, left = ring_pairs(count)
    ahead, behind = pieces[count - 1], pieces[count - 3]
    for hop in range(count // 2, 1, -1):
        ahead = lax.ppermute(ahead, "shard", right)
        ahead = (ahead.astype(full_type) + pieces[2 * hop - 2].astype(full_type)).astype(low_type)
    for hop in range(count // 2 - 1, 0, -1):
        behind = lax.ppermute(behind, "shard", left)
        if hop > 1:
            behind = (behind.astype(full_type) + pieces[2 * hop - 3].astype(full_type)).astype(
                low_type
            )
    return [pieces[0], ahead, behind]


def ring_finish(parts, count):
    if len(parts) == 1:
        return parts[0]
    last = lax.ppermute(parts[1], "shard", ring_pairs(count)[0])
    return sum(x.astype(full_type) for x in (parts[0], last, parts[2])).astype(low_type)


def ring_table(own, count):
    if count != len(CYCLE):
        return jnp.zeros((1,), jnp.int32)
    lines = []
    for s in range(count):
        at = CYCLE.index(s)
        line = [s]
        for hop in range(1, count // 2 + 1):
            line.append(CYCLE[(at - hop) % count])
            if hop < count // 2:
                line.append(CYCLE[(at + hop) % count])
        lines.append(line)
    return lax.dynamic_index_in_dim(jnp.array(lines, jnp.int32), own, 0, keepdims=False)


def permute_blocks(value, distance):
    size = value.shape[1] // 4
    return jnp.concatenate(
        [value[:, (r ^ distance) * size : ((r ^ distance) + 1) * size] for r in range(4)], 1
    )


def spread(value, axis, count):
    return lax.all_to_all(
        jnp.broadcast_to(value[None], (count,) + value.shape), axis, 0, 0, tiled=True
    )


def token_sum(tensor):
    return jnp.sum(tensor.astype(full_type), axis=0)


def shards(
    latents,
    cotangent,
    class_labels,
    time_buckets,
    class_table,
    time_table,
    ada_weight,
    qkv_weight,
    out_weight,
    up_weight,
    down_weight,
    biases,
    ada_first,
    qkv_first,
    out_first,
    up_first,
    down_first,
    bias_first,
    ada_second,
    qkv_second,
    out_second,
    up_second,
    down_second,
    bias_second,
    n_shard,
    n_seq,
):
    assert n_seq == 4 and latents.shape[0] == 1 and class_labels.shape[0] == n_shard
    s_own = lax.axis_index("shard")
    q_own = lax.axis_index("seq")
    tok_dev, width = latents.shape[1:]
    head_dim = width // HEADS
    score_scale = head_dim ** (-0.5)
    heads_own = HEADS // n_seq
    feats = heads_own * head_dim
    rows = ada_weight.shape[0]
    ff = up_weight.shape[1]
    ff_cell = ff // (n_shard * n_seq)
    ff_own = ff // n_seq

    table = jnp.concatenate([ring_table(s_own, n_shard), q_own[None].astype(jnp.int32)])
    own_index = q_own[None].astype(jnp.int32)
    first_part, rest_part = vmem_call(
        cut_kernel,
        "cut",
        (
            jax.ShapeDtypeStruct((rows, 4 * feats), low_type),
            jax.ShapeDtypeStruct((rows, width + ff_own), low_type),
        ),
        [pltpu.VMEM(x.shape, full_type) for x in (qkv_weight, out_weight, up_weight, down_weight)]
        + [pltpu.SemaphoreType.DMA((16,))],
        0,
        0,
        [own_index, qkv_weight, out_weight, up_weight, down_weight],
        space=pl.ANY,
        grant=60,
    )

    cond = jnp.take(class_table, class_labels, axis=0).astype(full_type) + jnp.take(
        time_table, time_buckets, axis=0
    ).astype(full_type)
    cond_cols = lax.dynamic_slice_in_dim(cond, s_own * rows, rows, 1)
    silu_cols = jax.nn.silu(cond_cols).astype(low_type)
    ada_low = ada_weight.astype(low_type)
    mod_partial = mm(silu_cols, ada_low)
    bias_low = biases.astype(low_type).astype(full_type).reshape(1, -1)
    payload = jnp.concatenate(
        [mod_partial, jnp.broadcast_to(bias_low, (n_shard, bias_low.shape[1]))], 1
    )
    arrived = lax.all_to_all(payload, "shard", split_axis=0, concat_axis=0, tiled=True)
    arrived, first_part = lax.optimization_barrier((arrived, first_part))
    first_pieces = ring_begin(first_part, n_shard)
    for _ in range(2):
        first_pieces = ring_hop(first_pieces, n_shard)
    both = jnp.concatenate([latents[0], cotangent[0]])
    far, first_pieces = lax.optimization_barrier((swap(both, 2), first_pieces))
    tokens = [both, swap(both, 1), far, swap(far, 1)]
    first_pieces = ring_hop(first_pieces, n_shard)
    n_piece = len(first_pieces)
    mod_sum = jnp.sum(arrived[:, : 6 * width], 0)
    bias_full = jnp.transpose(
        arrived[:, 6 * width :].reshape(n_shard, biases.shape[0], rows), (1, 0, 2)
    ).reshape(biases.shape[0], width)
    modulation = mod_sum.reshape(6, width) + bias_full[0:6]
    shift_a, scale_a, gate_a, shift_m, scale_m, gate_m = [modulation[i] for i in range(6)]

    n_tok = n_seq * tok_dev

    bias_query = lax.dynamic_slice_in_dim(bias_full[6], q_own * feats, feats)
    bias_value = lax.dynamic_slice_in_dim(bias_full[7], q_own * feats, feats)
    bias_qkv = jnp.concatenate([bias_query, jnp.zeros_like(bias_query), bias_value])[None]
    pair_count = heads_own * n_tok * n_tok
    bias_qkv, rest_pieces = lax.optimization_barrier((bias_qkv, ring_begin(rest_part, n_shard)))
    modulated_a, qkv_w, out_q, qkv = vmem_call(
        partial(project_kernel, n_piece),
        "project",
        (
            jax.ShapeDtypeStruct((n_tok, width), low_type),
            jax.ShapeDtypeStruct((width, 3 * feats), low_type),
            jax.ShapeDtypeStruct((width, feats), low_type),
            jax.ShapeDtypeStruct((n_tok, 3 * feats), low_type),
        ),
        [],
        6 * n_tok * width * feats,
        n_tok,
        [table, *tokens, modulation, bias_qkv, *first_pieces],
    )
    out_far = swap(out_q, 2)
    qkv, rest_pieces = lax.optimization_barrier((qkv, ring_hop(rest_pieces, n_shard)))
    rest_pieces = ring_hop(rest_pieces, n_shard)
    att_own, logs = vmem_call(
        partial(attend_forward_kernel, heads_own),
        "attend_forward",
        (
            jax.ShapeDtypeStruct((feats, n_tok), low_type),
            jax.ShapeDtypeStruct((8, n_tok), full_type),
        ),
        [],
        4 * pair_count * head_dim,
        pair_count,
        [qkv],
        0,
    )
    att_own, out_far, rest_pieces = lax.optimization_barrier((att_own, out_far, rest_pieces))
    out_parts = [out_q, swap(out_q, 1), out_far, swap(out_far, 1)]
    rest_pieces = ring_hop(rest_pieces, n_shard)
    att_far = swap(permute_blocks(att_own, 2), 2)
    att_far, rest_pieces = lax.optimization_barrier((att_far, rest_pieces))
    att_near = swap(permute_blocks(att_own, 1), 1)
    att_cross = swap(permute_blocks(att_far, 1), 1)

    bias_ff = lax.dynamic_index_in_dim(
        bias_full[9:13].reshape(n_shard, n_seq, ff_cell), q_own, 1, keepdims=False
    ).reshape(ff_own)
    bias_mlp = jnp.stack([bias_full[8], bias_full[13], bias_ff])
    attended, out_own, residual, branch_a, *mlp_out = (
        vmem_call(
            partial(mlp_kernel, n_piece),
            "mlp",
            (
                jax.ShapeDtypeStruct((width, n_tok), low_type),
                jax.ShapeDtypeStruct((feats, width), low_type),
            )
            + 4 * (jax.ShapeDtypeStruct((tok_dev, width), full_type),)
            + 2 * (jax.ShapeDtypeStruct((tok_dev, 1), full_type),)
            + 8 * (jax.ShapeDtypeStruct((tok_dev, width), low_type),)
            + (jax.ShapeDtypeStruct((16, width), full_type),)
            + n_piece * (jax.ShapeDtypeStruct((width // n_piece, width + ff_own), low_type),),
            [
                pltpu.VMEM((width, width + ff_own), low_type),
                pltpu.VMEM((width, width + ff_own), low_type),
                pltpu.VMEM((width, width), low_type),
            ]
            + [pltpu.VMEM((n_tok, width), low_type)] * 4,
            14 * n_tok * width * width,
            n_tok * width,
            [
                table,
                att_own,
                att_near,
                att_far,
                att_cross,
                *tokens,
                modulation,
                bias_mlp,
                *out_parts,
                *rest_pieces,
            ],
        )
    )
    normed_m, inverse_m = mlp_out[:2], mlp_out[2:4]
    branch_part, back, sums_mlp, grads_mlp = mlp_out[4:8], mlp_out[8:12], mlp_out[12], mlp_out[13:]
    near_zero, near_two, grads_mlp = lax.optimization_barrier(
        (swap(back[1], 1), swap(back[3], 1), grads_mlp)
    )
    chip = [
        (mine.astype(full_type) + theirs.astype(full_type)).astype(low_type)
        for mine, theirs in ((back[0], near_zero), (back[2], near_two))
    ]
    across = [swap(chip[1], 2), swap(chip[0], 2)]
    mlp_parts = ring_scatter(grads_mlp, n_shard)
    grad_residuals = [
        tokens[2 * i][tok_dev:].astype(full_type)
        + norm_back(
            (chip[i].astype(full_type) + across[i].astype(full_type)) * (1.0 + scale_m),
            normed_m[i],
            inverse_m[i],
        )
        for i in range(2)
    ]
    grad_residual = grad_residuals[0]
    grad_low = [(gate_a * part).astype(low_type) for part in grad_residuals]
    grad_branch_a = [grad_low[0], swap(grad_low[0], 1), grad_low[1], swap(grad_low[1], 1)]
    across, branch_part = lax.optimization_barrier((across, branch_part))
    branch_near = swap(branch_part[1], 1)
    branch_chip = branch_part[2].astype(full_type) + swap(branch_part[3], 1).astype(full_type)
    branch_far = swap(branch_chip.astype(low_type), 2)
    mlp_parts, grad_branch_a = lax.optimization_barrier((mlp_parts, grad_branch_a))
    grad_gate_a = token_sum(grad_residual * branch_a)
    grad_qkv, grads_att, sums_att = vmem_call(
        partial(attend_backward_kernel, heads_own),
        "attend_backward",
        (
            jax.ShapeDtypeStruct((n_tok, 3 * feats), low_type),
            jax.ShapeDtypeStruct((width, 4 * feats), low_type),
            jax.ShapeDtypeStruct((16, width), full_type),
        ),
        [
            pltpu.VMEM((n_tok, width), low_type),
            pltpu.VMEM((n_tok, feats), low_type),
            pltpu.VMEM((n_tok, feats), low_type),
            pltpu.VMEM((feats, n_tok), low_type),
            pltpu.VMEM((n_tok, feats), full_type),
            pltpu.VMEM((n_tok, feats), full_type),
        ],
        10 * n_tok * width * feats + 10 * pair_count * head_dim,
        pair_count,
        [own_index, *grad_branch_a, attended, out_own, qkv, logs, modulated_a],
    )
    *grad_mod_a_part, small = vmem_call(
        project_backward_kernel,
        "project_backward",
        4 * (jax.ShapeDtypeStruct((tok_dev, width), low_type),)
        + (jax.ShapeDtypeStruct((16, width), full_type),),
        [],
        6 * n_tok * width * feats,
        n_tok,
        [*tokens, grad_qkv, qkv_w, grad_gate_a[None], sums_mlp, sums_att],
        0,
    )
    arrived_att = lax.all_to_all(
        grads_att.reshape(n_shard, rows, 4 * feats), "shard", 0, 0, tiled=True
    )
    normed_a, inverse_a = layer_norm(latents[0].astype(full_type))
    latents_grad = grad_residual + norm_back(
        scatter_rel(grad_mod_a_part) * (1.0 + scale_a), normed_a, inverse_a
    )
    branch_own = sum(x.astype(full_type) for x in (branch_part[0], branch_near, branch_far))
    branch_own = branch_own + bias_full[13]
    block_out = (residual + gate_m * branch_own).astype(low_type)

    small = small + swap(small, 1)
    small = small + swap(small, 2)
    small, arrived_att = lax.optimization_barrier((small, arrived_att))
    every = spread(small, "shard", n_shard)
    ada_state = (ada_weight, ada_first, ada_second)
    bias_state = (biases, bias_first, bias_second)
    tables = tuple(jax.ShapeDtypeStruct((t.shape[0], rows), full_type) for t in (class_table, time_table))
    done = vmem_call(
        partial(finish_kernel, n_shard),
        "finish",
        tuple(jax.ShapeDtypeStruct(x.shape, full_type) for x in ada_state + bias_state) + tables,
        [
            pltpu.VMEM((16, width), full_type),
            pltpu.VMEM(biases.shape, full_type),
            pltpu.VMEM((n_shard, rows), full_type),
        ],
        24 * ada_weight.size,
        ada_weight.size,
        [
            s_own[None].astype(jnp.int32),
            class_labels,
            time_buckets,
            every,
            silu_cols,
            cond_cols,
            *ada_state,
            *bias_state,
        ],
        3,
    )
    ada_new, bias_new, class_grad, time_grad = done[:3], done[3:6], done[6], done[7]

    att_total = jnp.sum(arrived_att.astype(full_type), 0).astype(low_type)
    mlp_up, mlp_down = adam_call(
        adam_mlp_kernel,
        "adam_mlp",
        own_index,
        gather_rel(ring_finish(mlp_parts, n_shard)),
        [up_weight, down_weight, up_first, down_first, up_second, down_second],
    )
    att_qkv, att_out = adam_call(
        adam_att_kernel,
        "adam_att",
        own_index,
        gather_rel(att_total),
        [qkv_weight, out_weight, qkv_first, out_first, qkv_second, out_second],
    )

    updates = [
        ada_new,
        att_qkv,
        att_out,
        mlp_up,
        mlp_down,
        bias_new,
    ]
    return (
        block_out[None],
        latents_grad[None],
        class_grad,
        time_grad,
        *[update[0] for update in updates],
        *[update[1] for update in updates],
        *[update[2] for update in updates],
    )


def solution(mesh):
    tokens = P("shard", "seq", None)
    rows = P("shard", None)
    cols = P(None, "shard")
    state = (rows, rows, rows, rows, rows, cols)
    return jax.shard_map(
        partial(shards, n_shard=mesh.shape["shard"], n_seq=mesh.shape["seq"]),
        mesh=mesh,
        in_specs=(tokens, tokens, P(), P(), P(), P()) + 3 * state,
        out_specs=(tokens, tokens, cols, cols) + 3 * state,
        check_vma=False,
    )
```

```python
import math
from functools import partial

import jax
import jax.numpy as jnp
from jax import lax
from jax.experimental import pallas as pl
from jax.experimental.pallas import tpu as pltpu
from jax.sharding import PartitionSpec as P

HEADS = 12
ADAM_STEP = 10
BLOCK = 256


norm_eps = 1e-06
beta_one = 0.9
beta_two = 0.999
learn_rate = 0.05
adam_eps = 1e-08

low_type = jnp.bfloat16
full_type = jnp.float32


def layer_norm(values_in):
    centred = values_in - jnp.mean(values_in, -1, keepdims=True)
    inverse = lax.rsqrt(jnp.mean(centred * centred, -1, keepdims=True) + norm_eps)
    return (centred * inverse, inverse)


def norm_back(gradient, normed, inverse):
    return inverse * (
        gradient
        - jnp.mean(gradient, -1, keepdims=True)
        - normed * jnp.mean(gradient * normed, -1, keepdims=True)
    )


def dot(left, right, dims):
    return lax.dot_general(left, right, (dims, ((), ())), preferred_element_type=full_type)


def mm(left, right):
    return dot(left, right, ((1,), (0,)))


def mm_nt(left, right):
    return dot(left, right, ((1,), (1,)))


def mm_tn(left, right):
    return dot(left, right, ((0,), (0,)))


def vmem_call(kernel, name, out_shape, scratch, flops, exps, operands, n_scalar=1, space=None, grant=60):
    specs = [pl.BlockSpec(memory_space=pltpu.SMEM)] * n_scalar
    specs += [pl.BlockSpec(memory_space=space or pltpu.VMEM)] * (len(operands) - n_scalar)
    moved = sum(x.size * x.dtype.itemsize for x in operands)
    moved += sum(x.size * x.dtype.itemsize for x in out_shape)
    return pl.pallas_call(
        kernel,
        out_shape=out_shape,
        in_specs=specs,
        out_specs=tuple(pl.BlockSpec(memory_space=pltpu.VMEM) for _ in out_shape),
        scratch_shapes=scratch,
        compiler_params=pltpu.CompilerParams(vmem_limit_bytes=grant * 2**20),
        cost_estimate=pl.CostEstimate(flops=flops, bytes_accessed=moved, transcendentals=exps),
        name=name,
    )(*operands)


def assemble(table_ref, pieces, target):
    size = pieces[0].shape[0]
    for slot, piece in enumerate(pieces):
        target[pl.ds(pl.multiple_of(table_ref[slot] * size, size), size), :] = piece[...]


def cut_kernel(table_ref, qkv_all, out_all, up_all, down_all, first_ref, rest_ref, *scratch):
    held, sems = scratch[:4], scratch[4]
    qkv_ref, out_ref, up_ref, down_ref = held
    copies = []
    for source, target in zip((qkv_all, out_all, up_all, down_all), held):
        step = 768 if source.shape[1] > 768 else 256
        for start in range(0, source.shape[1], step):
            cut = (slice(None), pl.ds(start, step))
            copies.append(
                pltpu.make_async_copy(source.at[cut], target.at[cut], sems.at[len(copies)])
            )
    for copy in copies:
        copy.start()
    for copy in copies:
        copy.wait()
    rows, width = out_ref.shape
    feats = width // 4
    cell = down_ref.shape[0] // 4
    n_shard = up_ref.shape[1] // (4 * cell)
    for j in range(4):

        @pl.when(table_ref[0] == j)
        def _():
            for part in range(3):
                start = part * width + j * feats
                first_ref[:, part * feats : (part + 1) * feats] = qkv_ref[
                    :, start : start + feats
                ].astype(low_type)
            first_ref[:, 3 * feats :] = out_ref[:, j * feats : (j + 1) * feats].astype(low_type)
            for s in range(n_shard):
                start = (s * 4 + j) * cell
                rest_ref[:, s * cell : (s + 1) * cell] = up_ref[:, start : start + cell].astype(
                    low_type
                )
            rest_ref[:, width:] = down_ref[j * cell : (j + 1) * cell, :].astype(low_type)


def adam_mlp_kernel(table_ref, *refs):
    grads, state, outs = refs[:4], refs[4:10], refs[10:16]
    grad_up, grad_down = refs[16:]
    width = grad_down.shape[1]
    cell = grad_down.shape[0] // 4
    n_shard = grad_up.shape[1] // (4 * cell)
    for j in range(4):

        @pl.when(table_ref[0] == j)
        def _():
            for r in range(4):
                grad = grads[r][...].astype(full_type)
                for s in range(n_shard):
                    start = (s * 4 + (j ^ r)) * cell
                    grad_up[:, start : start + cell] = grad[:, s * cell : (s + 1) * cell]
                grad_down[(j ^ r) * cell : ((j ^ r) + 1) * cell, :] = grad[:, width:]

    for grad, part in ((grad_up, slice(0, 6, 2)), (grad_down, slice(1, 6, 2))):
        results = adam_step(*[ref[...] for ref in state[part]], grad[...])
        for ref, result in zip(outs[part], results):
            ref[...] = result


def adam_att_kernel(table_ref, *refs):
    grads, state, outs = refs[:4], refs[4:10], refs[10:16]
    grad_qkv, grad_out = refs[16:]
    width = grad_out.shape[1]
    feats = width // 4
    for j in range(4):

        @pl.when(table_ref[0] == j)
        def _():
            for r in range(4):
                grad = grads[r][...].astype(full_type)
                for part in range(3):
                    start = part * width + (j ^ r) * feats
                    grad_qkv[:, start : start + feats] = grad[:, part * feats : (part + 1) * feats]
                grad_out[:, (j ^ r) * feats : ((j ^ r) + 1) * feats] = grad[:, 3 * feats :]

    for grad, part in ((grad_qkv, slice(0, 6, 2)), (grad_out, slice(1, 6, 2))):
        results = adam_step(*[ref[...] for ref in state[part]], grad[...])
        for ref, result in zip(outs[part], results):
            ref[...] = result


def finish_kernel(n_shard, place_ref, *refs):
    every_ref, silu_ref, cond_ref, label_ref, bucket_ref = refs[:5]
    ada, bias = refs[5:8], refs[8:11]
    ada_out, bias_out, class_ref, time_ref = refs[11:14], refs[14:17], refs[17], refs[18]
    sums_ref, bias_grad = refs[19:]
    rows = cond_ref.shape[1]
    width = every_ref.shape[2]
    grad_silu = jnp.zeros((n_shard, rows), full_type)
    for slot in range(6):
        cut = slice(slot * width, (slot + 1) * width)
        grad_mod = every_ref[:, slot, :].astype(low_type)
        weight = ada[0][:, cut]
        results = adam_step(
            weight, ada[1][:, cut], ada[2][:, cut], mm_tn(silu_ref[...], grad_mod)
        )
        for ref, result in zip(ada_out, results):
            ref[:, cut] = result
        grad_silu += mm_nt(grad_mod, weight.astype(low_type))
        sums_ref[slot : slot + 1, :] = jnp.sum(grad_mod.astype(full_type), 0, keepdims=True)
    for slot in range(6, 14):
        sums_ref[slot : slot + 1, :] = jnp.sum(every_ref[:, slot, :], 0, keepdims=True)
    for s in range(n_shard):

        @pl.when(place_ref[0] == s)
        def _():
            for slot in range(14):
                row, cell = slot, s
                if 9 <= slot < 13:
                    row, cell = 9 + s % 4, (n_shard * (slot - 9) + s) // 4
                bias_grad[slot : slot + 1, :] = sums_ref[
                    row : row + 1, cell * rows : (cell + 1) * rows
                ]

    results = adam_step(*[ref[...] for ref in bias], bias_grad[...])
    for ref, result in zip(bias_out, results):
        ref[...] = result
    cond = cond_ref[...]
    gate = 1.0 / (1.0 + jnp.exp(-cond))
    cols = grad_silu * (gate * (1.0 + cond * (1.0 - gate)))
    for index_ref, table in ((label_ref, class_ref), (bucket_ref, time_ref)):
        places = lax.broadcasted_iota(jnp.int32, (n_shard, table.shape[1]), 1)
        hot = jnp.where(places == index_ref[...], 1.0, 0.0)
        table[...] = lax.dot_general(
            cols,
            hot,
            (((0,), (0,)), ((), ())),
            precision=lax.Precision.HIGHEST,
            preferred_element_type=full_type,
        )


def adam_call(kernel, name, own, grads, state):
    results = vmem_call(
        kernel,
        name,
        tuple(jax.ShapeDtypeStruct(x.shape, full_type) for x in state),
        [pltpu.VMEM(x.shape, full_type) for x in state[:2]],
        20 * (state[0].size + state[1].size),
        state[0].size + state[1].size,
        [own, *grads, *state],
    )
    return results[0::2], results[1::2]


def project_kernel(n_piece, table_ref, *refs):
    stream = refs[:4]
    mod_ref, bias_ref = refs[4:6]
    pieces = refs[6 : 6 + n_piece]
    low_ref, weight_ref, out_ref, qkv_ref = refs[6 + n_piece :]
    n_tok, cols = qkv_ref.shape
    size = pieces[0].shape[0]
    for slot, piece in enumerate(pieces):
        place = pl.ds(pl.multiple_of(table_ref[slot] * size, size), size)
        weight_ref[place, :] = piece[:, :cols]
        out_ref[place, :] = piece[:, cols:]
    for r in range(4):
        here = slice(r * n_tok // 4, (r + 1) * n_tok // 4)
        normed, _ = layer_norm(stream[r][: n_tok // 4, :].astype(full_type))
        low = (normed * (1.0 + mod_ref[1:2, :]) + mod_ref[0:1, :]).astype(low_type)
        low_ref[here, :] = low
        qkv_ref[here, :] = (mm(low, weight_ref[...]) + bias_ref[...]).astype(low_type)


def attend_forward_kernel(heads, qkv_ref, att_ref, log_ref):
    n_tok = qkv_ref.shape[0]
    feats = att_ref.shape[0]
    dim = feats // heads
    scale = dim ** (-0.5)
    log_ref[...] = jnp.zeros(log_ref.shape, full_type)

    def step(block, _):
        here = pl.ds(pl.multiple_of(block * BLOCK, BLOCK), BLOCK)
        for head in range(heads):
            queries = qkv_ref[here, head * dim : (head + 1) * dim] * scale
            keys = qkv_ref[:, feats + head * dim : feats + (head + 1) * dim]
            values = qkv_ref[:, 2 * feats + head * dim : 2 * feats + (head + 1) * dim]
            scores = mm_nt(queries.astype(low_type), keys)
            row_max = jnp.max(scores, -1, keepdims=True)
            expo = jnp.exp(scores - row_max)
            total = jnp.sum(expo, -1, keepdims=True)
            probs = (expo * (1.0 / total)).astype(low_type)
            att_ref[head * dim : (head + 1) * dim, here] = jnp.transpose(
                mm(probs, values)
            ).astype(low_type)
            logs = jnp.broadcast_to(row_max + jnp.log(total), (BLOCK, 128))
            log_ref[head : head + 1, here] = jnp.transpose(logs)[0:1]
        return 0

    lax.fori_loop(0, n_tok // BLOCK, step, 0)


def gelu_both(value):
    root = (2.0 / math.pi) ** 0.5
    square = value * value
    bend = jnp.tanh(root * value * (1.0 + 0.044715 * square))
    half = 0.5 * (1.0 + bend)
    slope = half + 0.5 * value * (1.0 - bend * bend) * (root * (1.0 + 3 * 0.044715 * square))
    return (value * half, slope)


def deal(table_ref, pieces, source):
    size = pieces[0].shape[0]
    for slot, piece in enumerate(pieces):
        piece[...] = source[pl.ds(pl.multiple_of(table_ref[slot] * size, size), size), :]


def mlp_kernel(n_piece, table_ref, *refs):
    att = refs[:4]
    tokens = refs[4:8]
    mod_ref, bias_ref = refs[8:10]
    out_parts = refs[10:14]
    pieces = refs[14 : 14 + n_piece]
    (
        att_all,
        out_own,
        residual_ref,
        branch_ref,
        *more,
        sums_ref,
    ) = refs[14 + n_piece : 31 + n_piece]
    normed_refs, inverse_refs, part_refs, back_refs = more[:2], more[2:4], more[4:8], more[8:12]
    dealt = refs[31 + n_piece : 31 + 2 * n_piece]
    weights, grads_ref, out_all, low_ref, act_ref, hid_ref, cot_ref = refs[31 + 2 * n_piece :]
    feats, n_tok = att[0].shape
    width = tokens[0].shape[1]
    size = n_tok // 4
    own = table_ref[n_piece]
    assemble(table_ref, pieces, weights)
    for r in range(4):
        start = pl.multiple_of((own ^ r) * feats, feats)
        att_all[pl.ds(start, feats), :] = att[r][...]
    for r in range(4):
        for j in range(4):

            @pl.when((own ^ r) == j)
            def _():
                out_all[:, j * feats : (j + 1) * feats] = out_parts[r][...]

    out_own[...] = out_all[pl.ds(pl.multiple_of(own * feats, feats), feats), :]
    shift_m, scale_m, gate_m = [mod_ref[i : i + 1, :] for i in (3, 4, 5)]
    totals = [jnp.zeros((1, width), full_type) for _ in range(5)]
    for r in range(4):
        here = slice(r * size, (r + 1) * size)
        branch = mm_tn(att_all[:, here], out_all[...]) + bias_ref[0:1, :]
        residual = tokens[r][:size, :].astype(full_type) + mod_ref[2:3, :] * branch
        if r == 0:
            residual_ref[...] = residual
            branch_ref[...] = branch
        normed, inverse = layer_norm(residual)
        if r % 2 == 0:
            normed_refs[r // 2][...] = normed
            inverse_refs[r // 2][...] = inverse
        low = (normed * (1.0 + scale_m) + shift_m).astype(low_type)
        low_ref[here, :] = low
        hidden = mm(low, weights[:, :width]) + bias_ref[2:3, :]
        active, slope = gelu_both(hidden)
        active = active.astype(low_type)
        act_ref[here, :] = active
        part = mm(active, weights[:, width:])
        part_refs[r][...] = part.astype(low_type)
        grad_y = tokens[r][size:, :].astype(full_type)
        totals[0] += jnp.sum(grad_y * part, 0, keepdims=True)
        if r == 0:
            totals[0] += jnp.sum(grad_y, 0, keepdims=True) * bias_ref[1:2, :]
        grad_low = (gate_m * grad_y).astype(low_type)
        cot_ref[here, :] = grad_low
        grad_hid = (mm_nt(grad_low, weights[:, width:]) * slope).astype(low_type)
        hid_ref[here, :] = grad_hid
        back = mm_nt(grad_hid, weights[:, :width])
        back_refs[r][...] = back.astype(low_type)
        totals[1] += jnp.sum(back * normed, 0, keepdims=True)
        totals[2] += jnp.sum(back, 0, keepdims=True)
        totals[3] += jnp.sum(grad_hid.astype(full_type), 0, keepdims=True)
        totals[4] += jnp.sum(grad_low.astype(full_type), 0, keepdims=True)
    sums_ref[...] = jnp.zeros(sums_ref.shape, full_type)
    sums_ref[3:4, :] = totals[2]
    sums_ref[4:5, :] = totals[1]
    sums_ref[5:6, :] = totals[0]
    sums_ref[pl.ds(9 + own, 1), :] = totals[3]
    sums_ref[13:14, :] = jnp.where(own == 0, totals[4], 0.0)
    grads_ref[:, :width] = mm_tn(low_ref[...], hid_ref[...]).astype(low_type)
    grads_ref[:, width:] = mm_tn(act_ref[...], cot_ref[...]).astype(low_type)
    deal(table_ref, dealt, grads_ref)


def attend_backward_kernel(heads, own_ref, *refs):
    grad = refs[:4]
    att_all, out_own, qkv_ref, log_ref, low_ref = refs[4:9]
    out_ref, grads_ref, sums_ref = refs[9:12]
    all_ref, cols_ref, grad_ref, keys_t, sum_k, sum_v = refs[12:]
    n_tok, width = low_ref.shape
    feats = out_own.shape[0]
    size = n_tok // 4
    dim = feats // heads
    scale = dim ** (-0.5)
    own = own_ref[0]
    for r in range(4):
        here = slice(r * size, (r + 1) * size)
        all_ref[here, :] = grad[r][...]
        grad_ref[here, :] = mm_nt(grad[r][...], out_own[...]).astype(low_type)
    for j in range(4):

        @pl.when(own == j)
        def _():
            cols_ref[...] = all_ref[:, j * feats : (j + 1) * feats]

    grads_ref[:, 3 * feats :] = mm(att_all[...], cols_ref[...]).astype(low_type)
    keys_t[...] = jnp.transpose(qkv_ref[:, feats : 2 * feats])
    sum_k[...] = jnp.zeros(sum_k.shape, full_type)
    sum_v[...] = jnp.zeros(sum_v.shape, full_type)

    def step(block, _):
        here = pl.ds(pl.multiple_of(block * BLOCK, BLOCK), BLOCK)
        for head in range(heads):
            cut = slice(head * dim, (head + 1) * dim)
            queries = (qkv_ref[here, cut] * scale).astype(low_type)
            keys = qkv_ref[:, feats + head * dim : feats + (head + 1) * dim]
            values = qkv_ref[:, 2 * feats + head * dim : 2 * feats + (head + 1) * dim]
            grad_att = grad_ref[here, cut]
            probs = jnp.exp(mm_nt(keys, queries) - log_ref[head : head + 1, here])
            grad_probs = mm_nt(values, grad_att)
            delta = jnp.sum(probs * grad_probs, 0, keepdims=True)
            grad_scores = (probs * (grad_probs - delta)).astype(low_type)
            sum_v[:, cut] += mm(probs.astype(low_type), grad_att)
            sum_k[:, cut] += mm(grad_scores, queries)
            grad_q = mm(keys_t[cut, :], grad_scores) * scale
            out_ref[here, cut] = jnp.transpose(grad_q).astype(low_type)
        return 0

    lax.fori_loop(0, n_tok // BLOCK, step, 0)
    out_ref[:, feats : 2 * feats] = sum_k[...].astype(low_type)
    out_ref[:, 2 * feats :] = sum_v[...].astype(low_type)
    grads_ref[:, : 3 * feats] = mm_tn(low_ref[...], out_ref[...]).astype(low_type)
    sums_ref[...] = jnp.zeros(sums_ref.shape, full_type)
    bias = jnp.sum(out_ref[...].astype(full_type), 0, keepdims=True)
    total = jnp.sum(all_ref[...].astype(full_type), 0, keepdims=True)
    sums_ref[8:9, :] = jnp.where(own == 0, total, 0.0)
    for j in range(4):

        @pl.when(own == j)
        def _():
            sums_ref[6:7, j * feats : (j + 1) * feats] = bias[:, :feats]
            sums_ref[7:8, j * feats : (j + 1) * feats] = bias[:, 2 * feats :]


def project_backward_kernel(*refs):
    tokens = refs[:4]
    grad_ref, weight_ref, gate_ref, sums_mlp, sums_att = refs[4:9]
    back_refs, sums_ref = refs[9:13], refs[13]
    size, width = back_refs[0].shape
    totals = [jnp.zeros((1, width), full_type) for _ in range(2)]
    for r in range(4):
        here = slice(r * size, (r + 1) * size)
        back = mm_nt(grad_ref[here, :], weight_ref[...])
        back_refs[r][...] = back.astype(low_type)
        normed, _ = layer_norm(tokens[r][:size, :].astype(full_type))
        totals[0] += jnp.sum(back, 0, keepdims=True)
        totals[1] += jnp.sum(back * normed, 0, keepdims=True)
    sums_ref[...] = sums_mlp[...] + sums_att[...]
    sums_ref[0:1, :] = totals[0]
    sums_ref[1:2, :] = totals[1]
    sums_ref[2:3, :] = gate_ref[...]


def adam_step(weight, first, second, grad):
    first_new = beta_one * first + (1.0 - beta_one) * grad
    second_new = beta_two * second + (1.0 - beta_two) * grad * grad
    corr_one = 1.0 - beta_one**ADAM_STEP
    corr_two = 1.0 - beta_two**ADAM_STEP
    weight_new = weight - learn_rate * (first_new / corr_one) / (
        jnp.sqrt(second_new / corr_two) + adam_eps
    )
    return (weight_new, first_new, second_new)


def swap(value, distance):
    return lax.ppermute(value, "seq", [(p, p ^ distance) for p in range(4)])


def gather_rel(value):
    far = swap(value, 2)
    near = swap(value, 1)
    cross = swap(far, 1)
    return [value, near, far, cross]


def scatter_rel(blocks):
    near_own, near_far = [swap(blocks[r], 1).astype(full_type) for r in (1, 3)]
    far_own = swap((blocks[2].astype(full_type) + near_far).astype(low_type), 2)
    return blocks[0].astype(full_type) + near_own + far_own.astype(full_type)


CYCLE = (0, 2, 4, 6, 7, 5, 3, 1)


def ring_pairs(count):
    right = [(CYCLE[i], CYCLE[(i + 1) % count]) for i in range(count)]
    return right, [(to, start) for start, to in right]


def ring_hop(pieces, count):
    if count != len(CYCLE):
        return pieces
    right, left = ring_pairs(count)
    hop = len(pieces) // 2
    ahead, behind = (pieces[-2], pieces[-1]) if hop else (pieces[0], pieces[0])
    more = [lax.ppermute(ahead, "shard", right)]
    if hop < count // 2 - 1:
        more.append(lax.ppermute(behind, "shard", left))
    return pieces + more


def ring_begin(value, count):
    if count != len(CYCLE):
        return [spread(value, "shard", count).reshape(-1, value.shape[-1])]
    return ring_hop([value], count)


def ring_scatter(pieces, count):
    if len(pieces) == 1:
        whole = pieces[0].reshape(count, -1, pieces[0].shape[-1])
        arrived = lax.all_to_all(whole, "shard", 0, 0, tiled=True)
        return [jnp.sum(arrived.astype(full_type), 0).astype(low_type)]
    right, left = ring_pairs(count)
    ahead, behind = pieces[count - 1], pieces[count - 3]
    for hop in range(count // 2, 1, -1):
        ahead = lax.ppermute(ahead, "shard", right)
        ahead = (ahead.astype(full_type) + pieces[2 * hop - 2].astype(full_type)).astype(low_type)
    for hop in range(count // 2 - 1, 0, -1):
        behind = lax.ppermute(behind, "shard", left)
        if hop > 1:
            behind = (behind.astype(full_type) + pieces[2 * hop - 3].astype(full_type)).astype(
                low_type
            )
    return [pieces[0], ahead, behind]


def ring_finish(parts, count):
    if len(parts) == 1:
        return parts[0]
    last = lax.ppermute(parts[1], "shard", ring_pairs(count)[0])
    return sum(x.astype(full_type) for x in (parts[0], last, parts[2])).astype(low_type)


def ring_table(own, count):
    if count != len(CYCLE):
        return jnp.zeros((1,), jnp.int32)
    lines = []
    for s in range(count):
        at = CYCLE.index(s)
        line = [s]
        for hop in range(1, count // 2 + 1):
            line.append(CYCLE[(at - hop) % count])
            if hop < count // 2:
                line.append(CYCLE[(at + hop) % count])
        lines.append(line)
    return lax.dynamic_index_in_dim(jnp.array(lines, jnp.int32), own, 0, keepdims=False)


def permute_blocks(value, distance):
    size = value.shape[1] // 4
    return jnp.concatenate(
        [value[:, (r ^ distance) * size : ((r ^ distance) + 1) * size] for r in range(4)], 1
    )


def spread(value, axis, count):
    return lax.all_to_all(
        jnp.broadcast_to(value[None], (count,) + value.shape), axis, 0, 0, tiled=True
    )


def token_sum(tensor):
    return jnp.sum(tensor.astype(full_type), axis=0)


def shards(
    latents,
    cotangent,
    class_labels,
    time_buckets,
    class_table,
    time_table,
    ada_weight,
    qkv_weight,
    out_weight,
    up_weight,
    down_weight,
    biases,
    ada_first,
    qkv_first,
    out_first,
    up_first,
    down_first,
    bias_first,
    ada_second,
    qkv_second,
    out_second,
    up_second,
    down_second,
    bias_second,
    n_shard,
    n_seq,
):
    assert n_seq == 4 and latents.shape[0] == 1 and class_labels.shape[0] == n_shard
    s_own = lax.axis_index("shard")
    q_own = lax.axis_index("seq")
    tok_dev, width = latents.shape[1:]
    head_dim = width // HEADS
    score_scale = head_dim ** (-0.5)
    heads_own = HEADS // n_seq
    feats = heads_own * head_dim
    rows = ada_weight.shape[0]
    ff = up_weight.shape[1]
    ff_cell = ff // (n_shard * n_seq)
    ff_own = ff // n_seq

    table = jnp.concatenate([ring_table(s_own, n_shard), q_own[None].astype(jnp.int32)])
    own_index = q_own[None].astype(jnp.int32)
    first_part, rest_part = vmem_call(
        cut_kernel,
        "cut",
        (
            jax.ShapeDtypeStruct((rows, 4 * feats), low_type),
            jax.ShapeDtypeStruct((rows, width + ff_own), low_type),
        ),
        [pltpu.VMEM(x.shape, full_type) for x in (qkv_weight, out_weight, up_weight, down_weight)]
        + [pltpu.SemaphoreType.DMA((16,))],
        0,
        0,
        [own_index, qkv_weight, out_weight, up_weight, down_weight],
        space=pl.ANY,
    )

    cond = jnp.take(class_table, class_labels, axis=0).astype(full_type) + jnp.take(
        time_table, time_buckets, axis=0
    ).astype(full_type)
    cond_cols = lax.dynamic_slice_in_dim(cond, s_own * rows, rows, 1)
    silu_cols = jax.nn.silu(cond_cols).astype(low_type)
    ada_low = ada_weight.astype(low_type)
    mod_partial = mm(silu_cols, ada_low)
    bias_low = biases.astype(low_type).astype(full_type).reshape(1, -1)
    payload = jnp.concatenate(
        [mod_partial, jnp.broadcast_to(bias_low, (n_shard, bias_low.shape[1]))], 1
    )
    arrived = lax.all_to_all(payload, "shard", split_axis=0, concat_axis=0, tiled=True)
    first_pieces = ring_begin(first_part, n_shard)
    for _ in range(2):
        first_pieces = ring_hop(first_pieces, n_shard)
    both = jnp.concatenate([latents[0], cotangent[0]])
    far, arrived, first_pieces = lax.optimization_barrier((swap(both, 2), arrived, first_pieces))
    tokens = [both, swap(both, 1), far, swap(far, 1)]
    first_pieces = ring_hop(first_pieces, n_shard)
    n_piece = len(first_pieces)
    mod_sum = jnp.sum(arrived[:, : 6 * width], 0)
    bias_full = jnp.transpose(
        arrived[:, 6 * width :].reshape(n_shard, biases.shape[0], rows), (1, 0, 2)
    ).reshape(biases.shape[0], width)
    modulation = mod_sum.reshape(6, width) + bias_full[0:6]
    shift_a, scale_a, gate_a, shift_m, scale_m, gate_m = [modulation[i] for i in range(6)]

    n_tok = n_seq * tok_dev

    bias_query = lax.dynamic_slice_in_dim(bias_full[6], q_own * feats, feats)
    bias_value = lax.dynamic_slice_in_dim(bias_full[7], q_own * feats, feats)
    bias_qkv = jnp.concatenate([bias_query, jnp.zeros_like(bias_query), bias_value])[None]
    pair_count = heads_own * n_tok * n_tok
    modulated_a, qkv_w, out_q, qkv = vmem_call(
        partial(project_kernel, n_piece),
        "project",
        (
            jax.ShapeDtypeStruct((n_tok, width), low_type),
            jax.ShapeDtypeStruct((width, 3 * feats), low_type),
            jax.ShapeDtypeStruct((width, feats), low_type),
            jax.ShapeDtypeStruct((n_tok, 3 * feats), low_type),
        ),
        [],
        6 * n_tok * width * feats,
        n_tok,
        [table, *tokens, modulation, bias_qkv, *first_pieces],
    )
    out_far = swap(out_q, 2)
    qkv, rest_pieces = lax.optimization_barrier((qkv, ring_begin(rest_part, n_shard)))
    rest_pieces = ring_hop(rest_pieces, n_shard)
    att_own, logs = vmem_call(
        partial(attend_forward_kernel, heads_own),
        "attend_forward",
        (
            jax.ShapeDtypeStruct((feats, n_tok), low_type),
            jax.ShapeDtypeStruct((8, n_tok), full_type),
        ),
        [],
        4 * pair_count * head_dim,
        pair_count,
        [qkv],
        0,
    )
    att_own, out_far, rest_pieces = lax.optimization_barrier((att_own, out_far, rest_pieces))
    out_parts = [out_q, swap(out_q, 1), out_far, swap(out_far, 1)]
    rest_pieces = ring_hop(rest_pieces, n_shard)
    att_far = swap(permute_blocks(att_own, 2), 2)
    att_far, rest_pieces = lax.optimization_barrier((att_far, rest_pieces))
    rest_pieces = ring_hop(rest_pieces, n_shard)
    att_near = swap(permute_blocks(att_own, 1), 1)
    att_cross = swap(permute_blocks(att_far, 1), 1)

    bias_ff = lax.dynamic_index_in_dim(
        bias_full[9:13].reshape(n_shard, n_seq, ff_cell), q_own, 1, keepdims=False
    ).reshape(ff_own)
    bias_mlp = jnp.stack([bias_full[8], bias_full[13], bias_ff])
    attended, out_own, residual, branch_a, *mlp_out = (
        vmem_call(
            partial(mlp_kernel, n_piece),
            "mlp",
            (
                jax.ShapeDtypeStruct((width, n_tok), low_type),
                jax.ShapeDtypeStruct((feats, width), low_type),
            )
            + 4 * (jax.ShapeDtypeStruct((tok_dev, width), full_type),)
            + 2 * (jax.ShapeDtypeStruct((tok_dev, 1), full_type),)
            + 8 * (jax.ShapeDtypeStruct((tok_dev, width), low_type),)
            + (jax.ShapeDtypeStruct((16, width), full_type),)
            + n_piece * (jax.ShapeDtypeStruct((width // n_piece, width + ff_own), low_type),),
            [
                pltpu.VMEM((width, width + ff_own), low_type),
                pltpu.VMEM((width, width + ff_own), low_type),
                pltpu.VMEM((width, width), low_type),
            ]
            + [pltpu.VMEM((n_tok, width), low_type)] * 4,
            14 * n_tok * width * width,
            n_tok * width,
            [
                table,
                att_own,
                att_near,
                att_far,
                att_cross,
                *tokens,
                modulation,
                bias_mlp,
                *out_parts,
                *rest_pieces,
            ],
        )
    )
    normed_m, inverse_m = mlp_out[:2], mlp_out[2:4]
    branch_part, back, sums_mlp, grads_mlp = mlp_out[4:8], mlp_out[8:12], mlp_out[12], mlp_out[13:]
    near_zero, near_two = swap(back[1], 1), swap(back[3], 1)
    chip = [
        (mine.astype(full_type) + theirs.astype(full_type)).astype(low_type)
        for mine, theirs in ((back[0], near_zero), (back[2], near_two))
    ]
    across = [swap(chip[1], 2), swap(chip[0], 2)]
    mlp_parts = ring_scatter(grads_mlp, n_shard)
    grad_residuals = [
        tokens[2 * i][tok_dev:].astype(full_type)
        + norm_back(
            (chip[i].astype(full_type) + across[i].astype(full_type)) * (1.0 + scale_m),
            normed_m[i],
            inverse_m[i],
        )
        for i in range(2)
    ]
    grad_residual = grad_residuals[0]
    grad_low = [(gate_a * part).astype(low_type) for part in grad_residuals]
    grad_low, mlp_parts = lax.optimization_barrier((grad_low, mlp_parts))
    grad_branch_a = [grad_low[0], swap(grad_low[0], 1), grad_low[1], swap(grad_low[1], 1)]
    across, branch_part = lax.optimization_barrier((across, branch_part))
    branch_near = swap(branch_part[1], 1)
    branch_chip = branch_part[2].astype(full_type) + swap(branch_part[3], 1).astype(full_type)
    branch_far = swap(branch_chip.astype(low_type), 2)
    mlp_total = ring_finish(mlp_parts, n_shard)
    mlp_total, grad_branch_a = lax.optimization_barrier((mlp_total, grad_branch_a))
    grad_gate_a = token_sum(grad_residual * branch_a)
    grad_qkv, grads_att, sums_att = vmem_call(
        partial(attend_backward_kernel, heads_own),
        "attend_backward",
        (
            jax.ShapeDtypeStruct((n_tok, 3 * feats), low_type),
            jax.ShapeDtypeStruct((width, 4 * feats), low_type),
            jax.ShapeDtypeStruct((16, width), full_type),
        ),
        [
            pltpu.VMEM((n_tok, width), low_type),
            pltpu.VMEM((n_tok, feats), low_type),
            pltpu.VMEM((n_tok, feats), low_type),
            pltpu.VMEM((feats, n_tok), low_type),
            pltpu.VMEM((n_tok, feats), full_type),
            pltpu.VMEM((n_tok, feats), full_type),
        ],
        10 * n_tok * width * feats + 10 * pair_count * head_dim,
        pair_count,
        [own_index, *grad_branch_a, attended, out_own, qkv, logs, modulated_a],
    )
    *grad_mod_a_part, small = vmem_call(
        project_backward_kernel,
        "project_backward",
        4 * (jax.ShapeDtypeStruct((tok_dev, width), low_type),)
        + (jax.ShapeDtypeStruct((16, width), full_type),),
        [],
        6 * n_tok * width * feats,
        n_tok,
        [*tokens, grad_qkv, qkv_w, grad_gate_a[None], sums_mlp, sums_att],
        0,
    )
    arrived_att = lax.all_to_all(
        grads_att.reshape(n_shard, rows, 4 * feats), "shard", 0, 0, tiled=True
    )
    normed_a, inverse_a = layer_norm(latents[0].astype(full_type))
    latents_grad = grad_residual + norm_back(
        scatter_rel(grad_mod_a_part) * (1.0 + scale_a), normed_a, inverse_a
    )
    branch_own = sum(x.astype(full_type) for x in (branch_part[0], branch_near, branch_far))
    branch_own = branch_own + bias_full[13]
    block_out = (residual + gate_m * branch_own).astype(low_type)

    small = small + swap(small, 1)
    small = small + swap(small, 2)
    small, arrived_att = lax.optimization_barrier((small, arrived_att))
    every = spread(small, "shard", n_shard)
    ada_state = (ada_weight, ada_first, ada_second)
    bias_state = (biases, bias_first, bias_second)
    tables = tuple(jax.ShapeDtypeStruct((rows, t.shape[0]), full_type) for t in (class_table, time_table))
    done = vmem_call(
        partial(finish_kernel, n_shard),
        "finish",
        tuple(jax.ShapeDtypeStruct(x.shape, full_type) for x in ada_state + bias_state) + tables,
        [
            pltpu.VMEM((16, width), full_type),
            pltpu.VMEM(biases.shape, full_type),
        ],
        24 * ada_weight.size,
        ada_weight.size,
        [
            s_own[None].astype(jnp.int32),
            every,
            silu_cols,
            cond_cols,
            class_labels[:, None],
            time_buckets[:, None],
            *ada_state,
            *bias_state,
        ],
    )
    ada_new, bias_new = done[:3], done[3:6]
    class_grad, time_grad = jnp.transpose(done[6]), jnp.transpose(done[7])

    att_total = jnp.sum(arrived_att.astype(full_type), 0).astype(low_type)
    mlp_up, mlp_down = adam_call(
        adam_mlp_kernel,
        "adam_mlp",
        own_index,
        gather_rel(mlp_total),
        [up_weight, down_weight, up_first, down_first, up_second, down_second],
    )
    att_qkv, att_out = adam_call(
        adam_att_kernel,
        "adam_att",
        own_index,
        gather_rel(att_total),
        [qkv_weight, out_weight, qkv_first, out_first, qkv_second, out_second],
    )

    updates = [
        ada_new,
        att_qkv,
        att_out,
        mlp_up,
        mlp_down,
        bias_new,
    ]
    return (
        block_out[None],
        latents_grad[None],
        class_grad,
        time_grad,
        *[update[0] for update in updates],
        *[update[1] for update in updates],
        *[update[2] for update in updates],
    )


def solution(mesh):
    tokens = P("shard", "seq", None)
    rows = P("shard", None)
    cols = P(None, "shard")
    state = (rows, rows, rows, rows, rows, cols)
    return jax.shard_map(
        partial(shards, n_shard=mesh.shape["shard"], n_seq=mesh.shape["seq"]),
        mesh=mesh,
        in_specs=(tokens, tokens, P(), P(), P(), P()) + 3 * state,
        out_specs=(tokens, tokens, cols, cols) + 3 * state,
        check_vma=False,
    )
```

```python
import math
from functools import partial

import jax
import jax.numpy as jnp
from jax import lax
from jax.experimental import pallas as pl
from jax.experimental.pallas import tpu as pltpu
from jax.sharding import PartitionSpec as P

HEADS = 12
ADAM_STEP = 10
BLOCK = 256


norm_eps = 1e-06
beta_one = 0.9
beta_two = 0.999
learn_rate = 0.05
adam_eps = 1e-08

low_type = jnp.bfloat16
full_type = jnp.float32


def layer_norm(values_in):
    centred = values_in - jnp.mean(values_in, -1, keepdims=True)
    inverse = lax.rsqrt(jnp.mean(centred * centred, -1, keepdims=True) + norm_eps)
    return (centred * inverse, inverse)


def norm_back(gradient, normed, inverse):
    return inverse * (
        gradient
        - jnp.mean(gradient, -1, keepdims=True)
        - normed * jnp.mean(gradient * normed, -1, keepdims=True)
    )


def dot(left, right, dims):
    return lax.dot_general(left, right, (dims, ((), ())), preferred_element_type=full_type)


def mm(left, right):
    return dot(left, right, ((1,), (0,)))


def mm_nt(left, right):
    return dot(left, right, ((1,), (1,)))


def mm_tn(left, right):
    return dot(left, right, ((0,), (0,)))


def vmem_call(
    kernel, name, out_shape, scratch, flops, exps, operands, n_scalar=1, far_in=(), far_out=()
):
    specs = [pl.BlockSpec(memory_space=pltpu.SMEM)] * n_scalar
    for place in range(n_scalar, len(operands)):
        specs.append(pl.BlockSpec(memory_space=pl.ANY if place in far_in else pltpu.VMEM))
    moved = sum(x.size * x.dtype.itemsize for x in operands)
    moved += sum(x.size * x.dtype.itemsize for x in out_shape)
    return pl.pallas_call(
        kernel,
        out_shape=out_shape,
        in_specs=specs,
        out_specs=tuple(
            pl.BlockSpec(memory_space=pl.ANY if place in far_out else pltpu.VMEM)
            for place in range(len(out_shape))
        ),
        scratch_shapes=scratch,
        compiler_params=pltpu.CompilerParams(vmem_limit_bytes=60 * 2**20),
        cost_estimate=pl.CostEstimate(flops=flops, bytes_accessed=moved, transcendentals=exps),
        name=name,
    )(*operands)


def after(value, *others):
    return lax.optimization_barrier((value, *others))[0]


def assemble(table_ref, pieces, target):
    size = pieces[0].shape[0]
    for slot, piece in enumerate(pieces):
        target[pl.ds(pl.multiple_of(table_ref[slot] * size, size), size), :] = piece[...]


def cut_kernel(table_ref, qkv_all, out_all, up_all, down_all, first_ref, rest_ref, *scratch):
    held, sems = scratch[:4], scratch[4]
    qkv_ref, out_ref, up_ref, down_ref = held
    copies = []
    for source, target in zip((qkv_all, out_all, up_all, down_all), held):
        step = 768 if source.shape[1] > 768 else 256
        for start in range(0, source.shape[1], step):
            cut = (slice(None), pl.ds(start, step))
            copies.append(
                pltpu.make_async_copy(source.at[cut], target.at[cut], sems.at[len(copies)])
            )
    for copy in copies:
        copy.start()
    for copy in copies:
        copy.wait()
    rows, width = out_ref.shape
    feats = width // 4
    cell = down_ref.shape[0] // 4
    n_shard = up_ref.shape[1] // (4 * cell)
    for j in range(4):

        @pl.when(table_ref[0] == j)
        def _():
            for part in range(3):
                start = part * width + j * feats
                first_ref[:, part * feats : (part + 1) * feats] = qkv_ref[
                    :, start : start + feats
                ].astype(low_type)
            first_ref[:, 3 * feats :] = out_ref[:, j * feats : (j + 1) * feats].astype(low_type)
            for s in range(n_shard):
                start = (s * 4 + j) * cell
                rest_ref[:, s * cell : (s + 1) * cell] = up_ref[:, start : start + cell].astype(
                    low_type
                )
            rest_ref[:, width:] = down_ref[j * cell : (j + 1) * cell, :].astype(low_type)


def pieces_of(shape):
    step = 768 if shape[1] > 768 else 256
    return [(slice(None), pl.ds(start, step)) for start in range(0, shape[1], step)]


class Stream:
    def __init__(self, state, outs, held, sems):
        self.cuts = pieces_of(state[0].shape)
        self.held, self.outs, self.sems = held, outs, sems
        self.loads = [
            [
                pltpu.make_async_copy(source.at[cut], target.at[cut], sems.at[0, 3 * at + i])
                for i, (source, target) in enumerate(zip(state, held))
            ]
            for at, cut in enumerate(self.cuts)
        ]
        self.stores = []

    def start(self):
        for group in self.loads:
            for copy in group:
                copy.start()

    def weight(self, at):
        for copy in self.loads[at]:
            copy.wait()
        return self.held[0][self.cuts[at]]

    def update(self, at, grad):
        cut = self.cuts[at]
        results = adam_step(*[ref[cut] for ref in self.held], grad)
        for i, (ref, result) in enumerate(zip(self.held, results)):
            ref[cut] = result
            copy = pltpu.make_async_copy(ref.at[cut], self.outs[i].at[cut], self.sems.at[1, 3 * at + i])
            copy.start()
            self.stores.append(copy)

    def finish(self):
        for copy in self.stores:
            copy.wait()


def adam_kernel(place, table_ref, *refs):
    grads, state, outs = refs[:4], refs[4:10], refs[10:16]
    held, sems, grad_refs = refs[16:22], refs[22:24], refs[24:]
    streams = [Stream(state[i::2], outs[i::2], held[i::2], sems[i]) for i in range(2)]
    for stream in streams:
        stream.start()
    for j in range(4):

        @pl.when(table_ref[0] == j)
        def _():
            for r in range(4):
                place(j ^ r, grads[r][...].astype(full_type), *grad_refs)

    for stream, grad in zip(streams, grad_refs):
        for at, cut in enumerate(stream.cuts):
            stream.weight(at)
            stream.update(at, grad[cut])
    for stream in streams:
        stream.finish()


def place_mlp(j, grad, grad_up, grad_down):
    width = grad_down.shape[1]
    cell = grad_down.shape[0] // 4
    for s in range(grad_up.shape[1] // (4 * cell)):
        start = (s * 4 + j) * cell
        grad_up[:, start : start + cell] = grad[:, s * cell : (s + 1) * cell]
    grad_down[j * cell : (j + 1) * cell, :] = grad[:, width:]


def place_att(j, grad, grad_qkv, grad_out):
    width = grad_out.shape[1]
    feats = width // 4
    for part in range(3):
        start = part * width + j * feats
        grad_qkv[:, start : start + feats] = grad[:, part * feats : (part + 1) * feats]
    grad_out[:, j * feats : (j + 1) * feats] = grad[:, 3 * feats :]


def finish_kernel(n_shard, place_ref, *refs):
    every_ref, silu_ref, cond_ref, label_ref, bucket_ref = refs[:5]
    ada, bias = refs[5:8], refs[8:11]
    ada_out, bias_out, class_ref, time_ref = refs[11:14], refs[14:17], refs[17], refs[18]
    sums_ref, bias_grad, *held, sems = refs[19:]
    stream = Stream(ada, ada_out, held, sems)
    stream.start()
    rows = cond_ref.shape[1]
    width = every_ref.shape[2]
    grad_silu = jnp.zeros((n_shard, rows), full_type)
    for slot in range(6):
        grad_mod = every_ref[:, slot, :].astype(low_type)
        grad_silu += mm_nt(grad_mod, stream.weight(slot).astype(low_type))
        stream.update(slot, mm_tn(silu_ref[...], grad_mod))
        sums_ref[slot : slot + 1, :] = jnp.sum(grad_mod.astype(full_type), 0, keepdims=True)
    for slot in range(6, 14):
        sums_ref[slot : slot + 1, :] = jnp.sum(every_ref[:, slot, :], 0, keepdims=True)
    for s in range(n_shard):

        @pl.when(place_ref[0] == s)
        def _():
            for slot in range(14):
                row, cell = slot, s
                if 9 <= slot < 13:
                    row, cell = 9 + s % 4, (n_shard * (slot - 9) + s) // 4
                bias_grad[slot : slot + 1, :] = sums_ref[
                    row : row + 1, cell * rows : (cell + 1) * rows
                ]

    results = adam_step(*[ref[...] for ref in bias], bias_grad[...])
    for ref, result in zip(bias_out, results):
        ref[...] = result
    cond = cond_ref[...]
    gate = 1.0 / (1.0 + jnp.exp(-cond))
    cols = grad_silu * (gate * (1.0 + cond * (1.0 - gate)))
    for index_ref, table in ((label_ref, class_ref), (bucket_ref, time_ref)):
        places = lax.broadcasted_iota(jnp.int32, (n_shard, table.shape[1]), 1)
        hot = jnp.where(places == index_ref[...], 1.0, 0.0)
        table[...] = lax.dot_general(
            cols,
            hot,
            (((0,), (0,)), ((), ())),
            precision=lax.Precision.HIGHEST,
            preferred_element_type=full_type,
        )
    stream.finish()


def adam_call(place, name, own, grads, state):
    results = vmem_call(
        partial(adam_kernel, place),
        name,
        tuple(jax.ShapeDtypeStruct(x.shape, full_type) for x in state),
        [pltpu.VMEM(x.shape, full_type) for x in state]
        + [pltpu.SemaphoreType.DMA((2, 3 * len(pieces_of(x.shape)))) for x in state[:2]]
        + [pltpu.VMEM(x.shape, full_type) for x in state[:2]],
        20 * (state[0].size + state[1].size),
        state[0].size + state[1].size,
        [own, *grads, *state],
        far_in=range(5, 11),
        far_out=range(6),
    )
    return results[0::2], results[1::2]


def project_kernel(n_piece, table_ref, *refs):
    stream = refs[:4]
    mod_ref, bias_ref = refs[4:6]
    pieces = refs[6 : 6 + n_piece]
    low_ref, weight_ref, out_ref, qkv_ref = refs[6 + n_piece :]
    n_tok, cols = qkv_ref.shape
    size = pieces[0].shape[0]
    for slot, piece in enumerate(pieces):
        place = pl.ds(pl.multiple_of(table_ref[slot] * size, size), size)
        weight_ref[place, :] = piece[:, :cols]
        out_ref[place, :] = piece[:, cols:]
    for r in range(4):
        here = slice(r * n_tok // 4, (r + 1) * n_tok // 4)
        normed, _ = layer_norm(stream[r][: n_tok // 4, :].astype(full_type))
        low = (normed * (1.0 + mod_ref[1:2, :]) + mod_ref[0:1, :]).astype(low_type)
        low_ref[here, :] = low
        qkv_ref[here, :] = (mm(low, weight_ref[...]) + bias_ref[...]).astype(low_type)


def attend_forward_kernel(heads, qkv_ref, att_ref, log_ref):
    n_tok = qkv_ref.shape[0]
    feats = att_ref.shape[0]
    dim = feats // heads
    scale = dim ** (-0.5)
    log_ref[...] = jnp.zeros(log_ref.shape, full_type)

    def step(block, _):
        here = pl.ds(pl.multiple_of(block * BLOCK, BLOCK), BLOCK)
        for head in range(heads):
            queries = qkv_ref[here, head * dim : (head + 1) * dim] * scale
            keys = qkv_ref[:, feats + head * dim : feats + (head + 1) * dim]
            values = qkv_ref[:, 2 * feats + head * dim : 2 * feats + (head + 1) * dim]
            scores = mm_nt(queries.astype(low_type), keys)
            row_max = jnp.max(scores, -1, keepdims=True)
            expo = jnp.exp(scores - row_max)
            total = jnp.sum(expo, -1, keepdims=True)
            probs = (expo * (1.0 / total)).astype(low_type)
            att_ref[head * dim : (head + 1) * dim, here] = jnp.transpose(
                mm(probs, values)
            ).astype(low_type)
            logs = jnp.broadcast_to(row_max + jnp.log(total), (BLOCK, 128))
            log_ref[head : head + 1, here] = jnp.transpose(logs)[0:1]
        return 0

    lax.fori_loop(0, n_tok // BLOCK, step, 0)


def gelu_both(value):
    root = (2.0 / math.pi) ** 0.5
    square = value * value
    bend = jnp.tanh(root * value * (1.0 + 0.044715 * square))
    half = 0.5 * (1.0 + bend)
    slope = half + 0.5 * value * (1.0 - bend * bend) * (root * (1.0 + 3 * 0.044715 * square))
    return (value * half, slope)


def deal(table_ref, pieces, source):
    size = pieces[0].shape[0]
    for slot, piece in enumerate(pieces):
        piece[...] = source[pl.ds(pl.multiple_of(table_ref[slot] * size, size), size), :]


def mlp_kernel(n_piece, table_ref, *refs):
    att = refs[:4]
    tokens = refs[4:8]
    mod_ref, bias_ref = refs[8:10]
    out_parts = refs[10:14]
    pieces = refs[14 : 14 + n_piece]
    (
        att_all,
        out_own,
        residual_ref,
        branch_ref,
        *more,
        sums_ref,
    ) = refs[14 + n_piece : 31 + n_piece]
    normed_refs, inverse_refs, part_refs, back_refs = more[:2], more[2:4], more[4:8], more[8:12]
    dealt = refs[31 + n_piece : 31 + 2 * n_piece]
    weights, grads_ref, out_all, low_ref, act_ref, hid_ref, cot_ref = refs[31 + 2 * n_piece :]
    feats, n_tok = att[0].shape
    width = tokens[0].shape[1]
    size = n_tok // 4
    own = table_ref[n_piece]
    assemble(table_ref, pieces, weights)
    for r in range(4):
        start = pl.multiple_of((own ^ r) * feats, feats)
        att_all[pl.ds(start, feats), :] = att[r][...]
    for r in range(4):
        for j in range(4):

            @pl.when((own ^ r) == j)
            def _():
                out_all[:, j * feats : (j + 1) * feats] = out_parts[r][...]

    out_own[...] = out_all[pl.ds(pl.multiple_of(own * feats, feats), feats), :]
    shift_m, scale_m, gate_m = [mod_ref[i : i + 1, :] for i in (3, 4, 5)]
    totals = [jnp.zeros((1, width), full_type) for _ in range(5)]
    for r in range(4):
        here = slice(r * size, (r + 1) * size)
        branch = mm_tn(att_all[:, here], out_all[...]) + bias_ref[0:1, :]
        residual = tokens[r][:size, :].astype(full_type) + mod_ref[2:3, :] * branch
        if r == 0:
            residual_ref[...] = residual
            branch_ref[...] = branch
        normed, inverse = layer_norm(residual)
        if r % 2 == 0:
            normed_refs[r // 2][...] = normed
            inverse_refs[r // 2][...] = inverse
        low = (normed * (1.0 + scale_m) + shift_m).astype(low_type)
        low_ref[here, :] = low
        hidden = mm(low, weights[:, :width]) + bias_ref[2:3, :]
        active, slope = gelu_both(hidden)
        active = active.astype(low_type)
        act_ref[here, :] = active
        part = mm(active, weights[:, width:])
        part_refs[r][...] = part.astype(low_type)
        grad_y = tokens[r][size:, :].astype(full_type)
        totals[0] += jnp.sum(grad_y * part, 0, keepdims=True)
        if r == 0:
            totals[0] += jnp.sum(grad_y, 0, keepdims=True) * bias_ref[1:2, :]
        grad_low = (gate_m * grad_y).astype(low_type)
        cot_ref[here, :] = grad_low
        grad_hid = (mm_nt(grad_low, weights[:, width:]) * slope).astype(low_type)
        hid_ref[here, :] = grad_hid
        back = mm_nt(grad_hid, weights[:, :width])
        back_refs[r][...] = back.astype(low_type)
        totals[1] += jnp.sum(back * normed, 0, keepdims=True)
        totals[2] += jnp.sum(back, 0, keepdims=True)
        totals[3] += jnp.sum(grad_hid.astype(full_type), 0, keepdims=True)
        totals[4] += jnp.sum(grad_low.astype(full_type), 0, keepdims=True)
    sums_ref[...] = jnp.zeros(sums_ref.shape, full_type)
    sums_ref[3:4, :] = totals[2]
    sums_ref[4:5, :] = totals[1]
    sums_ref[5:6, :] = totals[0]
    sums_ref[pl.ds(9 + own, 1), :] = totals[3]
    sums_ref[13:14, :] = jnp.where(own == 0, totals[4], 0.0)
    grads_ref[:, :width] = mm_tn(low_ref[...], hid_ref[...]).astype(low_type)
    grads_ref[:, width:] = mm_tn(act_ref[...], cot_ref[...]).astype(low_type)
    deal(table_ref, dealt, grads_ref)


def attend_backward_kernel(heads, own_ref, *refs):
    grad = refs[:4]
    att_all, out_own, qkv_ref, log_ref, low_ref = refs[4:9]
    out_ref, grads_ref, sums_ref = refs[9:12]
    all_ref, cols_ref, grad_ref, keys_t, sum_k, sum_v = refs[12:]
    n_tok, width = low_ref.shape
    feats = out_own.shape[0]
    size = n_tok // 4
    dim = feats // heads
    scale = dim ** (-0.5)
    own = own_ref[0]
    for r in range(4):
        here = slice(r * size, (r + 1) * size)
        all_ref[here, :] = grad[r][...]
        grad_ref[here, :] = mm_nt(grad[r][...], out_own[...]).astype(low_type)
    for j in range(4):

        @pl.when(own == j)
        def _():
            cols_ref[...] = all_ref[:, j * feats : (j + 1) * feats]

    grads_ref[:, 3 * feats :] = mm(att_all[...], cols_ref[...]).astype(low_type)
    keys_t[...] = jnp.transpose(qkv_ref[:, feats : 2 * feats])
    sum_k[...] = jnp.zeros(sum_k.shape, full_type)
    sum_v[...] = jnp.zeros(sum_v.shape, full_type)

    def step(block, _):
        here = pl.ds(pl.multiple_of(block * BLOCK, BLOCK), BLOCK)
        for head in range(heads):
            cut = slice(head * dim, (head + 1) * dim)
            queries = (qkv_ref[here, cut] * scale).astype(low_type)
            keys = qkv_ref[:, feats + head * dim : feats + (head + 1) * dim]
            values = qkv_ref[:, 2 * feats + head * dim : 2 * feats + (head + 1) * dim]
            grad_att = grad_ref[here, cut]
            probs = jnp.exp(mm_nt(keys, queries) - log_ref[head : head + 1, here])
            grad_probs = mm_nt(values, grad_att)
            delta = jnp.sum(probs * grad_probs, 0, keepdims=True)
            grad_scores = (probs * (grad_probs - delta)).astype(low_type)
            sum_v[:, cut] += mm(probs.astype(low_type), grad_att)
            sum_k[:, cut] += mm(grad_scores, queries)
            grad_q = mm(keys_t[cut, :], grad_scores) * scale
            out_ref[here, cut] = jnp.transpose(grad_q).astype(low_type)
        return 0

    lax.fori_loop(0, n_tok // BLOCK, step, 0)
    out_ref[:, feats : 2 * feats] = sum_k[...].astype(low_type)
    out_ref[:, 2 * feats :] = sum_v[...].astype(low_type)
    grads_ref[:, : 3 * feats] = mm_tn(low_ref[...], out_ref[...]).astype(low_type)
    sums_ref[...] = jnp.zeros(sums_ref.shape, full_type)
    bias = jnp.sum(out_ref[...].astype(full_type), 0, keepdims=True)
    total = jnp.sum(all_ref[...].astype(full_type), 0, keepdims=True)
    sums_ref[8:9, :] = jnp.where(own == 0, total, 0.0)
    for j in range(4):

        @pl.when(own == j)
        def _():
            sums_ref[6:7, j * feats : (j + 1) * feats] = bias[:, :feats]
            sums_ref[7:8, j * feats : (j + 1) * feats] = bias[:, 2 * feats :]


def project_backward_kernel(*refs):
    tokens = refs[:4]
    grad_ref, weight_ref, gate_ref, sums_mlp, sums_att = refs[4:9]
    back_refs, sums_ref = refs[9:13], refs[13]
    size, width = back_refs[0].shape
    totals = [jnp.zeros((1, width), full_type) for _ in range(2)]
    for r in range(4):
        here = slice(r * size, (r + 1) * size)
        back = mm_nt(grad_ref[here, :], weight_ref[...])
        back_refs[r][...] = back.astype(low_type)
        normed, _ = layer_norm(tokens[r][:size, :].astype(full_type))
        totals[0] += jnp.sum(back, 0, keepdims=True)
        totals[1] += jnp.sum(back * normed, 0, keepdims=True)
    sums_ref[...] = sums_mlp[...] + sums_att[...]
    sums_ref[0:1, :] = totals[0]
    sums_ref[1:2, :] = totals[1]
    sums_ref[2:3, :] = gate_ref[...]


def adam_step(weight, first, second, grad):
    first_new = beta_one * first + (1.0 - beta_one) * grad
    second_new = beta_two * second + (1.0 - beta_two) * grad * grad
    corr_one = 1.0 - beta_one**ADAM_STEP
    corr_two = 1.0 - beta_two**ADAM_STEP
    weight_new = weight - learn_rate * (first_new / corr_one) / (
        jnp.sqrt(second_new / corr_two) + adam_eps
    )
    return (weight_new, first_new, second_new)


def swap(value, distance):
    return lax.ppermute(value, "seq", [(p, p ^ distance) for p in range(4)])


def gather_rel(value):
    far = swap(value, 2)
    near = swap(value, 1)
    cross = swap(far, 1)
    return [value, near, far, cross]


def scatter_rel(blocks):
    near_own, near_far = [swap(blocks[r], 1).astype(full_type) for r in (1, 3)]
    far_own = swap((blocks[2].astype(full_type) + near_far).astype(low_type), 2)
    return blocks[0].astype(full_type) + near_own + far_own.astype(full_type)


CYCLE = (0, 2, 4, 6, 7, 5, 3, 1)


def ring_pairs(count):
    right = [(CYCLE[i], CYCLE[(i + 1) % count]) for i in range(count)]
    return right, [(to, start) for start, to in right]


def ring_hop(pieces, count):
    if count != len(CYCLE):
        return pieces
    right, left = ring_pairs(count)
    hop = len(pieces) // 2
    ahead, behind = (pieces[-2], pieces[-1]) if hop else (pieces[0], pieces[0])
    more = [lax.ppermute(ahead, "shard", right)]
    if hop < count // 2 - 1:
        more.append(lax.ppermute(behind, "shard", left))
    return pieces + more


def ring_begin(value, count):
    if count != len(CYCLE):
        return [spread(value, "shard", count).reshape(-1, value.shape[-1])]
    return ring_hop([value], count)


def ring_scatter(pieces, count, first):
    if len(pieces) == 1:
        whole = pieces[0].reshape(count, -1, pieces[0].shape[-1])
        arrived = lax.all_to_all(whole, "shard", 0, 0, tiled=True)
        return [jnp.sum(arrived.astype(full_type), 0).astype(low_type)]
    right, left = ring_pairs(count)
    ahead, behind = pieces[count - 1], pieces[count - 3]
    for hop in range(count // 2, 1, -1):
        ahead = after(lax.ppermute(ahead, "shard", right), *first)
        ahead = (ahead.astype(full_type) + pieces[2 * hop - 2].astype(full_type)).astype(low_type)
    for hop in range(count // 2 - 1, 0, -1):
        behind = after(lax.ppermute(behind, "shard", left), *first)
        if hop > 1:
            behind = (behind.astype(full_type) + pieces[2 * hop - 3].astype(full_type)).astype(
                low_type
            )
    return [pieces[0], ahead, behind]


def ring_finish(parts, count):
    if len(parts) == 1:
        return parts[0]
    last = lax.ppermute(parts[1], "shard", ring_pairs(count)[0])
    return sum(x.astype(full_type) for x in (parts[0], last, parts[2])).astype(low_type)


def ring_table(own, count):
    if count != len(CYCLE):
        return jnp.zeros((1,), jnp.int32)
    lines = []
    for s in range(count):
        at = CYCLE.index(s)
        line = [s]
        for hop in range(1, count // 2 + 1):
            line.append(CYCLE[(at - hop) % count])
            if hop < count // 2:
                line.append(CYCLE[(at + hop) % count])
        lines.append(line)
    return lax.dynamic_index_in_dim(jnp.array(lines, jnp.int32), own, 0, keepdims=False)


def permute_blocks(value, distance):
    size = value.shape[1] // 4
    return jnp.concatenate(
        [value[:, (r ^ distance) * size : ((r ^ distance) + 1) * size] for r in range(4)], 1
    )


def spread(value, axis, count):
    return lax.all_to_all(
        jnp.broadcast_to(value[None], (count,) + value.shape), axis, 0, 0, tiled=True
    )


def token_sum(tensor):
    return jnp.sum(tensor.astype(full_type), axis=0)


def shards(
    latents,
    cotangent,
    class_labels,
    time_buckets,
    class_table,
    time_table,
    ada_weight,
    qkv_weight,
    out_weight,
    up_weight,
    down_weight,
    biases,
    ada_first,
    qkv_first,
    out_first,
    up_first,
    down_first,
    bias_first,
    ada_second,
    qkv_second,
    out_second,
    up_second,
    down_second,
    bias_second,
    n_shard,
    n_seq,
):
    assert n_seq == 4 and latents.shape[0] == 1 and class_labels.shape[0] == n_shard
    s_own = lax.axis_index("shard")
    q_own = lax.axis_index("seq")
    tok_dev, width = latents.shape[1:]
    head_dim = width // HEADS
    score_scale = head_dim ** (-0.5)
    heads_own = HEADS // n_seq
    feats = heads_own * head_dim
    rows = ada_weight.shape[0]
    ff = up_weight.shape[1]
    ff_cell = ff // (n_shard * n_seq)
    ff_own = ff // n_seq

    table = jnp.concatenate([ring_table(s_own, n_shard), q_own[None].astype(jnp.int32)])
    own_index = q_own[None].astype(jnp.int32)
    first_part, rest_part = vmem_call(
        cut_kernel,
        "cut",
        (
            jax.ShapeDtypeStruct((rows, 4 * feats), low_type),
            jax.ShapeDtypeStruct((rows, width + ff_own), low_type),
        ),
        [pltpu.VMEM(x.shape, full_type) for x in (qkv_weight, out_weight, up_weight, down_weight)]
        + [pltpu.SemaphoreType.DMA((16,))],
        0,
        0,
        [own_index, qkv_weight, out_weight, up_weight, down_weight],
        far_in=range(1, 5),
    )

    cond = jnp.take(class_table, class_labels, axis=0).astype(full_type) + jnp.take(
        time_table, time_buckets, axis=0
    ).astype(full_type)
    cond_cols = lax.dynamic_slice_in_dim(cond, s_own * rows, rows, 1)
    silu_cols = jax.nn.silu(cond_cols).astype(low_type)
    ada_low = ada_weight.astype(low_type)
    mod_partial = mm(silu_cols, ada_low)
    bias_low = biases.astype(low_type).astype(full_type).reshape(1, -1)
    payload = jnp.concatenate(
        [mod_partial, jnp.broadcast_to(bias_low, (n_shard, bias_low.shape[1]))], 1
    )
    first_pieces = ring_begin(first_part, n_shard)
    payload = after(payload, *first_pieces)
    arrived = lax.all_to_all(payload, "shard", split_axis=0, concat_axis=0, tiled=True)
    for _ in range(2):
        first_pieces = ring_hop(first_pieces, n_shard)
    both = jnp.concatenate([latents[0], cotangent[0]])
    far, arrived, first_pieces = lax.optimization_barrier((swap(both, 2), arrived, first_pieces))
    tokens = [both, swap(both, 1), far, swap(far, 1)]
    first_pieces = ring_hop(first_pieces, n_shard)
    n_piece = len(first_pieces)
    mod_sum = jnp.sum(arrived[:, : 6 * width], 0)
    bias_full = jnp.transpose(
        arrived[:, 6 * width :].reshape(n_shard, biases.shape[0], rows), (1, 0, 2)
    ).reshape(biases.shape[0], width)
    modulation = mod_sum.reshape(6, width) + bias_full[0:6]
    shift_a, scale_a, gate_a, shift_m, scale_m, gate_m = [modulation[i] for i in range(6)]

    n_tok = n_seq * tok_dev

    bias_query = lax.dynamic_slice_in_dim(bias_full[6], q_own * feats, feats)
    bias_value = lax.dynamic_slice_in_dim(bias_full[7], q_own * feats, feats)
    bias_qkv = jnp.concatenate([bias_query, jnp.zeros_like(bias_query), bias_value])[None]
    pair_count = heads_own * n_tok * n_tok
    modulated_a, qkv_w, out_q, qkv = vmem_call(
        partial(project_kernel, n_piece),
        "project",
        (
            jax.ShapeDtypeStruct((n_tok, width), low_type),
            jax.ShapeDtypeStruct((width, 3 * feats), low_type),
            jax.ShapeDtypeStruct((width, feats), low_type),
            jax.ShapeDtypeStruct((n_tok, 3 * feats), low_type),
        ),
        [],
        6 * n_tok * width * feats,
        n_tok,
        [table, *tokens, modulation, bias_qkv, *first_pieces],
    )
    out_far = swap(out_q, 2)
    qkv, rest_pieces = lax.optimization_barrier((qkv, ring_begin(rest_part, n_shard)))
    rest_pieces = ring_hop(rest_pieces, n_shard)
    att_own, logs = vmem_call(
        partial(attend_forward_kernel, heads_own),
        "attend_forward",
        (
            jax.ShapeDtypeStruct((feats, n_tok), low_type),
            jax.ShapeDtypeStruct((8, n_tok), full_type),
        ),
        [],
        4 * pair_count * head_dim,
        pair_count,
        [qkv],
        0,
    )
    att_own, out_far, rest_pieces = lax.optimization_barrier((att_own, out_far, rest_pieces))
    out_parts = [out_q, swap(out_q, 1), out_far, swap(out_far, 1)]
    rest_pieces = ring_hop(rest_pieces, n_shard)
    att_far = swap(permute_blocks(att_own, 2), 2)
    att_far, rest_pieces = lax.optimization_barrier((att_far, rest_pieces))
    rest_pieces = ring_hop(rest_pieces, n_shard)
    att_near = swap(permute_blocks(att_own, 1), 1)
    att_cross = swap(permute_blocks(att_far, 1), 1)

    bias_ff = lax.dynamic_index_in_dim(
        bias_full[9:13].reshape(n_shard, n_seq, ff_cell), q_own, 1, keepdims=False
    ).reshape(ff_own)
    bias_mlp = jnp.stack([bias_full[8], bias_full[13], bias_ff])
    attended, out_own, residual, branch_a, *mlp_out = (
        vmem_call(
            partial(mlp_kernel, n_piece),
            "mlp",
            (
                jax.ShapeDtypeStruct((width, n_tok), low_type),
                jax.ShapeDtypeStruct((feats, width), low_type),
            )
            + 4 * (jax.ShapeDtypeStruct((tok_dev, width), full_type),)
            + 2 * (jax.ShapeDtypeStruct((tok_dev, 1), full_type),)
            + 8 * (jax.ShapeDtypeStruct((tok_dev, width), low_type),)
            + (jax.ShapeDtypeStruct((16, width), full_type),)
            + n_piece * (jax.ShapeDtypeStruct((width // n_piece, width + ff_own), low_type),),
            [
                pltpu.VMEM((width, width + ff_own), low_type),
                pltpu.VMEM((width, width + ff_own), low_type),
                pltpu.VMEM((width, width), low_type),
            ]
            + [pltpu.VMEM((n_tok, width), low_type)] * 4,
            14 * n_tok * width * width,
            n_tok * width,
            [
                table,
                att_own,
                att_near,
                att_far,
                att_cross,
                *tokens,
                modulation,
                bias_mlp,
                *out_parts,
                *rest_pieces,
            ],
        )
    )
    normed_m, inverse_m = mlp_out[:2], mlp_out[2:4]
    branch_part, back, sums_mlp, grads_mlp = mlp_out[4:8], mlp_out[8:12], mlp_out[12], mlp_out[13:]
    near_zero, near_two = swap(back[1], 1), swap(back[3], 1)
    chip = [
        (mine.astype(full_type) + theirs.astype(full_type)).astype(low_type)
        for mine, theirs in ((back[0], near_zero), (back[2], near_two))
    ]
    across = [swap(chip[1], 2), swap(chip[0], 2)]
    mlp_parts = ring_scatter(grads_mlp, n_shard, chip)
    grad_residuals = [
        tokens[2 * i][tok_dev:].astype(full_type)
        + norm_back(
            (chip[i].astype(full_type) + across[i].astype(full_type)) * (1.0 + scale_m),
            normed_m[i],
            inverse_m[i],
        )
        for i in range(2)
    ]
    grad_residual = grad_residuals[0]
    grad_low = [(gate_a * part).astype(low_type) for part in grad_residuals]
    grad_low, mlp_parts = lax.optimization_barrier((grad_low, mlp_parts))
    grad_branch_a = [grad_low[0], swap(grad_low[0], 1), grad_low[1], swap(grad_low[1], 1)]
    mlp_total = ring_finish(mlp_parts, n_shard)
    mlp_total, grad_branch_a = lax.optimization_barrier((mlp_total, grad_branch_a))
    grad_gate_a = token_sum(grad_residual * branch_a)
    grad_qkv, grads_att, sums_att = vmem_call(
        partial(attend_backward_kernel, heads_own),
        "attend_backward",
        (
            jax.ShapeDtypeStruct((n_tok, 3 * feats), low_type),
            jax.ShapeDtypeStruct((width, 4 * feats), low_type),
            jax.ShapeDtypeStruct((16, width), full_type),
        ),
        [
            pltpu.VMEM((n_tok, width), low_type),
            pltpu.VMEM((n_tok, feats), low_type),
            pltpu.VMEM((n_tok, feats), low_type),
            pltpu.VMEM((feats, n_tok), low_type),
            pltpu.VMEM((n_tok, feats), full_type),
            pltpu.VMEM((n_tok, feats), full_type),
        ],
        10 * n_tok * width * feats + 10 * pair_count * head_dim,
        pair_count,
        [own_index, *grad_branch_a, attended, out_own, qkv, logs, modulated_a],
    )
    *grad_mod_a_part, small = vmem_call(
        project_backward_kernel,
        "project_backward",
        4 * (jax.ShapeDtypeStruct((tok_dev, width), low_type),)
        + (jax.ShapeDtypeStruct((16, width), full_type),),
        [],
        6 * n_tok * width * feats,
        n_tok,
        [*tokens, grad_qkv, qkv_w, grad_gate_a[None], sums_mlp, sums_att],
        0,
    )
    small = small + swap(small, 1)
    small = small + swap(small, 2)
    arrived_att = lax.all_to_all(
        grads_att.reshape(n_shard, rows, 4 * feats), "shard", 0, 0, tiled=True
    )
    normed_a, inverse_a = layer_norm(latents[0].astype(full_type))
    latents_grad = grad_residual + norm_back(
        scatter_rel([after(x, small) for x in grad_mod_a_part]) * (1.0 + scale_a),
        normed_a,
        inverse_a,
    )
    branch_own = scatter_rel([after(x, small) for x in branch_part]) + bias_full[13]
    block_out = (residual + gate_m * branch_own).astype(low_type)

    every = spread(after(small, arrived_att), "shard", n_shard)
    ada_state = (ada_weight, ada_first, ada_second)
    bias_state = (biases, bias_first, bias_second)
    tables = tuple(jax.ShapeDtypeStruct((rows, t.shape[0]), full_type) for t in (class_table, time_table))
    done = vmem_call(
        partial(finish_kernel, n_shard),
        "finish",
        tuple(jax.ShapeDtypeStruct(x.shape, full_type) for x in ada_state + bias_state) + tables,
        [
            pltpu.VMEM((16, width), full_type),
            pltpu.VMEM(biases.shape, full_type),
        ]
        + [pltpu.VMEM(ada_weight.shape, full_type)] * 3
        + [pltpu.SemaphoreType.DMA((2, 18))],
        24 * ada_weight.size,
        ada_weight.size,
        [
            s_own[None].astype(jnp.int32),
            every,
            silu_cols,
            cond_cols,
            class_labels[:, None],
            time_buckets[:, None],
            *ada_state,
            *bias_state,
        ],
        far_in=range(6, 9),
        far_out=range(3),
    )
    ada_new, bias_new = done[:3], done[3:6]
    class_grad, time_grad = jnp.transpose(done[6]), jnp.transpose(done[7])

    att_total = jnp.sum(arrived_att.astype(full_type), 0).astype(low_type)
    mlp_up, mlp_down = adam_call(
        place_mlp,
        "adam_mlp",
        own_index,
        [after(x, att_total) for x in gather_rel(after(mlp_total, small))],
        [up_weight, down_weight, up_first, down_first, up_second, down_second],
    )
    att_qkv, att_out = adam_call(
        place_att,
        "adam_att",
        own_index,
        gather_rel(att_total),
        [qkv_weight, out_weight, qkv_first, out_first, qkv_second, out_second],
    )

    updates = [
        ada_new,
        att_qkv,
        att_out,
        mlp_up,
        mlp_down,
        bias_new,
    ]
    return (
        block_out[None],
        latents_grad[None],
        class_grad,
        time_grad,
        *[update[0] for update in updates],
        *[update[1] for update in updates],
        *[update[2] for update in updates],
    )


def solution(mesh):
    tokens = P("shard", "seq", None)
    rows = P("shard", None)
    cols = P(None, "shard")
    state = (rows, rows, rows, rows, rows, cols)
    return jax.shard_map(
        partial(shards, n_shard=mesh.shape["shard"], n_seq=mesh.shape["seq"]),
        mesh=mesh,
        in_specs=(tokens, tokens, P(), P(), P(), P()) + 3 * state,
        out_specs=(tokens, tokens, cols, cols) + 3 * state,
        check_vma=False,
    )
```

```python
import math
from functools import partial

import jax
import jax.numpy as jnp
from jax import lax
from jax.experimental import pallas as pl
from jax.experimental.pallas import tpu as pltpu
from jax.sharding import PartitionSpec as P

HEADS = 12
ADAM_STEP = 10
BLOCK = 256


norm_eps = 1e-06
beta_one = 0.9
beta_two = 0.999
learn_rate = 0.05
adam_eps = 1e-08

low_type = jnp.bfloat16
full_type = jnp.float32


def layer_norm(values_in):
    centred = values_in - jnp.mean(values_in, -1, keepdims=True)
    inverse = lax.rsqrt(jnp.mean(centred * centred, -1, keepdims=True) + norm_eps)
    return (centred * inverse, inverse)


def norm_back(gradient, normed, inverse):
    return inverse * (
        gradient
        - jnp.mean(gradient, -1, keepdims=True)
        - normed * jnp.mean(gradient * normed, -1, keepdims=True)
    )


def dot(left, right, dims):
    return lax.dot_general(left, right, (dims, ((), ())), preferred_element_type=full_type)


def mm(left, right):
    return dot(left, right, ((1,), (0,)))


def mm_nt(left, right):
    return dot(left, right, ((1,), (1,)))


def mm_tn(left, right):
    return dot(left, right, ((0,), (0,)))


def vmem_call(
    kernel, name, out_shape, scratch, flops, exps, operands, n_scalar=1, far_in=(), far_out=()
):
    specs = [pl.BlockSpec(memory_space=pltpu.SMEM)] * n_scalar
    for place in range(n_scalar, len(operands)):
        specs.append(pl.BlockSpec(memory_space=pl.ANY if place in far_in else pltpu.VMEM))
    moved = sum(x.size * x.dtype.itemsize for x in operands)
    moved += sum(x.size * x.dtype.itemsize for x in out_shape)
    return pl.pallas_call(
        kernel,
        out_shape=out_shape,
        in_specs=specs,
        out_specs=tuple(
            pl.BlockSpec(memory_space=pl.ANY if place in far_out else pltpu.VMEM)
            for place in range(len(out_shape))
        ),
        scratch_shapes=scratch,
        compiler_params=pltpu.CompilerParams(vmem_limit_bytes=60 * 2**20),
        cost_estimate=pl.CostEstimate(flops=flops, bytes_accessed=moved, transcendentals=exps),
        name=name,
    )(*operands)


def after(value, *others):
    return lax.optimization_barrier((value, *others))[0]


def assemble(table_ref, pieces, target):
    size = pieces[0].shape[0]
    for slot, piece in enumerate(pieces):
        target[pl.ds(pl.multiple_of(table_ref[slot] * size, size), size), :] = piece[...]


def cut_kernel(table_ref, qkv_all, out_all, up_all, down_all, first_ref, rest_ref, *scratch):
    held, sems = scratch[:4], scratch[4]
    qkv_ref, out_ref, up_ref, down_ref = held
    copies = []
    for source, target in zip((qkv_all, out_all, up_all, down_all), held):
        step = 768 if source.shape[1] > 768 else 256
        for start in range(0, source.shape[1], step):
            cut = (slice(None), pl.ds(start, step))
            copies.append(
                pltpu.make_async_copy(source.at[cut], target.at[cut], sems.at[len(copies)])
            )
    for copy in copies:
        copy.start()
    for copy in copies:
        copy.wait()
    rows, width = out_ref.shape
    feats = width // 4
    cell = down_ref.shape[0] // 4
    n_shard = up_ref.shape[1] // (4 * cell)
    for j in range(4):

        @pl.when(table_ref[0] == j)
        def _():
            for part in range(3):
                start = part * width + j * feats
                first_ref[:, part * feats : (part + 1) * feats] = qkv_ref[
                    :, start : start + feats
                ].astype(low_type)
            first_ref[:, 3 * feats :] = out_ref[:, j * feats : (j + 1) * feats].astype(low_type)
            for s in range(n_shard):
                start = (s * 4 + j) * cell
                rest_ref[:, s * cell : (s + 1) * cell] = up_ref[:, start : start + cell].astype(
                    low_type
                )
            rest_ref[:, width:] = down_ref[j * cell : (j + 1) * cell, :].astype(low_type)


def pieces_of(shape):
    step = 768 if shape[1] > 768 else 256
    return [(slice(None), pl.ds(start, step)) for start in range(0, shape[1], step)]


class Stream:
    def __init__(self, state, outs, held, sems):
        self.cuts = pieces_of(state[0].shape)
        self.held, self.outs, self.sems = held, outs, sems
        self.loads = [
            [
                pltpu.make_async_copy(source.at[cut], target.at[cut], sems.at[0, 3 * at + i])
                for i, (source, target) in enumerate(zip(state, held))
            ]
            for at, cut in enumerate(self.cuts)
        ]
        self.stores = []

    def start(self):
        for group in self.loads:
            for copy in group:
                copy.start()

    def weight(self, at):
        for copy in self.loads[at]:
            copy.wait()
        return self.held[0][self.cuts[at]]

    def update(self, at, grad):
        cut = self.cuts[at]
        results = adam_step(*[ref[cut] for ref in self.held], grad)
        for i, (ref, result) in enumerate(zip(self.held, results)):
            ref[cut] = result
            copy = pltpu.make_async_copy(ref.at[cut], self.outs[i].at[cut], self.sems.at[1, 3 * at + i])
            copy.start()
            self.stores.append(copy)

    def finish(self):
        for copy in self.stores:
            copy.wait()


def adam_kernel(place, table_ref, *refs):
    grads, state, outs = refs[:4], refs[4:10], refs[10:16]
    held, sems, grad_refs = refs[16:22], refs[22:24], refs[24:]
    streams = [Stream(state[i::2], outs[i::2], held[i::2], sems[i]) for i in range(2)]
    for stream in streams:
        stream.start()
    for j in range(4):

        @pl.when(table_ref[0] == j)
        def _():
            for r in range(4):
                place(j ^ r, grads[r][...].astype(full_type), *grad_refs)

    for stream, grad in zip(streams, grad_refs):
        for at, cut in enumerate(stream.cuts):
            stream.weight(at)
            stream.update(at, grad[cut])
    for stream in streams:
        stream.finish()


def place_mlp(j, grad, grad_up, grad_down):
    width = grad_down.shape[1]
    cell = grad_down.shape[0] // 4
    for s in range(grad_up.shape[1] // (4 * cell)):
        start = (s * 4 + j) * cell
        grad_up[:, start : start + cell] = grad[:, s * cell : (s + 1) * cell]
    grad_down[j * cell : (j + 1) * cell, :] = grad[:, width:]


def place_att(j, grad, grad_qkv, grad_out):
    width = grad_out.shape[1]
    feats = width // 4
    for part in range(3):
        start = part * width + j * feats
        grad_qkv[:, start : start + feats] = grad[:, part * feats : (part + 1) * feats]
    grad_out[:, j * feats : (j + 1) * feats] = grad[:, 3 * feats :]


def finish_kernel(n_shard, place_ref, *refs):
    every_ref, silu_ref, cond_ref, label_ref, bucket_ref = refs[:5]
    ada, bias = refs[5:8], refs[8:11]
    ada_out, bias_out, class_ref, time_ref = refs[11:14], refs[14:17], refs[17], refs[18]
    sums_ref, bias_grad, *held, sems = refs[19:]
    stream = Stream(ada, ada_out, held, sems)
    stream.start()
    rows = cond_ref.shape[1]
    width = every_ref.shape[2]
    grad_silu = jnp.zeros((n_shard, rows), full_type)
    for slot in range(6):
        grad_mod = every_ref[:, slot, :].astype(low_type)
        grad_silu += mm_nt(grad_mod, stream.weight(slot).astype(low_type))
        stream.update(slot, mm_tn(silu_ref[...], grad_mod))
        sums_ref[slot : slot + 1, :] = jnp.sum(grad_mod.astype(full_type), 0, keepdims=True)
    for slot in range(6, 14):
        sums_ref[slot : slot + 1, :] = jnp.sum(every_ref[:, slot, :], 0, keepdims=True)
    for s in range(n_shard):

        @pl.when(place_ref[0] == s)
        def _():
            for slot in range(14):
                row, cell = slot, s
                if 9 <= slot < 13:
                    row, cell = 9 + s % 4, (n_shard * (slot - 9) + s) // 4
                bias_grad[slot : slot + 1, :] = sums_ref[
                    row : row + 1, cell * rows : (cell + 1) * rows
                ]

    results = adam_step(*[ref[...] for ref in bias], bias_grad[...])
    for ref, result in zip(bias_out, results):
        ref[...] = result
    cond = cond_ref[...]
    gate = 1.0 / (1.0 + jnp.exp(-cond))
    cols = grad_silu * (gate * (1.0 + cond * (1.0 - gate)))
    for index_ref, table in ((label_ref, class_ref), (bucket_ref, time_ref)):
        places = lax.broadcasted_iota(jnp.int32, (n_shard, table.shape[1]), 1)
        hot = jnp.where(places == index_ref[...], 1.0, 0.0)
        table[...] = lax.dot_general(
            cols,
            hot,
            (((0,), (0,)), ((), ())),
            precision=lax.Precision.HIGHEST,
            preferred_element_type=full_type,
        )
    stream.finish()


def adam_call(place, name, own, grads, state):
    results = vmem_call(
        partial(adam_kernel, place),
        name,
        tuple(jax.ShapeDtypeStruct(x.shape, full_type) for x in state),
        [pltpu.VMEM(x.shape, full_type) for x in state]
        + [pltpu.SemaphoreType.DMA((2, 3 * len(pieces_of(x.shape)))) for x in state[:2]]
        + [pltpu.VMEM(x.shape, full_type) for x in state[:2]],
        20 * (state[0].size + state[1].size),
        state[0].size + state[1].size,
        [own, *grads, *state],
        far_in=range(5, 11),
        far_out=range(6),
    )
    return results[0::2], results[1::2]


def project_kernel(n_piece, table_ref, *refs):
    stream = refs[:4]
    mod_ref, bias_ref = refs[4:6]
    pieces = refs[6 : 6 + n_piece]
    low_ref, weight_ref, out_ref, qkv_ref = refs[6 + n_piece :]
    n_tok, cols = qkv_ref.shape
    size = pieces[0].shape[0]
    for slot, piece in enumerate(pieces):
        place = pl.ds(pl.multiple_of(table_ref[slot] * size, size), size)
        weight_ref[place, :] = piece[:, :cols]
        out_ref[place, :] = piece[:, cols:]
    for r in range(4):
        here = slice(r * n_tok // 4, (r + 1) * n_tok // 4)
        normed, _ = layer_norm(stream[r][: n_tok // 4, :].astype(full_type))
        low = (normed * (1.0 + mod_ref[1:2, :]) + mod_ref[0:1, :]).astype(low_type)
        low_ref[here, :] = low
        qkv_ref[here, :] = (mm(low, weight_ref[...]) + bias_ref[...]).astype(low_type)


def attend_forward_kernel(heads, qkv_ref, att_ref, log_ref):
    n_tok = qkv_ref.shape[0]
    feats = att_ref.shape[0]
    dim = feats // heads
    scale = dim ** (-0.5)
    log_ref[...] = jnp.zeros(log_ref.shape, full_type)

    def step(block, _):
        here = pl.ds(pl.multiple_of(block * BLOCK, BLOCK), BLOCK)
        for head in range(heads):
            queries = qkv_ref[here, head * dim : (head + 1) * dim] * scale
            keys = qkv_ref[:, feats + head * dim : feats + (head + 1) * dim]
            values = qkv_ref[:, 2 * feats + head * dim : 2 * feats + (head + 1) * dim]
            scores = mm_nt(queries.astype(low_type), keys)
            row_max = jnp.max(scores, -1, keepdims=True)
            expo = jnp.exp(scores - row_max)
            total = jnp.sum(expo, -1, keepdims=True)
            probs = (expo * (1.0 / total)).astype(low_type)
            att_ref[head * dim : (head + 1) * dim, here] = jnp.transpose(
                mm(probs, values)
            ).astype(low_type)
            logs = jnp.broadcast_to(row_max + jnp.log(total), (BLOCK, 128))
            log_ref[head : head + 1, here] = jnp.transpose(logs)[0:1]
        return 0

    lax.fori_loop(0, n_tok // BLOCK, step, 0)


def gelu_both(value):
    root = (2.0 / math.pi) ** 0.5
    square = value * value
    bend = jnp.tanh(root * value * (1.0 + 0.044715 * square))
    half = 0.5 * (1.0 + bend)
    slope = half + 0.5 * value * (1.0 - bend * bend) * (root * (1.0 + 3 * 0.044715 * square))
    return (value * half, slope)


def deal(table_ref, pieces, source):
    size = pieces[0].shape[0]
    for slot, piece in enumerate(pieces):
        piece[...] = source[pl.ds(pl.multiple_of(table_ref[slot] * size, size), size), :]


def mlp_kernel(n_piece, table_ref, *refs):
    att = refs[:4]
    tokens = refs[4:8]
    mod_ref, bias_ref = refs[8:10]
    out_parts = refs[10:14]
    pieces = refs[14 : 14 + n_piece]
    (
        att_all,
        out_own,
        residual_ref,
        branch_ref,
        *more,
        sums_ref,
    ) = refs[14 + n_piece : 31 + n_piece]
    normed_refs, inverse_refs, part_refs, back_refs = more[:2], more[2:4], more[4:8], more[8:12]
    dealt = refs[31 + n_piece : 31 + 2 * n_piece]
    weights, grads_ref, out_all, low_ref, act_ref, hid_ref, cot_ref = refs[31 + 2 * n_piece :]
    feats, n_tok = att[0].shape
    width = tokens[0].shape[1]
    size = n_tok // 4
    own = table_ref[n_piece]
    assemble(table_ref, pieces, weights)
    for r in range(4):
        start = pl.multiple_of((own ^ r) * feats, feats)
        att_all[pl.ds(start, feats), :] = att[r][...]
    for r in range(4):
        for j in range(4):

            @pl.when((own ^ r) == j)
            def _():
                out_all[:, j * feats : (j + 1) * feats] = out_parts[r][...]

    out_own[...] = out_all[pl.ds(pl.multiple_of(own * feats, feats), feats), :]
    shift_m, scale_m, gate_m = [mod_ref[i : i + 1, :] for i in (3, 4, 5)]
    totals = [jnp.zeros((1, width), full_type) for _ in range(5)]
    for r in range(4):
        here = slice(r * size, (r + 1) * size)
        branch = mm_tn(att_all[:, here], out_all[...]) + bias_ref[0:1, :]
        residual = tokens[r][:size, :].astype(full_type) + mod_ref[2:3, :] * branch
        if r == 0:
            residual_ref[...] = residual
            branch_ref[...] = branch
        normed, inverse = layer_norm(residual)
        if r % 2 == 0:
            normed_refs[r // 2][...] = normed
            inverse_refs[r // 2][...] = inverse
        low = (normed * (1.0 + scale_m) + shift_m).astype(low_type)
        low_ref[here, :] = low
        hidden = mm(low, weights[:, :width]) + bias_ref[2:3, :]
        active, slope = gelu_both(hidden)
        active = active.astype(low_type)
        act_ref[here, :] = active
        part = mm(active, weights[:, width:])
        part_refs[r][...] = part.astype(low_type)
        grad_y = tokens[r][size:, :].astype(full_type)
        totals[0] += jnp.sum(grad_y * part, 0, keepdims=True)
        if r == 0:
            totals[0] += jnp.sum(grad_y, 0, keepdims=True) * bias_ref[1:2, :]
        grad_low = (gate_m * grad_y).astype(low_type)
        cot_ref[here, :] = grad_low
        grad_hid = (mm_nt(grad_low, weights[:, width:]) * slope).astype(low_type)
        hid_ref[here, :] = grad_hid
        back = mm_nt(grad_hid, weights[:, :width])
        back_refs[r][...] = back.astype(low_type)
        totals[1] += jnp.sum(back * normed, 0, keepdims=True)
        totals[2] += jnp.sum(back, 0, keepdims=True)
        totals[3] += jnp.sum(grad_hid.astype(full_type), 0, keepdims=True)
        totals[4] += jnp.sum(grad_low.astype(full_type), 0, keepdims=True)
    sums_ref[...] = jnp.zeros(sums_ref.shape, full_type)
    sums_ref[3:4, :] = totals[2]
    sums_ref[4:5, :] = totals[1]
    sums_ref[5:6, :] = totals[0]
    sums_ref[pl.ds(9 + own, 1), :] = totals[3]
    sums_ref[13:14, :] = jnp.where(own == 0, totals[4], 0.0)
    grads_ref[:, :width] = mm_tn(low_ref[...], hid_ref[...]).astype(low_type)
    grads_ref[:, width:] = mm_tn(act_ref[...], cot_ref[...]).astype(low_type)
    deal(table_ref, dealt, grads_ref)


def attend_backward_kernel(heads, own_ref, *refs):
    grad = refs[:4]
    att_all, out_own, qkv_ref, log_ref, low_ref = refs[4:9]
    out_ref, grads_ref, sums_ref = refs[9:12]
    all_ref, cols_ref, grad_ref, keys_t, sum_k, sum_v = refs[12:]
    n_tok, width = low_ref.shape
    feats = out_own.shape[0]
    size = n_tok // 4
    dim = feats // heads
    scale = dim ** (-0.5)
    own = own_ref[0]
    for r in range(4):
        here = slice(r * size, (r + 1) * size)
        all_ref[here, :] = grad[r][...]
        grad_ref[here, :] = mm_nt(grad[r][...], out_own[...]).astype(low_type)
    for j in range(4):

        @pl.when(own == j)
        def _():
            cols_ref[...] = all_ref[:, j * feats : (j + 1) * feats]

    grads_ref[:, 3 * feats :] = mm(att_all[...], cols_ref[...]).astype(low_type)
    keys_t[...] = jnp.transpose(qkv_ref[:, feats : 2 * feats])
    sum_k[...] = jnp.zeros(sum_k.shape, full_type)
    sum_v[...] = jnp.zeros(sum_v.shape, full_type)

    def step(block, _):
        here = pl.ds(pl.multiple_of(block * BLOCK, BLOCK), BLOCK)
        for head in range(heads):
            cut = slice(head * dim, (head + 1) * dim)
            queries = (qkv_ref[here, cut] * scale).astype(low_type)
            keys = qkv_ref[:, feats + head * dim : feats + (head + 1) * dim]
            values = qkv_ref[:, 2 * feats + head * dim : 2 * feats + (head + 1) * dim]
            grad_att = grad_ref[here, cut]
            probs = jnp.exp(mm_nt(keys, queries) - log_ref[head : head + 1, here])
            grad_probs = mm_nt(values, grad_att)
            delta = jnp.sum(probs * grad_probs, 0, keepdims=True)
            grad_scores = (probs * (grad_probs - delta)).astype(low_type)
            sum_v[:, cut] += mm(probs.astype(low_type), grad_att)
            sum_k[:, cut] += mm(grad_scores, queries)
            grad_q = mm(keys_t[cut, :], grad_scores) * scale
            out_ref[here, cut] = jnp.transpose(grad_q).astype(low_type)
        return 0

    lax.fori_loop(0, n_tok // BLOCK, step, 0)
    out_ref[:, feats : 2 * feats] = sum_k[...].astype(low_type)
    out_ref[:, 2 * feats :] = sum_v[...].astype(low_type)
    grads_ref[:, : 3 * feats] = mm_tn(low_ref[...], out_ref[...]).astype(low_type)
    sums_ref[...] = jnp.zeros(sums_ref.shape, full_type)
    bias = jnp.sum(out_ref[...].astype(full_type), 0, keepdims=True)
    total = jnp.sum(all_ref[...].astype(full_type), 0, keepdims=True)
    sums_ref[8:9, :] = jnp.where(own == 0, total, 0.0)
    for j in range(4):

        @pl.when(own == j)
        def _():
            sums_ref[6:7, j * feats : (j + 1) * feats] = bias[:, :feats]
            sums_ref[7:8, j * feats : (j + 1) * feats] = bias[:, 2 * feats :]


def project_backward_kernel(*refs):
    tokens = refs[:4]
    grad_ref, weight_ref, gate_ref, sums_mlp, sums_att = refs[4:9]
    back_refs, sums_ref = refs[9:13], refs[13]
    size, width = back_refs[0].shape
    totals = [jnp.zeros((1, width), full_type) for _ in range(2)]
    for r in range(4):
        here = slice(r * size, (r + 1) * size)
        back = mm_nt(grad_ref[here, :], weight_ref[...])
        back_refs[r][...] = back.astype(low_type)
        normed, _ = layer_norm(tokens[r][:size, :].astype(full_type))
        totals[0] += jnp.sum(back, 0, keepdims=True)
        totals[1] += jnp.sum(back * normed, 0, keepdims=True)
    sums_ref[...] = sums_mlp[...] + sums_att[...]
    sums_ref[0:1, :] = totals[0]
    sums_ref[1:2, :] = totals[1]
    sums_ref[2:3, :] = gate_ref[...]


def adam_step(weight, first, second, grad):
    first_new = beta_one * first + (1.0 - beta_one) * grad
    second_new = beta_two * second + (1.0 - beta_two) * grad * grad
    corr_one = 1.0 - beta_one**ADAM_STEP
    corr_two = 1.0 - beta_two**ADAM_STEP
    weight_new = weight - (learn_rate / corr_one) * first_new / (
        jnp.sqrt(second_new * (1.0 / corr_two)) + adam_eps
    )
    return (weight_new, first_new, second_new)


def swap(value, distance):
    return lax.ppermute(value, "seq", [(p, p ^ distance) for p in range(4)])


def gather_rel(value):
    far = swap(value, 2)
    near = swap(value, 1)
    cross = swap(far, 1)
    return [value, near, far, cross]


def scatter_rel(blocks):
    near_own, near_far = [swap(blocks[r], 1).astype(full_type) for r in (1, 3)]
    far_own = swap((blocks[2].astype(full_type) + near_far).astype(low_type), 2)
    return blocks[0].astype(full_type) + near_own + far_own.astype(full_type)


CYCLE = (0, 2, 4, 6, 7, 5, 3, 1)


def ring_pairs(count):
    right = [(CYCLE[i], CYCLE[(i + 1) % count]) for i in range(count)]
    return right, [(to, start) for start, to in right]


def ring_hop(pieces, count):
    if count != len(CYCLE):
        return pieces
    right, left = ring_pairs(count)
    hop = len(pieces) // 2
    ahead, behind = (pieces[-2], pieces[-1]) if hop else (pieces[0], pieces[0])
    more = [lax.ppermute(ahead, "shard", right)]
    if hop < count // 2 - 1:
        more.append(lax.ppermute(behind, "shard", left))
    return pieces + more


def ring_begin(value, count):
    if count != len(CYCLE):
        return [spread(value, "shard", count).reshape(-1, value.shape[-1])]
    return ring_hop([value], count)


def ring_scatter(pieces, count, first):
    if len(pieces) == 1:
        whole = pieces[0].reshape(count, -1, pieces[0].shape[-1])
        arrived = lax.all_to_all(whole, "shard", 0, 0, tiled=True)
        return [jnp.sum(arrived.astype(full_type), 0).astype(low_type)]
    right, left = ring_pairs(count)
    ahead, behind = pieces[count - 1], pieces[count - 3]
    for hop in range(count // 2, 1, -1):
        ahead = after(lax.ppermute(ahead, "shard", right), *first)
        ahead = (ahead.astype(full_type) + pieces[2 * hop - 2].astype(full_type)).astype(low_type)
    for hop in range(count // 2 - 1, 0, -1):
        behind = after(lax.ppermute(behind, "shard", left), *first)
        if hop > 1:
            behind = (behind.astype(full_type) + pieces[2 * hop - 3].astype(full_type)).astype(
                low_type
            )
    return [pieces[0], ahead, behind]


def ring_finish(parts, count):
    if len(parts) == 1:
        return parts[0]
    last = lax.ppermute(parts[1], "shard", ring_pairs(count)[0])
    return sum(x.astype(full_type) for x in (parts[0], last, parts[2])).astype(low_type)


def ring_table(own, count):
    if count != len(CYCLE):
        return jnp.zeros((1,), jnp.int32)
    lines = []
    for s in range(count):
        at = CYCLE.index(s)
        line = [s]
        for hop in range(1, count // 2 + 1):
            line.append(CYCLE[(at - hop) % count])
            if hop < count // 2:
                line.append(CYCLE[(at + hop) % count])
        lines.append(line)
    return lax.dynamic_index_in_dim(jnp.array(lines, jnp.int32), own, 0, keepdims=False)


def permute_blocks(value, distance):
    size = value.shape[1] // 4
    return jnp.concatenate(
        [value[:, (r ^ distance) * size : ((r ^ distance) + 1) * size] for r in range(4)], 1
    )


def spread(value, axis, count):
    return lax.all_to_all(
        jnp.broadcast_to(value[None], (count,) + value.shape), axis, 0, 0, tiled=True
    )


def token_sum(tensor):
    return jnp.sum(tensor.astype(full_type), axis=0)


def shards(
    latents,
    cotangent,
    class_labels,
    time_buckets,
    class_table,
    time_table,
    ada_weight,
    qkv_weight,
    out_weight,
    up_weight,
    down_weight,
    biases,
    ada_first,
    qkv_first,
    out_first,
    up_first,
    down_first,
    bias_first,
    ada_second,
    qkv_second,
    out_second,
    up_second,
    down_second,
    bias_second,
    n_shard,
    n_seq,
):
    assert n_seq == 4 and latents.shape[0] == 1 and class_labels.shape[0] == n_shard
    s_own = lax.axis_index("shard")
    q_own = lax.axis_index("seq")
    tok_dev, width = latents.shape[1:]
    head_dim = width // HEADS
    score_scale = head_dim ** (-0.5)
    heads_own = HEADS // n_seq
    feats = heads_own * head_dim
    rows = ada_weight.shape[0]
    ff = up_weight.shape[1]
    ff_cell = ff // (n_shard * n_seq)
    ff_own = ff // n_seq

    table = jnp.concatenate([ring_table(s_own, n_shard), q_own[None].astype(jnp.int32)])
    own_index = q_own[None].astype(jnp.int32)
    first_part, rest_part = vmem_call(
        cut_kernel,
        "cut",
        (
            jax.ShapeDtypeStruct((rows, 4 * feats), low_type),
            jax.ShapeDtypeStruct((rows, width + ff_own), low_type),
        ),
        [pltpu.VMEM(x.shape, full_type) for x in (qkv_weight, out_weight, up_weight, down_weight)]
        + [pltpu.SemaphoreType.DMA((16,))],
        0,
        0,
        [own_index, qkv_weight, out_weight, up_weight, down_weight],
        far_in=range(1, 5),
    )

    cond = jnp.take(class_table, class_labels, axis=0).astype(full_type) + jnp.take(
        time_table, time_buckets, axis=0
    ).astype(full_type)
    cond_cols = lax.dynamic_slice_in_dim(cond, s_own * rows, rows, 1)
    silu_cols = jax.nn.silu(cond_cols).astype(low_type)
    ada_low = ada_weight.astype(low_type)
    mod_partial = mm(silu_cols, ada_low)
    bias_low = biases.astype(low_type).astype(full_type).reshape(1, -1)
    payload = jnp.concatenate(
        [mod_partial, jnp.broadcast_to(bias_low, (n_shard, bias_low.shape[1]))], 1
    )
    first_pieces, rest_pieces = ring_begin(first_part, n_shard), ring_begin(rest_part, n_shard)
    payload = after(payload, *first_pieces)
    arrived = lax.all_to_all(payload, "shard", split_axis=0, concat_axis=0, tiled=True)
    first_pieces, rest_pieces = lax.optimization_barrier((first_pieces, rest_pieces))
    for _ in range(2):
        first_pieces = ring_hop(first_pieces, n_shard)
    rest_pieces = ring_hop(rest_pieces, n_shard)
    both = jnp.concatenate([latents[0], cotangent[0]])
    far, arrived, first_pieces, rest_pieces = lax.optimization_barrier(
        (swap(both, 2), arrived, first_pieces, rest_pieces)
    )
    tokens = [both, swap(both, 1), far, swap(far, 1)]
    first_pieces = ring_hop(first_pieces, n_shard)
    n_piece = len(first_pieces)
    mod_sum = jnp.sum(arrived[:, : 6 * width], 0)
    bias_full = jnp.transpose(
        arrived[:, 6 * width :].reshape(n_shard, biases.shape[0], rows), (1, 0, 2)
    ).reshape(biases.shape[0], width)
    modulation = mod_sum.reshape(6, width) + bias_full[0:6]
    shift_a, scale_a, gate_a, shift_m, scale_m, gate_m = [modulation[i] for i in range(6)]

    n_tok = n_seq * tok_dev

    bias_query = lax.dynamic_slice_in_dim(bias_full[6], q_own * feats, feats)
    bias_value = lax.dynamic_slice_in_dim(bias_full[7], q_own * feats, feats)
    bias_qkv = jnp.concatenate([bias_query, jnp.zeros_like(bias_query), bias_value])[None]
    pair_count = heads_own * n_tok * n_tok
    modulated_a, qkv_w, out_q, qkv = vmem_call(
        partial(project_kernel, n_piece),
        "project",
        (
            jax.ShapeDtypeStruct((n_tok, width), low_type),
            jax.ShapeDtypeStruct((width, 3 * feats), low_type),
            jax.ShapeDtypeStruct((width, feats), low_type),
            jax.ShapeDtypeStruct((n_tok, 3 * feats), low_type),
        ),
        [],
        6 * n_tok * width * feats,
        n_tok,
        [table, *tokens, modulation, bias_qkv, *first_pieces],
    )
    out_far = swap(out_q, 2)
    qkv, rest_pieces = lax.optimization_barrier((qkv, ring_hop(rest_pieces, n_shard)))
    rest_pieces = ring_hop(rest_pieces, n_shard)
    att_own, logs = vmem_call(
        partial(attend_forward_kernel, heads_own),
        "attend_forward",
        (
            jax.ShapeDtypeStruct((feats, n_tok), low_type),
            jax.ShapeDtypeStruct((8, n_tok), full_type),
        ),
        [],
        4 * pair_count * head_dim,
        pair_count,
        [qkv],
        0,
    )
    att_own, out_far, rest_pieces = lax.optimization_barrier((att_own, out_far, rest_pieces))
    out_parts = [out_q, swap(out_q, 1), out_far, swap(out_far, 1)]
    att_far = swap(permute_blocks(att_own, 2), 2)
    att_near = swap(permute_blocks(att_own, 1), 1)
    att_cross = swap(permute_blocks(att_far, 1), 1)

    bias_ff = lax.dynamic_index_in_dim(
        bias_full[9:13].reshape(n_shard, n_seq, ff_cell), q_own, 1, keepdims=False
    ).reshape(ff_own)
    bias_mlp = jnp.stack([bias_full[8], bias_full[13], bias_ff])
    attended, out_own, residual, branch_a, *mlp_out = (
        vmem_call(
            partial(mlp_kernel, n_piece),
            "mlp",
            (
                jax.ShapeDtypeStruct((width, n_tok), low_type),
                jax.ShapeDtypeStruct((feats, width), low_type),
            )
            + 4 * (jax.ShapeDtypeStruct((tok_dev, width), full_type),)
            + 2 * (jax.ShapeDtypeStruct((tok_dev, 1), full_type),)
            + 8 * (jax.ShapeDtypeStruct((tok_dev, width), low_type),)
            + (jax.ShapeDtypeStruct((16, width), full_type),)
            + n_piece * (jax.ShapeDtypeStruct((width // n_piece, width + ff_own), low_type),),
            [
                pltpu.VMEM((width, width + ff_own), low_type),
                pltpu.VMEM((width, width + ff_own), low_type),
                pltpu.VMEM((width, width), low_type),
            ]
            + [pltpu.VMEM((n_tok, width), low_type)] * 4,
            14 * n_tok * width * width,
            n_tok * width,
            [
                table,
                att_own,
                att_near,
                att_far,
                att_cross,
                *tokens,
                modulation,
                bias_mlp,
                *out_parts,
                *rest_pieces,
            ],
        )
    )
    normed_m, inverse_m = mlp_out[:2], mlp_out[2:4]
    branch_part, back, sums_mlp, grads_mlp = mlp_out[4:8], mlp_out[8:12], mlp_out[12], mlp_out[13:]
    near_zero, near_two = swap(back[1], 1), swap(back[3], 1)
    chip = [
        (mine.astype(full_type) + theirs.astype(full_type)).astype(low_type)
        for mine, theirs in ((back[0], near_zero), (back[2], near_two))
    ]
    across = [swap(chip[1], 2), swap(chip[0], 2)]
    mlp_parts = ring_scatter(grads_mlp, n_shard, chip)
    grad_residuals = [
        tokens[2 * i][tok_dev:].astype(full_type)
        + norm_back(
            (chip[i].astype(full_type) + across[i].astype(full_type)) * (1.0 + scale_m),
            normed_m[i],
            inverse_m[i],
        )
        for i in range(2)
    ]
    grad_residual = grad_residuals[0]
    grad_low = [(gate_a * part).astype(low_type) for part in grad_residuals]
    grad_low, mlp_parts = lax.optimization_barrier((grad_low, mlp_parts))
    grad_branch_a = [grad_low[0], swap(grad_low[0], 1), grad_low[1], swap(grad_low[1], 1)]
    mlp_total = ring_finish(mlp_parts, n_shard)
    branch_part = [after(x, *chip) for x in branch_part]
    branch_near = swap(branch_part[1], 1)
    branch_chip = branch_part[2].astype(full_type) + swap(branch_part[3], 1).astype(full_type)
    mlp_total, branch_chip, branch_near, grad_branch_a = lax.optimization_barrier(
        (mlp_total, branch_chip.astype(low_type), branch_near, grad_branch_a)
    )
    mlp_far, branch_far = swap(mlp_total, 2), swap(branch_chip, 2)
    grad_gate_a = token_sum(grad_residual * branch_a)
    grad_qkv, grads_att, sums_att = vmem_call(
        partial(attend_backward_kernel, heads_own),
        "attend_backward",
        (
            jax.ShapeDtypeStruct((n_tok, 3 * feats), low_type),
            jax.ShapeDtypeStruct((width, 4 * feats), low_type),
            jax.ShapeDtypeStruct((16, width), full_type),
        ),
        [
            pltpu.VMEM((n_tok, width), low_type),
            pltpu.VMEM((n_tok, feats), low_type),
            pltpu.VMEM((n_tok, feats), low_type),
            pltpu.VMEM((feats, n_tok), low_type),
            pltpu.VMEM((n_tok, feats), full_type),
            pltpu.VMEM((n_tok, feats), full_type),
        ],
        10 * n_tok * width * feats + 10 * pair_count * head_dim,
        pair_count,
        [own_index, *grad_branch_a, attended, out_own, qkv, logs, modulated_a],
    )
    grads_att, mlp_far, branch_far = lax.optimization_barrier((grads_att, mlp_far, branch_far))
    *grad_mod_a_part, small = vmem_call(
        project_backward_kernel,
        "project_backward",
        4 * (jax.ShapeDtypeStruct((tok_dev, width), low_type),)
        + (jax.ShapeDtypeStruct((16, width), full_type),),
        [],
        6 * n_tok * width * feats,
        n_tok,
        [*tokens, grad_qkv, qkv_w, grad_gate_a[None], sums_mlp, sums_att],
        0,
    )
    small = small + swap(small, 1)
    small = small + swap(small, 2)
    arrived_att = lax.all_to_all(
        grads_att.reshape(n_shard, rows, 4 * feats), "shard", 0, 0, tiled=True
    )
    normed_a, inverse_a = layer_norm(latents[0].astype(full_type))
    latents_grad = grad_residual + norm_back(
        scatter_rel([after(x, small) for x in grad_mod_a_part]) * (1.0 + scale_a),
        normed_a,
        inverse_a,
    )
    branch_own = sum(x.astype(full_type) for x in (branch_part[0], branch_near, branch_far))
    branch_own = branch_own + bias_full[13]
    block_out = (residual + gate_m * branch_own).astype(low_type)

    mlp_up, mlp_down = adam_call(
        place_mlp,
        "adam_mlp",
        own_index,
        [mlp_total, swap(mlp_total, 1), mlp_far, swap(mlp_far, 1)],
        [up_weight, down_weight, up_first, down_first, up_second, down_second],
    )
    every = spread(after(small, arrived_att, mlp_up[0]), "shard", n_shard)
    ada_state = (ada_weight, ada_first, ada_second)
    bias_state = (biases, bias_first, bias_second)
    tables = tuple(jax.ShapeDtypeStruct((rows, t.shape[0]), full_type) for t in (class_table, time_table))
    done = vmem_call(
        partial(finish_kernel, n_shard),
        "finish",
        tuple(jax.ShapeDtypeStruct(x.shape, full_type) for x in ada_state + bias_state) + tables,
        [
            pltpu.VMEM((16, width), full_type),
            pltpu.VMEM(biases.shape, full_type),
        ]
        + [pltpu.VMEM(ada_weight.shape, full_type)] * 3
        + [pltpu.SemaphoreType.DMA((2, 18))],
        24 * ada_weight.size,
        ada_weight.size,
        [
            s_own[None].astype(jnp.int32),
            every,
            silu_cols,
            cond_cols,
            class_labels[:, None],
            time_buckets[:, None],
            *ada_state,
            *bias_state,
        ],
        far_in=range(6, 9),
        far_out=range(3),
    )
    ada_new, bias_new = done[:3], done[3:6]
    class_grad, time_grad = jnp.transpose(done[6]), jnp.transpose(done[7])

    att_total = jnp.sum(arrived_att.astype(full_type), 0).astype(low_type)
    att_qkv, att_out = adam_call(
        place_att,
        "adam_att",
        own_index,
        gather_rel(att_total),
        [qkv_weight, out_weight, qkv_first, out_first, qkv_second, out_second],
    )

    updates = [
        ada_new,
        att_qkv,
        att_out,
        mlp_up,
        mlp_down,
        bias_new,
    ]
    return (
        block_out[None],
        latents_grad[None],
        class_grad,
        time_grad,
        *[update[0] for update in updates],
        *[update[1] for update in updates],
        *[update[2] for update in updates],
    )


def solution(mesh):
    tokens = P("shard", "seq", None)
    rows = P("shard", None)
    cols = P(None, "shard")
    state = (rows, rows, rows, rows, rows, cols)
    return jax.shard_map(
        partial(shards, n_shard=mesh.shape["shard"], n_seq=mesh.shape["seq"]),
        mesh=mesh,
        in_specs=(tokens, tokens, P(), P(), P(), P()) + 3 * state,
        out_specs=(tokens, tokens, cols, cols) + 3 * state,
        check_vma=False,
    )
```

```python
import math
from functools import partial

import jax
import jax.numpy as jnp
from jax import lax
from jax.experimental import pallas as pl
from jax.experimental.pallas import tpu as pltpu
from jax.sharding import PartitionSpec as P

HEADS = 12
ADAM_STEP = 10
BLOCK = 256


norm_eps = 1e-06
beta_one = 0.9
beta_two = 0.999
learn_rate = 0.05
adam_eps = 1e-08

low_type = jnp.bfloat16
full_type = jnp.float32


def layer_norm(values_in):
    centred = values_in - jnp.mean(values_in, -1, keepdims=True)
    inverse = lax.rsqrt(jnp.mean(centred * centred, -1, keepdims=True) + norm_eps)
    return (centred * inverse, inverse)


def norm_back(gradient, normed, inverse):
    return inverse * (
        gradient
        - jnp.mean(gradient, -1, keepdims=True)
        - normed * jnp.mean(gradient * normed, -1, keepdims=True)
    )


def dot(left, right, dims):
    return lax.dot_general(left, right, (dims, ((), ())), preferred_element_type=full_type)


def mm(left, right):
    return dot(left, right, ((1,), (0,)))


def mm_nt(left, right):
    return dot(left, right, ((1,), (1,)))


def mm_tn(left, right):
    return dot(left, right, ((0,), (0,)))


def vmem_call(
    kernel, name, out_shape, scratch, flops, exps, operands, n_scalar=1, far_in=(), far_out=()
):
    specs = [pl.BlockSpec(memory_space=pltpu.SMEM)] * n_scalar
    for place in range(n_scalar, len(operands)):
        specs.append(pl.BlockSpec(memory_space=pl.ANY if place in far_in else pltpu.VMEM))
    moved = sum(x.size * x.dtype.itemsize for x in operands)
    moved += sum(x.size * x.dtype.itemsize for x in out_shape)
    return pl.pallas_call(
        kernel,
        out_shape=out_shape,
        in_specs=specs,
        out_specs=tuple(
            pl.BlockSpec(memory_space=pl.ANY if place in far_out else pltpu.VMEM)
            for place in range(len(out_shape))
        ),
        scratch_shapes=scratch,
        compiler_params=pltpu.CompilerParams(vmem_limit_bytes=60 * 2**20),
        cost_estimate=pl.CostEstimate(flops=flops, bytes_accessed=moved, transcendentals=exps),
        name=name,
    )(*operands)


def after(value, *others):
    return lax.optimization_barrier((value, *others))[0]


def assemble(table_ref, pieces, target):
    size = pieces[0].shape[0]
    for slot, piece in enumerate(pieces):
        target[pl.ds(pl.multiple_of(table_ref[slot] * size, size), size), :] = piece[...]


def cut_kernel(table_ref, qkv_all, out_all, up_all, down_all, first_ref, rest_ref, *scratch):
    held, sems = scratch[:4], scratch[4]
    qkv_ref, out_ref, up_ref, down_ref = held
    copies = []
    for source, target in zip((qkv_all, out_all, up_all, down_all), held):
        step = 768 if source.shape[1] > 768 else 256
        for start in range(0, source.shape[1], step):
            cut = (slice(None), pl.ds(start, step))
            copies.append(
                pltpu.make_async_copy(source.at[cut], target.at[cut], sems.at[len(copies)])
            )
    for copy in copies:
        copy.start()
    for copy in copies:
        copy.wait()
    rows, width = out_ref.shape
    feats = width // 4
    cell = down_ref.shape[0] // 4
    n_shard = up_ref.shape[1] // (4 * cell)
    for j in range(4):

        @pl.when(table_ref[0] == j)
        def _():
            for part in range(3):
                start = part * width + j * feats
                first_ref[:, part * feats : (part + 1) * feats] = qkv_ref[
                    :, start : start + feats
                ].astype(low_type)
            first_ref[:, 3 * feats :] = out_ref[:, j * feats : (j + 1) * feats].astype(low_type)
            for s in range(n_shard):
                start = (s * 4 + j) * cell
                rest_ref[:, s * cell : (s + 1) * cell] = up_ref[:, start : start + cell].astype(
                    low_type
                )
            rest_ref[:, width:] = down_ref[j * cell : (j + 1) * cell, :].astype(low_type)


def pieces_of(shape):
    step = 768 if shape[1] > 768 else 256
    return [(slice(None), pl.ds(start, step)) for start in range(0, shape[1], step)]


class Stream:
    def __init__(self, state, outs, held, sems):
        self.cuts = pieces_of(state[0].shape)
        self.held, self.outs, self.sems = held, outs, sems
        self.loads = [
            [
                pltpu.make_async_copy(source.at[cut], target.at[cut], sems.at[0, 3 * at + i])
                for i, (source, target) in enumerate(zip(state, held))
            ]
            for at, cut in enumerate(self.cuts)
        ]
        self.stores = []

    def start(self):
        for group in self.loads:
            for copy in group:
                copy.start()

    def weight(self, at):
        for copy in self.loads[at]:
            copy.wait()
        return self.held[0][self.cuts[at]]

    def update(self, at, grad):
        cut = self.cuts[at]
        results = adam_step(*[ref[cut] for ref in self.held], grad)
        for i, (ref, result) in enumerate(zip(self.held, results)):
            ref[cut] = result
            copy = pltpu.make_async_copy(ref.at[cut], self.outs[i].at[cut], self.sems.at[1, 3 * at + i])
            copy.start()
            self.stores.append(copy)

    def finish(self):
        for copy in self.stores:
            copy.wait()


def adam_kernel(place, table_ref, *refs):
    grads, state, outs = refs[:4], refs[4:10], refs[10:16]
    held, sems, grad_refs = refs[16:22], refs[22:24], refs[24:]
    streams = [Stream(state[i::2], outs[i::2], held[i::2], sems[i]) for i in range(2)]
    for stream in streams:
        stream.start()
    for j in range(4):

        @pl.when(table_ref[0] == j)
        def _():
            for r in range(4):
                place(j ^ r, grads[r][...].astype(full_type), *grad_refs)

    for stream, grad in zip(streams, grad_refs):
        for at, cut in enumerate(stream.cuts):
            stream.weight(at)
            stream.update(at, grad[cut])
    for stream in streams:
        stream.finish()


def place_mlp(j, grad, grad_up, grad_down):
    width = grad_down.shape[1]
    cell = grad_down.shape[0] // 4
    for s in range(grad_up.shape[1] // (4 * cell)):
        start = (s * 4 + j) * cell
        grad_up[:, start : start + cell] = grad[:, s * cell : (s + 1) * cell]
    grad_down[j * cell : (j + 1) * cell, :] = grad[:, width:]


def place_att(j, grad, grad_qkv, grad_out):
    width = grad_out.shape[1]
    feats = width // 4
    for part in range(3):
        start = part * width + j * feats
        grad_qkv[:, start : start + feats] = grad[:, part * feats : (part + 1) * feats]
    grad_out[:, j * feats : (j + 1) * feats] = grad[:, 3 * feats :]


def finish_kernel(n_shard, place_ref, *refs):
    every_ref, silu_ref, cond_ref, label_ref, bucket_ref = refs[:5]
    ada, bias = refs[5:8], refs[8:11]
    ada_out, bias_out, class_ref, time_ref = refs[11:14], refs[14:17], refs[17], refs[18]
    sums_ref, bias_grad, *held, sems = refs[19:]
    stream = Stream(ada, ada_out, held, sems)
    stream.start()
    rows = cond_ref.shape[1]
    width = every_ref.shape[2]
    grad_silu = jnp.zeros((n_shard, rows), full_type)
    for slot in range(6):
        grad_mod = every_ref[:, slot, :].astype(low_type)
        grad_silu += mm_nt(grad_mod, stream.weight(slot).astype(low_type))
        stream.update(slot, mm_tn(silu_ref[...], grad_mod))
        sums_ref[slot : slot + 1, :] = jnp.sum(grad_mod.astype(full_type), 0, keepdims=True)
    for slot in range(6, 14):
        sums_ref[slot : slot + 1, :] = jnp.sum(every_ref[:, slot, :], 0, keepdims=True)
    for s in range(n_shard):

        @pl.when(place_ref[0] == s)
        def _():
            for slot in range(14):
                row, cell = slot, s
                if 9 <= slot < 13:
                    row, cell = 9 + s % 4, (n_shard * (slot - 9) + s) // 4
                bias_grad[slot : slot + 1, :] = sums_ref[
                    row : row + 1, cell * rows : (cell + 1) * rows
                ]

    results = adam_step(*[ref[...] for ref in bias], bias_grad[...])
    for ref, result in zip(bias_out, results):
        ref[...] = result
    cond = cond_ref[...]
    gate = 1.0 / (1.0 + jnp.exp(-cond))
    cols = grad_silu * (gate * (1.0 + cond * (1.0 - gate)))
    for index_ref, table in ((label_ref, class_ref), (bucket_ref, time_ref)):
        places = lax.broadcasted_iota(jnp.int32, (n_shard, table.shape[1]), 1)
        hot = jnp.where(places == index_ref[...], 1.0, 0.0)
        table[...] = lax.dot_general(
            cols,
            hot,
            (((0,), (0,)), ((), ())),
            precision=lax.Precision.HIGHEST,
            preferred_element_type=full_type,
        )
    stream.finish()


def adam_call(place, name, own, grads, state):
    results = vmem_call(
        partial(adam_kernel, place),
        name,
        tuple(jax.ShapeDtypeStruct(x.shape, full_type) for x in state),
        [pltpu.VMEM(x.shape, full_type) for x in state]
        + [pltpu.SemaphoreType.DMA((2, 3 * len(pieces_of(x.shape)))) for x in state[:2]]
        + [pltpu.VMEM(x.shape, full_type) for x in state[:2]],
        20 * (state[0].size + state[1].size),
        state[0].size + state[1].size,
        [own, *grads, *state],
        far_in=range(5, 11),
        far_out=range(6),
    )
    return results[0::2], results[1::2]


def project_kernel(n_piece, table_ref, *refs):
    stream = refs[:4]
    mod_ref, bias_ref = refs[4:6]
    pieces = refs[6 : 6 + n_piece]
    low_ref, weight_ref, out_ref, qkv_ref = refs[6 + n_piece :]
    n_tok, cols = qkv_ref.shape
    size = pieces[0].shape[0]
    for slot, piece in enumerate(pieces):
        place = pl.ds(pl.multiple_of(table_ref[slot] * size, size), size)
        weight_ref[place, :] = piece[:, :cols]
        out_ref[place, :] = piece[:, cols:]
    for r in range(4):
        here = slice(r * n_tok // 4, (r + 1) * n_tok // 4)
        normed, _ = layer_norm(stream[r][: n_tok // 4, :].astype(full_type))
        low = (normed * (1.0 + mod_ref[1:2, :]) + mod_ref[0:1, :]).astype(low_type)
        low_ref[here, :] = low
        qkv_ref[here, :] = (mm(low, weight_ref[...]) + bias_ref[...]).astype(low_type)


def attend_forward_kernel(heads, qkv_ref, att_ref, log_ref):
    n_tok = qkv_ref.shape[0]
    feats = att_ref.shape[0]
    dim = feats // heads
    scale = dim ** (-0.5)
    log_ref[...] = jnp.zeros(log_ref.shape, full_type)

    def step(block, _):
        here = pl.ds(pl.multiple_of(block * BLOCK, BLOCK), BLOCK)
        for head in range(heads):
            queries = qkv_ref[here, head * dim : (head + 1) * dim] * scale
            keys = qkv_ref[:, feats + head * dim : feats + (head + 1) * dim]
            values = qkv_ref[:, 2 * feats + head * dim : 2 * feats + (head + 1) * dim]
            scores = mm_nt(queries.astype(low_type), keys)
            row_max = jnp.max(scores, -1, keepdims=True)
            expo = jnp.exp(scores - row_max)
            total = jnp.sum(expo, -1, keepdims=True)
            probs = (expo * (1.0 / total)).astype(low_type)
            att_ref[head * dim : (head + 1) * dim, here] = jnp.transpose(
                mm(probs, values)
            ).astype(low_type)
            logs = jnp.broadcast_to(row_max + jnp.log(total), (BLOCK, 128))
            log_ref[head : head + 1, here] = jnp.transpose(logs)[0:1]
        return 0

    lax.fori_loop(0, n_tok // BLOCK, step, 0)


def gelu_both(value):
    root = (2.0 / math.pi) ** 0.5
    square = value * value
    bend = jnp.tanh(root * value * (1.0 + 0.044715 * square))
    half = 0.5 * (1.0 + bend)
    slope = half + 0.5 * value * (1.0 - bend * bend) * (root * (1.0 + 3 * 0.044715 * square))
    return (value * half, slope)


def deal(table_ref, pieces, source):
    size = pieces[0].shape[0]
    for slot, piece in enumerate(pieces):
        piece[...] = source[pl.ds(pl.multiple_of(table_ref[slot] * size, size), size), :]


def mlp_kernel(n_piece, table_ref, *refs):
    att = refs[:4]
    tokens = refs[4:8]
    mod_ref, bias_ref = refs[8:10]
    out_parts = refs[10:14]
    pieces = refs[14 : 14 + n_piece]
    (
        att_all,
        out_own,
        residual_ref,
        branch_ref,
        *more,
        sums_ref,
    ) = refs[14 + n_piece : 31 + n_piece]
    normed_refs, inverse_refs, part_refs, back_refs = more[:2], more[2:4], more[4:8], more[8:12]
    dealt = refs[31 + n_piece : 31 + 2 * n_piece]
    weights, grads_ref, out_all, low_ref, act_ref, hid_ref, cot_ref = refs[31 + 2 * n_piece :]
    feats, n_tok = att[0].shape
    width = tokens[0].shape[1]
    size = n_tok // 4
    own = table_ref[n_piece]
    assemble(table_ref, pieces, weights)
    for r in range(4):
        start = pl.multiple_of((own ^ r) * feats, feats)
        att_all[pl.ds(start, feats), :] = att[r][...]
    for r in range(4):
        for j in range(4):

            @pl.when((own ^ r) == j)
            def _():
                out_all[:, j * feats : (j + 1) * feats] = out_parts[r][...]

    out_own[...] = out_all[pl.ds(pl.multiple_of(own * feats, feats), feats), :]
    shift_m, scale_m, gate_m = [mod_ref[i : i + 1, :] for i in (3, 4, 5)]
    totals = [jnp.zeros((1, width), full_type) for _ in range(5)]
    for r in range(4):
        here = slice(r * size, (r + 1) * size)
        branch = mm_tn(att_all[:, here], out_all[...]) + bias_ref[0:1, :]
        residual = tokens[r][:size, :].astype(full_type) + mod_ref[2:3, :] * branch
        if r == 0:
            residual_ref[...] = residual
            branch_ref[...] = branch
        normed, inverse = layer_norm(residual)
        if r % 2 == 0:
            normed_refs[r // 2][...] = normed
            inverse_refs[r // 2][...] = inverse
        low = (normed * (1.0 + scale_m) + shift_m).astype(low_type)
        low_ref[here, :] = low
        hidden = mm(low, weights[:, :width]) + bias_ref[2:3, :]
        active, slope = gelu_both(hidden)
        active = active.astype(low_type)
        act_ref[here, :] = active
        part = mm(active, weights[:, width:])
        part_refs[r][...] = part.astype(low_type)
        grad_y = tokens[r][size:, :].astype(full_type)
        totals[0] += jnp.sum(grad_y * part, 0, keepdims=True)
        if r == 0:
            totals[0] += jnp.sum(grad_y, 0, keepdims=True) * bias_ref[1:2, :]
        grad_low = (gate_m * grad_y).astype(low_type)
        cot_ref[here, :] = grad_low
        grad_hid = (mm_nt(grad_low, weights[:, width:]) * slope).astype(low_type)
        hid_ref[here, :] = grad_hid
        back = mm_nt(grad_hid, weights[:, :width])
        back_refs[r][...] = back.astype(low_type)
        totals[1] += jnp.sum(back * normed, 0, keepdims=True)
        totals[2] += jnp.sum(back, 0, keepdims=True)
        totals[3] += jnp.sum(grad_hid.astype(full_type), 0, keepdims=True)
        totals[4] += jnp.sum(grad_low.astype(full_type), 0, keepdims=True)
    sums_ref[...] = jnp.zeros(sums_ref.shape, full_type)
    sums_ref[3:4, :] = totals[2]
    sums_ref[4:5, :] = totals[1]
    sums_ref[5:6, :] = totals[0]
    sums_ref[pl.ds(9 + own, 1), :] = totals[3]
    sums_ref[13:14, :] = jnp.where(own == 0, totals[4], 0.0)
    grads_ref[:, :width] = mm_tn(low_ref[...], hid_ref[...]).astype(low_type)
    grads_ref[:, width:] = mm_tn(act_ref[...], cot_ref[...]).astype(low_type)
    deal(table_ref, dealt, grads_ref)


def attend_backward_kernel(heads, own_ref, *refs):
    grad = refs[:4]
    att_all, out_own, qkv_ref, log_ref, low_ref = refs[4:9]
    out_ref, grads_ref, sums_ref = refs[9:12]
    all_ref, cols_ref, grad_ref, keys_t, sum_k, sum_v = refs[12:]
    n_tok, width = low_ref.shape
    feats = out_own.shape[0]
    size = n_tok // 4
    dim = feats // heads
    scale = dim ** (-0.5)
    own = own_ref[0]
    for r in range(4):
        here = slice(r * size, (r + 1) * size)
        all_ref[here, :] = grad[r][...]
        grad_ref[here, :] = mm_nt(grad[r][...], out_own[...]).astype(low_type)
    for j in range(4):

        @pl.when(own == j)
        def _():
            cols_ref[...] = all_ref[:, j * feats : (j + 1) * feats]

    grads_ref[:, 3 * feats :] = mm(att_all[...], cols_ref[...]).astype(low_type)
    keys_t[...] = jnp.transpose(qkv_ref[:, feats : 2 * feats])
    sum_k[...] = jnp.zeros(sum_k.shape, full_type)
    sum_v[...] = jnp.zeros(sum_v.shape, full_type)

    def step(block, _):
        here = pl.ds(pl.multiple_of(block * BLOCK, BLOCK), BLOCK)
        for head in range(heads):
            cut = slice(head * dim, (head + 1) * dim)
            queries = (qkv_ref[here, cut] * scale).astype(low_type)
            keys = qkv_ref[:, feats + head * dim : feats + (head + 1) * dim]
            values = qkv_ref[:, 2 * feats + head * dim : 2 * feats + (head + 1) * dim]
            grad_att = grad_ref[here, cut]
            probs = jnp.exp(mm_nt(keys, queries) - log_ref[head : head + 1, here])
            grad_probs = mm_nt(values, grad_att)
            delta = jnp.sum(probs * grad_probs, 0, keepdims=True)
            grad_scores = (probs * (grad_probs - delta)).astype(low_type)
            sum_v[:, cut] += mm(probs.astype(low_type), grad_att)
            sum_k[:, cut] += mm(grad_scores, queries)
            grad_q = mm(keys_t[cut, :], grad_scores) * scale
            out_ref[here, cut] = jnp.transpose(grad_q).astype(low_type)
        return 0

    lax.fori_loop(0, n_tok // BLOCK, step, 0)
    out_ref[:, feats : 2 * feats] = sum_k[...].astype(low_type)
    out_ref[:, 2 * feats :] = sum_v[...].astype(low_type)
    grads_ref[:, : 3 * feats] = mm_tn(low_ref[...], out_ref[...]).astype(low_type)
    sums_ref[...] = jnp.zeros(sums_ref.shape, full_type)
    bias = jnp.sum(out_ref[...].astype(full_type), 0, keepdims=True)
    total = jnp.sum(all_ref[...].astype(full_type), 0, keepdims=True)
    sums_ref[8:9, :] = jnp.where(own == 0, total, 0.0)
    for j in range(4):

        @pl.when(own == j)
        def _():
            sums_ref[6:7, j * feats : (j + 1) * feats] = bias[:, :feats]
            sums_ref[7:8, j * feats : (j + 1) * feats] = bias[:, 2 * feats :]


def project_backward_kernel(*refs):
    tokens = refs[:4]
    grad_ref, weight_ref, gate_ref, sums_mlp, sums_att = refs[4:9]
    back_refs, sums_ref = refs[9:13], refs[13]
    size, width = back_refs[0].shape
    totals = [jnp.zeros((1, width), full_type) for _ in range(2)]
    for r in range(4):
        here = slice(r * size, (r + 1) * size)
        back = mm_nt(grad_ref[here, :], weight_ref[...])
        back_refs[r][...] = back.astype(low_type)
        normed, _ = layer_norm(tokens[r][:size, :].astype(full_type))
        totals[0] += jnp.sum(back, 0, keepdims=True)
        totals[1] += jnp.sum(back * normed, 0, keepdims=True)
    sums_ref[...] = sums_mlp[...] + sums_att[...]
    sums_ref[0:1, :] = totals[0]
    sums_ref[1:2, :] = totals[1]
    sums_ref[2:3, :] = gate_ref[...]


def adam_step(weight, first, second, grad):
    first_new = beta_one * first + (1.0 - beta_one) * grad
    second_new = beta_two * second + (1.0 - beta_two) * grad * grad
    corr_one = 1.0 - beta_one**ADAM_STEP
    corr_two = 1.0 - beta_two**ADAM_STEP
    weight_new = weight - (learn_rate / corr_one) * first_new / (
        jnp.sqrt(second_new * (1.0 / corr_two)) + adam_eps
    )
    return (weight_new, first_new, second_new)


def swap(value, distance):
    return lax.ppermute(value, "seq", [(p, p ^ distance) for p in range(4)])


def gather_rel(value):
    far = swap(value, 2)
    near = swap(value, 1)
    cross = swap(far, 1)
    return [value, near, far, cross]


def scatter_rel(blocks):
    near_own, near_far = [swap(blocks[r], 1).astype(full_type) for r in (1, 3)]
    far_own = swap((blocks[2].astype(full_type) + near_far).astype(low_type), 2)
    return blocks[0].astype(full_type) + near_own + far_own.astype(full_type)


CYCLE = (0, 2, 4, 6, 7, 5, 3, 1)


def ring_pairs(count):
    right = [(CYCLE[i], CYCLE[(i + 1) % count]) for i in range(count)]
    return right, [(to, start) for start, to in right]


def ring_hop(pieces, count):
    if count != len(CYCLE):
        return pieces
    right, left = ring_pairs(count)
    hop = len(pieces) // 2
    ahead, behind = (pieces[-2], pieces[-1]) if hop else (pieces[0], pieces[0])
    more = [lax.ppermute(ahead, "shard", right)]
    if hop < count // 2 - 1:
        more.append(lax.ppermute(behind, "shard", left))
    return pieces + more


def ring_begin(value, count):
    if count != len(CYCLE):
        return [spread(value, "shard", count).reshape(-1, value.shape[-1])]
    return ring_hop([value], count)


def ring_scatter(pieces, count, first):
    if len(pieces) == 1:
        whole = pieces[0].reshape(count, -1, pieces[0].shape[-1])
        arrived = lax.all_to_all(whole, "shard", 0, 0, tiled=True)
        return [jnp.sum(arrived.astype(full_type), 0).astype(low_type)]
    right, left = ring_pairs(count)
    ahead, behind = pieces[count - 1], pieces[count - 3]
    for hop in range(count // 2, 1, -1):
        ahead = after(lax.ppermute(ahead, "shard", right), *first)
        ahead = (ahead.astype(full_type) + pieces[2 * hop - 2].astype(full_type)).astype(low_type)
    for hop in range(count // 2 - 1, 0, -1):
        behind = after(lax.ppermute(behind, "shard", left), *first)
        if hop > 1:
            behind = (behind.astype(full_type) + pieces[2 * hop - 3].astype(full_type)).astype(
                low_type
            )
    return [pieces[0], ahead, behind]


def ring_finish(parts, count):
    if len(parts) == 1:
        return parts[0]
    last = lax.ppermute(parts[1], "shard", ring_pairs(count)[0])
    return sum(x.astype(full_type) for x in (parts[0], last, parts[2])).astype(low_type)


def ring_table(own, count):
    if count != len(CYCLE):
        return jnp.zeros((1,), jnp.int32)
    lines = []
    for s in range(count):
        at = CYCLE.index(s)
        line = [s]
        for hop in range(1, count // 2 + 1):
            line.append(CYCLE[(at - hop) % count])
            if hop < count // 2:
                line.append(CYCLE[(at + hop) % count])
        lines.append(line)
    return lax.dynamic_index_in_dim(jnp.array(lines, jnp.int32), own, 0, keepdims=False)


def permute_blocks(value, distance):
    size = value.shape[1] // 4
    return jnp.concatenate(
        [value[:, (r ^ distance) * size : ((r ^ distance) + 1) * size] for r in range(4)], 1
    )


def spread(value, axis, count):
    return lax.all_to_all(
        jnp.broadcast_to(value[None], (count,) + value.shape), axis, 0, 0, tiled=True
    )


def token_sum(tensor):
    return jnp.sum(tensor.astype(full_type), axis=0)


def shards(
    latents,
    cotangent,
    class_labels,
    time_buckets,
    class_table,
    time_table,
    ada_weight,
    qkv_weight,
    out_weight,
    up_weight,
    down_weight,
    biases,
    ada_first,
    qkv_first,
    out_first,
    up_first,
    down_first,
    bias_first,
    ada_second,
    qkv_second,
    out_second,
    up_second,
    down_second,
    bias_second,
    n_shard,
    n_seq,
):
    assert n_seq == 4 and latents.shape[0] == 1 and class_labels.shape[0] == n_shard
    s_own = lax.axis_index("shard")
    q_own = lax.axis_index("seq")
    tok_dev, width = latents.shape[1:]
    head_dim = width // HEADS
    score_scale = head_dim ** (-0.5)
    heads_own = HEADS // n_seq
    feats = heads_own * head_dim
    rows = ada_weight.shape[0]
    ff = up_weight.shape[1]
    ff_cell = ff // (n_shard * n_seq)
    ff_own = ff // n_seq

    table = jnp.concatenate([ring_table(s_own, n_shard), q_own[None].astype(jnp.int32)])
    own_index = q_own[None].astype(jnp.int32)
    first_part, rest_part = vmem_call(
        cut_kernel,
        "cut",
        (
            jax.ShapeDtypeStruct((rows, 4 * feats), low_type),
            jax.ShapeDtypeStruct((rows, width + ff_own), low_type),
        ),
        [pltpu.VMEM(x.shape, full_type) for x in (qkv_weight, out_weight, up_weight, down_weight)]
        + [pltpu.SemaphoreType.DMA((16,))],
        0,
        0,
        [own_index, qkv_weight, out_weight, up_weight, down_weight],
        far_in=range(1, 5),
    )

    cond = jnp.take(class_table, class_labels, axis=0).astype(full_type) + jnp.take(
        time_table, time_buckets, axis=0
    ).astype(full_type)
    cond_cols = lax.dynamic_slice_in_dim(cond, s_own * rows, rows, 1)
    silu_cols = jax.nn.silu(cond_cols).astype(low_type)
    ada_low = ada_weight.astype(low_type)
    mod_partial = mm(silu_cols, ada_low)
    bias_low = biases.astype(low_type).astype(full_type).reshape(1, -1)
    payload = jnp.concatenate(
        [mod_partial, jnp.broadcast_to(bias_low, (n_shard, bias_low.shape[1]))], 1
    )
    first_pieces, rest_pieces = ring_begin(first_part, n_shard), ring_begin(rest_part, n_shard)
    payload = after(payload, *first_pieces)
    arrived = lax.all_to_all(payload, "shard", split_axis=0, concat_axis=0, tiled=True)
    first_pieces, rest_pieces = lax.optimization_barrier((first_pieces, rest_pieces))
    for _ in range(2):
        first_pieces = ring_hop(first_pieces, n_shard)
    both = jnp.concatenate([latents[0], cotangent[0]])
    far, arrived, first_pieces = lax.optimization_barrier((swap(both, 2), arrived, first_pieces))
    tokens = [both, swap(both, 1), far, swap(far, 1)]
    first_pieces = ring_hop(first_pieces, n_shard)
    first_pieces, rest_pieces = lax.optimization_barrier((first_pieces, rest_pieces))
    n_piece = len(first_pieces)
    mod_sum = jnp.sum(arrived[:, : 6 * width], 0)
    bias_full = jnp.transpose(
        arrived[:, 6 * width :].reshape(n_shard, biases.shape[0], rows), (1, 0, 2)
    ).reshape(biases.shape[0], width)
    modulation = mod_sum.reshape(6, width) + bias_full[0:6]
    shift_a, scale_a, gate_a, shift_m, scale_m, gate_m = [modulation[i] for i in range(6)]

    n_tok = n_seq * tok_dev

    bias_query = lax.dynamic_slice_in_dim(bias_full[6], q_own * feats, feats)
    bias_value = lax.dynamic_slice_in_dim(bias_full[7], q_own * feats, feats)
    bias_qkv = jnp.concatenate([bias_query, jnp.zeros_like(bias_query), bias_value])[None]
    pair_count = heads_own * n_tok * n_tok
    modulated_a, qkv_w, out_q, qkv = vmem_call(
        partial(project_kernel, n_piece),
        "project",
        (
            jax.ShapeDtypeStruct((n_tok, width), low_type),
            jax.ShapeDtypeStruct((width, 3 * feats), low_type),
            jax.ShapeDtypeStruct((width, feats), low_type),
            jax.ShapeDtypeStruct((n_tok, 3 * feats), low_type),
        ),
        [],
        6 * n_tok * width * feats,
        n_tok,
        [table, *tokens, modulation, bias_qkv, *first_pieces],
    )
    out_far = swap(out_q, 2)
    qkv, rest_pieces = lax.optimization_barrier((qkv, ring_hop(rest_pieces, n_shard)))
    rest_pieces = ring_hop(rest_pieces, n_shard)
    att_own, logs = vmem_call(
        partial(attend_forward_kernel, heads_own),
        "attend_forward",
        (
            jax.ShapeDtypeStruct((feats, n_tok), low_type),
            jax.ShapeDtypeStruct((8, n_tok), full_type),
        ),
        [],
        4 * pair_count * head_dim,
        pair_count,
        [qkv],
        0,
    )
    att_own, out_far, rest_pieces = lax.optimization_barrier((att_own, out_far, rest_pieces))
    out_parts = [out_q, swap(out_q, 1), out_far, swap(out_far, 1)]
    rest_pieces = ring_hop(rest_pieces, n_shard)
    att_far = swap(permute_blocks(att_own, 2), 2)
    att_far, rest_pieces = lax.optimization_barrier((att_far, rest_pieces))
    att_near = swap(permute_blocks(att_own, 1), 1)
    att_cross = swap(permute_blocks(att_far, 1), 1)

    bias_ff = lax.dynamic_index_in_dim(
        bias_full[9:13].reshape(n_shard, n_seq, ff_cell), q_own, 1, keepdims=False
    ).reshape(ff_own)
    bias_mlp = jnp.stack([bias_full[8], bias_full[13], bias_ff])
    attended, out_own, residual, branch_a, *mlp_out = (
        vmem_call(
            partial(mlp_kernel, n_piece),
            "mlp",
            (
                jax.ShapeDtypeStruct((width, n_tok), low_type),
                jax.ShapeDtypeStruct((feats, width), low_type),
            )
            + 4 * (jax.ShapeDtypeStruct((tok_dev, width), full_type),)
            + 2 * (jax.ShapeDtypeStruct((tok_dev, 1), full_type),)
            + 8 * (jax.ShapeDtypeStruct((tok_dev, width), low_type),)
            + (jax.ShapeDtypeStruct((16, width), full_type),)
            + n_piece * (jax.ShapeDtypeStruct((width // n_piece, width + ff_own), low_type),),
            [
                pltpu.VMEM((width, width + ff_own), low_type),
                pltpu.VMEM((width, width + ff_own), low_type),
                pltpu.VMEM((width, width), low_type),
            ]
            + [pltpu.VMEM((n_tok, width), low_type)] * 4,
            14 * n_tok * width * width,
            n_tok * width,
            [
                table,
                att_own,
                att_near,
                att_far,
                att_cross,
                *tokens,
                modulation,
                bias_mlp,
                *out_parts,
                *rest_pieces,
            ],
        )
    )
    normed_m, inverse_m = mlp_out[:2], mlp_out[2:4]
    branch_part, back, sums_mlp, grads_mlp = mlp_out[4:8], mlp_out[8:12], mlp_out[12], mlp_out[13:]
    near_zero, near_two = swap(back[1], 1), swap(back[3], 1)
    chip = [
        (mine.astype(full_type) + theirs.astype(full_type)).astype(low_type)
        for mine, theirs in ((back[0], near_zero), (back[2], near_two))
    ]
    across = [swap(chip[1], 2), swap(chip[0], 2)]
    mlp_parts = ring_scatter(grads_mlp, n_shard, chip)
    grad_residuals = [
        tokens[2 * i][tok_dev:].astype(full_type)
        + norm_back(
            (chip[i].astype(full_type) + across[i].astype(full_type)) * (1.0 + scale_m),
            normed_m[i],
            inverse_m[i],
        )
        for i in range(2)
    ]
    grad_residual = grad_residuals[0]
    grad_low = [(gate_a * part).astype(low_type) for part in grad_residuals]
    grad_low, mlp_parts = lax.optimization_barrier((grad_low, mlp_parts))
    grad_branch_a = [grad_low[0], swap(grad_low[0], 1), grad_low[1], swap(grad_low[1], 1)]
    mlp_total = ring_finish(mlp_parts, n_shard)
    branch_part = [after(x, *chip) for x in branch_part]
    branch_near = swap(branch_part[1], 1)
    branch_chip = branch_part[2].astype(full_type) + swap(branch_part[3], 1).astype(full_type)
    mlp_total, branch_chip, branch_near, grad_branch_a = lax.optimization_barrier(
        (mlp_total, branch_chip.astype(low_type), branch_near, grad_branch_a)
    )
    mlp_far, branch_far = swap(mlp_total, 2), swap(branch_chip, 2)
    grad_gate_a = token_sum(grad_residual * branch_a)
    grad_qkv, grads_att, sums_att = vmem_call(
        partial(attend_backward_kernel, heads_own),
        "attend_backward",
        (
            jax.ShapeDtypeStruct((n_tok, 3 * feats), low_type),
            jax.ShapeDtypeStruct((width, 4 * feats), low_type),
            jax.ShapeDtypeStruct((16, width), full_type),
        ),
        [
            pltpu.VMEM((n_tok, width), low_type),
            pltpu.VMEM((n_tok, feats), low_type),
            pltpu.VMEM((n_tok, feats), low_type),
            pltpu.VMEM((feats, n_tok), low_type),
            pltpu.VMEM((n_tok, feats), full_type),
            pltpu.VMEM((n_tok, feats), full_type),
        ],
        10 * n_tok * width * feats + 10 * pair_count * head_dim,
        pair_count,
        [own_index, *grad_branch_a, attended, out_own, qkv, logs, modulated_a],
    )
    grads_att, mlp_far, branch_far = lax.optimization_barrier((grads_att, mlp_far, branch_far))
    *grad_mod_a_part, small = vmem_call(
        project_backward_kernel,
        "project_backward",
        4 * (jax.ShapeDtypeStruct((tok_dev, width), low_type),)
        + (jax.ShapeDtypeStruct((16, width), full_type),),
        [],
        6 * n_tok * width * feats,
        n_tok,
        [*tokens, grad_qkv, qkv_w, grad_gate_a[None], sums_mlp, sums_att],
        0,
    )
    small = small + swap(small, 1)
    small = small + swap(small, 2)
    arrived_att = lax.all_to_all(
        grads_att.reshape(n_shard, rows, 4 * feats), "shard", 0, 0, tiled=True
    )
    normed_a, inverse_a = layer_norm(latents[0].astype(full_type))
    latents_grad = grad_residual + norm_back(
        scatter_rel([after(x, small) for x in grad_mod_a_part]) * (1.0 + scale_a),
        normed_a,
        inverse_a,
    )
    branch_own = sum(x.astype(full_type) for x in (branch_part[0], branch_near, branch_far))
    branch_own = branch_own + bias_full[13]
    block_out = (residual + gate_m * branch_own).astype(low_type)

    every = spread(after(small, arrived_att), "shard", n_shard)
    ada_state = (ada_weight, ada_first, ada_second)
    bias_state = (biases, bias_first, bias_second)
    tables = tuple(jax.ShapeDtypeStruct((rows, t.shape[0]), full_type) for t in (class_table, time_table))
    done = vmem_call(
        partial(finish_kernel, n_shard),
        "finish",
        tuple(jax.ShapeDtypeStruct(x.shape, full_type) for x in ada_state + bias_state) + tables,
        [
            pltpu.VMEM((16, width), full_type),
            pltpu.VMEM(biases.shape, full_type),
        ]
        + [pltpu.VMEM(ada_weight.shape, full_type)] * 3
        + [pltpu.SemaphoreType.DMA((2, 18))],
        24 * ada_weight.size,
        ada_weight.size,
        [
            s_own[None].astype(jnp.int32),
            every,
            silu_cols,
            cond_cols,
            class_labels[:, None],
            time_buckets[:, None],
            *ada_state,
            *bias_state,
        ],
        far_in=range(6, 9),
        far_out=range(3),
    )
    ada_new, bias_new = done[:3], done[3:6]
    class_grad, time_grad = jnp.transpose(done[6]), jnp.transpose(done[7])

    att_total = jnp.sum(arrived_att.astype(full_type), 0).astype(low_type)
    att_near, att_far = swap(att_total, 1), swap(att_total, 2)
    mlp_up, mlp_down = adam_call(
        place_mlp,
        "adam_mlp",
        own_index,
        [after(mlp_total, att_total), swap(mlp_total, 1), mlp_far, swap(mlp_far, 1)],
        [up_weight, down_weight, up_first, down_first, up_second, down_second],
    )
    att_qkv, att_out = adam_call(
        place_att,
        "adam_att",
        own_index,
        [att_total, att_near, att_far, swap(after(att_far, mlp_up[0]), 1)],
        [qkv_weight, out_weight, qkv_first, out_first, qkv_second, out_second],
    )

    updates = [
        ada_new,
        att_qkv,
        att_out,
        mlp_up,
        mlp_down,
        bias_new,
    ]
    return (
        block_out[None],
        latents_grad[None],
        class_grad,
        time_grad,
        *[update[0] for update in updates],
        *[update[1] for update in updates],
        *[update[2] for update in updates],
    )


def solution(mesh):
    tokens = P("shard", "seq", None)
    rows = P("shard", None)
    cols = P(None, "shard")
    state = (rows, rows, rows, rows, rows, cols)
    return jax.shard_map(
        partial(shards, n_shard=mesh.shape["shard"], n_seq=mesh.shape["seq"]),
        mesh=mesh,
        in_specs=(tokens, tokens, P(), P(), P(), P()) + 3 * state,
        out_specs=(tokens, tokens, cols, cols) + 3 * state,
        check_vma=False,
    )
```

```python
import math
from functools import partial

import jax
import jax.numpy as jnp
from jax import lax
from jax.experimental import pallas as pl
from jax.experimental.pallas import tpu as pltpu
from jax.sharding import PartitionSpec as P

HEADS = 12
ADAM_STEP = 10
BLOCK = 256


norm_eps = 1e-06
beta_one = 0.9
beta_two = 0.999
learn_rate = 0.05
adam_eps = 1e-08

low_type = jnp.bfloat16
full_type = jnp.float32


def layer_norm(values_in):
    centred = values_in - jnp.mean(values_in, -1, keepdims=True)
    inverse = lax.rsqrt(jnp.mean(centred * centred, -1, keepdims=True) + norm_eps)
    return (centred * inverse, inverse)


def norm_back(gradient, normed, inverse):
    return inverse * (
        gradient
        - jnp.mean(gradient, -1, keepdims=True)
        - normed * jnp.mean(gradient * normed, -1, keepdims=True)
    )


def dot(left, right, dims):
    return lax.dot_general(left, right, (dims, ((), ())), preferred_element_type=full_type)


def mm(left, right):
    return dot(left, right, ((1,), (0,)))


def mm_nt(left, right):
    return dot(left, right, ((1,), (1,)))


def mm_tn(left, right):
    return dot(left, right, ((0,), (0,)))


def vmem_call(
    kernel, name, out_shape, scratch, flops, exps, operands, n_scalar=1, far_in=(), far_out=()
):
    specs = [pl.BlockSpec(memory_space=pltpu.SMEM)] * n_scalar
    for place in range(n_scalar, len(operands)):
        specs.append(pl.BlockSpec(memory_space=pl.ANY if place in far_in else pltpu.VMEM))
    moved = sum(x.size * x.dtype.itemsize for x in operands)
    moved += sum(x.size * x.dtype.itemsize for x in out_shape)
    return pl.pallas_call(
        kernel,
        out_shape=out_shape,
        in_specs=specs,
        out_specs=tuple(
            pl.BlockSpec(memory_space=pl.ANY if place in far_out else pltpu.VMEM)
            for place in range(len(out_shape))
        ),
        scratch_shapes=scratch,
        compiler_params=pltpu.CompilerParams(vmem_limit_bytes=60 * 2**20),
        cost_estimate=pl.CostEstimate(flops=flops, bytes_accessed=moved, transcendentals=exps),
        name=name,
    )(*operands)


def after(value, *others):
    return lax.optimization_barrier((value, *others))[0]


def assemble(table_ref, pieces, target):
    size = pieces[0].shape[0]
    for slot, piece in enumerate(pieces):
        target[pl.ds(pl.multiple_of(table_ref[slot] * size, size), size), :] = piece[...]


def cut_kernel(table_ref, qkv_all, out_all, up_all, down_all, first_ref, rest_ref, *scratch):
    held, sems = scratch[:4], scratch[4]
    qkv_ref, out_ref, up_ref, down_ref = held
    copies = []
    for source, target in zip((qkv_all, out_all, up_all, down_all), held):
        step = 768 if source.shape[1] > 768 else 256
        for start in range(0, source.shape[1], step):
            cut = (slice(None), pl.ds(start, step))
            copies.append(
                pltpu.make_async_copy(source.at[cut], target.at[cut], sems.at[len(copies)])
            )
    for copy in copies:
        copy.start()
    for copy in copies:
        copy.wait()
    rows, width = out_ref.shape
    feats = width // 4
    cell = down_ref.shape[0] // 4
    n_shard = up_ref.shape[1] // (4 * cell)
    for j in range(4):

        @pl.when(table_ref[0] == j)
        def _():
            for part in range(3):
                start = part * width + j * feats
                first_ref[:, part * feats : (part + 1) * feats] = qkv_ref[
                    :, start : start + feats
                ].astype(low_type)
            first_ref[:, 3 * feats :] = out_ref[:, j * feats : (j + 1) * feats].astype(low_type)
            for s in range(n_shard):
                start = (s * 4 + j) * cell
                rest_ref[:, s * cell : (s + 1) * cell] = up_ref[:, start : start + cell].astype(
                    low_type
                )
            rest_ref[:, width:] = down_ref[j * cell : (j + 1) * cell, :].astype(low_type)


def pieces_of(shape):
    step = 768 if shape[1] > 768 else 256
    return [(slice(None), pl.ds(start, step)) for start in range(0, shape[1], step)]


class Stream:
    def __init__(self, state, outs, held, sems):
        self.cuts = pieces_of(state[0].shape)
        self.held, self.outs, self.sems = held, outs, sems
        self.loads = [
            [
                pltpu.make_async_copy(source.at[cut], target.at[cut], sems.at[0, 3 * at + i])
                for i, (source, target) in enumerate(zip(state, held))
            ]
            for at, cut in enumerate(self.cuts)
        ]
        self.stores = []

    def start(self):
        for group in self.loads:
            for copy in group:
                copy.start()

    def weight(self, at):
        for copy in self.loads[at]:
            copy.wait()
        return self.held[0][self.cuts[at]]

    def update(self, at, grad):
        cut = self.cuts[at]
        results = adam_step(*[ref[cut] for ref in self.held], grad)
        for i, (ref, result) in enumerate(zip(self.held, results)):
            ref[cut] = result
            copy = pltpu.make_async_copy(ref.at[cut], self.outs[i].at[cut], self.sems.at[1, 3 * at + i])
            copy.start()
            self.stores.append(copy)

    def finish(self):
        for copy in self.stores:
            copy.wait()


def adam_kernel(place, table_ref, *refs):
    grads, state, outs = refs[:4], refs[4:10], refs[10:16]
    held, sems, grad_refs = refs[16:22], refs[22:24], refs[24:]
    streams = [Stream(state[i::2], outs[i::2], held[i::2], sems[i]) for i in range(2)]
    for stream in streams:
        stream.start()
    for j in range(4):

        @pl.when(table_ref[0] == j)
        def _():
            for r in range(4):
                place(j ^ r, grads[r][...].astype(full_type), *grad_refs)

    for stream, grad in zip(streams, grad_refs):
        for at, cut in enumerate(stream.cuts):
            stream.weight(at)
            stream.update(at, grad[cut])
    for stream in streams:
        stream.finish()


def place_mlp(j, grad, grad_up, grad_down):
    width = grad_down.shape[1]
    cell = grad_down.shape[0] // 4
    for s in range(grad_up.shape[1] // (4 * cell)):
        start = (s * 4 + j) * cell
        grad_up[:, start : start + cell] = grad[:, s * cell : (s + 1) * cell]
    grad_down[j * cell : (j + 1) * cell, :] = grad[:, width:]


def place_att(j, grad, grad_qkv, grad_out):
    width = grad_out.shape[1]
    feats = width // 4
    for part in range(3):
        start = part * width + j * feats
        grad_qkv[:, start : start + feats] = grad[:, part * feats : (part + 1) * feats]
    grad_out[:, j * feats : (j + 1) * feats] = grad[:, 3 * feats :]


def finish_kernel(n_shard, place_ref, *refs):
    every_ref, silu_ref, cond_ref, label_ref, bucket_ref = refs[:5]
    ada, bias = refs[5:8], refs[8:11]
    ada_out, bias_out, class_ref, time_ref = refs[11:14], refs[14:17], refs[17], refs[18]
    sums_ref, bias_grad, *held, sems = refs[19:]
    stream = Stream(ada, ada_out, held, sems)
    stream.start()
    rows = cond_ref.shape[1]
    width = every_ref.shape[2]
    grad_silu = jnp.zeros((n_shard, rows), full_type)
    for slot in range(6):
        grad_mod = every_ref[:, slot, :].astype(low_type)
        grad_silu += mm_nt(grad_mod, stream.weight(slot).astype(low_type))
        stream.update(slot, mm_tn(silu_ref[...], grad_mod))
        sums_ref[slot : slot + 1, :] = jnp.sum(grad_mod.astype(full_type), 0, keepdims=True)
    for slot in range(6, 14):
        sums_ref[slot : slot + 1, :] = jnp.sum(every_ref[:, slot, :], 0, keepdims=True)
    for s in range(n_shard):

        @pl.when(place_ref[0] == s)
        def _():
            for slot in range(14):
                row, cell = slot, s
                if 9 <= slot < 13:
                    row, cell = 9 + s % 4, (n_shard * (slot - 9) + s) // 4
                bias_grad[slot : slot + 1, :] = sums_ref[
                    row : row + 1, cell * rows : (cell + 1) * rows
                ]

    results = adam_step(*[ref[...] for ref in bias], bias_grad[...])
    for ref, result in zip(bias_out, results):
        ref[...] = result
    cond = cond_ref[...]
    gate = 1.0 / (1.0 + jnp.exp(-cond))
    cols = grad_silu * (gate * (1.0 + cond * (1.0 - gate)))
    for index_ref, table in ((label_ref, class_ref), (bucket_ref, time_ref)):
        places = lax.broadcasted_iota(jnp.int32, (n_shard, table.shape[1]), 1)
        hot = jnp.where(places == index_ref[...], 1.0, 0.0)
        table[...] = lax.dot_general(
            cols,
            hot,
            (((0,), (0,)), ((), ())),
            precision=lax.Precision.HIGHEST,
            preferred_element_type=full_type,
        )
    stream.finish()


def adam_call(place, name, own, grads, state):
    results = vmem_call(
        partial(adam_kernel, place),
        name,
        tuple(jax.ShapeDtypeStruct(x.shape, full_type) for x in state),
        [pltpu.VMEM(x.shape, full_type) for x in state]
        + [pltpu.SemaphoreType.DMA((2, 3 * len(pieces_of(x.shape)))) for x in state[:2]]
        + [pltpu.VMEM(x.shape, full_type) for x in state[:2]],
        20 * (state[0].size + state[1].size),
        state[0].size + state[1].size,
        [own, *grads, *state],
        far_in=range(5, 11),
        far_out=range(6),
    )
    return results[0::2], results[1::2]


def project_kernel(n_piece, table_ref, *refs):
    stream = refs[:4]
    mod_ref, bias_ref = refs[4:6]
    pieces = refs[6 : 6 + n_piece]
    low_ref, weight_ref, out_ref, qkv_ref = refs[6 + n_piece :]
    n_tok, cols = qkv_ref.shape
    size = pieces[0].shape[0]
    for slot, piece in enumerate(pieces):
        place = pl.ds(pl.multiple_of(table_ref[slot] * size, size), size)
        weight_ref[place, :] = piece[:, :cols]
        out_ref[place, :] = piece[:, cols:]
    for r in range(4):
        here = slice(r * n_tok // 4, (r + 1) * n_tok // 4)
        normed, _ = layer_norm(stream[r][: n_tok // 4, :].astype(full_type))
        low = (normed * (1.0 + mod_ref[1:2, :]) + mod_ref[0:1, :]).astype(low_type)
        low_ref[here, :] = low
        qkv_ref[here, :] = (mm(low, weight_ref[...]) + bias_ref[...]).astype(low_type)


def attend_forward_kernel(heads, qkv_ref, att_ref, log_ref):
    n_tok = qkv_ref.shape[0]
    feats = att_ref.shape[0]
    dim = feats // heads
    scale = dim ** (-0.5)
    log_ref[...] = jnp.zeros(log_ref.shape, full_type)

    def step(block, _):
        here = pl.ds(pl.multiple_of(block * BLOCK, BLOCK), BLOCK)
        for head in range(heads):
            queries = qkv_ref[here, head * dim : (head + 1) * dim] * scale
            keys = qkv_ref[:, feats + head * dim : feats + (head + 1) * dim]
            values = qkv_ref[:, 2 * feats + head * dim : 2 * feats + (head + 1) * dim]
            scores = mm_nt(queries.astype(low_type), keys)
            row_max = jnp.max(scores, -1, keepdims=True)
            expo = jnp.exp(scores - row_max)
            total = jnp.sum(expo, -1, keepdims=True)
            probs = (expo * (1.0 / total)).astype(low_type)
            att_ref[head * dim : (head + 1) * dim, here] = jnp.transpose(
                mm(probs, values)
            ).astype(low_type)
            logs = jnp.broadcast_to(row_max + jnp.log(total), (BLOCK, 128))
            log_ref[head : head + 1, here] = jnp.transpose(logs)[0:1]
        return 0

    lax.fori_loop(0, n_tok // BLOCK, step, 0)


def gelu_both(value):
    root = (2.0 / math.pi) ** 0.5
    square = value * value
    bend = jnp.tanh(root * value * (1.0 + 0.044715 * square))
    half = 0.5 * (1.0 + bend)
    slope = half + 0.5 * value * (1.0 - bend * bend) * (root * (1.0 + 3 * 0.044715 * square))
    return (value * half, slope)


def deal(table_ref, pieces, source):
    size = pieces[0].shape[0]
    for slot, piece in enumerate(pieces):
        piece[...] = source[pl.ds(pl.multiple_of(table_ref[slot] * size, size), size), :]


def mlp_kernel(n_piece, table_ref, *refs):
    att = refs[:4]
    tokens = refs[4:8]
    mod_ref, bias_ref = refs[8:10]
    out_parts = refs[10:14]
    pieces = refs[14 : 14 + n_piece]
    (
        att_all,
        out_own,
        residual_ref,
        branch_ref,
        *more,
        sums_ref,
    ) = refs[14 + n_piece : 31 + n_piece]
    normed_refs, inverse_refs, part_refs, back_refs = more[:2], more[2:4], more[4:8], more[8:12]
    dealt = refs[31 + n_piece : 31 + 2 * n_piece]
    weights, grads_ref, out_all, low_ref, act_ref, hid_ref, cot_ref = refs[31 + 2 * n_piece :]
    feats, n_tok = att[0].shape
    width = tokens[0].shape[1]
    size = n_tok // 4
    own = table_ref[n_piece]
    assemble(table_ref, pieces, weights)
    for r in range(4):
        start = pl.multiple_of((own ^ r) * feats, feats)
        att_all[pl.ds(start, feats), :] = att[r][...]
    for r in range(4):
        for j in range(4):

            @pl.when((own ^ r) == j)
            def _():
                out_all[:, j * feats : (j + 1) * feats] = out_parts[r][...]

    out_own[...] = out_all[pl.ds(pl.multiple_of(own * feats, feats), feats), :]
    shift_m, scale_m, gate_m = [mod_ref[i : i + 1, :] for i in (3, 4, 5)]
    totals = [jnp.zeros((1, width), full_type) for _ in range(5)]
    for r in range(4):
        here = slice(r * size, (r + 1) * size)
        branch = mm_tn(att_all[:, here], out_all[...]) + bias_ref[0:1, :]
        residual = tokens[r][:size, :].astype(full_type) + mod_ref[2:3, :] * branch
        if r == 0:
            residual_ref[...] = residual
            branch_ref[...] = branch
        normed, inverse = layer_norm(residual)
        if r % 2 == 0:
            normed_refs[r // 2][...] = normed
            inverse_refs[r // 2][...] = inverse
        low = (normed * (1.0 + scale_m) + shift_m).astype(low_type)
        low_ref[here, :] = low
        hidden = mm(low, weights[:, :width]) + bias_ref[2:3, :]
        active, slope = gelu_both(hidden)
        active = active.astype(low_type)
        act_ref[here, :] = active
        part = mm(active, weights[:, width:])
        part_refs[r][...] = part.astype(low_type)
        grad_y = tokens[r][size:, :].astype(full_type)
        totals[0] += jnp.sum(grad_y * part, 0, keepdims=True)
        if r == 0:
            totals[0] += jnp.sum(grad_y, 0, keepdims=True) * bias_ref[1:2, :]
        grad_low = (gate_m * grad_y).astype(low_type)
        cot_ref[here, :] = grad_low
        grad_hid = (mm_nt(grad_low, weights[:, width:]) * slope).astype(low_type)
        hid_ref[here, :] = grad_hid
        back = mm_nt(grad_hid, weights[:, :width])
        back_refs[r][...] = back.astype(low_type)
        totals[1] += jnp.sum(back * normed, 0, keepdims=True)
        totals[2] += jnp.sum(back, 0, keepdims=True)
        totals[3] += jnp.sum(grad_hid.astype(full_type), 0, keepdims=True)
        totals[4] += jnp.sum(grad_low.astype(full_type), 0, keepdims=True)
    sums_ref[...] = jnp.zeros(sums_ref.shape, full_type)
    sums_ref[3:4, :] = totals[2]
    sums_ref[4:5, :] = totals[1]
    sums_ref[5:6, :] = totals[0]
    sums_ref[pl.ds(9 + own, 1), :] = totals[3]
    sums_ref[13:14, :] = jnp.where(own == 0, totals[4], 0.0)
    grads_ref[:, :width] = mm_tn(low_ref[...], hid_ref[...]).astype(low_type)
    grads_ref[:, width:] = mm_tn(act_ref[...], cot_ref[...]).astype(low_type)
    deal(table_ref, dealt, grads_ref)


def attend_backward_kernel(heads, own_ref, *refs):
    grad = refs[:4]
    att_all, out_own, qkv_ref, log_ref, low_ref = refs[4:9]
    out_ref, grads_ref, sums_ref = refs[9:12]
    all_ref, cols_ref, grad_ref, keys_t, sum_k, sum_v = refs[12:]
    n_tok, width = low_ref.shape
    feats = out_own.shape[0]
    size = n_tok // 4
    dim = feats // heads
    scale = dim ** (-0.5)
    own = own_ref[0]
    for r in range(4):
        here = slice(r * size, (r + 1) * size)
        all_ref[here, :] = grad[r][...]
        grad_ref[here, :] = mm_nt(grad[r][...], out_own[...]).astype(low_type)
    for j in range(4):

        @pl.when(own == j)
        def _():
            cols_ref[...] = all_ref[:, j * feats : (j + 1) * feats]

    grads_ref[:, 3 * feats :] = mm(att_all[...], cols_ref[...]).astype(low_type)
    keys_t[...] = jnp.transpose(qkv_ref[:, feats : 2 * feats])
    sum_k[...] = jnp.zeros(sum_k.shape, full_type)
    sum_v[...] = jnp.zeros(sum_v.shape, full_type)

    def step(block, _):
        here = pl.ds(pl.multiple_of(block * BLOCK, BLOCK), BLOCK)
        for head in range(heads):
            cut = slice(head * dim, (head + 1) * dim)
            queries = (qkv_ref[here, cut] * scale).astype(low_type)
            keys = qkv_ref[:, feats + head * dim : feats + (head + 1) * dim]
            values = qkv_ref[:, 2 * feats + head * dim : 2 * feats + (head + 1) * dim]
            grad_att = grad_ref[here, cut]
            probs = jnp.exp(mm_nt(keys, queries) - log_ref[head : head + 1, here])
            grad_probs = mm_nt(values, grad_att)
            delta = jnp.sum(probs * grad_probs, 0, keepdims=True)
            grad_scores = (probs * (grad_probs - delta)).astype(low_type)
            sum_v[:, cut] += mm(probs.astype(low_type), grad_att)
            sum_k[:, cut] += mm(grad_scores, queries)
            grad_q = mm(keys_t[cut, :], grad_scores) * scale
            out_ref[here, cut] = jnp.transpose(grad_q).astype(low_type)
        return 0

    lax.fori_loop(0, n_tok // BLOCK, step, 0)
    out_ref[:, feats : 2 * feats] = sum_k[...].astype(low_type)
    out_ref[:, 2 * feats :] = sum_v[...].astype(low_type)
    grads_ref[:, : 3 * feats] = mm_tn(low_ref[...], out_ref[...]).astype(low_type)
    sums_ref[...] = jnp.zeros(sums_ref.shape, full_type)
    bias = jnp.sum(out_ref[...].astype(full_type), 0, keepdims=True)
    total = jnp.sum(all_ref[...].astype(full_type), 0, keepdims=True)
    sums_ref[8:9, :] = jnp.where(own == 0, total, 0.0)
    for j in range(4):

        @pl.when(own == j)
        def _():
            sums_ref[6:7, j * feats : (j + 1) * feats] = bias[:, :feats]
            sums_ref[7:8, j * feats : (j + 1) * feats] = bias[:, 2 * feats :]


def project_backward_kernel(*refs):
    tokens = refs[:4]
    grad_ref, weight_ref, gate_ref, sums_mlp, sums_att = refs[4:9]
    back_refs, sums_ref = refs[9:13], refs[13]
    size, width = back_refs[0].shape
    totals = [jnp.zeros((1, width), full_type) for _ in range(2)]
    for r in range(4):
        here = slice(r * size, (r + 1) * size)
        back = mm_nt(grad_ref[here, :], weight_ref[...])
        back_refs[r][...] = back.astype(low_type)
        normed, _ = layer_norm(tokens[r][:size, :].astype(full_type))
        totals[0] += jnp.sum(back, 0, keepdims=True)
        totals[1] += jnp.sum(back * normed, 0, keepdims=True)
    sums_ref[...] = sums_mlp[...] + sums_att[...]
    sums_ref[0:1, :] = totals[0]
    sums_ref[1:2, :] = totals[1]
    sums_ref[2:3, :] = gate_ref[...]


def adam_step(weight, first, second, grad):
    first_new = beta_one * first + (1.0 - beta_one) * grad
    second_new = beta_two * second + (1.0 - beta_two) * grad * grad
    corr_one = 1.0 - beta_one**ADAM_STEP
    corr_two = 1.0 - beta_two**ADAM_STEP
    weight_new = weight - (learn_rate / corr_one) * first_new / (
        jnp.sqrt(second_new * (1.0 / corr_two)) + adam_eps
    )
    return (weight_new, first_new, second_new)


def swap(value, distance):
    return lax.ppermute(value, "seq", [(p, p ^ distance) for p in range(4)])


def gather_rel(value):
    far = swap(value, 2)
    near = swap(value, 1)
    cross = swap(far, 1)
    return [value, near, far, cross]


def scatter_rel(blocks):
    near_own, near_far = [swap(blocks[r], 1).astype(full_type) for r in (1, 3)]
    far_own = swap((blocks[2].astype(full_type) + near_far).astype(low_type), 2)
    return blocks[0].astype(full_type) + near_own + far_own.astype(full_type)


CYCLE = (0, 2, 4, 6, 7, 5, 3, 1)


def ring_pairs(count):
    right = [(CYCLE[i], CYCLE[(i + 1) % count]) for i in range(count)]
    return right, [(to, start) for start, to in right]


def ring_hop(pieces, count):
    if count != len(CYCLE):
        return pieces
    right, left = ring_pairs(count)
    hop = len(pieces) // 2
    ahead, behind = (pieces[-2], pieces[-1]) if hop else (pieces[0], pieces[0])
    more = [lax.ppermute(ahead, "shard", right)]
    if hop < count // 2 - 1:
        more.append(lax.ppermute(behind, "shard", left))
    return pieces + more


def ring_begin(value, count):
    if count != len(CYCLE):
        return [spread(value, "shard", count).reshape(-1, value.shape[-1])]
    return ring_hop([value], count)


def ring_scatter(pieces, count, first):
    if len(pieces) == 1:
        whole = pieces[0].reshape(count, -1, pieces[0].shape[-1])
        arrived = lax.all_to_all(whole, "shard", 0, 0, tiled=True)
        return [jnp.sum(arrived.astype(full_type), 0).astype(low_type)]
    right, left = ring_pairs(count)
    ahead, behind = pieces[count - 1], pieces[count - 3]
    for hop in range(count // 2, 1, -1):
        ahead = after(lax.ppermute(ahead, "shard", right), *first)
        ahead = (ahead.astype(full_type) + pieces[2 * hop - 2].astype(full_type)).astype(low_type)
    for hop in range(count // 2 - 1, 0, -1):
        behind = after(lax.ppermute(behind, "shard", left), *first)
        if hop > 1:
            behind = (behind.astype(full_type) + pieces[2 * hop - 3].astype(full_type)).astype(
                low_type
            )
    return [pieces[0], ahead, behind]


def ring_last(parts, count):
    if len(parts) == 1:
        return []
    return [lax.ppermute(parts[1], "shard", ring_pairs(count)[0])]


def ring_total(parts, last):
    if not last:
        return parts[0]
    return sum(x.astype(full_type) for x in (parts[0], last[0], parts[2])).astype(low_type)


def ring_table(own, count):
    if count != len(CYCLE):
        return jnp.zeros((1,), jnp.int32)
    lines = []
    for s in range(count):
        at = CYCLE.index(s)
        line = [s]
        for hop in range(1, count // 2 + 1):
            line.append(CYCLE[(at - hop) % count])
            if hop < count // 2:
                line.append(CYCLE[(at + hop) % count])
        lines.append(line)
    return lax.dynamic_index_in_dim(jnp.array(lines, jnp.int32), own, 0, keepdims=False)


def permute_blocks(value, distance):
    size = value.shape[1] // 4
    return jnp.concatenate(
        [value[:, (r ^ distance) * size : ((r ^ distance) + 1) * size] for r in range(4)], 1
    )


def spread(value, axis, count):
    return lax.all_to_all(
        jnp.broadcast_to(value[None], (count,) + value.shape), axis, 0, 0, tiled=True
    )


def token_sum(tensor):
    return jnp.sum(tensor.astype(full_type), axis=0)


def shards(
    latents,
    cotangent,
    class_labels,
    time_buckets,
    class_table,
    time_table,
    ada_weight,
    qkv_weight,
    out_weight,
    up_weight,
    down_weight,
    biases,
    ada_first,
    qkv_first,
    out_first,
    up_first,
    down_first,
    bias_first,
    ada_second,
    qkv_second,
    out_second,
    up_second,
    down_second,
    bias_second,
    n_shard,
    n_seq,
):
    assert n_seq == 4 and latents.shape[0] == 1 and class_labels.shape[0] == n_shard
    s_own = lax.axis_index("shard")
    q_own = lax.axis_index("seq")
    tok_dev, width = latents.shape[1:]
    head_dim = width // HEADS
    score_scale = head_dim ** (-0.5)
    heads_own = HEADS // n_seq
    feats = heads_own * head_dim
    rows = ada_weight.shape[0]
    ff = up_weight.shape[1]
    ff_cell = ff // (n_shard * n_seq)
    ff_own = ff // n_seq

    table = jnp.concatenate([ring_table(s_own, n_shard), q_own[None].astype(jnp.int32)])
    own_index = q_own[None].astype(jnp.int32)
    first_part, rest_part = vmem_call(
        cut_kernel,
        "cut",
        (
            jax.ShapeDtypeStruct((rows, 4 * feats), low_type),
            jax.ShapeDtypeStruct((rows, width + ff_own), low_type),
        ),
        [pltpu.VMEM(x.shape, full_type) for x in (qkv_weight, out_weight, up_weight, down_weight)]
        + [pltpu.SemaphoreType.DMA((16,))],
        0,
        0,
        [own_index, qkv_weight, out_weight, up_weight, down_weight],
        far_in=range(1, 5),
    )

    cond = jnp.take(class_table, class_labels, axis=0).astype(full_type) + jnp.take(
        time_table, time_buckets, axis=0
    ).astype(full_type)
    cond_cols = lax.dynamic_slice_in_dim(cond, s_own * rows, rows, 1)
    silu_cols = jax.nn.silu(cond_cols).astype(low_type)
    ada_low = ada_weight.astype(low_type)
    mod_partial = mm(silu_cols, ada_low)
    bias_low = biases.astype(low_type).astype(full_type).reshape(1, -1)
    payload = jnp.concatenate(
        [mod_partial, jnp.broadcast_to(bias_low, (n_shard, bias_low.shape[1]))], 1
    )
    first_pieces, rest_pieces = ring_begin(first_part, n_shard), ring_begin(rest_part, n_shard)
    payload = after(payload, *first_pieces)
    arrived = lax.all_to_all(payload, "shard", split_axis=0, concat_axis=0, tiled=True)
    first_pieces, rest_pieces = lax.optimization_barrier((first_pieces, rest_pieces))
    for _ in range(2):
        first_pieces = ring_hop(first_pieces, n_shard)
    both = jnp.concatenate([latents[0], cotangent[0]])
    far, arrived, first_pieces = lax.optimization_barrier((swap(both, 2), arrived, first_pieces))
    tokens = [both, swap(both, 1), far, swap(far, 1)]
    first_pieces = ring_hop(first_pieces, n_shard)
    first_pieces, rest_pieces = lax.optimization_barrier((first_pieces, rest_pieces))
    n_piece = len(first_pieces)
    mod_sum = jnp.sum(arrived[:, : 6 * width], 0)
    bias_full = jnp.transpose(
        arrived[:, 6 * width :].reshape(n_shard, biases.shape[0], rows), (1, 0, 2)
    ).reshape(biases.shape[0], width)
    modulation = mod_sum.reshape(6, width) + bias_full[0:6]
    shift_a, scale_a, gate_a, shift_m, scale_m, gate_m = [modulation[i] for i in range(6)]

    n_tok = n_seq * tok_dev

    bias_query = lax.dynamic_slice_in_dim(bias_full[6], q_own * feats, feats)
    bias_value = lax.dynamic_slice_in_dim(bias_full[7], q_own * feats, feats)
    bias_qkv = jnp.concatenate([bias_query, jnp.zeros_like(bias_query), bias_value])[None]
    pair_count = heads_own * n_tok * n_tok
    modulated_a, qkv_w, out_q, qkv = vmem_call(
        partial(project_kernel, n_piece),
        "project",
        (
            jax.ShapeDtypeStruct((n_tok, width), low_type),
            jax.ShapeDtypeStruct((width, 3 * feats), low_type),
            jax.ShapeDtypeStruct((width, feats), low_type),
            jax.ShapeDtypeStruct((n_tok, 3 * feats), low_type),
        ),
        [],
        6 * n_tok * width * feats,
        n_tok,
        [table, *tokens, modulation, bias_qkv, *first_pieces],
    )
    out_far = swap(out_q, 2)
    qkv, rest_pieces = lax.optimization_barrier((qkv, ring_hop(rest_pieces, n_shard)))
    rest_pieces = ring_hop(rest_pieces, n_shard)
    att_own, logs = vmem_call(
        partial(attend_forward_kernel, heads_own),
        "attend_forward",
        (
            jax.ShapeDtypeStruct((feats, n_tok), low_type),
            jax.ShapeDtypeStruct((8, n_tok), full_type),
        ),
        [],
        4 * pair_count * head_dim,
        pair_count,
        [qkv],
        0,
    )
    att_own, out_far, rest_pieces = lax.optimization_barrier((att_own, out_far, rest_pieces))
    out_parts = [out_q, swap(out_q, 1), out_far, swap(out_far, 1)]
    rest_pieces = ring_hop(rest_pieces, n_shard)
    att_far = swap(permute_blocks(att_own, 2), 2)
    att_far, rest_pieces = lax.optimization_barrier((att_far, rest_pieces))
    att_near = swap(permute_blocks(att_own, 1), 1)
    att_cross = swap(permute_blocks(att_far, 1), 1)

    bias_ff = lax.dynamic_index_in_dim(
        bias_full[9:13].reshape(n_shard, n_seq, ff_cell), q_own, 1, keepdims=False
    ).reshape(ff_own)
    bias_mlp = jnp.stack([bias_full[8], bias_full[13], bias_ff])
    attended, out_own, residual, branch_a, *mlp_out = (
        vmem_call(
            partial(mlp_kernel, n_piece),
            "mlp",
            (
                jax.ShapeDtypeStruct((width, n_tok), low_type),
                jax.ShapeDtypeStruct((feats, width), low_type),
            )
            + 4 * (jax.ShapeDtypeStruct((tok_dev, width), full_type),)
            + 2 * (jax.ShapeDtypeStruct((tok_dev, 1), full_type),)
            + 8 * (jax.ShapeDtypeStruct((tok_dev, width), low_type),)
            + (jax.ShapeDtypeStruct((16, width), full_type),)
            + n_piece * (jax.ShapeDtypeStruct((width // n_piece, width + ff_own), low_type),),
            [
                pltpu.VMEM((width, width + ff_own), low_type),
                pltpu.VMEM((width, width + ff_own), low_type),
                pltpu.VMEM((width, width), low_type),
            ]
            + [pltpu.VMEM((n_tok, width), low_type)] * 4,
            14 * n_tok * width * width,
            n_tok * width,
            [
                table,
                att_own,
                att_near,
                att_far,
                att_cross,
                *tokens,
                modulation,
                bias_mlp,
                *out_parts,
                *rest_pieces,
            ],
        )
    )
    normed_m, inverse_m = mlp_out[:2], mlp_out[2:4]
    branch_part, back, sums_mlp, grads_mlp = mlp_out[4:8], mlp_out[8:12], mlp_out[12], mlp_out[13:]
    near_zero, near_two = swap(back[1], 1), swap(back[3], 1)
    chip = [
        (mine.astype(full_type) + theirs.astype(full_type)).astype(low_type)
        for mine, theirs in ((back[0], near_zero), (back[2], near_two))
    ]
    across = [swap(chip[1], 2), swap(chip[0], 2)]
    mlp_parts = ring_scatter(grads_mlp, n_shard, chip)
    grad_residuals = [
        tokens[2 * i][tok_dev:].astype(full_type)
        + norm_back(
            (chip[i].astype(full_type) + across[i].astype(full_type)) * (1.0 + scale_m),
            normed_m[i],
            inverse_m[i],
        )
        for i in range(2)
    ]
    grad_residual = grad_residuals[0]
    grad_low = [(gate_a * part).astype(low_type) for part in grad_residuals]
    grad_low, mlp_parts = lax.optimization_barrier((grad_low, mlp_parts))
    grad_branch_a = [grad_low[0], swap(grad_low[0], 1), grad_low[1], swap(grad_low[1], 1)]
    branch_part = [after(x, *chip) for x in branch_part]
    branch_near = swap(branch_part[1], 1)
    branch_chip = branch_part[2].astype(full_type) + swap(branch_part[3], 1).astype(full_type)
    mlp_parts, branch_chip, branch_near, grad_branch_a = lax.optimization_barrier(
        (mlp_parts, branch_chip.astype(low_type), branch_near, grad_branch_a)
    )
    mlp_last, branch_far = ring_last(mlp_parts, n_shard), swap(branch_chip, 2)
    grad_gate_a = token_sum(grad_residual * branch_a)
    grad_qkv, grads_att, sums_att = vmem_call(
        partial(attend_backward_kernel, heads_own),
        "attend_backward",
        (
            jax.ShapeDtypeStruct((n_tok, 3 * feats), low_type),
            jax.ShapeDtypeStruct((width, 4 * feats), low_type),
            jax.ShapeDtypeStruct((16, width), full_type),
        ),
        [
            pltpu.VMEM((n_tok, width), low_type),
            pltpu.VMEM((n_tok, feats), low_type),
            pltpu.VMEM((n_tok, feats), low_type),
            pltpu.VMEM((feats, n_tok), low_type),
            pltpu.VMEM((n_tok, feats), full_type),
            pltpu.VMEM((n_tok, feats), full_type),
        ],
        10 * n_tok * width * feats + 10 * pair_count * head_dim,
        pair_count,
        [own_index, *grad_branch_a, attended, out_own, qkv, logs, modulated_a],
    )
    grads_att, mlp_last, branch_far = lax.optimization_barrier((grads_att, mlp_last, branch_far))
    mlp_total = ring_total(mlp_parts, mlp_last)
    mlp_near, mlp_far = swap(mlp_total, 1), swap(mlp_total, 2)
    *grad_mod_a_part, small = vmem_call(
        project_backward_kernel,
        "project_backward",
        4 * (jax.ShapeDtypeStruct((tok_dev, width), low_type),)
        + (jax.ShapeDtypeStruct((16, width), full_type),),
        [],
        6 * n_tok * width * feats,
        n_tok,
        [*tokens, grad_qkv, qkv_w, grad_gate_a[None], sums_mlp, sums_att],
        0,
    )
    small = small + swap(small, 1)
    small = small + swap(small, 2)
    arrived_att = lax.all_to_all(
        grads_att.reshape(n_shard, rows, 4 * feats), "shard", 0, 0, tiled=True
    )
    normed_a, inverse_a = layer_norm(latents[0].astype(full_type))
    latents_grad = grad_residual + norm_back(
        scatter_rel([after(x, arrived_att) for x in grad_mod_a_part]) * (1.0 + scale_a),
        normed_a,
        inverse_a,
    )
    branch_own = sum(x.astype(full_type) for x in (after(branch_part[0], arrived_att), branch_near, branch_far))
    branch_own = branch_own + bias_full[13]
    block_out = (residual + gate_m * branch_own).astype(low_type)

    mlp_up, mlp_down = adam_call(
        place_mlp,
        "adam_mlp",
        own_index,
        [mlp_total, mlp_near, mlp_far, swap(mlp_far, 1)],
        [up_weight, down_weight, up_first, down_first, up_second, down_second],
    )
    every = spread(after(small, arrived_att, mlp_up[0]), "shard", n_shard)
    ada_state = (ada_weight, ada_first, ada_second)
    bias_state = (biases, bias_first, bias_second)
    tables = tuple(jax.ShapeDtypeStruct((rows, t.shape[0]), full_type) for t in (class_table, time_table))
    done = vmem_call(
        partial(finish_kernel, n_shard),
        "finish",
        tuple(jax.ShapeDtypeStruct(x.shape, full_type) for x in ada_state + bias_state) + tables,
        [
            pltpu.VMEM((16, width), full_type),
            pltpu.VMEM(biases.shape, full_type),
        ]
        + [pltpu.VMEM(ada_weight.shape, full_type)] * 3
        + [pltpu.SemaphoreType.DMA((2, 18))],
        24 * ada_weight.size,
        ada_weight.size,
        [
            s_own[None].astype(jnp.int32),
            every,
            silu_cols,
            cond_cols,
            class_labels[:, None],
            time_buckets[:, None],
            *ada_state,
            *bias_state,
        ],
        far_in=range(6, 9),
        far_out=range(3),
    )
    ada_new, bias_new = done[:3], done[3:6]
    class_grad, time_grad = jnp.transpose(done[6]), jnp.transpose(done[7])

    att_total = jnp.sum(arrived_att.astype(full_type), 0).astype(low_type)
    att_near, att_far = swap(att_total, 1), swap(att_total, 2)
    att_qkv, att_out = adam_call(
        place_att,
        "adam_att",
        own_index,
        [att_total, att_near, att_far, swap(att_far, 1)],
        [qkv_weight, out_weight, qkv_first, out_first, qkv_second, out_second],
    )

    updates = [
        ada_new,
        att_qkv,
        att_out,
        mlp_up,
        mlp_down,
        bias_new,
    ]
    return (
        block_out[None],
        latents_grad[None],
        class_grad,
        time_grad,
        *[update[0] for update in updates],
        *[update[1] for update in updates],
        *[update[2] for update in updates],
    )


def solution(mesh):
    tokens = P("shard", "seq", None)
    rows = P("shard", None)
    cols = P(None, "shard")
    state = (rows, rows, rows, rows, rows, cols)
    return jax.shard_map(
        partial(shards, n_shard=mesh.shape["shard"], n_seq=mesh.shape["seq"]),
        mesh=mesh,
        in_specs=(tokens, tokens, P(), P(), P(), P()) + 3 * state,
        out_specs=(tokens, tokens, cols, cols) + 3 * state,
        check_vma=False,
    )
```
